32 devices in a mesh: views: 8 (over z, x), chan: 4 (over y, core).
Axes of the slice: x: 2, y: 2, z: 4, core: 2. Of those that a mesh axis runs over, the one named last changes fastest.
Arguments:
- block_input: bfloat16 [25088, 2048], P('views', 'chan'), may hold values from -6 to 6
- conv_first: bfloat16 [2048, 512], P(None, 'chan'), may hold values from -0.125 to 0.125
- conv_mid: bfloat16 [4608, 512], P(None, 'chan'), may hold values from -0.09375 to 0.09375
- conv_last: bfloat16 [2048, 512], P(None, 'chan'), may hold values from -0.25 to 0.25
- gain_first: float32 [512], P('chan'), may hold values from 0.25 to 1.75
- shift_first: float32 [512], P('chan'), may hold values from -3 to 3
- gain_mid: float32 [512], P('chan'), may hold values from 0.25 to 1.75
- shift_mid: float32 [512], P('chan'), may hold values from -3 to 3
- gain_last: float32 [2048], P('chan'), may hold values from 0.25 to 1.75
- shift_last: float32 [2048], P('chan'), may hold values from -3 to 3
- head_first: bfloat16 [2048, 1024], P('chan'), may hold values from -0.125 to 0.125
- gain_head: float32 [1024], replicated, may hold values from 0.25 to 1.75
- shift_head: float32 [1024], replicated, may hold values from -3 to 3
- head_last: bfloat16 [1024, 128], replicated, may hold values from -0.1875 to 0.1875
- image_of: int32 [512], replicated, may hold values from 0 to 127, as said below
- partner: int32 [512], replicated, may hold values from 0 to 511, as said below
- sub_of: int32 [512], replicated, may hold values from 0 to 1, as said below
Outputs:
- loss: float32 [], replicated
- grad_input: float32 [25088, 2048], P('views', 'chan')
- grad_conv_first: float32 [2048, 512], P('views', 'chan')
- grad_conv_mid: float32 [4608, 512], P('views', 'chan')
- grad_conv_last: float32 [2048, 512], P('views', 'chan')
- grad_head_first: float32 [2048, 1024], P('chan', 'views')
- grad_head_last: float32 [1024, 128], P('views')
- grad_gain_first: float32 [512], P('chan')
- grad_shift_first: float32 [512], P('chan')
- grad_gain_mid: float32 [512], P('chan')
- grad_shift_mid: float32 [512], P('chan')
- grad_gain_last: float32 [2048], P('chan')
- grad_shift_last: float32 [2048], P('chan')
- grad_gain_head: float32 [1024], replicated
- grad_shift_head: float32 [1024], replicated
The draws below stay inside these ranges and needn't reach their ends.
Inputs may be any that keep to these rules, and one draw needn't show every extreme that they name: `image_of`: every image holds 2 to 6 views; both counts occur. A permutation of the views; each view's partner is another view of the same image. `sub_of`: every sub-batch holds exactly 256 views, one in each aligned block of 2 views.
All inputs are finite; a program needn't handle non-finite values.
Results may differ from the reference program's by a relative error of at most 0.03.
Values may be sent and summed in bfloat16 or wider, within the bound.
A program may use at most 256 MiB of HBM per device.

```python
import jax
import jax.numpy as jnp
from jax import lax

C_IN = 2048
C_MID = 512
HID = 1024
EMB = 128
SIDE = 7
SUB = 256
VIEWS = 512
PIXELS = 25088


def image_pairs(key):
    blocks = VIEWS // 8
    split_key, offset_key, order_key = jax.random.split(key, 3)
    first_size = jax.random.randint(split_key, (blocks,), 2, 7)
    first_size = first_size.at[0].set(2).at[1].set(6)
    position = jnp.arange(8, dtype=jnp.int32)[None, :]
    in_first = position < first_size[:, None]
    extent = jnp.where(in_first, first_size[:, None], 8 - first_size[:, None])
    anchor = jnp.where(in_first, 0, first_size[:, None])
    offsets = jax.random.randint(offset_key, (blocks, 2), 0, 1 << 20)
    offset = jnp.where(in_first, offsets[:, 0:1], offsets[:, 1:2]) % (extent - 1) + 1
    block_base = jnp.arange(blocks, dtype=jnp.int32)[:, None] * 8
    target = anchor + (position - anchor + offset) % extent + block_base
    labels = jnp.arange(blocks, dtype=jnp.int32)[:, None] * 2 + jnp.where(in_first, 0, 1)
    shuffle = jax.random.permutation(order_key, VIEWS).astype(jnp.int32)
    image_of = jnp.zeros((VIEWS,), jnp.int32).at[shuffle].set(labels.reshape(-1).astype(jnp.int32))
    partner = jnp.zeros((VIEWS,), jnp.int32).at[shuffle].set(shuffle[target.reshape(-1)])
    return (image_of, partner)


def draw_image_of(key, part):
    return image_pairs(key)[0]


def draw_partner(key, part):
    return image_pairs(key)[1]


def draw_sub_of(key, part):
    key = jax.random.fold_in(key, 7)
    sub_count = VIEWS // SUB
    block_keys = jax.random.split(key, SUB)
    rows = jax.vmap(lambda one_key: jax.random.permutation(one_key, sub_count))(block_keys)
    return rows.reshape(-1).astype(jnp.int32)


def block_scale(key, dims, shards, smallest, high):
    gain, own = 1.0, jax.random.fold_in(key, 6)
    for dim, shards_of in shards:
        draws = jnp.exp(jax.random.uniform(jax.random.fold_in(own, dim), (shards_of,), jnp.float32, smallest / len(shards), high / len(shards)))
        gain = gain * jnp.repeat(draws, dims[dim] // shards_of).reshape([-1 if axis == dim else 1 for axis in range(len(dims))])
    return gain


def normal_values(own_key, dims, width, bound, pieces=(), kind=jnp.bfloat16):
    entries = width * jax.random.normal(own_key, dims, jnp.float32)
    if pieces:
        entries = entries * block_scale(own_key, dims, pieces, -0.22, 0.18)
    return jnp.clip(entries, -bound, bound).astype(kind)


def setup_inputs(seed: int = 0) -> dict:
    arg_keys = jax.random.split(jax.random.key(seed), 18)
    return {
        "block_input": normal_values(arg_keys[0], (PIXELS, C_IN), 1.0, 6.0, ((0, 8), (1, 4))),
        "conv_first": normal_values(arg_keys[1], (C_IN, C_MID), C_IN ** -0.5, 0.125, ((1, 4),)),
        "conv_mid": normal_values(arg_keys[2], (9 * C_MID, C_MID), (9 * C_MID) ** -0.5, 0.09375, ((1, 4),)),
        "conv_last": normal_values(arg_keys[3], (C_IN, C_MID), C_MID ** -0.5, 0.25, ((1, 4),)),
        "gain_first": jnp.clip(1.0 + 0.15 * jax.random.normal(arg_keys[4], (C_MID,), jnp.float32), 0.25, 1.75),
        "shift_first": normal_values(arg_keys[5], (C_MID,), 0.5, 3.0, ((0, 4),), jnp.float32),
        "gain_mid": jnp.clip(1.0 + 0.15 * jax.random.normal(arg_keys[6], (C_MID,), jnp.float32), 0.25, 1.75),
        "shift_mid": normal_values(arg_keys[7], (C_MID,), 0.5, 3.0, ((0, 4),), jnp.float32),
        "gain_last": jnp.clip(1.0 + 0.15 * jax.random.normal(arg_keys[8], (C_IN,), jnp.float32), 0.25, 1.75),
        "shift_last": normal_values(arg_keys[9], (C_IN,), 0.5, 3.0, ((0, 4),), jnp.float32),
        "head_first": normal_values(arg_keys[10], (C_IN, HID), C_IN ** -0.5, 0.125, ((0, 4),)),
        "gain_head": jnp.clip(1.0 + 0.15 * jax.random.normal(arg_keys[11], (HID,), jnp.float32), 0.25, 1.75),
        "shift_head": normal_values(arg_keys[12], (HID,), 0.5, 3.0, (), jnp.float32),
        "head_last": normal_values(arg_keys[13], (HID, EMB), HID ** -0.5, 0.1875),
        "image_of": draw_image_of(jax.random.fold_in(arg_keys[17], 71), 0),
        "partner": draw_partner(jax.random.fold_in(arg_keys[17], 71), 0),
        "sub_of": draw_sub_of(jax.random.fold_in(arg_keys[17], 71), 0),
    }


norm_eps = 1e-05
ridge_value = 0.5
highest = lax.Precision.HIGHEST

@jax.custom_vjp
def low(v):
    return lax.optimization_barrier(v.astype(jnp.bfloat16)).astype(jnp.float32)

@jax.custom_vjp
def low_back(v):
    return v

def low_keep(v):
    return (low(v), None)

def low_pass(kept, grad):
    return (grad,)

def back_keep(v):
    return (v, None)

def back_low(kept, grad):
    return (low(grad),)
low.defvjp(low_keep, low_pass)
low_back.defvjp(back_keep, back_low)

def product(left, right):
    return jnp.dot(left, right, precision=highest)

def batch_norm(hidden, norm_gain, norm_shift):
    row_total = hidden.shape[0]
    average = lax.optimization_barrier(jnp.sum(hidden, axis=0)) / row_total
    squares = lax.optimization_barrier(jnp.sum(hidden * hidden, axis=0)) / row_total
    inverse_std = lax.rsqrt(squares - average * average + norm_eps)
    return (hidden - average) * inverse_std * norm_gain + norm_shift

def conv_three(activation, weight):
    view_count = activation.shape[0] // (SIDE * SIDE)
    channels = activation.shape[1]
    padded = jnp.pad(activation.reshape(view_count, SIDE, SIDE, channels), ((0, 0), (1, 1), (1, 1), (0, 0)))
    summed = jnp.zeros((activation.shape[0], weight.shape[1]), activation.dtype)
    for kernel_tap in range(9):
        tap_row, tap_col = (kernel_tap // 3, kernel_tap % 3)
        window = padded[:, tap_row:tap_row + SIDE, tap_col:tap_col + SIDE, :].reshape(-1, channels)
        summed = summed + product(window, weight[kernel_tap * channels:(kernel_tap + 1) * channels])
    return summed

def moments(embed, sub_mask):
    first_sum = lax.dot_general(sub_mask, embed, (((0,), (0,)), ((), ())), precision=highest)
    stacked = (sub_mask[:, :, None] * embed[:, None, :]).reshape(embed.shape[0], -1)
    second_sum = lax.dot_general(stacked, embed, (((0,), (0,)), ((), ())), precision=highest)
    return (first_sum, second_sum.reshape(sub_mask.shape[1], embed.shape[1], embed.shape[1]))

def white_local(embed, sub_mask, first_sum, second_sum):
    average = first_sum / SUB
    identity = jnp.eye(embed.shape[1], dtype=embed.dtype)
    covariance = second_sum / SUB - average[:, :, None] * average[:, None, :] + ridge_value * identity
    factor = jnp.linalg.cholesky(covariance)
    inverse = lax.linalg.triangular_solve(factor, jnp.broadcast_to(identity, covariance.shape), left_side=True, lower=True)
    centered = embed - jnp.dot(sub_mask, average, precision=highest)
    per_sub = jnp.einsum('sij,vj->vsi', inverse, centered, precision=highest)
    whitened = jnp.einsum('vs,vsi->vi', sub_mask, per_sub, precision=highest)
    return whitened / jnp.sqrt(lax.optimization_barrier(jnp.sum(whitened * whitened, axis=1, keepdims=True)) + norm_eps)

def view_weights(image_of, view_count):
    members = jax.ops.segment_sum(jnp.ones_like(image_of), image_of, num_segments=view_count)
    return 1.0 / members[image_of].astype(jnp.float32)

def pair_loss(unit_rows, partner, pair_weight):
    difference = unit_rows - unit_rows[partner]
    return jnp.sum(lax.optimization_barrier(jnp.sum(difference * difference, axis=1)) * pair_weight) * (2.0 / unit_rows.shape[0])

def forward(block_input, conv_first, conv_mid, conv_last, gain_first, shift_first, gain_mid, shift_mid, gain_last, shift_last, head_first, gain_head, shift_head, head_last, sub_mask, partner, pair_weight):
    hidden_one = low_back(product(block_input, conv_first))
    act_one = low(jax.nn.silu(batch_norm(hidden_one, gain_first, shift_first)))
    hidden_two = low_back(conv_three(act_one, conv_mid))
    act_two = low(jax.nn.silu(batch_norm(hidden_two, gain_mid, shift_mid)))
    hidden_three = low_back(product(act_two, conv_last.T))
    after = jax.nn.silu(block_input + batch_norm(hidden_three, gain_last, shift_last))
    pooled = lax.optimization_barrier(jnp.mean(after.reshape(VIEWS, SIDE * SIDE, C_IN), axis=1))
    head_hidden = product(pooled, head_first)
    act_four = jax.nn.silu(batch_norm(head_hidden, gain_head, shift_head))
    embed = product(act_four, head_last)
    first_sum, second_sum = moments(embed, sub_mask)
    unit_rows = white_local(embed, sub_mask, first_sum, second_sum)
    return pair_loss(unit_rows, partner, pair_weight)

def reference(block_input, conv_first, conv_mid, conv_last, gain_first, shift_first, gain_mid, shift_mid, gain_last, shift_last, head_first, gain_head, shift_head, head_last, image_of, partner, sub_of):
    sub_mask = (sub_of[:, None] == jnp.arange(VIEWS // SUB, dtype=jnp.int32)[None, :]).astype(jnp.float32)
    pair_weight = view_weights(image_of, VIEWS)
    primals = tuple((initial.astype(jnp.float32) for initial in (block_input, conv_first, conv_mid, conv_last, gain_first, shift_first, gain_mid, shift_mid, gain_last, shift_last, head_first, gain_head, shift_head, head_last)))

    def objective(*params):
        return forward(*params, sub_mask, partner, pair_weight)
    value, backward = jax.vjp(objective, *primals)
    grads = backward(jnp.ones_like(value))
    return (value, grads[0], grads[1], grads[2], grads[3], grads[10], grads[13], grads[4], grads[5], grads[6], grads[7], grads[8], grads[9], grads[11], grads[12])
```

```python
import functools

import jax
import jax.numpy as jnp
from jax import lax
from jax.experimental import pallas as pl
from jax.experimental.pallas import tpu as pltpu
from jax.sharding import PartitionSpec as P

SIDE = 7
PIX = SIDE * SIDE
PAD = SIDE + 2
SUB = 256
EPS = 1e-05
RIDGE = 0.5
MESH = pl.DeviceIdType.MESH
BF16 = jnp.bfloat16
F32 = jnp.float32
VMEM_BYTES = 60 << 20


def place():
    view_at, chan_at = lax.axis_index("views"), lax.axis_index("chan")
    return view_at, chan_at, lax.div(chan_at, 2), lax.rem(chan_at, 2)


def greet(peers, groups=()):
    barrier = pltpu.get_barrier_semaphore()
    total = len(peers)
    for peer in peers:
        pl.semaphore_signal(barrier, inc=1, device_id=peer, device_id_type=MESH)
    for size, own, device in groups:

        def tell(step, carry, size=size, own=own, device=device):
            pl.semaphore_signal(
                barrier, inc=1, device_id=device(lax.rem(own + step, size)), device_id_type=MESH
            )
            return carry

        lax.fori_loop(1, size, tell, 0)
        total += size - 1
    return lambda: pl.semaphore_wait(barrier, total)


class Mail:
    def __init__(self, send_sems, recv_sems):
        self.send_sems, self.recv_sems, self.copies = send_sems, recv_sems, []

    def send(self, source, target, peer):
        spot = len(self.copies)
        copy = pltpu.make_async_remote_copy(
            src_ref=source,
            dst_ref=target,
            send_sem=self.send_sems.at[spot],
            recv_sem=self.recv_sems.at[spot],
            device_id=peer,
            device_id_type=MESH,
        )
        copy.start()
        self.copies.append(copy)
        return copy

    def finish(self):
        for copy in self.copies:
            copy.wait_send()


def group_copy(source, slots, sends, recvs, size, own, device, step):
    to = lax.rem(own + step, size)
    return pltpu.make_async_remote_copy(
        src_ref=source,
        dst_ref=slots.at[own],
        send_sem=sends.at[step],
        recv_sem=recvs.at[own],
        device_id=device(to),
        device_id_type=MESH,
    )


def group_arrival(source, slots, sends, recvs, size, own, device, step):
    origin = lax.rem(own + step, size)
    return pltpu.make_async_remote_copy(
        src_ref=source,
        dst_ref=slots.at[origin],
        send_sem=sends.at[step],
        recv_sem=recvs.at[origin],
        device_id=device(origin),
        device_id_type=MESH,
    )


def share_start(source, slots, sends, recvs, group):
    def start(step, carry):
        group_copy(source, slots, sends, recvs, *group, step).start()
        return carry

    lax.fori_loop(1, group[0], start, 0)
    slots[group[1]] = source[...]


def share_end(source, slots, sends, recvs, group):
    def end(step, carry):
        group_arrival(source, slots, sends, recvs, *group, step).wait_recv()
        group_copy(source, slots, sends, recvs, *group, step).wait_send()
        return carry

    lax.fori_loop(1, group[0], end, 0)


def add_slots(slots, size):
    def add(at, total):
        return total + slots[at]

    return lax.fori_loop(1, size, add, slots[0])


def share(source, slots, sends, recvs, group):
    share_start(source, slots, sends, recvs, group)
    share_end(source, slots, sends, recvs, group)
    return add_slots(slots, group[0])


def gather_start(slots, sends, recvs, group):
    source = slots.at[group[1]]

    def start(step, carry):
        group_copy(source, slots, sends, recvs, *group, step).start()
        return carry

    lax.fori_loop(1, group[0], start, 0)


def gather_end(slots, sends, recvs, group):
    share_end(slots.at[group[1]], slots, sends, recvs, group)


def scatter_start(parts, slots, sends, recvs, group):
    size, own, device = group

    def start(step, carry):
        to = lax.rem(own + step, size)
        group_copy(parts.at[to], slots, sends, recvs, *group, step).start()
        return carry

    lax.fori_loop(1, size, start, 0)
    slots[own] = parts[own]


def scatter_end(parts, slots, sends, recvs, group):
    share_end(parts.at[group[1]], slots, sends, recvs, group)


def chan_group():
    view_at, chan_at, y, c = place()
    return (4, chan_at, lambda at: (view_at, at))


def half_group(views):
    view_at, chan_at, y, c = place()
    return (
        2 * views,
        2 * view_at + c,
        lambda at: (lax.div(at, 2), 2 * y + lax.rem(at, 2)),
    )


def view_group(views):
    view_at, chan_at, y, c = place()
    return (views, view_at, lambda at: (at, chan_at))


def all_group(views):
    view_at, chan_at, y, c = place()
    return (4 * views, 4 * view_at + chan_at, lambda at: (lax.div(at, 4), lax.rem(at, 4)))


def dot(left, right):
    return jnp.dot(left, right, preferred_element_type=F32)


def dot_nt(left, right):
    return lax.dot_general(left, right, (((1,), (1,)), ((), ())), preferred_element_type=F32)


def dot_tn(left, right):
    return lax.dot_general(left, right, (((0,), (0,)), ((), ())), preferred_element_type=F32)


def gate(level):
    return 0.5 + 0.5 * jnp.tanh(0.5 * level)


def silu_slope(level):
    open_part = gate(level)
    return open_part * (1.0 + level * (1.0 - open_part))


def call(body, name, outs, ins, scratch, collective=None, flops=0, aliases=None, any_ins=()):
    return pl.pallas_call(
        body,
        out_shape=outs,
        in_specs=[
            pl.BlockSpec(memory_space=pl.ANY if at in any_ins else pltpu.VMEM) for at in range(ins)
        ],
        out_specs=jax.tree.map(lambda _: pl.BlockSpec(memory_space=pltpu.VMEM), outs),
        scratch_shapes=scratch,
        name=name,
        compiler_params=pltpu.CompilerParams(
            collective_id=collective,
            has_side_effects=collective is not None,
            vmem_limit_bytes=VMEM_BYTES,
        ),
    )


def shape(*dims, kind=F32):
    return jax.ShapeDtypeStruct(dims, kind)


def dma(*dims):
    return pltpu.SemaphoreType.DMA(dims)


def first_body(
    views, x, w1in, w2in, w3in, small, perm,
    pad, h1q, stat, w2, w3, w1_own, smalls,
    xm, xp, w1, out_part, in_part, h1, st, slots,
    sends, recvs, part_sends, part_recvs, group_sends, group_recvs, local_sems,
):
    view_at, chan_at, y, c = place()
    mate, opposite = (view_at, 2 * y + 1 - c), (view_at, 2 * (1 - y) + c)
    diagonal = (view_at, 2 * (1 - y) + 1 - c)
    group = half_group(views)
    quarter = x.shape[1]
    depth = x.shape[2]
    near, far = 2 * y + c, 2 * (1 - y) + c
    met = greet([opposite, diagonal], [group])
    locals_ = []
    for at, (source, target) in enumerate(
        [
            (w1in.at[pl.ds(2 * depth * y, 2 * depth)], w1.at[near]),
            (w3in.at[pl.ds(2 * depth * y, 2 * depth)], w3.at[near]),
            (w2in, w2.at[c]),
        ]
    ):
        copy = pltpu.make_async_copy(source, target, local_sems.at[at])
        copy.start()
        locals_.append(copy)
    met()
    mail = Mail(sends, recvs)
    w1_far = mail.send(w1in.at[pl.ds(2 * depth * (1 - y), 2 * depth)], w1.at[near], opposite)
    w1_mate = mail.send(w1in.at[pl.ds(2 * depth * y, 2 * depth)], w1.at[near], mate)
    x_mate = [mail.send(x.at[2 * q + 1 - c], xm.at[q], mate) for q in range(2)]
    small_copies = [mail.send(small, smalls.at[chan_at], to) for to in (mate, opposite, diagonal)]
    smalls[chan_at] = small[...]
    w2_mate = mail.send(w2in, w2.at[c], mate)
    w3_mate = mail.send(w3in.at[pl.ds(2 * depth * y, 2 * depth)], w3.at[near], mate)
    pad[...] = jnp.zeros(pad.shape, pad.dtype)
    for q in range(2):
        xp[q, c] = dot(perm[...], x[2 * q + c]).astype(BF16)
    for q in range(2):
        x_mate[q].wait_recv()
        xp[q, 1 - c] = dot(perm[...], xm[q]).astype(BF16)
    locals_[0].wait()
    w1_mate.wait_recv()

    def part_copy(half, q):
        return pltpu.make_async_remote_copy(
            src_ref=out_part.at[half, q],
            dst_ref=in_part.at[half, q],
            send_sem=part_sends.at[half, q],
            recv_sem=part_recvs.at[half, q],
            device_id=opposite,
            device_id_type=MESH,
        )

    def parts(half):
        def one(q, carry):
            both = jnp.concatenate([w1[2 * half], w1[2 * half + 1]], axis=1)
            out_part[half, q] = (
                dot(xp[q, 0], both[:depth]) + dot(xp[q, 1], both[depth:])
            ).astype(BF16)
            part_copy(half, q).start()
            return carry

        lax.fori_loop(0, 2, one, 0)

    parts(y)
    w1_far.wait_recv()
    w1_on = mail.send(w1.at[far], w1.at[far], mate)
    w1_on.wait_recv()
    parts(1 - y)
    st[...] = jnp.zeros(st.shape, st.dtype)
    step_rows = quarter // SIDE

    def sums(half):
        def one(q, carry):
            part_copy(half, q).wait_recv()

            def rows_of(at, inner):
                rows = pl.ds(at * step_rows, step_rows)
                value = out_part[half, q, rows].astype(F32) + in_part[half, q, rows].astype(F32)
                h1[half, q, rows] = value
                st[half, 0:1] += jnp.sum(value, axis=0, keepdims=True)
                st[half, 1:2] += jnp.sum(value * value, axis=0, keepdims=True)
                return inner

            return lax.fori_loop(0, SIDE, rows_of, carry)

        lax.fori_loop(0, 2, one, 0)

    sums(1 - y)
    sums(y)
    w3_far = mail.send(w3in.at[pl.ds(2 * depth * (1 - y), 2 * depth)], w3.at[near], opposite)
    totals = share(st, slots, group_sends, group_recvs, group)
    count = float(views * 4 * quarter)
    for copy in small_copies:
        copy.wait_recv()
    mean = totals[:, 0:1] / count
    rstd = lax.rsqrt(totals[:, 1:2] / count - mean * mean + EPS)
    stat[...] = jnp.concatenate([mean, rstd], axis=1)
    for half in range(2):
        gains = jnp.concatenate([smalls[2 * half], smalls[2 * half + 1]], axis=1)
        scale = rstd[half] * gains[0:1]
        bias = gains[1:2] - mean[half] * scale

        def act_rows(at, carry, half=half, scale=scale, bias=bias):
            q, i = lax.div(at, SIDE), lax.rem(at, SIDE)
            level = h1[half, q, pl.ds(i * step_rows, step_rows)] * scale + bias
            value = (level * gate(level)).astype(BF16)
            pad[q, i + 1, 1 : SIDE + 1, :, 256 * half : 256 * half + 256] = value.reshape(
                SIDE, step_rows // SIDE, 256
            )
            return carry

        lax.fori_loop(0, 2 * SIDE, act_rows, 0)
    h1q[...] = h1[:, y]
    own_rows = pl.ds(pl.multiple_of(depth * c, depth), depth)
    w1_own[...] = jnp.concatenate([w1[k, own_rows] for k in range(4)], axis=1)
    w3_far.wait_recv()
    w3_on = mail.send(w3.at[far], w3.at[far], mate)
    w3_on.wait_recv()
    w2_mate.wait_recv()
    w3_mate.wait_recv()
    locals_[1].wait()
    locals_[2].wait()
    mail.finish()
    for half in range(2):
        for q in range(2):
            part_copy(half, q).wait_send()


def first_stage(views, x, conv_first, conv_mid, conv_last, small, perm):
    quarter, depth = x.shape[0] // 4, x.shape[1]
    mid = conv_mid.shape[1] * 4
    block = quarter // PIX
    group = 2 * views
    return call(
        functools.partial(first_body, views),
        "first_conv",
        (
            shape(2, PAD, PAD, block, mid, kind=BF16),
            shape(2, quarter, mid // 2),
            shape(2, 2, mid // 2),
            shape(2, *conv_mid.shape, kind=BF16),
            shape(4, 2 * depth, mid // 4, kind=BF16),
            shape(depth, mid, kind=BF16),
            shape(4, *small.shape),
        ),
        6,
        [
            pltpu.VMEM((2, quarter, depth), BF16),
            pltpu.VMEM((2, 2, quarter, depth), BF16),
            pltpu.VMEM((4, 2 * depth, mid // 4), BF16),
            pltpu.VMEM((2, 2, quarter, mid // 2), BF16),
            pltpu.VMEM((2, 2, quarter, mid // 2), BF16),
            pltpu.VMEM((2, 2, quarter, mid // 2), F32),
            pltpu.VMEM((2, 2, mid // 2), F32),
            pltpu.VMEM((group, 2, 2, mid // 2), F32),
            dma(12),
            dma(12),
            dma(2, 2),
            dma(2, 2),
            dma(group),
            dma(group),
            dma(3),
        ],
        collective=1,
    )(x.reshape(4, quarter, depth), conv_first, conv_mid, conv_last, small, perm)


def mid_body(
    views, pad, w2, unperm, smalls,
    act, h2, stat,
    hidden, st, slots,
    sends, recvs, group_sends, group_recvs,
):
    view_at, chan_at, y, c = place()
    mate, opposite = (view_at, 2 * y + 1 - c), (view_at, 2 * (1 - y) + c)
    group = half_group(views)
    quarter, width = hidden.shape[1], hidden.shape[2]
    channels = pad.shape[4]
    met = greet([opposite], [group])
    st[...] = jnp.zeros(st.shape, st.dtype)

    def convolve(q, carry):
        total = None
        for tap in range(9):
            a, b = tap // 3, tap % 3
            window = pad[q, a : a + SIDE, b : b + SIDE].reshape(quarter, channels)
            weight = jnp.concatenate(
                [w2[0, tap * channels : (tap + 1) * channels], w2[1, tap * channels : (tap + 1) * channels]],
                axis=1,
            )
            term = dot(window, weight)
            if total is None:
                hidden[q] = term
            else:
                hidden[q] += term
            total = tap
        value = hidden[q]
        h2[q] = value.astype(BF16)
        st[0:1] += jnp.sum(value, axis=0, keepdims=True)
        st[1:2] += jnp.sum(value * value, axis=0, keepdims=True)
        return carry

    lax.fori_loop(0, 2, convolve, 0)
    met()
    totals = share(st, slots, group_sends, group_recvs, group)
    count = float(views * 4 * quarter)
    mean = totals[0:1] / count
    rstd = lax.rsqrt(totals[1:2] / count - mean * mean + EPS)
    stat[...] = jnp.concatenate([mean, rstd], axis=0)
    gains = jnp.concatenate([smalls[2 * y], smalls[2 * y + 1]], axis=1)
    scale = rstd * gains[2:3]
    bias = gains[3:4] - mean * scale
    mail = Mail(sends, recvs)
    across, beside = [], []
    for q in range(2):
        level = hidden[q] * scale + bias
        value = (level * gate(level)).astype(BF16)
        spot = act.at[y, 2 * q + c]
        act[y, 2 * q + c] = dot(unperm[...], value).astype(BF16)
        across.append(mail.send(spot, spot, opposite))
        beside.append(mail.send(spot, spot, mate))
    for q in range(2):
        across[q].wait_recv()
        spot = act.at[1 - y, 2 * q + c]
        beside.append(mail.send(spot, spot, mate))
    for copy in beside:
        copy.wait_recv()
    mail.finish()


def mid_stage(views, pad, w2, unperm, smalls):
    quarter = unperm.shape[0]
    mid = pad.shape[4]
    group = 2 * views
    return call(
        functools.partial(mid_body, views),
        "mid_conv",
        (
            shape(2, 4, quarter, mid // 2, kind=BF16),
            shape(2, quarter, mid // 2, kind=BF16),
            shape(2, mid // 2),
        ),
        4,
        [
            pltpu.VMEM((2, quarter, mid // 2), F32),
            pltpu.VMEM((2, mid // 2), F32),
            pltpu.VMEM((group, 2, mid // 2), F32),
            dma(6),
            dma(6),
            dma(group),
            dma(group),
        ],
        collective=2,
    )(pad, w2, unperm, smalls)


def orders(quarter):
    block = quarter // PIX
    row = jnp.arange(quarter, dtype=jnp.int32)
    source = (row % block) * PIX + row // block
    hot = (source[:, None] == row[None, :]).astype(BF16)
    back = (source[None, :] == row[:, None]).astype(BF16)
    return hot, back


def split_rows(value):
    high = value.astype(BF16)
    rest = value - high.astype(F32)
    middle = rest.astype(BF16)
    low = (rest - middle.astype(F32)).astype(BF16)
    return jnp.concatenate([high, middle, low], axis=0)


def join_rows(stacked):
    rows = stacked.shape[0] // 3
    return stacked[2 * rows :] + stacked[rows : 2 * rows] + stacked[:rows]


def split_pair(value):
    high = value.astype(BF16)
    return high, (value - high.astype(F32)).astype(BF16)


def exact(left, right, left_dim, right_dim):
    return lax.dot_general(
        left,
        right,
        (((left_dim,), (right_dim,)), ((), ())),
        precision=lax.Precision.HIGHEST,
        preferred_element_type=F32,
    )


def over(count, body, start):
    return body(0, start) if count == 1 else lax.fori_loop(0, count, body, start)


def factor_inverse(work, inverse, subs, width):
    panel = 8
    lane = lax.broadcasted_iota(jnp.int32, (panel, width), 1)
    row = lax.broadcasted_iota(jnp.int32, (panel, 1), 0)
    row_small = lax.broadcasted_iota(jnp.int32, (panel, width), 0)
    together = min(subs, 2)

    def eliminate(s, first):
        rows = work[s, first : first + panel]
        for j in range(panel - 1):
            column = rows[:, first + j : first + j + 1]
            pivot = column[j : j + 1]
            ratio = jnp.where(row > j, column / pivot, 0.0)
            rows = rows - ratio * rows[j : j + 1]
        diagonal = jnp.sum(
            jnp.where(lane == row_small + first, rows[:, :width], 0.0), axis=1, keepdims=True
        )
        inverse[s, first : first + panel] = rows[:, width:] * lax.rsqrt(diagonal)
        if first + panel < width:
            scaled = rows[:, :width] / diagonal
            work[s, first + panel :] -= exact(scaled, rows, 0, 0)[first + panel :]

    def some(at, carry):
        for first in range(0, width, panel):
            for k in range(together):
                eliminate(at * together + k, first)
        return carry

    over(subs // together, some, 0)


def whiten(embed, sub_col, image_col, image_row, partner_col, partner_row, refs, own_rows):
    work, inverse, white, unit, unit_parts, back = refs
    total, width = embed.shape
    subs = inverse.shape[0]
    eye = (
        lax.broadcasted_iota(jnp.int32, (width, width), 0)
        == lax.broadcasted_iota(jnp.int32, (width, width), 1)
    ).astype(F32)
    size = min(total, 512)
    pieces = total // size

    def rows_at(at):
        return pl.ds(pl.multiple_of(at * size, size), size)

    means = []
    for s in range(subs):

        def moments(at, sums, s=s):
            rows = rows_at(at)
            picked = embed[rows] * (sub_col[rows] == s).astype(F32)
            first = sums[0] + jnp.sum(picked, axis=0, keepdims=True)
            return first, sums[1] + exact(picked, embed[rows], 0, 0)

        first, second = over(
            pieces, moments, (jnp.zeros((1, width), F32), jnp.zeros((width, width), F32))
        )
        mean = first / SUB
        work[s, :, :width] = second / SUB - exact(mean, mean, 0, 0) + RIDGE * eye
        work[s, :, width:] = eye
        means.append(mean)
    factor_inverse(work, inverse, subs, width)

    def whitening(at, carry):
        rows = rows_at(at)
        value = None
        for s in range(subs):
            mask = (sub_col[rows] == s).astype(F32)
            term = exact((embed[rows] - means[s]) * mask, inverse[s], 1, 1)
            value = term if value is None else value + term
        white[rows] = value
        value = value * lax.rsqrt(jnp.sum(value * value, axis=1, keepdims=True) + EPS)
        unit[rows] = value
        high = value.astype(BF16)
        rest = value - high.astype(F32)
        middle = rest.astype(BF16)
        unit_parts[rows] = jnp.concatenate(
            [high, middle, (rest - middle.astype(F32)).astype(BF16)], axis=1
        )
        return carry

    over(pieces, whitening, 0)
    chunk = min(total, 262144 // total)

    def pairs(at, loss):
        rows = pl.ds(pl.multiple_of(at * chunk, chunk), chunk)
        across = lax.broadcasted_iota(jnp.int32, (chunk, total), 1)
        down = lax.broadcasted_iota(jnp.int32, (chunk, total), 0) + at * chunk

        def pick(hot):
            found = dot(hot.astype(F32).astype(BF16), unit_parts[...])
            return found[:, 2 * width :] + found[:, width : 2 * width] + found[:, :width]

        mine = unit[rows]
        ahead = pick(partner_col[rows] == across)
        behind = pick(partner_row[...] == down)
        members = jnp.sum((image_col[rows] == image_row[...]).astype(F32), axis=1, keepdims=True)
        weight = 1.0 / members
        apart = mine - ahead
        grad = (4.0 / total) * weight * (2.0 * mine - ahead - behind)
        length = lax.rsqrt(jnp.sum(white[rows] * white[rows], axis=1, keepdims=True) + EPS)
        back[rows] = length * (grad - mine * jnp.sum(mine * grad, axis=1, keepdims=True))
        per_view = jnp.sum(apart * apart, axis=1, keepdims=True) * weight
        return loss + jnp.sum(per_view, axis=0, keepdims=True)

    loss = over(total // chunk, pairs, jnp.zeros((1, 1), F32)) * (2.0 / total)
    lower = lax.broadcasted_iota(jnp.int32, (width, width), 0) >= lax.broadcasted_iota(
        jnp.int32, (width, width), 1
    )
    own_white, own_back = white[own_rows], back[own_rows]
    gradient = jnp.zeros(own_white.shape, F32)
    for s in range(subs):

        def pulled(at, sums, s=s):
            rows = rows_at(at)
            picked = back[rows] * (sub_col[rows] == s).astype(F32)
            spread = sums[0] + jnp.sum(picked, axis=0, keepdims=True)
            return spread, sums[1] + exact(picked, white[rows], 0, 0)

        spread, sums = over(
            pieces, pulled, (jnp.zeros((1, width), F32), jnp.zeros((width, width), F32))
        )
        low_part = jnp.where(lower, sums, 0.0)
        mirrored = low_part + low_part.T - sums * eye
        moved = own_back - (exact(own_white, mirrored, 1, 0) + spread) / SUB
        own_mask = (sub_col[own_rows] == s).astype(F32)
        gradient = gradient + own_mask * exact(moved, inverse[s], 1, 0)
    return loss, gradient


def head_body(
    views, act, w3, x, last_vectors, head_first, head_vectors, head_last, w2, h2, stat2,
    pool, sub_col, image_col, image_row, partner_col, partner_row,
    h3, slope, stat3, back3, pooled_all, grad_pooled_out, act4, grad_embed_out, grad_p1, back4, loss_out, w2_far, h2q, stats2,
    embed_all, part, part_in, mean_sums, slope_sums, st3, slots3, st4, slots4, bk4, bslots4, bk3, bslots3, embed_own,
    work, inverse, white, unit, unit_parts, back,
    sends, recvs, group_sends, group_recvs, local_sems,
):
    view_at, chan_at, y, c = place()
    mate, opposite = (view_at, 2 * y + 1 - c), (view_at, 2 * (1 - y) + c)
    group = view_group(views)
    quarter, width = h3.shape[1], h3.shape[2]
    block = quarter // PIX
    views_own = 4 * block
    met = greet([mate, opposite], [group])
    keep = pltpu.make_async_copy(h2.at[y], h2q.at[y], local_sems.at[0])
    keep.start()
    pooled_out = pooled_all.at[view_at]
    own_out = pl.ds(pl.multiple_of(width * c, width), width)
    st3[...] = jnp.zeros(st3.shape, F32)

    def last_conv(q, carry):
        total = None
        for half in range(2):
            weight = jnp.concatenate([w3[2 * half, own_out], w3[2 * half + 1, own_out]], axis=1)
            term = dot_nt(act[half, q], weight)
            total = term if total is None else total + term
        low = total.astype(BF16)
        h3[q] = low
        value = low.astype(F32)
        st3[0:1] += jnp.sum(value, axis=0, keepdims=True)
        st3[1:2] += jnp.sum(value * value, axis=0, keepdims=True)
        return carry

    lax.fori_loop(0, 4, last_conv, 0)
    met()
    totals = share(st3, slots3, group_sends.at[0], group_recvs.at[0], group)
    count = float(views * 4 * quarter)
    mean = totals[0:1] / count
    rstd = lax.rsqrt(totals[1:2] / count - mean * mean + EPS)
    stat3[...] = jnp.concatenate([mean, rstd], axis=0)
    scale = rstd * last_vectors[0:1]
    bias = last_vectors[1:2] - mean * scale

    def pool_block(q, carry):
        before = x[q].astype(F32) + (h3[q].astype(F32) * scale + bias)
        after = before * gate(before)
        high, low = split_pair(after)
        sums = dot(pool[...], high) + dot(pool[...], low)
        pooled_out[pl.ds(pl.multiple_of(q * block, block), block)] = sums * (1.0 / PIX)
        return carry

    lax.fori_loop(0, 4, pool_block, 0)
    mail = Mail(sends, recvs)
    hidden = join_rows(dot(split_rows(pooled_out[...]), head_first[...]))
    wide = hidden.shape[1] // 2
    part[0] = hidden[:, :wide]
    part[1] = hidden[:, wide:]
    beside = mail.send(part, part_in.at[pl.ds(0, 2)], mate)

    def slope_block(q, carry):
        level3 = h3[q].astype(F32)
        before = x[q].astype(F32) + (level3 * scale + bias)
        low = silu_slope(before).astype(BF16)
        slope[q] = low
        normed = (level3 - mean) * rstd
        high_part, low_part = split_pair(low.astype(F32) * normed)
        rows = pl.ds(pl.multiple_of(q * block, block), block)
        slope_sums[0, rows] = dot(pool[...], low)
        slope_sums[1, rows] = dot(pool[...], high_part) + dot(pool[...], low_part)
        return carry

    beside.wait()
    mean_sums[...] = part[...] + part_in[0:2]
    across = mail.send(mean_sums.at[c], part_in.at[2], opposite)
    lax.fori_loop(0, 2, slope_block, 0)
    across.wait_recv()
    part_in[4 + c] = mean_sums[c] + part_in[2]
    gathered = mail.send(part_in.at[4 + c], part_in.at[4 + c], mate)
    h2_far = mail.send(h2.at[1 - y], h2q.at[y], opposite)
    w2_over = mail.send(w2.at[c], w2_far.at[c], opposite)
    stats2[y] = stat2[...]
    stat2_far = mail.send(stat2, stats2.at[y], opposite)
    gathered.wait_recv()
    p1 = part_in[4:6]
    st4[0:2] = jnp.sum(p1, axis=1)
    st4[2:4] = jnp.sum(p1 * p1, axis=1)
    share_start(st4, slots4, group_sends.at[1], group_recvs.at[1], group)
    lax.fori_loop(2, 4, slope_block, 0)
    share_end(st4, slots4, group_sends.at[1], group_recvs.at[1], group)
    totals4 = add_slots(slots4, views)
    count4 = float(views * views_own)
    mean4 = totals4[0:2] / count4
    rstd4 = lax.rsqrt(totals4[2:4] / count4 - mean4 * mean4 + EPS)
    embed = None
    for half in range(2):
        normed = (part_in[4 + half] - mean4[half : half + 1]) * rstd4[half : half + 1]
        level = normed * head_vectors[half : half + 1] + head_vectors[2 + half : 3 + half]
        value = level * gate(level)
        act4[half] = value
        term = join_rows(dot(split_rows(value), head_last[half * wide : (half + 1) * wide]))
        embed = term if embed is None else embed + term
    embed_own[...] = embed
    share_start(embed_own, embed_all, group_sends.at[2], group_recvs.at[2], group)
    share_end(embed_own, embed_all, group_sends.at[2], group_recvs.at[2], group)
    gather_start(pooled_all, group_sends.at[5], group_recvs.at[5], group)
    own_rows = pl.ds(pl.multiple_of(view_at * views_own, views_own), views_own)
    every = embed_all.reshape(views * views_own, embed.shape[1])
    loss, grad_embed = whiten(
        every, sub_col, image_col, image_row, partner_col, partner_row,
        (work, inverse, white, unit, unit_parts, back), own_rows,
    )
    loss_out[...] = loss
    grad_embed_out[...] = grad_embed
    stacked = split_rows(grad_embed)
    for half in range(2):
        normed = (part_in[4 + half] - mean4[half : half + 1]) * rstd4[half : half + 1]
        level = normed * head_vectors[half : half + 1] + head_vectors[2 + half : 3 + half]
        grad = join_rows(dot_nt(stacked, head_last[half * wide : (half + 1) * wide]))
        grad = grad * silu_slope(level)
        part[half] = grad
        bk4[half : half + 1] = jnp.sum(grad, axis=0, keepdims=True)
        bk4[2 + half : 3 + half] = jnp.sum(grad * normed, axis=0, keepdims=True)
    tot4 = share(bk4, bslots4, group_sends.at[3], group_recvs.at[3], group)
    back4[...] = tot4
    grad_pooled = None
    for half in range(2):
        normed = (part_in[4 + half] - mean4[half : half + 1]) * rstd4[half : half + 1]
        grad = (
            head_vectors[half : half + 1]
            * rstd4[half : half + 1]
            * (
                part[half]
                - tot4[half : half + 1] / count4
                - normed * (tot4[2 + half : 3 + half] / count4)
            )
        )
        grad_p1[half] = grad
        term = join_rows(dot_nt(split_rows(grad), head_first[:, half * wide : (half + 1) * wide]))
        grad_pooled = term if grad_pooled is None else grad_pooled + term
    grad_pooled = grad_pooled * (1.0 / PIX)
    grad_pooled_out[...] = grad_pooled
    bk3[0:1] = jnp.sum(grad_pooled * slope_sums[0], axis=0, keepdims=True)
    bk3[1:2] = jnp.sum(grad_pooled * slope_sums[1], axis=0, keepdims=True)
    share_start(bk3, bslots3, group_sends.at[4], group_recvs.at[4], group)
    w2_over.wait_recv()
    w2_on = mail.send(w2_far.at[c], w2_far.at[c], mate)
    share_end(bk3, bslots3, group_sends.at[4], group_recvs.at[4], group)
    back3[...] = add_slots(bslots3, views)
    keep.wait()
    h2_far.wait_recv()
    stat2_far.wait_recv()
    w2_on.wait_recv()
    gather_end(pooled_all, group_sends.at[5], group_recvs.at[5], group)
    for copy in mail.copies[1:]:
        copy.wait_send()


def head_stage(
    views, act, w3, x, last_vectors, head_first, head_vectors, head_last, w2, h2, stat2, pool, tables
):
    quarter = act.shape[2]
    width = x.shape[1]
    block = quarter // PIX
    own = 4 * block
    total = views * own
    hid, emb = head_last.shape
    wide = hid // 2
    subs = total // SUB
    return call(
        functools.partial(head_body, views),
        "head",
        (
            shape(4, quarter, width, kind=BF16),
            shape(4, quarter, width, kind=BF16),
            shape(2, width),
            shape(2, width),
            shape(views, own, width),
            shape(own, width),
            shape(2, own, wide),
            shape(own, emb),
            shape(2, own, wide),
            shape(4, wide),
            shape(1, 1),
            shape(*w2.shape, kind=BF16),
            shape(*h2.shape, kind=BF16),
            shape(2, *stat2.shape),
        ),
        16,
        [
            pltpu.VMEM((views, own, emb), F32),
            pltpu.VMEM((2, own, wide), F32),
            pltpu.VMEM((6, own, wide), F32),
            pltpu.VMEM((2, own, wide), F32),
            pltpu.VMEM((2, own, width), F32),
            pltpu.VMEM((2, width), F32),
            pltpu.VMEM((views, 2, width), F32),
            pltpu.VMEM((4, wide), F32),
            pltpu.VMEM((views, 4, wide), F32),
            pltpu.VMEM((4, wide), F32),
            pltpu.VMEM((views, 4, wide), F32),
            pltpu.VMEM((2, width), F32),
            pltpu.VMEM((views, 2, width), F32),
            pltpu.VMEM((own, emb), F32),
            pltpu.VMEM((subs, emb, 2 * emb), F32),
            pltpu.VMEM((subs, emb, emb), F32),
            pltpu.VMEM((total, emb), F32),
            pltpu.VMEM((total, emb), F32),
            pltpu.VMEM((total, 3 * emb), BF16),
            pltpu.VMEM((total, emb), F32),
            dma(8),
            dma(8),
            dma(6, views),
            dma(6, views),
            dma(1),
        ],
        collective=3,
    )(
        act, w3, x.reshape(4, quarter, width), last_vectors, head_first, head_vectors, head_last, w2, h2,
        stat2, pool, *tables,
    )


def link_kind(rows):
    return BF16 if rows % 16 == 0 else F32


def back_body(
    views, h3, slope, stat3, back3, grad_pooled, last_vectors, w3, expand,
    h2q, stats2, smalls, stat1, act4, grad_embed, grad_p1,
    perm_any, unperm_any, pad_any, h1q_any, w2_any, w2_far_any, act_any, x_any, pooled_any,
    gh1, mid_slots, pair_out, head_last_out, head_first_out, smalls_out,
    gh3, gh3_mate, out_part, in_part, ga2, gh2, gh2_far, gpad, ga1, st, chan_slots, view_slots,
    order, pad, h1q, w2, w2_far, act, pooled,
    wsum, wsend, mid_parts, last_parts, last_slots, first_slots, pair_parts,
    hl_parts, hl_slots, p1_parts, p1_slots,
    sends, recvs, chan_sends, chan_recvs, group_sends, group_recvs, pair_sends, pair_recvs, local_sems,
):
    view_at, chan_at, y, c = place()
    mate, opposite = (view_at, 2 * y + 1 - c), (view_at, 2 * (1 - y) + c)
    group, chans, everyone = view_group(views), chan_group(), all_group(views)
    quarter, width = h3.shape[1], h3.shape[2]
    block = quarter // PIX
    half_width = h2q.shape[2]
    met = greet([], [everyone])
    fetch = []
    for at, (source, target) in enumerate(
        [
            (act_any, act), (perm_any, order), (w2_any, w2), (w2_far_any, w2_far),
            (h1q_any, h1q), (pad_any, pad),
        ]
    ):
        copy = pltpu.make_async_copy(source, target, local_sems.at[at])
        copy.start()
        fetch.append(copy)
    count = float(views * 4 * quarter)
    mean, rstd = stat3[0:1], stat3[1:2]
    scale = rstd * last_vectors[0:1]
    shift_part, gain_part = back3[0:1] / count, back3[1:2] / count

    def grad_rows(q):
        rows = pl.ds(pl.multiple_of(q * block, block), block)
        high, low = split_pair(grad_pooled[rows])
        spread = dot(expand[...], jnp.concatenate([high, low], axis=0))
        grad = spread * slope[q].astype(F32)
        normed = (h3[q].astype(F32) - mean) * rstd
        gh3[q] = (scale * (grad - shift_part - normed * gain_part)).astype(BF16)

    mail = Mail(sends, recvs)
    beside = []
    for i in (0, 1):
        grad_rows(2 * i + 1 - c)
        if i == 0:
            met()
        beside.append(mail.send(gh3.at[2 * i + 1 - c], gh3_mate.at[i], mate))
    for i in (0, 1):
        grad_rows(2 * i + c)
    for copy in beside:
        copy.wait_recv()
    mate_out = pl.ds(pl.multiple_of(width * (1 - c), width), width)
    own_out = pl.ds(pl.multiple_of(width * c, width), width)

    def part_of(i):
        def weight(rows):
            return jnp.concatenate([w3[k, rows] for k in range(4)], axis=1)

        value = dot(gh3[2 * i + c], weight(own_out)) + dot(gh3_mate[i], weight(mate_out))
        return dot(order[...], value.astype(BF16))

    fetch[1].wait()
    out_part[...] = part_of(1 - y).astype(BF16)
    across = mail.send(out_part, in_part, opposite)
    ga2[...] = part_of(y)
    unperm_fetch = pltpu.make_async_copy(unperm_any, order, local_sems.at[1])
    unperm_fetch.start()

    hid_block, hid_split = hl_parts.shape[1], head_last_out.shape[0]
    for half in range(2):
        product = exact(act4[half], grad_embed[...], 0, 0)
        ga1[: product.shape[0], : product.shape[1]] = product
        per_half = views // 2

        def spread_hidden(to, carry, half=half, per_half=per_half):
            spot = (4 * to + chan_at) * hid_block if hid_split == 4 else to * hid_block
            rows = pl.ds(pl.multiple_of(spot, hid_block), hid_block)
            hl_parts[half * per_half + to] = ga1[rows, : hl_parts.shape[2]]
            return carry

        lax.fori_loop(0, per_half, spread_hidden, 0)
        wide = grad_p1.shape[2] // per_half
        for to in range(per_half):
            p1_parts[half * per_half + to] = grad_p1[half, :, to * wide : (to + 1) * wide]
    scatter_start(hl_parts, hl_slots, group_sends.at[0], group_recvs.at[0], group)
    scatter_start(p1_parts, p1_slots, group_sends.at[1], group_recvs.at[1], group)
    fetch[0].wait()
    share_rows = last_parts.shape[1]
    for half in range(2):
        total = None
        for q in range(4):
            term = dot_tn(gh3[q], act[half, q])
            total = term if total is None else total + term
        low = total.astype(last_parts.dtype)
        for to in range(views):
            last_parts[to, :, half * half_width : (half + 1) * half_width] = low[
                to * share_rows : (to + 1) * share_rows
            ]
    scatter_start(last_parts, last_slots, group_sends.at[2], group_recvs.at[2], group)
    for copy in beside:
        copy.wait_send()
    x = gh3
    x_fetch = pltpu.make_async_copy(x_any, x, local_sems.at[6])
    x_fetch.start()

    def sums_everywhere(at):
        return share(
            share_value(st, chan_slots.at[at], chan_sends.at[at], chan_recvs.at[at], chans),
            view_slots.at[at], group_sends.at[3 + at], group_recvs.at[3 + at], group,
        )

    def share_value(source, slots, send, recv, who):
        source[...] = share(source, slots, send, recv, who)
        return source

    gpad[...] = jnp.zeros(gpad.shape, gpad.dtype)
    across.wait()
    ga2[...] += in_part[...].astype(F32)
    halves = (y, 1 - y)

    def mid_norm(near):
        half = halves[near]
        gains = jnp.concatenate([smalls[2 * half], smalls[2 * half + 1]], axis=1)
        mean2, rstd2 = stats2[half, 0:1], stats2[half, 1:2]
        return mean2, rstd2, gains[2:3], gains[3:4]

    def half_cols(ref, near):
        low, high = ref[:, :half_width], ref[:, half_width:]
        return jnp.where(halves[near] == 0, low, high)

    for near in range(2):
        mean2, rstd2, gain2, shift2 = mid_norm(near)
        normed = (h2q[halves[near]].astype(F32) - mean2) * rstd2
        grad = half_cols(ga2, near) * silu_slope(normed * gain2 + shift2)
        ga1[:, near * half_width : (near + 1) * half_width] = grad
        st[halves[near], 0:1] = jnp.sum(grad, axis=0, keepdims=True)
        st[halves[near], 1:2] = jnp.sum(grad * normed, axis=0, keepdims=True)
    totals2 = sums_everywhere(0)
    view_slots[0, 0] = totals2
    for near in range(2):
        mean2, rstd2, gain2, shift2 = mid_norm(near)
        tot = view_slots[0, 0, halves[near]]
        normed = (h2q[halves[near]].astype(F32) - mean2) * rstd2
        grad = ga1[:, near * half_width : (near + 1) * half_width]
        low = (gain2 * rstd2 * (grad - tot[0:1] / count - normed * (tot[1:2] / count))).astype(BF16)
        gh2[near] = low
        gpad[near, 1 : SIDE + 1, 1 : SIDE + 1] = low.reshape(SIDE, SIDE, block, half_width)
    tot = view_slots[0, 0, y]
    smalls_out[0:2] = jnp.where(c == 0, tot[:, : half_width // 2], tot[:, half_width // 2 :])
    far_copy = mail.send(gh2.at[1], gh2_far, opposite)
    fetch[2].wait()
    fetch[3].wait()
    channels = w2.shape[1] // 9
    for tap in range(9):
        a, b = 2 - tap // 3, 2 - tap % 3
        taps = slice(tap * channels, (tap + 1) * channels)
        term = None
        for near, weight in enumerate((w2, w2_far)):
            window = gpad[near, a : a + SIDE, b : b + SIDE].reshape(quarter, half_width)
            both = jnp.concatenate([weight[0, taps], weight[1, taps]], axis=1)
            piece = dot_nt(window, both)
            term = piece if term is None else term + piece
        if tap == 0:
            ga1[...] = term
        else:
            ga1[...] += term
    fetch[4].wait()
    for half in range(2):
        gains = jnp.concatenate([smalls[2 * half], smalls[2 * half + 1]], axis=1)
        normed = (h1q[half] - stat1[half, 0:1]) * stat1[half, 1:2]
        cols = slice(half * half_width, (half + 1) * half_width)
        grad = ga1[:, cols] * silu_slope(normed * gains[0:1] + gains[1:2])
        ga2[:, cols] = grad
        st[half, 0:1] = jnp.sum(grad, axis=0, keepdims=True)
        st[half, 1:2] = jnp.sum(grad * normed, axis=0, keepdims=True)
    totals1 = sums_everywhere(1)
    view_slots[1, 0] = totals1
    tot = view_slots[1, 0, y]
    smalls_out[2:4] = jnp.where(c == 0, tot[:, : half_width // 2], tot[:, half_width // 2 :])
    unperm_fetch.wait()
    for half in range(2):
        gains = jnp.concatenate([smalls[2 * half], smalls[2 * half + 1]], axis=1)
        normed = (h1q[half] - stat1[half, 0:1]) * stat1[half, 1:2]
        cols = slice(half * half_width, (half + 1) * half_width)
        tot = totals1[half]
        low = (
            gains[0:1]
            * stat1[half, 1:2]
            * (ga2[:, cols] - tot[0:1] / count - normed * (tot[1:2] / count))
        ).astype(BF16)
        out_part[:, cols] = low
    gh1[chan_at] = dot(order[...], out_part[...]).astype(BF16)
    spot = gh1.at[chan_at]
    gh1_across = mail.send(spot, spot, opposite)
    gh1_beside = mail.send(spot, spot, mate)

    far_copy.wait_recv()
    fetch[5].wait()
    for tap in range(9):
        a, b = tap // 3, tap % 3

        def tap_term(at, grads):
            window = pad[at, a : a + SIDE, b : b + SIDE].reshape(quarter, channels)
            return dot_tn(window, grads)

        total = tap_term(y, gh2[0]) + tap_term(1 - y, gh2_far[...])
        taps = slice(tap * channels, (tap + 1) * channels)
        wsum[0, taps] = total[:, : half_width // 2]
        wsum[1, taps] = total[:, half_width // 2 :]
    mid_rows = mid_parts.shape[1]
    mid_flat = mid_parts.reshape(views * mid_rows, mid_parts.shape[2])
    if mid_parts.dtype == F32:
        mid_mate = mail.send(wsum.at[1 - c], mid_flat, mate)
    else:
        wsend[...] = wsum[1 - c].astype(wsend.dtype)
        mid_mate = mail.send(wsend, mid_flat, mate)
    scatter_end(p1_parts, p1_slots, group_sends.at[1], group_recvs.at[1], group)
    few = pooled.shape[0]

    def head_first_term(at, total):
        views_at = pl.ds(at * few, few)
        copy = pltpu.make_async_copy(pooled_any.at[views_at], pooled, local_sems.at[7])
        copy.start()
        copy.wait()
        rows = pooled[...].reshape(-1, width)
        return total + exact(rows, p1_slots[views_at].reshape(rows.shape[0], -1), 0, 0)

    head_first_out[...] = over(views // few, head_first_term, jnp.zeros(head_first_out.shape, F32))
    mid_mate.wait_recv()

    def mid_block(to, carry):
        rows = pl.ds(pl.multiple_of(to * mid_rows, mid_rows), mid_rows)
        mid_parts[to] = (wsum[c, rows] + mid_parts[to].astype(F32)).astype(mid_parts.dtype)
        return carry

    lax.fori_loop(0, views, mid_block, 0)
    scatter_start(mid_parts, mid_slots, group_sends.at[5], group_recvs.at[5], group)
    gh1_across.wait_recv()
    far_spot = gh1.at[2 * (1 - y) + c]
    gh1_on = mail.send(far_spot, far_spot, mate)
    gh1_beside.wait_recv()
    gh1_on.wait_recv()
    x_fetch.wait()
    scatter_end(last_parts, last_slots, group_sends.at[2], group_recvs.at[2], group)
    first_parts = last_parts
    total = None
    for q in range(4):
        term = dot_tn(x[q], gh1[q])
        total = term if total is None else total + term
    low = total.astype(first_parts.dtype)
    for to in range(views):
        first_parts[to] = low[to * share_rows : (to + 1) * share_rows]
    scatter_start(first_parts, first_slots, group_sends.at[6], group_recvs.at[6], group)

    scatter_end(hl_parts, hl_slots, group_sends.at[0], group_recvs.at[0], group)
    if hid_split == 4:
        head_last_out[chan_at] = add_slots(hl_slots, views)
        gather_start(head_last_out, chan_sends.at[2], chan_recvs.at[2], chans)
    else:
        head_last_out[0] = add_slots(hl_slots, views)

    def blocks(kind, summed):
        wide = summed.shape[1] // 4
        for to in range(4):
            pair_parts[to, kind] = summed[:, to * wide : (to + 1) * wide]

    def summed_slots(slots):
        def add(at, total):
            return total + slots[at].astype(F32)

        return lax.fori_loop(1, views, add, slots[0].astype(F32))

    blocks(1, summed_slots(last_slots))
    scatter_end(first_parts, first_slots, group_sends.at[6], group_recvs.at[6], group)
    blocks(0, summed_slots(first_slots))
    row_views = views // 4
    to_view = chan_at * row_views + lax.div(view_at, 4)
    slot = lax.rem(view_at, 4)

    def pair_copy(to):
        return pltpu.make_async_remote_copy(
            src_ref=pair_parts.at[to],
            dst_ref=pair_out.at[slot],
            send_sem=pair_sends.at[to],
            recv_sem=pair_recvs.at[slot],
            device_id=(to_view, to),
            device_id_type=MESH,
        )

    def pair_arrival(origin):
        return pltpu.make_async_remote_copy(
            src_ref=pair_parts.at[0],
            dst_ref=pair_out.at[origin],
            send_sem=pair_sends.at[0],
            recv_sem=pair_recvs.at[origin],
            device_id=(from_view + origin, from_chan),
            device_id_type=MESH,
        )

    from_view, from_chan = 4 * lax.rem(view_at, row_views), lax.div(view_at, row_views)
    for to in range(4):
        own = jnp.logical_and(to_view == view_at, chan_at == to)

        @pl.when(own)
        def _():
            pair_out[slot] = pair_parts[to]

        @pl.when(jnp.logical_not(own))
        def _():
            pair_copy(to).start()

    for origin in range(4):
        own = jnp.logical_and(from_view + origin == view_at, chan_at == from_chan)

        @pl.when(jnp.logical_not(own))
        def _():
            pair_arrival(origin).wait_recv()

    for to in range(4):
        own = jnp.logical_and(to_view == view_at, chan_at == to)

        @pl.when(jnp.logical_not(own))
        def _():
            pair_copy(to).wait_send()

    if hid_split == 4:
        gather_end(head_last_out, chan_sends.at[2], chan_recvs.at[2], chans)
    scatter_end(mid_parts, mid_slots, group_sends.at[5], group_recvs.at[5], group)
    for copy in mail.copies[3:]:
        copy.wait_send()


def back_stage(views, head_outs, first_outs, act, x, last_vectors, perm, unperm, expand):
    (h3, slope, stat3, back3, pooled_all, grad_pooled, act4, grad_embed, grad_p1, back4, loss, w2_far, h2q, stats2) = head_outs
    pad, h1q, stat1, w2, w3, smalls = first_outs
    quarter, width = h3.shape[1], h3.shape[2]
    block = quarter // PIX
    own = 4 * block
    mid = pad.shape[4]
    half = mid // 2
    hid, emb = 2 * act4.shape[2], grad_embed.shape[1]
    taps = w2.shape[1]
    hid_split = 4 if hid // views % 32 == 0 else 1
    hid_block = hid // views // hid_split
    mid_kind, row_kind = link_kind(taps // views), link_kind(width // views)
    vm = pltpu.VMEM
    return call(
        functools.partial(back_body, views),
        "back",
        (
            shape(4, quarter, mid, kind=BF16),
            shape(views, taps // views, half // 2, kind=mid_kind),
            shape(4, 2, width // views, mid // 4),
            shape(hid_split, hid_block, emb),
            shape(width, hid // views),
            shape(4, half // 2),
        ),
        24,
        [
            vm((4, quarter, width), BF16),
            vm((2, quarter, width), BF16),
            vm((quarter, mid), BF16),
            vm((quarter, mid), BF16),
            vm((quarter, mid), F32),
            vm((2, quarter, half), BF16),
            vm((quarter, half), BF16),
            vm((2, PAD, PAD, block, half), BF16),
            vm((quarter, mid), F32),
            vm((2, 2, half), F32),
            vm((2, 4, 2, 2, half), F32),
            vm((2, views, 2, 2, half), F32),
            vm(unperm.shape, BF16),
            vm(pad.shape, BF16),
            vm(h1q.shape, F32),
            vm(w2.shape, BF16),
            vm(w2_far.shape, BF16),
            vm(act.shape, BF16),
            vm((min(views, 8), own, width), F32),
            vm((2, taps, half // 2), F32),
            vm((taps if mid_kind == BF16 else 16, half // 2), BF16),
            vm((views, taps // views, half // 2), mid_kind),
            vm((views, width // views, mid), row_kind),
            vm((views, width // views, mid), row_kind),
            vm((views, width // views, mid), row_kind),
            vm((4, 2, width // views, mid // 4), F32),
            vm((views, hid_block, emb), F32),
            vm((views, hid_block, emb), F32),
            vm((views, own, hid // views), F32),
            vm((views, own, hid // views), F32),
            dma(10),
            dma(10),
            dma(3, 4),
            dma(3, 4),
            dma(7, views),
            dma(7, views),
            dma(4),
            dma(4),
            dma(8),
        ],
        collective=4,
        any_ins=range(15, 24),
    )(
        h3, slope, stat3, back3, grad_pooled, last_vectors, w3, expand,
        h2q, stats2, smalls, stat1, act4, grad_embed, grad_p1,
        perm, unperm, pad, h1q, w2, w2_far, act, x.reshape(4, quarter, width), pooled_all,
    )


def last_body(
    gh1, w1_own, slope, grad_pooled, expand, mid_slots, pair_out, head_last_in, head_first_in,
    grad_input, grad_mid, grad_first, grad_last, grad_head_last, grad_head_first,
):
    at = pl.program_id(0)
    high, low = split_pair(grad_pooled[0])
    spread = dot(expand[...], jnp.concatenate([high, low], axis=0))
    grad_input[0] = dot_nt(gh1[0], w1_own[...]) + spread * slope[0].astype(F32)

    @pl.when(at == 0)
    def _():
        views = mid_slots.shape[0]

        def add(slot, total):
            return total + mid_slots[slot].astype(F32)

        grad_mid[...] = lax.fori_loop(1, views, add, mid_slots[0].astype(F32))
        rows = pair_out.shape[2]
        for origin in range(4):
            grad_first[origin * rows : (origin + 1) * rows] = pair_out[origin, 0]
            grad_last[origin * rows : (origin + 1) * rows] = pair_out[origin, 1]
        grad_head_first[...] = head_first_in[...]
        rows = head_last_in.shape[1]
        for origin in range(head_last_in.shape[0]):
            grad_head_last[origin * rows : (origin + 1) * rows] = head_last_in[origin]


def last_stage(gh1, w1_own, slope, grad_pooled, expand, mid_slots, pair_out, head_last_in, head_first_in):
    quarter, mid = gh1.shape[1], gh1.shape[2]
    width = slope.shape[2]
    block = quarter // PIX

    def whole(array):
        dims = array.shape
        return pl.BlockSpec(dims, lambda q: (0,) * len(dims))

    def part(*dims):
        return pl.BlockSpec((1, *dims), lambda q: (q, 0, 0))

    outs = (
        shape(4, quarter, width),
        shape(*mid_slots.shape[1:]),
        shape(4 * pair_out.shape[2], pair_out.shape[3]),
        shape(4 * pair_out.shape[2], pair_out.shape[3]),
        shape(head_last_in.shape[0] * head_last_in.shape[1], head_last_in.shape[2]),
        shape(*head_first_in.shape),
    )
    return pl.pallas_call(
        last_body,
        grid=(4,),
        out_shape=outs,
        in_specs=[
            part(quarter, mid), whole(w1_own), part(quarter, width), part(block, width), whole(expand),
            whole(mid_slots), whole(pair_out), whole(head_last_in), whole(head_first_in),
        ],
        out_specs=(part(quarter, width), *(whole(out) for out in outs[1:])),
        name="results",
        compiler_params=pltpu.CompilerParams(
            vmem_limit_bytes=VMEM_BYTES, dimension_semantics=("arbitrary",)
        ),
    )(
        gh1, w1_own, slope, grad_pooled.reshape(4, block, width), expand,
        mid_slots, pair_out, head_last_in, head_first_in,
    )


def per_device(
    views,
    block_input,
    conv_first,
    conv_mid,
    conv_last,
    gain_first,
    shift_first,
    gain_mid,
    shift_mid,
    gain_last,
    shift_last,
    head_first,
    gain_head,
    shift_head,
    head_last,
    image_of,
    partner,
    sub_of,
):
    rows, width = block_input.shape
    quarter = rows // 4
    block = quarter // PIX
    perm, unperm = orders(quarter)
    small = jnp.stack([gain_first, shift_first, gain_mid, shift_mid] * 2)
    last_vectors = jnp.stack([gain_last, shift_last])
    head_vectors = jnp.concatenate([gain_head.reshape(2, -1), shift_head.reshape(2, -1)], axis=0)
    at_row, at_view = jnp.arange(quarter, dtype=jnp.int32), jnp.arange(block, dtype=jnp.int32)
    pool = (at_row[None, :] // PIX == at_view[:, None]).astype(BF16)
    twice = jnp.arange(2 * block, dtype=jnp.int32) % block
    expand = (at_row[:, None] // PIX == twice[None, :]).astype(BF16)
    tables = (sub_of[:, None], image_of[:, None], image_of[None], partner[:, None], partner[None])
    first_outs = first_stage(views, block_input, conv_first, conv_mid, conv_last, small, perm)
    pad, h1q, stat1, w2, w3, w1, smalls = first_outs
    first_outs = (pad, h1q, stat1, w2, w3, smalls)
    act, h2, stat2 = mid_stage(views, pad, w2, unperm, smalls)
    head_outs = head_stage(
        views, act, w3, block_input, last_vectors, head_first, head_vectors, head_last, w2, h2, stat2, pool, tables
    )
    slope, back3, grad_pooled = head_outs[1], head_outs[3], head_outs[5]
    back4, loss = head_outs[9], head_outs[10]
    gh1, mid_slots, pair_out, head_last_in, head_first_in, smalls_out = back_stage(
        views, head_outs, first_outs, act, block_input, last_vectors, perm, unperm, expand
    )
    grad_input, grad_mid, grad_first, grad_last, grad_head_last, grad_head_first = last_stage(
        gh1, w1, slope, grad_pooled, expand, mid_slots, pair_out, head_last_in, head_first_in
    )
    return (
        loss[0, 0],
        grad_input.reshape(rows, width),
        grad_first,
        grad_mid,
        grad_last,
        grad_head_first,
        grad_head_last,
        smalls_out[3],
        smalls_out[2],
        smalls_out[1],
        smalls_out[0],
        back3[1],
        back3[0],
        back4[2:4].reshape(-1),
        back4[0:2].reshape(-1),
    )


def solution(mesh):
    views = mesh.shape["views"]
    return jax.shard_map(
        functools.partial(per_device, views),
        mesh=mesh,
        in_specs=(
            P("views", "chan"),
            P(None, "chan"),
            P(None, "chan"),
            P(None, "chan"),
            P("chan"),
            P("chan"),
            P("chan"),
            P("chan"),
            P("chan"),
            P("chan"),
            P("chan", None),
            P(),
            P(),
            P(),
            P(),
            P(),
            P(),
        ),
        out_specs=(
            P(),
            P("views", "chan"),
            P("views", "chan"),
            P("views", "chan"),
            P("views", "chan"),
            P("chan", "views"),
            P("views", None),
            P("chan"),
            P("chan"),
            P("chan"),
            P("chan"),
            P("chan"),
            P("chan"),
            P(),
            P(),
        ),
        check_vma=False,
    )
```

```python
import functools

import jax
import jax.numpy as jnp
import numpy as np
from jax import lax
from jax.experimental import pallas as pl
from jax.experimental.pallas import tpu as pltpu
from jax.sharding import PartitionSpec as P

SIDE = 7
PIX = SIDE * SIDE
PAD = SIDE + 2
SUB = 256
EPS = 1e-05
RIDGE = 0.5
MESH = pl.DeviceIdType.MESH
BF16 = jnp.bfloat16
F32 = jnp.float32
VMEM_BYTES = 60 << 20


def place():
    view_at, chan_at = lax.axis_index("views"), lax.axis_index("chan")
    return view_at, chan_at, lax.div(chan_at, 2), lax.rem(chan_at, 2)


def greet(peers, groups=()):
    barrier = pltpu.get_barrier_semaphore()
    total = len(peers)
    for peer in peers:
        pl.semaphore_signal(barrier, inc=1, device_id=peer, device_id_type=MESH)
    for size, own, device in groups:

        def tell(step, carry, size=size, own=own, device=device):
            pl.semaphore_signal(
                barrier, inc=1, device_id=device(lax.rem(own + step, size)), device_id_type=MESH
            )
            return carry

        lax.fori_loop(1, size, tell, 0)
        total += size - 1
    return lambda: pl.semaphore_wait(barrier, total)


class Mail:
    def __init__(self, send_sems, recv_sems):
        self.send_sems, self.recv_sems, self.copies = send_sems, recv_sems, []

    def send(self, source, target, peer):
        spot = len(self.copies)
        copy = pltpu.make_async_remote_copy(
            src_ref=source,
            dst_ref=target,
            send_sem=self.send_sems.at[spot],
            recv_sem=self.recv_sems.at[spot],
            device_id=peer,
            device_id_type=MESH,
        )
        copy.start()
        self.copies.append(copy)
        return copy

    def finish(self):
        for copy in self.copies:
            copy.wait_send()


class Local:
    def __init__(self, sems):
        self.sems, self.used = sems, 0

    def fetch(self, source, target):
        copy = pltpu.make_async_copy(source, target, self.sems.at[self.used])
        copy.start()
        self.used += 1
        return copy


def group_copy(source, slots, sends, recvs, size, own, device, step):
    to = lax.rem(own + step, size)
    return pltpu.make_async_remote_copy(
        src_ref=source,
        dst_ref=slots.at[own],
        send_sem=sends.at[step],
        recv_sem=recvs.at[own],
        device_id=device(to),
        device_id_type=MESH,
    )


def group_arrival(source, slots, sends, recvs, size, own, device, step):
    origin = lax.rem(own + step, size)
    return pltpu.make_async_remote_copy(
        src_ref=source,
        dst_ref=slots.at[origin],
        send_sem=sends.at[step],
        recv_sem=recvs.at[origin],
        device_id=device(origin),
        device_id_type=MESH,
    )


def share_start(source, slots, sends, recvs, group):
    def start(step, carry):
        group_copy(source, slots, sends, recvs, *group, step).start()
        return carry

    lax.fori_loop(1, group[0], start, 0)
    slots[group[1]] = source[...]


def share_end(source, slots, sends, recvs, group):
    def end(step, carry):
        group_arrival(source, slots, sends, recvs, *group, step).wait_recv()
        group_copy(source, slots, sends, recvs, *group, step).wait_send()
        return carry

    lax.fori_loop(1, group[0], end, 0)


def add_slots(slots, size):
    def add(at, total):
        return total + slots[at]

    return lax.fori_loop(1, size, add, slots[0])


def share(source, slots, sends, recvs, group):
    share_start(source, slots, sends, recvs, group)
    share_end(source, slots, sends, recvs, group)
    return add_slots(slots, group[0])


def gather_start(source, slots, sends, recvs, group):
    def start(step, carry):
        group_copy(source, slots, sends, recvs, *group, step).start()
        return carry

    lax.fori_loop(1, group[0], start, 0)


def scatter_start(parts, slots, sends, recvs, group, keep=True):
    size, own, device = group

    def start(step, carry):
        to = lax.rem(own + step, size)
        group_copy(parts.at[to], slots, sends, recvs, *group, step).start()
        return carry

    lax.fori_loop(1, size, start, 0)
    if keep:
        slots[own] = parts[own]


def scatter_end(parts, slots, sends, recvs, group):
    share_end(parts.at[group[1]], slots, sends, recvs, group)


def chan_group():
    view_at, chan_at, y, c = place()
    return (4, chan_at, lambda at: (view_at, at))


def half_group(views):
    view_at, chan_at, y, c = place()
    return (
        2 * views,
        2 * view_at + c,
        lambda at: (lax.div(at, 2), 2 * y + lax.rem(at, 2)),
    )


def view_group(views):
    view_at, chan_at, y, c = place()
    return (views, view_at, lambda at: (at, chan_at))


def all_group(views):
    view_at, chan_at, y, c = place()
    return (4 * views, 4 * view_at + chan_at, lambda at: (lax.div(at, 4), lax.rem(at, 4)))


def dot(left, right):
    return jnp.dot(left, right, preferred_element_type=F32)


def dot_nt(left, right):
    return lax.dot_general(left, right, (((1,), (1,)), ((), ())), preferred_element_type=F32)


def dot_tn(left, right):
    return lax.dot_general(left, right, (((0,), (0,)), ((), ())), preferred_element_type=F32)


def gate(level):
    return 0.5 + 0.5 * jnp.tanh(0.5 * level)


def silu_slope(level):
    open_part = gate(level)
    return open_part * (1.0 + level * (1.0 - open_part))


def call(body, name, outs, ins, scratch, collective, any_ins=(), any_outs=()):
    def spec(at, places):
        return pl.BlockSpec(memory_space=pl.ANY if at in places else pltpu.VMEM)

    return pl.pallas_call(
        body,
        out_shape=outs,
        in_specs=[spec(at, any_ins) for at in range(ins)],
        out_specs=tuple(spec(at, any_outs) for at in range(len(outs))),
        scratch_shapes=scratch,
        name=name,
        compiler_params=pltpu.CompilerParams(
            collective_id=collective, has_side_effects=True, vmem_limit_bytes=VMEM_BYTES
        ),
    )


def shape(*dims, kind=F32):
    return jax.ShapeDtypeStruct(dims, kind)


def dma(*dims):
    return pltpu.SemaphoreType.DMA(dims)


EARLY_TAPS = 6


def forward_body(
    views, g1, b1, g2, b2, x, w1in, w2in, w3in, perm_any, unperm_any,
    pad_out, h1_out, w2_out, w2_far_out, w3, act, h2_out, stat, stat2, w1_own, smalls,
    xo, xm, xp, w1, out_part, in_part, h1, st, slots, st2, slots2,
    perm, unperm, pad, w2, hidden, act_own, h2, small,
    sends, recvs, part_sends, part_recvs, group_sends, group_recvs, local_sems,
):
    view_at, chan_at, y, c = place()
    mate, opposite = (view_at, 2 * y + 1 - c), (view_at, 2 * (1 - y) + c)
    diagonal = (view_at, 2 * (1 - y) + 1 - c)
    group = half_group(views)
    quarter, depth = x.shape[1], x.shape[2]
    near, far = 2 * y + c, 2 * (1 - y) + c
    near_rows = pl.ds(pl.multiple_of(2 * depth * y, 2 * depth), 2 * depth)
    far_rows = pl.ds(pl.multiple_of(2 * depth * (1 - y), 2 * depth), 2 * depth)
    met = greet([opposite, diagonal], [group])
    local = Local(local_sems)
    x_own = [local.fetch(x.at[2 * q + c], xo.at[q]) for q in range(2)]
    perm_here = local.fetch(perm_any, perm)
    w1_here = local.fetch(w1in.at[near_rows], w1.at[near])
    w2_here = local.fetch(w2in, w2.at[c])
    unperm_here = local.fetch(unperm_any, unperm)
    rest = [local.fetch(w3in.at[near_rows], w3.at[near])]
    for at, vector in enumerate((g1, b1, g2, b2)):
        small[at : at + 1] = vector[...]
        small[4 + at : 5 + at] = vector[...]
    smalls[chan_at] = small[...]
    pad[...] = jnp.zeros(pad.shape, pad.dtype)
    met()
    mail = Mail(sends, recvs)
    x_mate = [mail.send(x.at[1 - c], xm.at[0], mate)]
    w1_mate = mail.send(w1in.at[near_rows], w1.at[near], mate)
    w1_far = mail.send(w1in.at[far_rows], w1.at[near], opposite)
    x_mate.append(mail.send(x.at[3 - c], xm.at[1], mate))
    small_copies = [mail.send(small, smalls.at[chan_at], to) for to in (mate, opposite, diagonal)]
    w2_mate = mail.send(w2in, w2.at[c], mate)
    w3_mate = mail.send(w3in.at[near_rows], w3.at[near], mate)

    def part_copy(half, q):
        return pltpu.make_async_remote_copy(
            src_ref=out_part.at[half, q],
            dst_ref=in_part.at[half, q],
            send_sem=part_sends.at[half, q],
            recv_sem=part_recvs.at[half, q],
            device_id=opposite,
            device_id_type=MESH,
        )

    def part(half, q):
        both = jnp.concatenate([w1[2 * half], w1[2 * half + 1]], axis=1)
        out_part[half, q] = (dot(xp[q, 0], both[:depth]) + dot(xp[q, 1], both[depth:])).astype(BF16)
        part_copy(half, q).start()

    perm_here.wait()
    for q in range(2):
        x_own[q].wait()
        xp[q, c] = dot(perm[...], xo[q]).astype(BF16)
        x_mate[q].wait_recv()
        xp[q, 1 - c] = dot(perm[...], xm[q]).astype(BF16)
        if q == 0:
            w1_here.wait()
            w1_mate.wait_recv()
        part(y, q)
    w1_far.wait_recv()
    w1_on = mail.send(w1.at[far], w1.at[far], mate)
    w1_on.wait_recv()
    for q in range(2):
        part(1 - y, q)
    w2_here.wait()
    w2_mate.wait_recv()
    rest.append(local.fetch(w2, w2_out))
    own_rows = pl.ds(pl.multiple_of(depth * c, depth), depth)
    w1_own[...] = jnp.concatenate([w1[k, own_rows] for k in range(4)], axis=1)
    st[...] = jnp.zeros(st.shape, st.dtype)
    step_rows = quarter // SIDE

    def sums(half):
        def one(q, carry):
            part_copy(half, q).wait_recv()

            def rows_of(at, inner):
                rows = pl.ds(at * step_rows, step_rows)
                value = out_part[half, q, rows].astype(F32) + in_part[half, q, rows].astype(F32)
                h1[half, q, rows] = value
                st[half, 0:1] += jnp.sum(value, axis=0, keepdims=True)
                st[half, 1:2] += jnp.sum(value * value, axis=0, keepdims=True)
                return inner

            return lax.fori_loop(0, SIDE, rows_of, carry)

        lax.fori_loop(0, 2, one, 0)

    sums(1 - y)
    sums(y)
    share_start(st, slots, group_sends.at[0], group_recvs.at[0], group)
    w3_far = mail.send(w3in.at[far_rows], w3.at[near], opposite)
    channels = pad.shape[4]
    w2_far = []
    for tap in range(EARLY_TAPS):
        rows = pl.ds(tap * channels, channels)
        w2_far.append(mail.send(w2in.at[rows], w2_far_out.at[c, rows], opposite))
    share_end(st, slots, group_sends.at[0], group_recvs.at[0], group)
    totals = add_slots(slots, group[0])
    count = float(views * 4 * quarter)
    for copy in small_copies:
        copy.wait_recv()
    mean = totals[:, 0:1] / count
    rstd = lax.rsqrt(totals[:, 1:2] / count - mean * mean + EPS)
    stat[...] = jnp.concatenate([mean, rstd], axis=1)
    for half in range(2):
        gains = jnp.concatenate([smalls[2 * half], smalls[2 * half + 1]], axis=1)
        scale = rstd[half] * gains[0:1]
        bias = gains[1:2] - mean[half] * scale

        def act_rows(at, carry, half=half, scale=scale, bias=bias):
            q, i = lax.div(at, SIDE), lax.rem(at, SIDE)
            level = h1[half, q, pl.ds(i * step_rows, step_rows)] * scale + bias
            value = (level * gate(level)).astype(BF16)
            pad[q, i + 1, 1 : SIDE + 1, :, 256 * half : 256 * half + 256] = value.reshape(
                SIDE, step_rows // SIDE, 256
            )
            return carry

        lax.fori_loop(0, 2 * SIDE, act_rows, 0)
    rest.append(local.fetch(pad, pad_out))
    rest += [local.fetch(h1.at[half, y], h1_out.at[half]) for half in range(2)]
    w3_far.wait_recv()
    w3_on = mail.send(w3.at[far], w3.at[far], mate)
    st2[...] = jnp.zeros(st2.shape, F32)

    def convolve(q, carry):
        for tap in range(9):
            a, b = tap // 3, tap % 3
            window = pad[q, a : a + SIDE, b : b + SIDE].reshape(quarter, channels)
            taps = slice(tap * channels, (tap + 1) * channels)
            term = dot(window, jnp.concatenate([w2[0, taps], w2[1, taps]], axis=1))
            if tap == 0:
                hidden[q] = term
            else:
                hidden[q] += term
        value = hidden[q]
        h2[q] = value.astype(BF16)
        st2[0:1] += jnp.sum(value, axis=0, keepdims=True)
        st2[1:2] += jnp.sum(value * value, axis=0, keepdims=True)
        return carry

    lax.fori_loop(0, 2, convolve, 0)
    share_start(st2, slots2, group_sends.at[1], group_recvs.at[1], group)
    rest.append(local.fetch(h2, h2_out))
    w2_on = []

    def pass_on(taps):
        for tap in taps:
            w2_far[tap].wait_recv()
            rows = pl.ds(tap * channels, channels)
            w2_on.append(mail.send(w2_far_out.at[c, rows], w2_far_out.at[c, rows], mate))

    pass_on(range(EARLY_TAPS // 2))
    share_end(st2, slots2, group_sends.at[1], group_recvs.at[1], group)
    totals2 = add_slots(slots2, group[0])
    mean2 = totals2[0:1] / count
    rstd2 = lax.rsqrt(totals2[1:2] / count - mean2 * mean2 + EPS)
    stat2[...] = jnp.concatenate([mean2, rstd2], axis=0)
    gains = jnp.concatenate([smalls[2 * y], smalls[2 * y + 1]], axis=1)
    scale2 = rstd2 * gains[2:3]
    bias2 = gains[3:4] - mean2 * scale2
    across, beside = [], []
    unperm_here.wait()
    for q in range(2):
        level = hidden[q] * scale2 + bias2
        value = (level * gate(level)).astype(BF16)
        act_own[q] = dot(unperm[...], value).astype(BF16)
        spot = act.at[y, 2 * q + c]
        across.append(mail.send(act_own.at[q], spot, opposite))
        beside.append(mail.send(act_own.at[q], spot, mate))
        rest.append(local.fetch(act_own.at[q], spot))
    pass_on(range(EARLY_TAPS // 2, EARLY_TAPS))
    for q in range(2):
        across[q].wait_recv()
        spot = act.at[1 - y, 2 * q + c]
        beside.append(mail.send(spot, spot, mate))
    for copy in [w3_mate, w3_on, *w2_on, *beside]:
        copy.wait_recv()
    for copy in rest:
        copy.wait()
    mail.finish()
    for half in range(2):
        for q in range(2):
            part_copy(half, q).wait_send()


def forward_stage(views, x, conv_first, conv_mid, conv_last, vectors, perm, unperm):
    quarter, depth = x.shape[0] // 4, x.shape[1]
    mid = conv_mid.shape[1] * 4
    half, taps = mid // 2, conv_mid.shape[0]
    block = quarter // PIX
    group = 2 * views
    vm = pltpu.VMEM
    return call(
        functools.partial(forward_body, views),
        "forward",
        (
            shape(2, PAD, PAD, block, mid, kind=BF16),
            shape(2, quarter, half),
            shape(2, *conv_mid.shape, kind=BF16),
            shape(2, taps // 9 * EARLY_TAPS, conv_mid.shape[1], kind=BF16),
            shape(4, 2 * depth, mid // 4, kind=BF16),
            shape(2, 4, quarter, half, kind=BF16),
            shape(2, quarter, half, kind=BF16),
            shape(2, 2, half),
            shape(2, half),
            shape(depth, mid, kind=BF16),
            shape(4, 8, mid // 4),
        ),
        10,
        [
            vm((2, quarter, depth), BF16),
            vm((2, quarter, depth), BF16),
            vm((2, 2, quarter, depth), BF16),
            vm((4, 2 * depth, mid // 4), BF16),
            vm((2, 2, quarter, half), BF16),
            vm((2, 2, quarter, half), BF16),
            vm((2, 2, quarter, half), F32),
            vm((2, 2, half), F32),
            vm((group, 2, 2, half), F32),
            vm((2, half), F32),
            vm((group, 2, half), F32),
            vm((quarter, quarter), BF16),
            vm((quarter, quarter), BF16),
            vm((2, PAD, PAD, block, mid), BF16),
            vm((2, *conv_mid.shape), BF16),
            vm((2, quarter, half), F32),
            vm((2, quarter, half), BF16),
            vm((2, quarter, half), BF16),
            vm((8, mid // 4), F32),
            dma(32),
            dma(32),
            dma(2, 2),
            dma(2, 2),
            dma(2, group),
            dma(2, group),
            dma(20),
        ],
        collective=1,
        any_ins=range(4, 10),
        any_outs=range(7),
    )(*vectors, x.reshape(4, quarter, depth), conv_first, conv_mid, conv_last, perm, unperm)


def orders(quarter):
    block = quarter // PIX
    row = np.arange(quarter)
    source = (row % block) * PIX + row // block
    hot = (source[:, None] == row[None, :]).astype(BF16)
    return jnp.asarray(hot), jnp.asarray(hot.T)


def split_rows(value):
    high = value.astype(BF16)
    rest = value - high.astype(F32)
    middle = rest.astype(BF16)
    low = (rest - middle.astype(F32)).astype(BF16)
    return jnp.concatenate([high, middle, low], axis=0)


def join_rows(stacked):
    rows = stacked.shape[0] // 3
    return stacked[2 * rows :] + stacked[rows : 2 * rows] + stacked[:rows]


def split_pair(value):
    high = value.astype(BF16)
    return high, (value - high.astype(F32)).astype(BF16)


def exact(left, right, left_dim, right_dim):
    return lax.dot_general(
        left,
        right,
        (((left_dim,), (right_dim,)), ((), ())),
        precision=lax.Precision.HIGHEST,
        preferred_element_type=F32,
    )


def over(count, body, start):
    return body(0, start) if count == 1 else lax.fori_loop(0, count, body, start)


def factor_inverse(work, inverse, subs, width):
    panel = 8
    lane = lax.broadcasted_iota(jnp.int32, (panel, width), 1)
    row = lax.broadcasted_iota(jnp.int32, (panel, 1), 0)
    row_small = lax.broadcasted_iota(jnp.int32, (panel, width), 0)
    together = min(subs, 2)

    def eliminate(s, first):
        rows = work[s, first : first + panel]
        for j in range(panel - 1):
            column = rows[:, first + j : first + j + 1]
            pivot = column[j : j + 1]
            ratio = jnp.where(row > j, column / pivot, 0.0)
            rows = rows - ratio * rows[j : j + 1]
        diagonal = jnp.sum(
            jnp.where(lane == row_small + first, rows[:, :width], 0.0), axis=1, keepdims=True
        )
        inverse[s, first : first + panel] = rows[:, width:] * lax.rsqrt(diagonal)
        if first + panel < width:
            scaled = rows[:, :width] / diagonal
            work[s, first + panel :] -= exact(scaled, rows, 0, 0)[first + panel :]

    def some(at, carry):
        for first in range(0, width, panel):
            for k in range(together):
                eliminate(at * together + k, first)
        return carry

    over(subs // together, some, 0)


def columns_of(row, column):
    tile = column.shape[1]

    def one(at, carry):
        cols = pl.ds(pl.multiple_of(at * tile, tile), tile)
        column[cols] = jnp.broadcast_to(row[:, cols].astype(F32), (tile, tile)).T
        return carry

    lax.fori_loop(0, row.shape[1] // tile, one, 0)


def whiten(embed, sub_col, image_col, image_row, partner_col, partner_row, refs, own_rows):
    work, inverse, white, unit, unit_parts, back = refs
    total, width = embed.shape
    subs = inverse.shape[0]
    eye = (
        lax.broadcasted_iota(jnp.int32, (width, width), 0)
        == lax.broadcasted_iota(jnp.int32, (width, width), 1)
    ).astype(F32)
    size = min(total, 512)
    pieces = total // size

    def rows_at(at):
        return pl.ds(pl.multiple_of(at * size, size), size)

    means = []
    for s in range(subs):

        def moments(at, sums, s=s):
            rows = rows_at(at)
            picked = embed[rows] * (sub_col[rows] == float(s)).astype(F32)
            first = sums[0] + jnp.sum(picked, axis=0, keepdims=True)
            return first, sums[1] + exact(picked, embed[rows], 0, 0)

        first, second = over(
            pieces, moments, (jnp.zeros((1, width), F32), jnp.zeros((width, width), F32))
        )
        mean = first / SUB
        work[s, :, :width] = second / SUB - exact(mean, mean, 0, 0) + RIDGE * eye
        work[s, :, width:] = eye
        means.append(mean)
    factor_inverse(work, inverse, subs, width)

    def whitening(at, carry):
        rows = rows_at(at)
        value = None
        for s in range(subs):
            mask = (sub_col[rows] == float(s)).astype(F32)
            term = exact((embed[rows] - means[s]) * mask, inverse[s], 1, 1)
            value = term if value is None else value + term
        white[rows] = value
        value = value * lax.rsqrt(jnp.sum(value * value, axis=1, keepdims=True) + EPS)
        unit[rows] = value
        high = value.astype(BF16)
        rest = value - high.astype(F32)
        middle = rest.astype(BF16)
        unit_parts[rows] = jnp.concatenate(
            [high, middle, (rest - middle.astype(F32)).astype(BF16)], axis=1
        )
        return carry

    over(pieces, whitening, 0)
    chunk = min(total, 262144 // total)

    def pairs(at, loss):
        rows = pl.ds(pl.multiple_of(at * chunk, chunk), chunk)
        across = lax.broadcasted_iota(jnp.int32, (chunk, total), 1).astype(F32)
        down = lax.broadcasted_iota(jnp.int32, (chunk, total), 0) + at * chunk

        def pick(hot):
            found = dot(hot.astype(F32).astype(BF16), unit_parts[...])
            return found[:, 2 * width :] + found[:, width : 2 * width] + found[:, :width]

        mine = unit[rows]
        ahead = pick(partner_col[rows][:, :1] == across)
        behind = pick(partner_row[...] == down)
        members = jnp.sum(
            (image_col[rows][:, :1] == image_row[...].astype(F32)).astype(F32), axis=1, keepdims=True
        )
        weight = 1.0 / members
        apart = mine - ahead
        grad = (4.0 / total) * weight * (2.0 * mine - ahead - behind)
        length = lax.rsqrt(jnp.sum(white[rows] * white[rows], axis=1, keepdims=True) + EPS)
        back[rows] = length * (grad - mine * jnp.sum(mine * grad, axis=1, keepdims=True))
        per_view = jnp.sum(apart * apart, axis=1, keepdims=True) * weight
        return loss + jnp.sum(per_view, axis=0, keepdims=True)

    loss = over(total // chunk, pairs, jnp.zeros((1, 1), F32)) * (2.0 / total)
    lower = lax.broadcasted_iota(jnp.int32, (width, width), 0) >= lax.broadcasted_iota(
        jnp.int32, (width, width), 1
    )
    own_white, own_back = white[own_rows], back[own_rows]
    gradient = jnp.zeros(own_white.shape, F32)
    for s in range(subs):

        def pulled(at, sums, s=s):
            rows = rows_at(at)
            picked = back[rows] * (sub_col[rows] == float(s)).astype(F32)
            spread = sums[0] + jnp.sum(picked, axis=0, keepdims=True)
            return spread, sums[1] + exact(picked, white[rows], 0, 0)

        spread, sums = over(
            pieces, pulled, (jnp.zeros((1, width), F32), jnp.zeros((width, width), F32))
        )
        low_part = jnp.where(lower, sums, 0.0)
        mirrored = low_part + low_part.T - sums * eye
        moved = own_back - (exact(own_white, mirrored, 1, 0) + spread) / SUB
        own_mask = (sub_col[own_rows] == float(s)).astype(F32)
        gradient = gradient + own_mask * exact(moved, inverse[s], 1, 0)
    return loss, gradient


def head_body(
    views, gain_last, shift_last, gain_head, shift_head, sub_row, image_row, partner_row, stat2, pool,
    act_any, w3_any, x_any, head_first_any, head_last_any, w2in, h2,
    h3_out, slope_out, pooled_all, w2_late, h2q,
    stat3, grad_shift_last, grad_gain_last, grad_shift_head, grad_gain_head,
    grad_pooled_out, act4, grad_embed_out, grad_p1, loss_out, stats2, pooled_means,
    act, w3, x, head_first, head_last, h3, slope, pooled_own, pooled_low, sub_col, image_col, partner_col,
    embed_all, part, part_in, mean_sums, slope_sums, st3, slots3, st4, slots4, bk4, bslots4, bk3, bslots3, embed_own,
    work, inverse, white, unit, unit_parts, back,
    sends, recvs, group_sends, group_recvs, local_sems,
):
    view_at, chan_at, y, c = place()
    mate, opposite = (view_at, 2 * y + 1 - c), (view_at, 2 * (1 - y) + c)
    group = view_group(views)
    quarter, width = h3.shape[1], h3.shape[2]
    block = quarter // PIX
    views_own = 4 * block
    met = greet([mate, opposite], [group])
    local = Local(local_sems)
    w3_here = local.fetch(w3_any, w3)
    act_here = [local.fetch(act_any.at[:, q], act.at[:, q]) for q in range(4)]
    x_here = local.fetch(x_any, x)
    head_first_here = local.fetch(head_first_any, head_first)
    head_last_here = local.fetch(head_last_any, head_last)
    rest = [local.fetch(h2.at[y], h2q.at[y])]
    own_out = pl.ds(pl.multiple_of(width * c, width), width)
    st3[...] = jnp.zeros(st3.shape, F32)
    w3_here.wait()
    for q in range(4):
        act_here[q].wait()

    def last_conv(q, carry):
        total = None
        for half in range(2):
            weight = jnp.concatenate([w3[2 * half, own_out], w3[2 * half + 1, own_out]], axis=1)
            term = dot_nt(act[half, q], weight)
            total = term if total is None else total + term
        low = total.astype(BF16)
        h3[q] = low
        value = low.astype(F32)
        st3[0:1] += jnp.sum(value, axis=0, keepdims=True)
        st3[1:2] += jnp.sum(value * value, axis=0, keepdims=True)
        return carry

    lax.fori_loop(0, 4, last_conv, 0)
    met()
    share_start(st3, slots3, group_sends.at[0], group_recvs.at[0], group)
    rest.append(local.fetch(h3, h3_out))
    for row, column in ((sub_row, sub_col), (image_row, image_col), (partner_row, partner_col)):
        columns_of(row, column)
    share_end(st3, slots3, group_sends.at[0], group_recvs.at[0], group)
    totals = add_slots(slots3, views)
    count = float(views * 4 * quarter)
    mean = totals[0:1] / count
    rstd = lax.rsqrt(totals[1:2] / count - mean * mean + EPS)
    stat3[...] = jnp.concatenate([mean, rstd], axis=0)
    scale = rstd * gain_last[...]
    bias = shift_last[...] - mean * scale
    x_here.wait()

    def pool_block(q, carry):
        before = x[q].astype(F32) + (h3[q].astype(F32) * scale + bias)
        after = before * gate(before)
        high, low = split_pair(after)
        sums = dot(pool[...], high) + dot(pool[...], low)
        pooled_own[pl.ds(pl.multiple_of(q * block, block), block)] = sums * (1.0 / PIX)
        return carry

    lax.fori_loop(0, 4, pool_block, 0)
    mail = Mail(sends, recvs)
    head_first_here.wait()
    hidden = join_rows(dot(split_rows(pooled_own[...]), head_first[...]))
    wide = hidden.shape[1] // 2
    part[0] = hidden[:, :wide]
    part[1] = hidden[:, wide:]
    beside = mail.send(part, part_in.at[pl.ds(0, 2)], mate)

    def slope_block(q, carry):
        level3 = h3[q].astype(F32)
        before = x[q].astype(F32) + (level3 * scale + bias)
        low = silu_slope(before).astype(BF16)
        slope[q] = low
        normed = (level3 - mean) * rstd
        high_part, low_part = split_pair(low.astype(F32) * normed)
        rows = pl.ds(pl.multiple_of(q * block, block), block)
        slope_sums[0, rows] = dot(pool[...], low)
        slope_sums[1, rows] = dot(pool[...], high_part) + dot(pool[...], low_part)
        return carry

    beside.wait()
    mean_sums[...] = part[...] + part_in[0:2]
    across = mail.send(mean_sums.at[c], part_in.at[2], opposite)
    stats2[y] = stat2[...]
    stat2_far = mail.send(stat2, stats2.at[y], opposite)
    lax.fori_loop(0, 2, slope_block, 0)
    across.wait_recv()
    part_in[4 + c] = mean_sums[c] + part_in[2]
    gathered = mail.send(part_in.at[4 + c], part_in.at[4 + c], mate)
    h2_far = mail.send(h2.at[1 - y], h2q.at[y], opposite)
    late_rows = pl.ds(w2in.shape[0] - w2_late.shape[1], w2_late.shape[1])
    w2_over = mail.send(w2in.at[late_rows], w2_late.at[c], opposite)
    gathered.wait_recv()
    p1 = part_in[4:6]
    st4[0:2] = jnp.sum(p1, axis=1)
    st4[2:4] = jnp.sum(p1 * p1, axis=1)
    share_start(st4, slots4, group_sends.at[1], group_recvs.at[1], group)
    lax.fori_loop(2, 4, slope_block, 0)
    rest.append(local.fetch(slope, slope_out))
    share_end(st4, slots4, group_sends.at[1], group_recvs.at[1], group)
    totals4 = add_slots(slots4, views)
    count4 = float(views * views_own)
    mean4 = totals4[0:2] / count4
    rstd4 = lax.rsqrt(totals4[2:4] / count4 - mean4 * mean4 + EPS)
    head_last_here.wait()

    def level4(half):
        cols = slice(half * wide, (half + 1) * wide)
        normed = (part_in[4 + half] - mean4[half : half + 1]) * rstd4[half : half + 1]
        return normed, normed * gain_head[:, cols] + shift_head[:, cols]

    embed = None
    for half in range(2):
        normed, level = level4(half)
        value = level * gate(level)
        act4[half] = value
        term = join_rows(dot(split_rows(value), head_last[half * wide : (half + 1) * wide]))
        embed = term if embed is None else embed + term
    embed_own[...] = embed
    share_start(embed_own, embed_all, group_sends.at[2], group_recvs.at[2], group)
    share_end(embed_own, embed_all, group_sends.at[2], group_recvs.at[2], group)
    pooled_mean = jnp.sum(pooled_own[...], axis=0, keepdims=True) / views_own
    bk3[2:3] = pooled_mean
    pooled_low[...] = (pooled_own[...] - pooled_mean).astype(BF16)
    gather_start(pooled_low, pooled_all, group_sends.at[5], group_recvs.at[5], group)
    rest.append(local.fetch(pooled_low, pooled_all.at[view_at]))
    own_rows = pl.ds(pl.multiple_of(view_at * views_own, views_own), views_own)
    every = embed_all.reshape(views * views_own, embed.shape[1])
    loss, grad_embed = whiten(
        every, sub_col, image_col, image_row, partner_col, partner_row,
        (work, inverse, white, unit, unit_parts, back), own_rows,
    )
    loss_out[...] = loss
    grad_embed_out[...] = grad_embed
    stacked = split_rows(grad_embed)
    for half in range(2):
        normed, level = level4(half)
        grad = join_rows(dot_nt(stacked, head_last[half * wide : (half + 1) * wide]))
        grad = grad * silu_slope(level)
        part[half] = grad
        bk4[half : half + 1] = jnp.sum(grad, axis=0, keepdims=True)
        bk4[2 + half : 3 + half] = jnp.sum(grad * normed, axis=0, keepdims=True)
    tot4 = share(bk4, bslots4, group_sends.at[3], group_recvs.at[3], group)
    grad_pooled = None
    for half in range(2):
        cols = slice(half * wide, (half + 1) * wide)
        normed, level = level4(half)
        shift_sum, gain_sum = tot4[half : half + 1], tot4[2 + half : 3 + half]
        grad_shift_head[:, cols] = shift_sum
        grad_gain_head[:, cols] = gain_sum
        grad = (
            gain_head[:, cols]
            * rstd4[half : half + 1]
            * (part[half] - shift_sum / count4 - normed * (gain_sum / count4))
        )
        grad_p1[half] = grad
        term = join_rows(dot_nt(split_rows(grad), head_first[:, cols]))
        grad_pooled = term if grad_pooled is None else grad_pooled + term
    grad_pooled = grad_pooled * (1.0 / PIX)
    grad_pooled_out[...] = grad_pooled
    bk3[0:1] = jnp.sum(grad_pooled * slope_sums[0], axis=0, keepdims=True)
    bk3[1:2] = jnp.sum(grad_pooled * slope_sums[1], axis=0, keepdims=True)
    share_start(bk3, bslots3, group_sends.at[4], group_recvs.at[4], group)
    w2_over.wait_recv()
    w2_on = mail.send(w2_late.at[c], w2_late.at[c], mate)
    share_end(bk3, bslots3, group_sends.at[4], group_recvs.at[4], group)
    tot3 = add_slots(bslots3, views)
    grad_shift_last[...] = tot3[0:1]
    grad_gain_last[...] = tot3[1:2]
    pooled_means[...] = bslots3[:, 2]
    h2_far.wait_recv()
    stat2_far.wait_recv()
    w2_on.wait_recv()
    share_end(pooled_low, pooled_all, group_sends.at[5], group_recvs.at[5], group)
    for copy in rest:
        copy.wait()
    for copy in mail.copies[1:]:
        copy.wait_send()


def head_stage(
    views, vectors, tables, stat2, pool, act, w3, x, head_first, head_last, w2in, h2
):
    quarter, width = act.shape[2], x.shape[1]
    block = quarter // PIX
    own = 4 * block
    total = views * own
    hid, emb = head_last.shape
    wide = hid // 2
    subs = total // SUB
    taps = w2in.shape[0]
    vm = pltpu.VMEM
    return call(
        functools.partial(head_body, views),
        "head",
        (
            shape(4, quarter, width, kind=BF16),
            shape(4, quarter, width, kind=BF16),
            shape(views, own, width, kind=BF16),
            shape(2, taps // 9 * (9 - EARLY_TAPS), w2in.shape[1], kind=BF16),
            shape(*h2.shape, kind=BF16),
            shape(2, width),
            shape(1, width),
            shape(1, width),
            shape(1, hid),
            shape(1, hid),
            shape(own, width),
            shape(2, own, wide),
            shape(own, emb),
            shape(2, own, wide),
            shape(1, 1),
            shape(2, *stat2.shape),
            shape(views, width),
        ),
        16,
        [
            vm(act.shape, BF16),
            vm(w3.shape, BF16),
            vm((4, quarter, width), BF16),
            vm(head_first.shape, BF16),
            vm(head_last.shape, BF16),
            vm((4, quarter, width), BF16),
            vm((4, quarter, width), BF16),
            vm((own, width), F32),
            vm((own, width), BF16),
            vm((total, 128), F32),
            vm((total, 128), F32),
            vm((total, 128), F32),
            vm((views, own, emb), F32),
            vm((2, own, wide), F32),
            vm((6, own, wide), F32),
            vm((2, own, wide), F32),
            vm((2, own, width), F32),
            vm((2, width), F32),
            vm((views, 2, width), F32),
            vm((4, wide), F32),
            vm((views, 4, wide), F32),
            vm((4, wide), F32),
            vm((views, 4, wide), F32),
            vm((3, width), F32),
            vm((views, 3, width), F32),
            vm((own, emb), F32),
            vm((subs, emb, 2 * emb), F32),
            vm((subs, emb, emb), F32),
            vm((total, emb), F32),
            vm((total, emb), F32),
            vm((total, 3 * emb), BF16),
            vm((total, emb), F32),
            dma(8),
            dma(8),
            dma(6, views),
            dma(6, views),
            dma(16),
        ],
        collective=3,
        any_ins=range(9, 16),
        any_outs=range(5),
    )(
        *vectors, *tables, stat2, pool, act, w3, x.reshape(4, quarter, width),
        head_first, head_last, w2in, h2,
    )


def link_kind(rows):
    return BF16 if rows % 16 == 0 else F32


def back_body(
    views, stat3, grad_shift_last, grad_gain_last, grad_pooled, gain_last, expand,
    stats2, smalls, stat1, act4, grad_embed, grad_p1, pooled_means,
    h3_any, slope_any, w3_any, h2q_any, perm_any, unperm_any, pad_any, h1q_any, w2_any,
    w2_early_any, w2_late_any, act_any, x_any, pooled_any,
    gh1_out, mid_slots, pair_out, head_last_out, head_first_out,
    grad_shift_mid, grad_gain_mid, grad_shift_first, grad_gain_first,
    h3, slope, w3, h2q, gh1, gh3, gh3_mate, out_part, in_part, ga2, gh2, gh2_far, gpad, ga1, st, chan_slots, view_slots,
    order, pad, h1q, w2, w2_far, act, pooled,
    wsum, wsend, mid_parts, last_parts, last_slots, first_slots, pair_parts,
    hl_parts, hl_slots, p1_parts, p1_slots,
    sends, recvs, chan_sends, chan_recvs, group_sends, group_recvs, pair_sends, pair_recvs, local_sems,
):
    view_at, chan_at, y, c = place()
    mate, opposite = (view_at, 2 * y + 1 - c), (view_at, 2 * (1 - y) + c)
    group, chans, everyone = view_group(views), chan_group(), all_group(views)
    quarter, width = h3.shape[1], h3.shape[2]
    block = quarter // PIX
    half_width = h2q.shape[2]
    met = greet([], [everyone])
    local = Local(local_sems)
    near_half, own_half = [2 * i + 1 - c for i in range(2)], [2 * i + c for i in range(2)]
    rows_here = []
    for q in near_half + own_half:
        rows_here.append((local.fetch(h3_any.at[q], h3.at[q]), local.fetch(slope_any.at[q], slope.at[q])))
    w3_here = local.fetch(w3_any, w3)
    perm_here = local.fetch(perm_any, order)
    act_here = local.fetch(act_any, act)
    h2q_here = local.fetch(h2q_any, h2q)
    w2_here = local.fetch(w2_any, w2)
    early = w2_early_any.shape[1]
    w2_far_here = [
        local.fetch(w2_early_any, w2_far.at[:, pl.ds(0, early)]),
        local.fetch(w2_late_any, w2_far.at[:, pl.ds(early, w2_far.shape[1] - early)]),
    ]
    h1q_here = local.fetch(h1q_any, h1q)
    pad_here = local.fetch(pad_any, pad)
    count = float(views * 4 * quarter)
    mean, rstd = stat3[0:1], stat3[1:2]
    scale = rstd * gain_last[...]
    shift_part, gain_part = grad_shift_last[...] / count, grad_gain_last[...] / count

    def grad_rows(q):
        rows = pl.ds(pl.multiple_of(q * block, block), block)
        high, low = split_pair(grad_pooled[rows])
        spread = dot(expand[...], jnp.concatenate([high, low], axis=0))
        grad = spread * slope[q].astype(F32)
        normed = (h3[q].astype(F32) - mean) * rstd
        gh3[q] = (scale * (grad - shift_part - normed * gain_part)).astype(BF16)

    mail = Mail(sends, recvs)
    beside = []
    for i in (0, 1):
        for copy in rows_here[i]:
            copy.wait()
        grad_rows(2 * i + 1 - c)
        if i == 0:
            met()
        beside.append(mail.send(gh3.at[2 * i + 1 - c], gh3_mate.at[i], mate))
    for i in (0, 1):
        for copy in rows_here[2 + i]:
            copy.wait()
        grad_rows(2 * i + c)
    for copy in beside:
        copy.wait_recv()
    mate_out = pl.ds(pl.multiple_of(width * (1 - c), width), width)
    own_out = pl.ds(pl.multiple_of(width * c, width), width)

    def part_of(i):
        def weight(rows):
            return jnp.concatenate([w3[k, rows] for k in range(4)], axis=1)

        value = dot(gh3[2 * i + c], weight(own_out)) + dot(gh3_mate[i], weight(mate_out))
        return dot(order[...], value.astype(BF16))

    w3_here.wait()
    perm_here.wait()
    out_part[...] = part_of(1 - y).astype(BF16)
    across = mail.send(out_part, in_part, opposite)
    ga2[...] = part_of(y)
    unperm_here = local.fetch(unperm_any, order)

    hid_block, hid_split = hl_parts.shape[1], head_last_out.shape[0]
    for half in range(2):
        product = exact(act4[half], grad_embed[...], 0, 0)
        ga1[: product.shape[0], : product.shape[1]] = product
        per_half = views // 2

        def spread_hidden(to, carry, half=half, per_half=per_half):
            spot = (4 * to + chan_at) * hid_block if hid_split == 4 else to * hid_block
            rows = pl.ds(pl.multiple_of(spot, hid_block), hid_block)
            hl_parts[half * per_half + to] = ga1[rows, : hl_parts.shape[2]]
            return carry

        lax.fori_loop(0, per_half, spread_hidden, 0)
        wide = grad_p1.shape[2] // per_half
        for to in range(per_half):
            p1_parts[half * per_half + to] = grad_p1[half, :, to * wide : (to + 1) * wide]
    scatter_start(hl_parts, hl_slots, group_sends.at[0], group_recvs.at[0], group)
    scatter_start(p1_parts, p1_slots, group_sends.at[1], group_recvs.at[1], group)
    act_here.wait()
    share_rows = last_parts.shape[1]
    for half in range(2):
        total = None
        for q in range(4):
            term = dot_tn(gh3[q], act[half, q])
            total = term if total is None else total + term
        low = total.astype(last_parts.dtype)
        for to in range(views):
            last_parts[to, :, half * half_width : (half + 1) * half_width] = low[
                to * share_rows : (to + 1) * share_rows
            ]
    scatter_start(last_parts, last_slots, group_sends.at[2], group_recvs.at[2], group)
    for copy in beside:
        copy.wait_send()
    x = gh3
    x_here = local.fetch(x_any, x)
    h2q_here.wait()

    def sums_everywhere(at):
        return share(
            share_value(st, chan_slots.at[at], chan_sends.at[at], chan_recvs.at[at], chans),
            view_slots.at[at], group_sends.at[3 + at], group_recvs.at[3 + at], group,
        )

    def share_value(source, slots, send, recv, who):
        source[...] = share(source, slots, send, recv, who)
        return source

    gpad[...] = jnp.zeros(gpad.shape, gpad.dtype)
    across.wait()
    ga2[...] += in_part[...].astype(F32)
    halves = (y, 1 - y)

    def mid_norm(near):
        half = halves[near]
        gains = jnp.concatenate([smalls[2 * half], smalls[2 * half + 1]], axis=1)
        mean2, rstd2 = stats2[half, 0:1], stats2[half, 1:2]
        return mean2, rstd2, gains[2:3], gains[3:4]

    def half_cols(ref, near):
        low, high = ref[:, :half_width], ref[:, half_width:]
        return jnp.where(halves[near] == 0, low, high)

    for near in range(2):
        mean2, rstd2, gain2, shift2 = mid_norm(near)
        normed = (h2q[halves[near]].astype(F32) - mean2) * rstd2
        grad = half_cols(ga2, near) * silu_slope(normed * gain2 + shift2)
        ga1[:, near * half_width : (near + 1) * half_width] = grad
        st[halves[near], 0:1] = jnp.sum(grad, axis=0, keepdims=True)
        st[halves[near], 1:2] = jnp.sum(grad * normed, axis=0, keepdims=True)
    totals2 = sums_everywhere(0)
    view_slots[0, 0] = totals2
    for near in range(2):
        mean2, rstd2, gain2, shift2 = mid_norm(near)
        tot = view_slots[0, 0, halves[near]]
        normed = (h2q[halves[near]].astype(F32) - mean2) * rstd2
        grad = ga1[:, near * half_width : (near + 1) * half_width]
        low = (gain2 * rstd2 * (grad - tot[0:1] / count - normed * (tot[1:2] / count))).astype(BF16)
        gh2[near] = low
        gpad[near, 1 : SIDE + 1, 1 : SIDE + 1] = low.reshape(SIDE, SIDE, block, half_width)
    tot = view_slots[0, 0, y]
    own_cols = jnp.where(c == 0, tot[:, : half_width // 2], tot[:, half_width // 2 :])
    grad_shift_mid[...] = own_cols[0:1]
    grad_gain_mid[...] = own_cols[1:2]
    far_copy = mail.send(gh2.at[1], gh2_far, opposite)
    w2_here.wait()
    for copy in w2_far_here:
        copy.wait()
    channels = w2.shape[1] // 9
    for tap in range(9):
        a, b = 2 - tap // 3, 2 - tap % 3
        taps = slice(tap * channels, (tap + 1) * channels)
        term = None
        for near, weight in enumerate((w2, w2_far)):
            window = gpad[near, a : a + SIDE, b : b + SIDE].reshape(quarter, half_width)
            both = jnp.concatenate([weight[0, taps], weight[1, taps]], axis=1)
            piece = dot_nt(window, both)
            term = piece if term is None else term + piece
        if tap == 0:
            ga1[...] = term
        else:
            ga1[...] += term
    h1q_here.wait()
    for half in range(2):
        gains = jnp.concatenate([smalls[2 * half], smalls[2 * half + 1]], axis=1)
        normed = (h1q[half] - stat1[half, 0:1]) * stat1[half, 1:2]
        cols = slice(half * half_width, (half + 1) * half_width)
        grad = ga1[:, cols] * silu_slope(normed * gains[0:1] + gains[1:2])
        ga2[:, cols] = grad
        st[half, 0:1] = jnp.sum(grad, axis=0, keepdims=True)
        st[half, 1:2] = jnp.sum(grad * normed, axis=0, keepdims=True)
    totals1 = sums_everywhere(1)
    view_slots[1, 0] = totals1
    tot = view_slots[1, 0, y]
    own_cols = jnp.where(c == 0, tot[:, : half_width // 2], tot[:, half_width // 2 :])
    grad_shift_first[...] = own_cols[0:1]
    grad_gain_first[...] = own_cols[1:2]
    unperm_here.wait()
    for half in range(2):
        gains = jnp.concatenate([smalls[2 * half], smalls[2 * half + 1]], axis=1)
        normed = (h1q[half] - stat1[half, 0:1]) * stat1[half, 1:2]
        cols = slice(half * half_width, (half + 1) * half_width)
        tot = totals1[half]
        low = (
            gains[0:1]
            * stat1[half, 1:2]
            * (ga2[:, cols] - tot[0:1] / count - normed * (tot[1:2] / count))
        ).astype(BF16)
        out_part[:, cols] = low
    gh1[chan_at] = dot(order[...], out_part[...]).astype(BF16)
    spot = gh1.at[chan_at]
    gh1_across = mail.send(spot, spot, opposite)
    gh1_beside = mail.send(spot, spot, mate)

    far_copy.wait_recv()
    pad_here.wait()
    for tap in range(9):
        a, b = tap // 3, tap % 3

        def tap_term(at, grads):
            window = pad[at, a : a + SIDE, b : b + SIDE].reshape(quarter, channels)
            return dot_tn(window, grads)

        total = tap_term(y, gh2[0]) + tap_term(1 - y, gh2_far[...])
        taps = slice(tap * channels, (tap + 1) * channels)
        wsum[0, taps] = total[:, : half_width // 2]
        wsum[1, taps] = total[:, half_width // 2 :]
    mid_rows = mid_parts.shape[1]
    mid_flat = mid_parts.reshape(views * mid_rows, mid_parts.shape[2])
    if mid_parts.dtype == F32:
        mid_mate = mail.send(wsum.at[1 - c], mid_flat, mate)
    else:
        wsend[...] = wsum[1 - c].astype(wsend.dtype)
        mid_mate = mail.send(wsend, mid_flat, mate)
    scatter_end(p1_parts, p1_slots, group_sends.at[1], group_recvs.at[1], group)
    few = pooled.shape[0]

    def head_first_term(at, total):
        views_at = pl.ds(at * few, few)
        copy = pltpu.make_async_copy(pooled_any.at[views_at], pooled, local_sems.at[29])
        copy.start()
        copy.wait()
        rows = pooled[...].astype(F32).reshape(-1, width)
        return total + exact(rows, p1_slots[views_at].reshape(rows.shape[0], -1), 0, 0)

    head_first_out[...] = over(
        views // few, head_first_term, exact(pooled_means[...], jnp.sum(p1_slots[...], axis=1), 0, 0)
    )
    mid_mate.wait_recv()

    def mid_block(to, carry):
        rows = pl.ds(pl.multiple_of(to * mid_rows, mid_rows), mid_rows)
        mid_parts[to] = (wsum[c, rows] + mid_parts[to].astype(F32)).astype(mid_parts.dtype)
        return carry

    lax.fori_loop(0, views, mid_block, 0)
    scatter_start(mid_parts, mid_slots, group_sends.at[5], group_recvs.at[5], group, False)
    rest = [local.fetch(mid_parts.at[view_at], mid_slots.at[view_at])]
    gh1_across.wait_recv()
    far_spot = gh1.at[2 * (1 - y) + c]
    gh1_on = mail.send(far_spot, far_spot, mate)
    gh1_beside.wait_recv()
    gh1_on.wait_recv()
    rest.append(local.fetch(gh1, gh1_out))
    x_here.wait()
    scatter_end(last_parts, last_slots, group_sends.at[2], group_recvs.at[2], group)
    first_parts = last_parts
    total = None
    for q in range(4):
        term = dot_tn(x[q], gh1[q])
        total = term if total is None else total + term
    low = total.astype(first_parts.dtype)
    for to in range(views):
        first_parts[to] = low[to * share_rows : (to + 1) * share_rows]
    scatter_start(first_parts, first_slots, group_sends.at[6], group_recvs.at[6], group)

    scatter_end(hl_parts, hl_slots, group_sends.at[0], group_recvs.at[0], group)
    if hid_split == 4:
        head_last_out[chan_at] = add_slots(hl_slots, views)
        gather_start(head_last_out.at[chan_at], head_last_out, chan_sends.at[2], chan_recvs.at[2], chans)
    else:
        head_last_out[0] = add_slots(hl_slots, views)

    def blocks(kind, summed):
        wide = summed.shape[1] // 4
        for to in range(4):
            pair_parts[to, kind] = summed[:, to * wide : (to + 1) * wide]

    def summed_slots(slots):
        def add(at, total):
            return total + slots[at].astype(F32)

        return lax.fori_loop(1, views, add, slots[0].astype(F32))

    blocks(1, summed_slots(last_slots))
    scatter_end(first_parts, first_slots, group_sends.at[6], group_recvs.at[6], group)
    blocks(0, summed_slots(first_slots))
    row_views = views // 4
    to_view = chan_at * row_views + lax.div(view_at, 4)
    slot = lax.rem(view_at, 4)

    def pair_copy(to):
        return pltpu.make_async_remote_copy(
            src_ref=pair_parts.at[to],
            dst_ref=pair_out.at[slot],
            send_sem=pair_sends.at[to],
            recv_sem=pair_recvs.at[slot],
            device_id=(to_view, to),
            device_id_type=MESH,
        )

    def pair_arrival(origin):
        return pltpu.make_async_remote_copy(
            src_ref=pair_parts.at[0],
            dst_ref=pair_out.at[origin],
            send_sem=pair_sends.at[0],
            recv_sem=pair_recvs.at[origin],
            device_id=(from_view + origin, from_chan),
            device_id_type=MESH,
        )

    from_view, from_chan = 4 * lax.rem(view_at, row_views), lax.div(view_at, row_views)
    for to in range(4):
        own = jnp.logical_and(to_view == view_at, chan_at == to)

        @pl.when(own)
        def _():
            pair_out[slot] = pair_parts[to]

        @pl.when(jnp.logical_not(own))
        def _():
            pair_copy(to).start()

    for origin in range(4):
        own = jnp.logical_and(from_view + origin == view_at, chan_at == from_chan)

        @pl.when(jnp.logical_not(own))
        def _():
            pair_arrival(origin).wait_recv()

    for to in range(4):
        own = jnp.logical_and(to_view == view_at, chan_at == to)

        @pl.when(jnp.logical_not(own))
        def _():
            pair_copy(to).wait_send()

    if hid_split == 4:
        share_end(head_last_out.at[chan_at], head_last_out, chan_sends.at[2], chan_recvs.at[2], chans)
    scatter_end(mid_parts, mid_slots, group_sends.at[5], group_recvs.at[5], group)
    for copy in rest:
        copy.wait()
    for copy in mail.copies[3:]:
        copy.wait_send()


def back_stage(views, head_outs, forward_outs, x, gain_last, perm, unperm, expand):
    (h3, slope, pooled_all, w2_late, h2q, stat3, grad_shift_last, grad_gain_last, _, _,
     grad_pooled, act4, grad_embed, grad_p1, _, stats2, pooled_means) = head_outs
    pad, h1q, w2, w2_early, w3, act, _, stat1, _, _, smalls = forward_outs
    quarter, width = h3.shape[1], h3.shape[2]
    block = quarter // PIX
    own = 4 * block
    mid = pad.shape[4]
    half = mid // 2
    hid, emb = 2 * act4.shape[2], grad_embed.shape[1]
    taps = w2.shape[1]
    hid_split = 4 if hid // views % 32 == 0 else 1
    hid_block = hid // views // hid_split
    mid_kind, row_kind = link_kind(taps // views), link_kind(width // views)
    vm = pltpu.VMEM
    return call(
        functools.partial(back_body, views),
        "back",
        (
            shape(4, quarter, mid, kind=BF16),
            shape(views, taps // views, half // 2, kind=mid_kind),
            shape(4, 2, width // views, mid // 4),
            shape(hid_split, hid_block, emb),
            shape(width, hid // views),
            *[shape(1, half // 2)] * 4,
        ),
        27,
        [
            vm((4, quarter, width), BF16),
            vm((4, quarter, width), BF16),
            vm(w3.shape, BF16),
            vm(h2q.shape, BF16),
            vm((4, quarter, mid), BF16),
            vm((4, quarter, width), BF16),
            vm((2, quarter, width), BF16),
            vm((quarter, mid), BF16),
            vm((quarter, mid), BF16),
            vm((quarter, mid), F32),
            vm((2, quarter, half), BF16),
            vm((quarter, half), BF16),
            vm((2, PAD, PAD, block, half), BF16),
            vm((quarter, mid), F32),
            vm((2, 2, half), F32),
            vm((2, 4, 2, 2, half), F32),
            vm((2, views, 2, 2, half), F32),
            vm(unperm.shape, BF16),
            vm(pad.shape, BF16),
            vm(h1q.shape, F32),
            vm(w2.shape, BF16),
            vm(w2.shape, BF16),
            vm(act.shape, BF16),
            vm((min(views, 8), own, width), BF16),
            vm((2, taps, half // 2), F32),
            vm((taps if mid_kind == BF16 else 16, half // 2), BF16),
            vm((views, taps // views, half // 2), mid_kind),
            vm((views, width // views, mid), row_kind),
            vm((views, width // views, mid), row_kind),
            vm((views, width // views, mid), row_kind),
            vm((4, 2, width // views, mid // 4), F32),
            vm((views, hid_block, emb), F32),
            vm((views, hid_block, emb), F32),
            vm((views, own, hid // views), F32),
            vm((views, own, hid // views), F32),
            dma(10),
            dma(10),
            dma(3, 4),
            dma(3, 4),
            dma(7, views),
            dma(7, views),
            dma(4),
            dma(4),
            dma(30),
        ],
        collective=4,
        any_ins=range(13, 27),
        any_outs=range(2),
    )(
        stat3, grad_shift_last, grad_gain_last, grad_pooled, gain_last, expand,
        stats2, smalls, stat1, act4, grad_embed, grad_p1, pooled_means,
        h3, slope, w3, h2q, perm, unperm, pad, h1q, w2, w2_early, w2_late, act,
        x.reshape(4, quarter, width), pooled_all,
    )


def last_body(
    gh1, w1_own, slope, grad_pooled, expand, mid_slots, pair_out, head_last_in, head_first_in, *more
):
    small_ins, small_outs = more[: len(more) // 2 - 3], more[len(more) // 2 + 3 :]
    grad_input, grad_mid, grad_first, grad_last, grad_head_last, grad_head_first = more[
        len(small_ins) : len(small_ins) + 6
    ]
    at = pl.program_id(0)
    high, low = split_pair(grad_pooled[...])
    spread = dot(expand[...], jnp.concatenate([high, low], axis=0))
    grad_input[...] = dot_nt(gh1[...], w1_own[...]) + spread * slope[...].astype(F32)

    @pl.when(at == 0)
    def _():
        views = mid_slots.shape[0]

        def add(slot, total):
            return total + mid_slots[slot].astype(F32)

        grad_mid[...] = lax.fori_loop(1, views, add, mid_slots[0].astype(F32))
        rows = pair_out.shape[2]
        for origin in range(4):
            grad_first[origin * rows : (origin + 1) * rows] = pair_out[origin, 0]
            grad_last[origin * rows : (origin + 1) * rows] = pair_out[origin, 1]
        for source, target in zip(small_ins, small_outs):
            target[...] = source[...]
        grad_head_first[...] = head_first_in[...]
        rows = head_last_in.shape[1]
        for origin in range(head_last_in.shape[0]):
            grad_head_last[origin * rows : (origin + 1) * rows] = head_last_in[origin]


def last_stage(gh1, w1_own, slope, grad_pooled, mid_slots, pair_out, head_last_in, head_first_in, small):
    rows, mid, width = 4 * gh1.shape[1], gh1.shape[2], slope.shape[2]
    own = rows // PIX
    hot = np.arange(rows)[:, None] // PIX == np.arange(2 * own)[None, :] % own
    steps = 7

    def whole(array):
        dims = array.shape
        return pl.BlockSpec(dims, lambda q: (0,) * len(dims))

    def part(columns):
        return pl.BlockSpec((rows // steps, columns), lambda q: (q, 0))

    outs = (
        shape(rows, width),
        shape(*mid_slots.shape[1:]),
        shape(4 * pair_out.shape[2], pair_out.shape[3]),
        shape(4 * pair_out.shape[2], pair_out.shape[3]),
        shape(head_last_in.shape[0] * head_last_in.shape[1], head_last_in.shape[2]),
        shape(*head_first_in.shape),
        *[shape(*array.shape) for array in small],
    )
    return pl.pallas_call(
        last_body,
        grid=(steps,),
        out_shape=outs,
        in_specs=[
            part(mid), whole(w1_own), part(width), whole(grad_pooled), part(2 * own),
            whole(mid_slots), whole(pair_out), whole(head_last_in), whole(head_first_in),
            *[whole(array) for array in small],
        ],
        out_specs=(part(width), *(whole(out) for out in outs[1:])),
        name="results",
        compiler_params=pltpu.CompilerParams(
            vmem_limit_bytes=VMEM_BYTES, dimension_semantics=("arbitrary",)
        ),
    )(
        gh1.reshape(rows, mid), w1_own, slope.reshape(rows, width), grad_pooled,
        jnp.asarray(hot.astype(BF16)), mid_slots, pair_out, head_last_in, head_first_in, *small,
    )


def per_device(
    views,
    block_input,
    conv_first,
    conv_mid,
    conv_last,
    gain_first,
    shift_first,
    gain_mid,
    shift_mid,
    gain_last,
    shift_last,
    head_first,
    gain_head,
    shift_head,
    head_last,
    image_of,
    partner,
    sub_of,
):
    rows, width = block_input.shape
    quarter = rows // 4
    block = quarter // PIX
    perm, unperm = orders(quarter)
    at_row = np.arange(quarter)
    pool = jnp.asarray((at_row[None, :] // PIX == np.arange(block)[:, None]).astype(BF16))
    twice = np.arange(2 * block) % block
    expand = jnp.asarray((at_row[:, None] // PIX == twice[None, :]).astype(BF16))

    def line(vector):
        return vector.reshape(1, -1)

    forward_outs = forward_stage(
        views, block_input, conv_first, conv_mid, conv_last,
        [line(v) for v in (gain_first, shift_first, gain_mid, shift_mid)], perm, unperm,
    )
    w3, act, h2, stat2, w1_own = (forward_outs[at] for at in (4, 5, 6, 8, 9))
    head_outs = head_stage(
        views, [line(v) for v in (gain_last, shift_last, gain_head, shift_head)],
        [line(v) for v in (sub_of, image_of, partner)], stat2, pool,
        act, w3, block_input, head_first, head_last, conv_mid, h2,
    )
    slope, grad_pooled, loss = head_outs[1], head_outs[10], head_outs[14]
    (gh1, mid_slots, pair_out, head_last_in, head_first_in,
     grad_shift_mid, grad_gain_mid, grad_shift_first, grad_gain_first) = back_stage(
        views, head_outs, forward_outs, block_input, line(gain_last), perm, unperm, expand
    )
    small = [
        grad_gain_first, grad_shift_first, grad_gain_mid, grad_shift_mid,
        head_outs[7], head_outs[6], head_outs[9], head_outs[8], loss,
    ]
    grad_input, grad_mid, grad_first, grad_last, grad_head_last, grad_head_first, *small = last_stage(
        gh1, w1_own, slope, grad_pooled, mid_slots, pair_out, head_last_in, head_first_in, small
    )
    return (
        small[8].reshape(()),
        grad_input,
        grad_first,
        grad_mid,
        grad_last,
        grad_head_first,
        grad_head_last,
        *[vector.reshape(-1) for vector in small[:8]],
    )


def solution(mesh):
    views = mesh.shape["views"]
    return jax.shard_map(
        functools.partial(per_device, views),
        mesh=mesh,
        in_specs=(
            P("views", "chan"),
            P(None, "chan"),
            P(None, "chan"),
            P(None, "chan"),
            P("chan"),
            P("chan"),
            P("chan"),
            P("chan"),
            P("chan"),
            P("chan"),
            P("chan", None),
            P(),
            P(),
            P(),
            P(),
            P(),
            P(),
        ),
        out_specs=(
            P(),
            P("views", "chan"),
            P("views", "chan"),
            P("views", "chan"),
            P("views", "chan"),
            P("chan", "views"),
            P("views", None),
            P("chan"),
            P("chan"),
            P("chan"),
            P("chan"),
            P("chan"),
            P("chan"),
            P(),
            P(),
        ),
        check_vma=False,
    )
```

```python
import functools

import jax
import jax.numpy as jnp
import numpy as np
from jax import lax
from jax.experimental import pallas as pl
from jax.experimental.pallas import tpu as pltpu
from jax.sharding import PartitionSpec as P

SIDE = 7
PIX = SIDE * SIDE
PAD = SIDE + 2
SUB = 256
EPS = 1e-05
RIDGE = 0.5
MESH = pl.DeviceIdType.MESH
BF16 = jnp.bfloat16
F32 = jnp.float32
VMEM_BYTES = 60 << 20


def place():
    view_at, chan_at = lax.axis_index("views"), lax.axis_index("chan")
    return view_at, chan_at, lax.div(chan_at, 2), lax.rem(chan_at, 2)


def greet(peers, groups=()):
    barrier = pltpu.get_barrier_semaphore()
    total = len(peers)
    for peer in peers:
        pl.semaphore_signal(barrier, inc=1, device_id=peer, device_id_type=MESH)
    for size, own, device in groups:

        def tell(step, carry, size=size, own=own, device=device):
            pl.semaphore_signal(
                barrier, inc=1, device_id=device(lax.rem(own + step, size)), device_id_type=MESH
            )
            return carry

        lax.fori_loop(1, size, tell, 0)
        total += size - 1
    return lambda: pl.semaphore_wait(barrier, total)


class Mail:
    def __init__(self, send_sems, recv_sems):
        self.send_sems, self.recv_sems, self.copies = send_sems, recv_sems, []

    def send(self, source, target, peer):
        spot = len(self.copies)
        copy = pltpu.make_async_remote_copy(
            src_ref=source,
            dst_ref=target,
            send_sem=self.send_sems.at[spot],
            recv_sem=self.recv_sems.at[spot],
            device_id=peer,
            device_id_type=MESH,
        )
        copy.start()
        self.copies.append(copy)
        return copy

    def finish(self):
        for copy in self.copies:
            copy.wait_send()


class Local:
    def __init__(self, sems):
        self.sems, self.used = sems, 0

    def fetch(self, source, target):
        copy = pltpu.make_async_copy(source, target, self.sems.at[self.used])
        copy.start()
        self.used += 1
        return copy


def group_copy(source, slots, sends, recvs, size, own, device, step):
    to = lax.rem(own + step, size)
    return pltpu.make_async_remote_copy(
        src_ref=source,
        dst_ref=slots.at[own],
        send_sem=sends.at[step],
        recv_sem=recvs.at[own],
        device_id=device(to),
        device_id_type=MESH,
    )


def group_arrival(source, slots, sends, recvs, size, own, device, step):
    origin = lax.rem(own + step, size)
    return pltpu.make_async_remote_copy(
        src_ref=source,
        dst_ref=slots.at[origin],
        send_sem=sends.at[step],
        recv_sem=recvs.at[origin],
        device_id=device(origin),
        device_id_type=MESH,
    )


def share_start(source, slots, sends, recvs, group):
    def start(step, carry):
        group_copy(source, slots, sends, recvs, *group, step).start()
        return carry

    lax.fori_loop(1, group[0], start, 0)
    slots[group[1]] = source[...]


def share_end(source, slots, sends, recvs, group):
    def end(step, carry):
        group_arrival(source, slots, sends, recvs, *group, step).wait_recv()
        group_copy(source, slots, sends, recvs, *group, step).wait_send()
        return carry

    lax.fori_loop(1, group[0], end, 0)


def add_slots(slots, size):
    def add(at, total):
        return total + slots[at]

    return lax.fori_loop(1, size, add, slots[0])


def share(source, slots, sends, recvs, group):
    share_start(source, slots, sends, recvs, group)
    share_end(source, slots, sends, recvs, group)
    return add_slots(slots, group[0])


def gather_start(source, slots, sends, recvs, group):
    def start(step, carry):
        group_copy(source, slots, sends, recvs, *group, step).start()
        return carry

    lax.fori_loop(1, group[0], start, 0)


def scatter_start(parts, slots, sends, recvs, group, keep=True):
    size, own, device = group

    def start(step, carry):
        to = lax.rem(own + step, size)
        group_copy(parts.at[to], slots, sends, recvs, *group, step).start()
        return carry

    lax.fori_loop(1, size, start, 0)
    if keep:
        slots[own] = parts[own]


def scatter_end(parts, slots, sends, recvs, group):
    share_end(parts.at[group[1]], slots, sends, recvs, group)


class Fold:
    def __init__(self, parts, fold_in, slots, sems, views, keep=True):
        view_at, chan_at, _, _ = place()
        self.parts, self.fold_in, self.slots, self.sems, self.keep = parts, fold_in, slots, sems, keep
        self.size, self.outer, self.inner = views // 2, lax.div(view_at, 2), lax.rem(view_at, 2)
        self.pair = (2 * self.outer + 1 - self.inner, chan_at)
        self.chan_at = chan_at

    def block(self, step):
        return lax.rem(self.outer + step, self.size)

    def pair_copy(self, step):
        at = self.block(step)
        return pltpu.make_async_remote_copy(
            src_ref=self.parts.at[2 * at + 1 - self.inner],
            dst_ref=self.fold_in.at[at],
            send_sem=self.sems[0].at[at],
            recv_sem=self.sems[1].at[at],
            device_id=self.pair,
            device_id_type=MESH,
        )

    def out_copy(self, step, slot):
        at = self.block(step)
        return pltpu.make_async_remote_copy(
            src_ref=self.parts.at[2 * at + self.inner],
            dst_ref=self.slots.at[slot],
            send_sem=self.sems[2].at[at],
            recv_sem=self.sems[3].at[slot],
            device_id=(2 * at + self.inner, self.chan_at),
            device_id_type=MESH,
        )

    def start(self):
        def one(step, carry):
            self.pair_copy(step).start()
            return carry

        lax.fori_loop(1, self.size + 1, one, 0)

    def add(self, step):
        self.pair_copy(step).wait_recv()
        at, mine = self.block(step), 2 * self.block(step) + self.inner
        total = self.parts[mine].astype(F32) + self.fold_in[at].astype(F32)
        self.parts[mine] = total.astype(self.parts.dtype)

    def pass_on(self, first, last):
        def one(step, carry):
            self.add(step)
            self.out_copy(step, self.outer).start()
            return carry

        lax.fori_loop(first, min(last, self.size), one, 0)
        if last > self.size:
            self.add(self.size)
            if self.keep:
                self.slots[self.outer] = self.parts[2 * self.outer + self.inner]

    def end(self):
        def one(step, carry):
            self.out_copy(step, self.block(step)).wait_recv()
            self.out_copy(step, self.outer).wait_send()
            return carry

        lax.fori_loop(1, self.size, one, 0)

        def sent(step, carry):
            self.pair_copy(step).wait_send()
            return carry

        lax.fori_loop(1, self.size + 1, sent, 0)


def chan_group():
    view_at, chan_at, y, c = place()
    return (4, chan_at, lambda at: (view_at, at))


def half_group(views):
    view_at, chan_at, y, c = place()
    return (
        2 * views,
        2 * view_at + c,
        lambda at: (lax.div(at, 2), 2 * y + lax.rem(at, 2)),
    )


def view_group(views):
    view_at, chan_at, y, c = place()
    return (views, view_at, lambda at: (at, chan_at))


def all_group(views):
    view_at, chan_at, y, c = place()
    return (4 * views, 4 * view_at + chan_at, lambda at: (lax.div(at, 4), lax.rem(at, 4)))


def dot(left, right):
    return jnp.dot(left, right, preferred_element_type=F32)


def dot_nt(left, right):
    return lax.dot_general(left, right, (((1,), (1,)), ((), ())), preferred_element_type=F32)


def dot_tn(left, right):
    return lax.dot_general(left, right, (((0,), (0,)), ((), ())), preferred_element_type=F32)


def gate(level):
    return 0.5 + 0.5 * jnp.tanh(0.5 * level)


def silu_slope(level):
    open_part = gate(level)
    return open_part * (1.0 + level * (1.0 - open_part))


def call(body, name, outs, ins, scratch, collective, any_ins=(), any_outs=()):
    def spec(at, places):
        return pl.BlockSpec(memory_space=pl.ANY if at in places else pltpu.VMEM)

    return pl.pallas_call(
        body,
        out_shape=outs,
        in_specs=[spec(at, any_ins) for at in range(ins)],
        out_specs=tuple(spec(at, any_outs) for at in range(len(outs))),
        scratch_shapes=scratch,
        name=name,
        compiler_params=pltpu.CompilerParams(
            collective_id=collective, has_side_effects=True, vmem_limit_bytes=VMEM_BYTES
        ),
    )


def shape(*dims, kind=F32):
    return jax.ShapeDtypeStruct(dims, kind)


def dma(*dims):
    return pltpu.SemaphoreType.DMA(dims)


EARLY_TAPS = 3


def forward_body(
    views, g1, b1, g2, b2, x, w1in, w2in, w3in, perm_any, unperm_any,
    pad_out, h1_out, w2_out, w2_far_out, w3, act, h2_out, stat, stat2, w1_own, smalls,
    xo, xm, xp, w1, out_part, in_part, h1, st, slots, st2, slots2,
    perm, unperm, pad, w2, hidden, act_own, h2, small,
    sends, recvs, part_sends, part_recvs, group_sends, group_recvs, local_sems,
):
    view_at, chan_at, y, c = place()
    mate, opposite = (view_at, 2 * y + 1 - c), (view_at, 2 * (1 - y) + c)
    diagonal = (view_at, 2 * (1 - y) + 1 - c)
    group = half_group(views)
    quarter, depth = x.shape[1], x.shape[2]
    near, far = 2 * y + c, 2 * (1 - y) + c
    near_rows = pl.ds(pl.multiple_of(2 * depth * y, 2 * depth), 2 * depth)
    far_rows = pl.ds(pl.multiple_of(2 * depth * (1 - y), 2 * depth), 2 * depth)
    met = greet([opposite, diagonal], [group])
    local = Local(local_sems)
    x_own = [local.fetch(x.at[2 * q + c], xo.at[q]) for q in range(2)]
    perm_here = local.fetch(perm_any, perm)
    w1_here = local.fetch(w1in.at[near_rows], w1.at[near])
    w2_here = local.fetch(w2in, w2.at[c])
    unperm_here = local.fetch(unperm_any, unperm)
    rest = [local.fetch(w3in.at[near_rows], w3.at[near])]
    for at, vector in enumerate((g1, b1, g2, b2)):
        small[at : at + 1] = vector[...]
        small[4 + at : 5 + at] = vector[...]
    smalls[chan_at] = small[...]
    pad[...] = jnp.zeros(pad.shape, pad.dtype)
    met()
    mail = Mail(sends, recvs)
    x_mate = [mail.send(x.at[1 - c], xm.at[0], mate)]
    w1_mate = mail.send(w1in.at[near_rows], w1.at[near], mate)
    w1_far = mail.send(w1in.at[far_rows], w1.at[near], opposite)
    x_mate.append(mail.send(x.at[3 - c], xm.at[1], mate))
    small_copies = [mail.send(small, smalls.at[chan_at], to) for to in (mate, opposite, diagonal)]
    w2_mate = mail.send(w2in, w2.at[c], mate)
    w3_mate = mail.send(w3in.at[near_rows], w3.at[near], mate)

    def part_copy(half, q):
        return pltpu.make_async_remote_copy(
            src_ref=out_part.at[half, q],
            dst_ref=in_part.at[half, q],
            send_sem=part_sends.at[half, q],
            recv_sem=part_recvs.at[half, q],
            device_id=opposite,
            device_id_type=MESH,
        )

    def part(half, q):
        both = jnp.concatenate([w1[2 * half], w1[2 * half + 1]], axis=1)
        out_part[half, q] = (dot(xp[q, 0], both[:depth]) + dot(xp[q, 1], both[depth:])).astype(BF16)
        part_copy(half, q).start()

    perm_here.wait()
    for q in range(2):
        x_own[q].wait()
        xp[q, c] = dot(perm[...], xo[q]).astype(BF16)
        x_mate[q].wait_recv()
        xp[q, 1 - c] = dot(perm[...], xm[q]).astype(BF16)
        if q == 0:
            w1_here.wait()
            w1_mate.wait_recv()
        part(y, q)
    w1_far.wait_recv()
    w1_on = mail.send(w1.at[far], w1.at[far], mate)
    w1_on.wait_recv()
    for q in range(2):
        part(1 - y, q)
    w2_here.wait()
    w2_mate.wait_recv()
    rest.append(local.fetch(w2, w2_out))
    own_rows = pl.ds(pl.multiple_of(depth * c, depth), depth)
    w1_own[...] = jnp.concatenate([w1[k, own_rows] for k in range(4)], axis=1)
    st[...] = jnp.zeros(st.shape, st.dtype)
    step_rows = quarter // SIDE

    def sums(half):
        def one(q, carry):
            part_copy(half, q).wait_recv()

            def rows_of(at, inner):
                rows = pl.ds(at * step_rows, step_rows)
                value = out_part[half, q, rows].astype(F32) + in_part[half, q, rows].astype(F32)
                h1[half, q, rows] = value
                st[half, 0:1] += jnp.sum(value, axis=0, keepdims=True)
                st[half, 1:2] += jnp.sum(value * value, axis=0, keepdims=True)
                return inner

            return lax.fori_loop(0, SIDE, rows_of, carry)

        lax.fori_loop(0, 2, one, 0)

    sums(1 - y)
    sums(y)
    share_start(st, slots, group_sends.at[0], group_recvs.at[0], group)
    w3_far = mail.send(w3in.at[far_rows], w3.at[near], opposite)
    channels = pad.shape[4]
    w2_far = []
    for tap in range(EARLY_TAPS):
        rows = pl.ds(tap * channels, channels)
        w2_far.append(mail.send(w2in.at[rows], w2_far_out.at[c, rows], opposite))
    share_end(st, slots, group_sends.at[0], group_recvs.at[0], group)
    totals = add_slots(slots, group[0])
    count = float(views * 4 * quarter)
    for copy in small_copies:
        copy.wait_recv()
    mean = totals[:, 0:1] / count
    rstd = lax.rsqrt(totals[:, 1:2] / count - mean * mean + EPS)
    stat[...] = jnp.concatenate([mean, rstd], axis=1)
    for half in range(2):
        gains = jnp.concatenate([smalls[2 * half], smalls[2 * half + 1]], axis=1)
        scale = rstd[half] * gains[0:1]
        bias = gains[1:2] - mean[half] * scale

        def act_rows(at, carry, half=half, scale=scale, bias=bias):
            q, i = lax.div(at, SIDE), lax.rem(at, SIDE)
            level = h1[half, q, pl.ds(i * step_rows, step_rows)] * scale + bias
            value = (level * gate(level)).astype(BF16)
            pad[q, i + 1, 1 : SIDE + 1, :, 256 * half : 256 * half + 256] = value.reshape(
                SIDE, step_rows // SIDE, 256
            )
            return carry

        lax.fori_loop(0, 2 * SIDE, act_rows, 0)
    rest.append(local.fetch(pad, pad_out))
    rest += [local.fetch(h1.at[half, y], h1_out.at[half]) for half in range(2)]
    w3_far.wait_recv()
    w3_on = mail.send(w3.at[far], w3.at[far], mate)
    st2[...] = jnp.zeros(st2.shape, F32)

    def convolve(q, carry):
        for tap in range(9):
            a, b = tap // 3, tap % 3
            window = pad[q, a : a + SIDE, b : b + SIDE].reshape(quarter, channels)
            taps = slice(tap * channels, (tap + 1) * channels)
            term = dot(window, jnp.concatenate([w2[0, taps], w2[1, taps]], axis=1))
            if tap == 0:
                hidden[q] = term
            else:
                hidden[q] += term
        value = hidden[q]
        h2[q] = value.astype(BF16)
        st2[0:1] += jnp.sum(value, axis=0, keepdims=True)
        st2[1:2] += jnp.sum(value * value, axis=0, keepdims=True)
        return carry

    lax.fori_loop(0, 2, convolve, 0)
    share_start(st2, slots2, group_sends.at[1], group_recvs.at[1], group)
    rest.append(local.fetch(h2, h2_out))
    w2_on = []

    def pass_on(taps):
        for tap in taps:
            w2_far[tap].wait_recv()
            rows = pl.ds(tap * channels, channels)
            w2_on.append(mail.send(w2_far_out.at[c, rows], w2_far_out.at[c, rows], mate))

    pass_on(range(EARLY_TAPS - 1))
    share_end(st2, slots2, group_sends.at[1], group_recvs.at[1], group)
    totals2 = add_slots(slots2, group[0])
    mean2 = totals2[0:1] / count
    rstd2 = lax.rsqrt(totals2[1:2] / count - mean2 * mean2 + EPS)
    stat2[...] = jnp.concatenate([mean2, rstd2], axis=0)
    gains = jnp.concatenate([smalls[2 * y], smalls[2 * y + 1]], axis=1)
    scale2 = rstd2 * gains[2:3]
    bias2 = gains[3:4] - mean2 * scale2
    across, beside = [], []
    unperm_here.wait()
    for q in range(2):
        level = hidden[q] * scale2 + bias2
        value = (level * gate(level)).astype(BF16)
        act_own[q] = dot(unperm[...], value).astype(BF16)
        spot = act.at[y, 2 * q + c]
        across.append(mail.send(act_own.at[q], spot, opposite))
        beside.append(mail.send(act_own.at[q], spot, mate))
        rest.append(local.fetch(act_own.at[q], spot))
    pass_on(range(EARLY_TAPS - 1, EARLY_TAPS))
    for q in range(2):
        across[q].wait_recv()
        spot = act.at[1 - y, 2 * q + c]
        beside.append(mail.send(spot, spot, mate))
    for copy in [w3_mate, w3_on, *w2_on, *beside]:
        copy.wait_recv()
    for copy in rest:
        copy.wait()
    mail.finish()
    for half in range(2):
        for q in range(2):
            part_copy(half, q).wait_send()


def forward_stage(views, x, conv_first, conv_mid, conv_last, vectors, perm, unperm):
    quarter, depth = x.shape[0] // 4, x.shape[1]
    mid = conv_mid.shape[1] * 4
    half, taps = mid // 2, conv_mid.shape[0]
    block = quarter // PIX
    group = 2 * views
    vm = pltpu.VMEM
    return call(
        functools.partial(forward_body, views),
        "forward",
        (
            shape(2, PAD, PAD, block, mid, kind=BF16),
            shape(2, quarter, half),
            shape(2, *conv_mid.shape, kind=BF16),
            shape(2, taps // 9 * EARLY_TAPS, conv_mid.shape[1], kind=BF16),
            shape(4, 2 * depth, mid // 4, kind=BF16),
            shape(2, 4, quarter, half, kind=BF16),
            shape(2, quarter, half, kind=BF16),
            shape(2, 2, half),
            shape(2, half),
            shape(depth, mid, kind=BF16),
            shape(4, 8, mid // 4),
        ),
        10,
        [
            vm((2, quarter, depth), BF16),
            vm((2, quarter, depth), BF16),
            vm((2, 2, quarter, depth), BF16),
            vm((4, 2 * depth, mid // 4), BF16),
            vm((2, 2, quarter, half), BF16),
            vm((2, 2, quarter, half), BF16),
            vm((2, 2, quarter, half), F32),
            vm((2, 2, half), F32),
            vm((group, 2, 2, half), F32),
            vm((2, half), F32),
            vm((group, 2, half), F32),
            vm((quarter, quarter), BF16),
            vm((quarter, quarter), BF16),
            vm((2, PAD, PAD, block, mid), BF16),
            vm((2, *conv_mid.shape), BF16),
            vm((2, quarter, half), F32),
            vm((2, quarter, half), BF16),
            vm((2, quarter, half), BF16),
            vm((8, mid // 4), F32),
            dma(32),
            dma(32),
            dma(2, 2),
            dma(2, 2),
            dma(2, group),
            dma(2, group),
            dma(20),
        ],
        collective=1,
        any_ins=range(4, 10),
        any_outs=range(7),
    )(*vectors, x.reshape(4, quarter, depth), conv_first, conv_mid, conv_last, perm, unperm)


def orders(quarter):
    block = quarter // PIX
    row = np.arange(quarter)
    source = (row % block) * PIX + row // block
    hot = (source[:, None] == row[None, :]).astype(BF16)
    return jnp.asarray(hot), jnp.asarray(hot.T)


def split_rows(value):
    high = value.astype(BF16)
    rest = value - high.astype(F32)
    middle = rest.astype(BF16)
    low = (rest - middle.astype(F32)).astype(BF16)
    return jnp.concatenate([high, middle, low], axis=0)


def join_rows(stacked):
    rows = stacked.shape[0] // 3
    return stacked[2 * rows :] + stacked[rows : 2 * rows] + stacked[:rows]


def split_pair(value):
    high = value.astype(BF16)
    return high, (value - high.astype(F32)).astype(BF16)


def exact(left, right, left_dim, right_dim):
    return lax.dot_general(
        left,
        right,
        (((left_dim,), (right_dim,)), ((), ())),
        precision=lax.Precision.HIGHEST,
        preferred_element_type=F32,
    )


def over(count, body, start):
    return body(0, start) if count == 1 else lax.fori_loop(0, count, body, start)


def split_three(value):
    high = value.astype(BF16)
    rest = value - high.astype(F32)
    middle = rest.astype(BF16)
    return high, middle, (rest - middle.astype(F32)).astype(BF16)


def short_product(left, right):
    lh, lm, ll = split_three(left)
    rh, rm, rl = split_three(right)
    return dot_tn(
        jnp.concatenate([lh, lh, lm, lh, lm, ll], axis=0),
        jnp.concatenate([rh, rm, rh, rl, rm, rh], axis=0),
    )


def factor_inverse(work, inverse, subs, width):
    panel = 16
    row = lax.broadcasted_iota(jnp.int32, (panel, width), 0)

    def wide(part):
        return jnp.broadcast_to(part, (panel, width))

    def eliminate(s, first):
        rows = work[s, first : first + panel]
        columns = [wide(rows[:, first + j : first + j + 1]) for j in range(panel)]
        diagonal = jnp.zeros((panel, width), F32)
        for j in range(panel):
            pivot = wide(columns[j][j : j + 1])
            diagonal = jnp.where(row == j, pivot, diagonal)
            if j == panel - 1:
                break
            ratio = jnp.where(row > j, columns[j] * (1.0 / pivot), 0.0)
            for k in range(j + 1, panel):
                columns[k] = columns[k] - ratio * wide(columns[k][j : j + 1])
            rows = rows - jnp.concatenate([ratio, ratio], axis=1) * rows[j : j + 1]
        inverse[s, first : first + panel] = rows[:, width:] * lax.rsqrt(diagonal)
        if first + panel < width:
            scaled = rows[:, :width] / diagonal
            work[s, first + panel :] -= short_product(scaled, rows)[first + panel :]

    def some(at, carry):
        for first in range(0, width, panel):
            for k in range(2):
                eliminate(2 * at + k, first)
        return carry

    over(subs // 2, some, 0)


def view_sums(value, block):
    return jnp.concatenate(
        [jnp.sum(value[PIX * v : PIX * (v + 1)], axis=0, keepdims=True) for v in range(block)], axis=0
    )


def columns_of(row, column):
    tile = column.shape[1]

    def one(at, carry):
        cols = pl.ds(pl.multiple_of(at * tile, tile), tile)
        column[cols] = jnp.broadcast_to(row[:, cols].astype(F32), (tile, tile)).T
        return carry

    lax.fori_loop(0, row.shape[1] // tile, one, 0)


def whiten(embed, sub_col, image_col, image_row, partner_col, partner_row, refs, own_rows):
    work, inverse, white, unit, unit_parts, back = refs
    total, width = embed.shape
    subs = inverse.shape[0]
    eye = (
        lax.broadcasted_iota(jnp.int32, (width, width), 0)
        == lax.broadcasted_iota(jnp.int32, (width, width), 1)
    ).astype(F32)
    size = min(total, 512)
    pieces = total // size

    def rows_at(at):
        return pl.ds(pl.multiple_of(at * size, size), size)

    means = []

    def masks(rows, s):
        column = sub_col[rows]
        return (column == float(s)).astype(F32), (column == float(s + 1)).astype(F32)

    for s in range(0, subs, 2):

        def moments(at, sums, s=s):
            rows = rows_at(at)
            value = embed[rows]
            picked = jnp.concatenate([value * mask for mask in masks(rows, s)], axis=1)
            first = sums[0] + jnp.sum(picked, axis=0, keepdims=True)
            return first, sums[1] + exact(picked, value, 0, 0)

        first, second = over(
            pieces, moments, (jnp.zeros((1, 2 * width), F32), jnp.zeros((2 * width, width), F32))
        )
        for k in range(2):
            mean = first[:, k * width : (k + 1) * width] / SUB
            cov = second[k * width : (k + 1) * width] / SUB - exact(mean, mean, 0, 0)
            work[s + k, :, :width] = cov + RIDGE * eye
            work[s + k, :, width:] = eye
            means.append(mean)
    factor_inverse(work, inverse, subs, width)

    def whitening(at, carry):
        rows = rows_at(at)
        value = None
        for s in range(0, subs, 2):
            centred = jnp.concatenate(
                [(embed[rows] - means[s + k]) * mask for k, mask in enumerate(masks(rows, s))], axis=1
            )
            term = exact(centred, jnp.concatenate([inverse[s], inverse[s + 1]], axis=1), 1, 1)
            value = term if value is None else value + term
        white[rows] = value
        value = value * lax.rsqrt(jnp.sum(value * value, axis=1, keepdims=True) + EPS)
        unit[rows] = value
        high = value.astype(BF16)
        rest = value - high.astype(F32)
        middle = rest.astype(BF16)
        unit_parts[rows] = jnp.concatenate(
            [high, middle, (rest - middle.astype(F32)).astype(BF16)], axis=1
        )
        return carry

    over(pieces, whitening, 0)
    chunk = min(total, 262144 // total)

    def pairs(at, loss):
        rows = pl.ds(pl.multiple_of(at * chunk, chunk), chunk)
        across = lax.broadcasted_iota(jnp.int32, (chunk, total), 1).astype(F32)
        down = lax.broadcasted_iota(jnp.int32, (chunk, total), 0) + at * chunk

        def pick(hot):
            found = dot(hot.astype(F32).astype(BF16), unit_parts[...])
            return found[:, 2 * width :] + found[:, width : 2 * width] + found[:, :width]

        mine = unit[rows]
        ahead = pick(partner_col[rows][:, :1] == across)
        behind = pick(partner_row[...] == down)
        members = jnp.sum(
            (image_col[rows][:, :1] == image_row[...].astype(F32)).astype(F32), axis=1, keepdims=True
        )
        weight = 1.0 / members
        apart = mine - ahead
        grad = (4.0 / total) * weight * (2.0 * mine - ahead - behind)
        length = lax.rsqrt(jnp.sum(white[rows] * white[rows], axis=1, keepdims=True) + EPS)
        back[rows] = length * (grad - mine * jnp.sum(mine * grad, axis=1, keepdims=True))
        per_view = jnp.sum(apart * apart, axis=1, keepdims=True) * weight
        return loss + jnp.sum(per_view, axis=0, keepdims=True)

    loss = over(total // chunk, pairs, jnp.zeros((1, 1), F32)) * (2.0 / total)
    lower = lax.broadcasted_iota(jnp.int32, (width, width), 0) >= lax.broadcasted_iota(
        jnp.int32, (width, width), 1
    )
    own_white, own_back = white[own_rows], back[own_rows]
    gradient = jnp.zeros(own_white.shape, F32)
    for s in range(0, subs, 2):

        def pulled(at, sums, s=s):
            rows = rows_at(at)
            picked = jnp.concatenate([back[rows] * mask for mask in masks(rows, s)], axis=1)
            spread = sums[0] + jnp.sum(picked, axis=0, keepdims=True)
            return spread, sums[1] + exact(picked, white[rows], 0, 0)

        spread, sums = over(
            pieces, pulled, (jnp.zeros((1, 2 * width), F32), jnp.zeros((2 * width, width), F32))
        )
        for k, own_mask in enumerate(masks(own_rows, s)):
            cols = slice(k * width, (k + 1) * width)
            low_part = jnp.where(lower, sums[cols], 0.0)
            mirrored = low_part + low_part.T - sums[cols] * eye
            moved = own_back - (exact(own_white, mirrored, 1, 0) + spread[:, cols]) / SUB
            gradient = gradient + own_mask * exact(moved, inverse[s + k], 1, 0)
    return loss, gradient


def head_body(
    views, gain_last, shift_last, gain_head, shift_head, sub_row, image_row, partner_row, stat2,
    act_any, w3_any, x_any, head_first_any, head_last_any, w2in, h2,
    h3_out, slope_out, pooled_all, w2_late, h2q,
    stat3, grad_shift_last, grad_gain_last, grad_shift_head, grad_gain_head,
    grad_pooled_out, act4, grad_embed_out, grad_p1, loss_out, stats2, pooled_means,
    act, w3, x, head_first, head_last, h3, slope, pooled_own, pooled_low, sub_col, image_col, partner_col,
    embed_all, part, part_in, mean_sums, slope_sums, st3, slots3, st4, slots4, bk4, bslots4, bk3, bslots3, embed_own,
    work, inverse, white, unit, unit_parts, back,
    sends, recvs, group_sends, group_recvs, local_sems,
):
    view_at, chan_at, y, c = place()
    mate, opposite = (view_at, 2 * y + 1 - c), (view_at, 2 * (1 - y) + c)
    group = view_group(views)
    quarter, width = h3.shape[1], h3.shape[2]
    block = quarter // PIX
    views_own = 4 * block
    met = greet([mate, opposite], [group])
    local = Local(local_sems)
    w3_here = local.fetch(w3_any, w3)
    act_here = [local.fetch(act_any.at[:, q], act.at[:, q]) for q in range(4)]
    x_here = local.fetch(x_any, x)
    head_first_here = local.fetch(head_first_any, head_first)
    head_last_here = local.fetch(head_last_any, head_last)
    rest = [local.fetch(h2.at[y], h2q.at[y])]
    own_out = pl.ds(pl.multiple_of(width * c, width), width)
    st3[...] = jnp.zeros(st3.shape, F32)
    w3_here.wait()
    for q in range(4):
        act_here[q].wait()

    def last_conv(q, carry):
        total = None
        for half in range(2):
            weight = jnp.concatenate([w3[2 * half, own_out], w3[2 * half + 1, own_out]], axis=1)
            term = dot_nt(act[half, q], weight)
            total = term if total is None else total + term
        low = total.astype(BF16)
        h3[q] = low
        value = low.astype(F32)
        st3[0:1] += jnp.sum(value, axis=0, keepdims=True)
        st3[1:2] += jnp.sum(value * value, axis=0, keepdims=True)
        return carry

    lax.fori_loop(0, 4, last_conv, 0)
    met()
    share_start(st3, slots3, group_sends.at[0], group_recvs.at[0], group)
    rest.append(local.fetch(h3, h3_out))
    for row, column in ((sub_row, sub_col), (image_row, image_col), (partner_row, partner_col)):
        columns_of(row, column)
    share_end(st3, slots3, group_sends.at[0], group_recvs.at[0], group)
    totals = add_slots(slots3, views)
    count = float(views * 4 * quarter)
    mean = totals[0:1] / count
    rstd = lax.rsqrt(totals[1:2] / count - mean * mean + EPS)
    stat3[...] = jnp.concatenate([mean, rstd], axis=0)
    scale = rstd * gain_last[...]
    bias = shift_last[...] - mean * scale
    x_here.wait()

    def pool_block(q, carry):
        before = x[q].astype(F32) + (h3[q].astype(F32) * scale + bias)
        sums = view_sums(before * gate(before), block)
        pooled_own[pl.ds(pl.multiple_of(q * block, block), block)] = sums * (1.0 / PIX)
        return carry

    lax.fori_loop(0, 4, pool_block, 0)
    mail = Mail(sends, recvs)
    head_first_here.wait()
    hidden = join_rows(dot(split_rows(pooled_own[...]), head_first[...]))
    wide = hidden.shape[1] // 2
    part[0] = hidden[:, :wide]
    part[1] = hidden[:, wide:]
    beside = mail.send(part, part_in.at[pl.ds(0, 2)], mate)

    def slope_block(q, carry):
        level3 = h3[q].astype(F32)
        before = x[q].astype(F32) + (level3 * scale + bias)
        low = silu_slope(before).astype(BF16)
        slope[q] = low
        normed = (level3 - mean) * rstd
        kept = low.astype(F32)
        rows = pl.ds(pl.multiple_of(q * block, block), block)
        slope_sums[0, rows] = view_sums(kept, block)
        slope_sums[1, rows] = view_sums(kept * normed, block)
        return carry

    beside.wait()
    mean_sums[...] = part[...] + part_in[0:2]
    across = mail.send(mean_sums.at[c], part_in.at[2], opposite)
    stats2[y] = stat2[...]
    stat2_far = mail.send(stat2, stats2.at[y], opposite)
    lax.fori_loop(0, 2, slope_block, 0)
    across.wait_recv()
    part_in[4 + c] = mean_sums[c] + part_in[2]
    gathered = mail.send(part_in.at[4 + c], part_in.at[4 + c], mate)
    h2_far = mail.send(h2.at[1 - y], h2q.at[y], opposite)
    late_rows = pl.ds(w2in.shape[0] - w2_late.shape[1], w2_late.shape[1])
    w2_over = mail.send(w2in.at[late_rows], w2_late.at[c], opposite)
    gathered.wait_recv()
    p1 = part_in[4:6]
    st4[0:2] = jnp.sum(p1, axis=1)
    st4[2:4] = jnp.sum(p1 * p1, axis=1)
    share_start(st4, slots4, group_sends.at[1], group_recvs.at[1], group)
    lax.fori_loop(2, 4, slope_block, 0)
    rest.append(local.fetch(slope, slope_out))
    share_end(st4, slots4, group_sends.at[1], group_recvs.at[1], group)
    totals4 = add_slots(slots4, views)
    count4 = float(views * views_own)
    mean4 = totals4[0:2] / count4
    rstd4 = lax.rsqrt(totals4[2:4] / count4 - mean4 * mean4 + EPS)
    head_last_here.wait()

    def level4(half):
        cols = slice(half * wide, (half + 1) * wide)
        normed = (part_in[4 + half] - mean4[half : half + 1]) * rstd4[half : half + 1]
        return normed, normed * gain_head[:, cols] + shift_head[:, cols]

    embed = None
    for half in range(2):
        normed, level = level4(half)
        value = level * gate(level)
        act4[half] = value
        term = join_rows(dot(split_rows(value), head_last[half * wide : (half + 1) * wide]))
        embed = term if embed is None else embed + term
    embed_own[...] = embed
    share_start(embed_own, embed_all, group_sends.at[2], group_recvs.at[2], group)
    share_end(embed_own, embed_all, group_sends.at[2], group_recvs.at[2], group)
    pooled_mean = jnp.sum(pooled_own[...], axis=0, keepdims=True) / views_own
    bk3[2:3] = pooled_mean
    pooled_low[...] = (pooled_own[...] - pooled_mean).astype(BF16)
    gather_start(pooled_low, pooled_all, group_sends.at[5], group_recvs.at[5], group)
    rest.append(local.fetch(pooled_low, pooled_all.at[view_at]))
    own_rows = pl.ds(pl.multiple_of(view_at * views_own, views_own), views_own)
    every = embed_all.reshape(views * views_own, embed.shape[1])
    loss, grad_embed = whiten(
        every, sub_col, image_col, image_row, partner_col, partner_row,
        (work, inverse, white, unit, unit_parts, back), own_rows,
    )
    loss_out[...] = loss
    grad_embed_out[...] = grad_embed
    stacked = split_rows(grad_embed)
    for half in range(2):
        normed, level = level4(half)
        grad = join_rows(dot_nt(stacked, head_last[half * wide : (half + 1) * wide]))
        grad = grad * silu_slope(level)
        part[half] = grad
        bk4[half : half + 1] = jnp.sum(grad, axis=0, keepdims=True)
        bk4[2 + half : 3 + half] = jnp.sum(grad * normed, axis=0, keepdims=True)
    tot4 = share(bk4, bslots4, group_sends.at[3], group_recvs.at[3], group)
    grad_pooled = None
    for half in range(2):
        cols = slice(half * wide, (half + 1) * wide)
        normed, level = level4(half)
        shift_sum, gain_sum = tot4[half : half + 1], tot4[2 + half : 3 + half]
        grad_shift_head[:, cols] = shift_sum
        grad_gain_head[:, cols] = gain_sum
        grad = (
            gain_head[:, cols]
            * rstd4[half : half + 1]
            * (part[half] - shift_sum / count4 - normed * (gain_sum / count4))
        )
        grad_p1[half] = grad
        term = join_rows(dot_nt(split_rows(grad), head_first[:, cols]))
        grad_pooled = term if grad_pooled is None else grad_pooled + term
    grad_pooled = grad_pooled * (1.0 / PIX)
    grad_pooled_out[...] = grad_pooled
    bk3[0:1] = jnp.sum(grad_pooled * slope_sums[0], axis=0, keepdims=True)
    bk3[1:2] = jnp.sum(grad_pooled * slope_sums[1], axis=0, keepdims=True)
    share_start(bk3, bslots3, group_sends.at[4], group_recvs.at[4], group)
    w2_over.wait_recv()
    w2_on = mail.send(w2_late.at[c], w2_late.at[c], mate)
    share_end(bk3, bslots3, group_sends.at[4], group_recvs.at[4], group)
    tot3 = add_slots(bslots3, views)
    grad_shift_last[...] = tot3[0:1]
    grad_gain_last[...] = tot3[1:2]
    pooled_means[...] = bslots3[:, 2]
    h2_far.wait_recv()
    stat2_far.wait_recv()
    w2_on.wait_recv()
    share_end(pooled_low, pooled_all, group_sends.at[5], group_recvs.at[5], group)
    for copy in rest:
        copy.wait()
    for copy in mail.copies[1:]:
        copy.wait_send()


def head_stage(
    views, vectors, tables, stat2, act, w3, x, head_first, head_last, w2in, h2
):
    quarter, width = act.shape[2], x.shape[1]
    block = quarter // PIX
    own = 4 * block
    total = views * own
    hid, emb = head_last.shape
    wide = hid // 2
    subs = total // SUB
    taps = w2in.shape[0]
    vm = pltpu.VMEM
    return call(
        functools.partial(head_body, views),
        "head",
        (
            shape(4, quarter, width, kind=BF16),
            shape(4, quarter, width, kind=BF16),
            shape(views, own, width, kind=BF16),
            shape(2, taps // 9 * (9 - EARLY_TAPS), w2in.shape[1], kind=BF16),
            shape(*h2.shape, kind=BF16),
            shape(2, width),
            shape(1, width),
            shape(1, width),
            shape(1, hid),
            shape(1, hid),
            shape(own, width),
            shape(2, own, wide),
            shape(own, emb),
            shape(2, own, wide),
            shape(1, 1),
            shape(2, *stat2.shape),
            shape(views, width),
        ),
        15,
        [
            vm(act.shape, BF16),
            vm(w3.shape, BF16),
            vm((4, quarter, width), BF16),
            vm(head_first.shape, BF16),
            vm(head_last.shape, BF16),
            vm((4, quarter, width), BF16),
            vm((4, quarter, width), BF16),
            vm((own, width), F32),
            vm((own, width), BF16),
            vm((total, 128), F32),
            vm((total, 128), F32),
            vm((total, 128), F32),
            vm((views, own, emb), F32),
            vm((2, own, wide), F32),
            vm((6, own, wide), F32),
            vm((2, own, wide), F32),
            vm((2, own, width), F32),
            vm((2, width), F32),
            vm((views, 2, width), F32),
            vm((4, wide), F32),
            vm((views, 4, wide), F32),
            vm((4, wide), F32),
            vm((views, 4, wide), F32),
            vm((3, width), F32),
            vm((views, 3, width), F32),
            vm((own, emb), F32),
            vm((subs, emb, 2 * emb), F32),
            vm((subs, emb, emb), F32),
            vm((total, emb), F32),
            vm((total, emb), F32),
            vm((total, 3 * emb), BF16),
            vm((total, emb), F32),
            dma(8),
            dma(8),
            dma(6, views),
            dma(6, views),
            dma(16),
        ],
        collective=3,
        any_ins=range(8, 15),
        any_outs=range(5),
    )(
        *vectors, *tables, stat2, act, w3, x.reshape(4, quarter, width),
        head_first, head_last, w2in, h2,
    )


def link_kind(rows):
    return BF16 if rows % 16 == 0 else F32


def back_body(
    views, stat3, grad_shift_last, grad_gain_last, grad_pooled, gain_last, expand,
    stats2, smalls, stat1, act4, grad_embed, grad_p1, pooled_means,
    h3_any, slope_any, w3_any, h2q_any, perm_any, unperm_any, pad_any, h1q_any, w2_any,
    w2_early_any, w2_late_any, act_any, x_any, pooled_any,
    gh1_out, mid_slots, pair_out, head_last_out, head_first_out,
    grad_shift_mid, grad_gain_mid, grad_shift_first, grad_gain_first,
    h3, slope, w3, h2q, gh1, gh3, gh3_mate, out_part, in_part, ga2, gh2, gh2_far, gpad, ga1, st, chan_slots, view_slots,
    order, pad, h1q, w2, w2_far, act, pooled,
    wsum, wsend, mid_parts, mid_in, last_parts, last_in, last_slots, first_slots, pair_parts,
    hl_parts, hl_slots, p1_parts, p1_slots,
    sends, recvs, chan_sends, chan_recvs, group_sends, group_recvs, pair_sends, pair_recvs,
    pair1_sends, pair1_recvs, pair2_sends, pair2_recvs, local_sems,
):
    view_at, chan_at, y, c = place()
    mate, opposite = (view_at, 2 * y + 1 - c), (view_at, 2 * (1 - y) + c)
    group, chans, everyone = view_group(views), chan_group(), all_group(views)
    quarter, width = h3.shape[1], h3.shape[2]
    block = quarter // PIX
    half_width = h2q.shape[2]
    met = greet([], [everyone])
    local = Local(local_sems)
    near_half, own_half = [2 * i + 1 - c for i in (1 - y, y)], [2 * i + c for i in (1 - y, y)]
    rows_here = []
    for q in near_half + own_half:
        rows_here.append((local.fetch(h3_any.at[q], h3.at[q]), local.fetch(slope_any.at[q], slope.at[q])))
    w3_here = local.fetch(w3_any, w3)
    perm_here = local.fetch(perm_any, order)
    act_here = local.fetch(act_any, act)
    h2q_here = local.fetch(h2q_any, h2q)
    w2_here = local.fetch(w2_any, w2)
    early = w2_early_any.shape[1]
    w2_far_here = [
        local.fetch(w2_early_any, w2_far.at[:, pl.ds(0, early)]),
        local.fetch(w2_late_any, w2_far.at[:, pl.ds(early, w2_far.shape[1] - early)]),
    ]
    h1q_here = local.fetch(h1q_any, h1q)
    pad_here = local.fetch(pad_any, pad)
    count = float(views * 4 * quarter)
    mean, rstd = stat3[0:1], stat3[1:2]
    scale = rstd * gain_last[...]
    shift_part, gain_part = grad_shift_last[...] / count, grad_gain_last[...] / count

    def grad_rows(q):
        rows = pl.ds(pl.multiple_of(q * block, block), block)
        high, low = split_pair(grad_pooled[rows])
        spread = dot(expand[...], jnp.concatenate([high, low], axis=0))
        grad = spread * slope[q].astype(F32)
        normed = (h3[q].astype(F32) - mean) * rstd
        gh3[q] = (scale * (grad - shift_part - normed * gain_part)).astype(BF16)

    mate_out = pl.ds(pl.multiple_of(width * (1 - c), width), width)
    own_out = pl.ds(pl.multiple_of(width * c, width), width)

    def part_of(i):
        def weight(rows):
            return jnp.concatenate([w3[k, rows] for k in range(4)], axis=1)

        value = dot(gh3[2 * i + c], weight(own_out)) + dot(gh3_mate[i], weight(mate_out))
        return dot(order[...], value.astype(BF16))

    mail = Mail(sends, recvs)
    beside = []
    for at, i in enumerate((1 - y, y)):
        for copy in rows_here[at]:
            copy.wait()
        grad_rows(2 * i + 1 - c)
        if at == 0:
            met()
        beside.append(mail.send(gh3.at[2 * i + 1 - c], gh3_mate.at[i], mate))
    for at, i in enumerate((1 - y, y)):
        for copy in rows_here[2 + at]:
            copy.wait()
        grad_rows(2 * i + c)
        if at == 0:
            w3_here.wait()
            perm_here.wait()
            beside[0].wait_recv()
            out_part[...] = part_of(1 - y).astype(BF16)
            across = mail.send(out_part, in_part, opposite)
    beside[1].wait_recv()
    ga2[...] = part_of(y)
    unperm_here = local.fetch(unperm_any, order)
    def fold_sems(at):
        return [sems.at[at] for sems in (pair1_sends, pair1_recvs, pair2_sends, pair2_recvs)]

    hid_block, hid_split = hl_parts.shape[1], head_last_out.shape[0]
    for half in range(2):
        product = exact(act4[half], grad_embed[...], 0, 0)
        ga1[: product.shape[0], : product.shape[1]] = product
        per_half = views // 2

        def spread_hidden(to, carry, half=half, per_half=per_half):
            spot = (4 * to + chan_at) * hid_block if hid_split == 4 else to * hid_block
            rows = pl.ds(pl.multiple_of(spot, hid_block), hid_block)
            hl_parts[half * per_half + to] = ga1[rows, : hl_parts.shape[2]]
            return carry

        lax.fori_loop(0, per_half, spread_hidden, 0)
        wide = grad_p1.shape[2] // per_half
        for to in range(per_half):
            p1_parts[half * per_half + to] = grad_p1[half, :, to * wide : (to + 1) * wide]
    scatter_start(hl_parts, hl_slots, group_sends.at[0], group_recvs.at[0], group)
    scatter_start(p1_parts, p1_slots, group_sends.at[1], group_recvs.at[1], group)
    act_here.wait()
    share_rows = last_parts.shape[1]
    for half in range(2):
        total = None
        for q in range(4):
            term = dot_tn(gh3[q], act[half, q])
            total = term if total is None else total + term
        low = total.astype(last_parts.dtype)
        for to in range(views):
            last_parts[to, :, half * half_width : (half + 1) * half_width] = low[
                to * share_rows : (to + 1) * share_rows
            ]
    fold_last = Fold(last_parts, last_in, last_slots, fold_sems(0), views)
    fold_last.start()
    for copy in beside:
        copy.wait_send()
    x = gh3
    x_here = local.fetch(x_any, x)
    h2q_here.wait()
    fold_last.pass_on(1, fold_last.size + 1)

    def sums_everywhere(at):
        return share(
            share_value(st, chan_slots.at[at], chan_sends.at[at], chan_recvs.at[at], chans),
            view_slots.at[at], group_sends.at[3 + at], group_recvs.at[3 + at], group,
        )

    def share_value(source, slots, send, recv, who):
        source[...] = share(source, slots, send, recv, who)
        return source

    gpad[...] = jnp.zeros(gpad.shape, gpad.dtype)
    across.wait()
    ga2[...] += in_part[...].astype(F32)
    halves = (y, 1 - y)

    def mid_norm(near):
        half = halves[near]
        gains = jnp.concatenate([smalls[2 * half], smalls[2 * half + 1]], axis=1)
        mean2, rstd2 = stats2[half, 0:1], stats2[half, 1:2]
        return mean2, rstd2, gains[2:3], gains[3:4]

    def half_cols(ref, near):
        low, high = ref[:, :half_width], ref[:, half_width:]
        return jnp.where(halves[near] == 0, low, high)

    for near in range(2):
        mean2, rstd2, gain2, shift2 = mid_norm(near)
        normed = (h2q[halves[near]].astype(F32) - mean2) * rstd2
        grad = half_cols(ga2, near) * silu_slope(normed * gain2 + shift2)
        ga1[:, near * half_width : (near + 1) * half_width] = grad
        st[halves[near], 0:1] = jnp.sum(grad, axis=0, keepdims=True)
        st[halves[near], 1:2] = jnp.sum(grad * normed, axis=0, keepdims=True)
    totals2 = sums_everywhere(0)
    view_slots[0, 0] = totals2
    for near in range(2):
        mean2, rstd2, gain2, shift2 = mid_norm(near)
        tot = view_slots[0, 0, halves[near]]
        normed = (h2q[halves[near]].astype(F32) - mean2) * rstd2
        grad = ga1[:, near * half_width : (near + 1) * half_width]
        low = (gain2 * rstd2 * (grad - tot[0:1] / count - normed * (tot[1:2] / count))).astype(BF16)
        gh2[near] = low
        gpad[near, 1 : SIDE + 1, 1 : SIDE + 1] = low.reshape(SIDE, SIDE, block, half_width)
    tot = view_slots[0, 0, y]
    own_cols = jnp.where(c == 0, tot[:, : half_width // 2], tot[:, half_width // 2 :])
    grad_shift_mid[...] = own_cols[0:1]
    grad_gain_mid[...] = own_cols[1:2]
    cut = quarter // 32 * 16
    far_pieces = [pl.ds(0, cut), pl.ds(cut, quarter - cut)]
    far_copies = [mail.send(gh2.at[1, far_pieces[0]], gh2_far.at[far_pieces[0]], opposite)]
    w2_here.wait()
    for copy in w2_far_here:
        copy.wait()
    channels = w2.shape[1] // 9
    for tap in range(9):
        a, b = 2 - tap // 3, 2 - tap % 3
        taps = slice(tap * channels, (tap + 1) * channels)
        term = None
        for near, weight in enumerate((w2, w2_far)):
            window = gpad[near, a : a + SIDE, b : b + SIDE].reshape(quarter, half_width)
            both = jnp.concatenate([weight[0, taps], weight[1, taps]], axis=1)
            piece = dot_nt(window, both)
            term = piece if term is None else term + piece
        if tap == 0:
            ga1[...] = term
        else:
            ga1[...] += term
    h1q_here.wait()
    for half in range(2):
        gains = jnp.concatenate([smalls[2 * half], smalls[2 * half + 1]], axis=1)
        normed = (h1q[half] - stat1[half, 0:1]) * stat1[half, 1:2]
        cols = slice(half * half_width, (half + 1) * half_width)
        grad = ga1[:, cols] * silu_slope(normed * gains[0:1] + gains[1:2])
        ga2[:, cols] = grad
        st[half, 0:1] = jnp.sum(grad, axis=0, keepdims=True)
        st[half, 1:2] = jnp.sum(grad * normed, axis=0, keepdims=True)
    share_value(st, chan_slots.at[1], chan_sends.at[1], chan_recvs.at[1], chans)
    far_copies.append(mail.send(gh2.at[1, far_pieces[1]], gh2_far.at[far_pieces[1]], opposite))
    share_start(st, view_slots.at[1], group_sends.at[4], group_recvs.at[4], group)

    pad_here.wait()

    def tap_term(at, tap, grads):
        a, b = tap // 3, tap % 3
        window = pad[at, a : a + SIDE, b : b + SIDE].reshape(quarter, channels)
        return dot_tn(window, grads)

    for tap in range(9):
        total = tap_term(y, tap, gh2[0])
        taps = slice(tap * channels, (tap + 1) * channels)
        wsum[0, taps] = total[:, : half_width // 2]
        wsum[1, taps] = total[:, half_width // 2 :]
    share_end(st, view_slots.at[1], group_sends.at[4], group_recvs.at[4], group)
    totals1 = add_slots(view_slots.at[1], views)
    view_slots[1, 0] = totals1
    tot = view_slots[1, 0, y]
    own_cols = jnp.where(c == 0, tot[:, : half_width // 2], tot[:, half_width // 2 :])
    grad_shift_first[...] = own_cols[0:1]
    grad_gain_first[...] = own_cols[1:2]
    unperm_here.wait()
    for half in range(2):
        gains = jnp.concatenate([smalls[2 * half], smalls[2 * half + 1]], axis=1)
        normed = (h1q[half] - stat1[half, 0:1]) * stat1[half, 1:2]
        cols = slice(half * half_width, (half + 1) * half_width)
        tot = totals1[half]
        low = (
            gains[0:1]
            * stat1[half, 1:2]
            * (ga2[:, cols] - tot[0:1] / count - normed * (tot[1:2] / count))
        ).astype(BF16)
        out_part[:, cols] = low
    gh1[chan_at] = dot(order[...], out_part[...]).astype(BF16)
    spot = gh1.at[chan_at]
    gh1_across = mail.send(spot, spot, opposite)
    gh1_beside = mail.send(spot, spot, mate)

    for copy in far_copies:
        copy.wait_recv()
    for tap in range(9):
        total = tap_term(1 - y, tap, gh2_far[...])
        taps = slice(tap * channels, (tap + 1) * channels)
        wsum[0, taps] += total[:, : half_width // 2]
        wsum[1, taps] += total[:, half_width // 2 :]
    mid_rows = mid_parts.shape[1]
    mid_flat = mid_parts.reshape(views * mid_rows, mid_parts.shape[2])
    if mid_parts.dtype == F32:
        mid_mate = mail.send(wsum.at[1 - c], mid_flat, mate)
    else:
        wsend[...] = wsum[1 - c].astype(wsend.dtype)
        mid_mate = mail.send(wsend, mid_flat, mate)
    mid_mate.wait_recv()

    def mid_block(to, carry):
        rows = pl.ds(pl.multiple_of(to * mid_rows, mid_rows), mid_rows)
        mid_parts[to] = (wsum[c, rows] + mid_parts[to].astype(F32)).astype(mid_parts.dtype)
        return carry

    lax.fori_loop(0, views, mid_block, 0)
    fold_mid = Fold(mid_parts, mid_in, mid_slots, fold_sems(1), views, False)
    fold_mid.start()
    scatter_end(p1_parts, p1_slots, group_sends.at[1], group_recvs.at[1], group)
    few = pooled.shape[0]

    def head_first_term(at, total):
        views_at = pl.ds(at * few, few)
        copy = pltpu.make_async_copy(pooled_any.at[views_at], pooled, local_sems.at[29])
        copy.start()
        copy.wait()
        rows = pooled[...].astype(F32).reshape(-1, width)
        return total + exact(rows, p1_slots[views_at].reshape(rows.shape[0], -1), 0, 0)

    head_first_out[...] = over(
        views // few, head_first_term, exact(pooled_means[...], jnp.sum(p1_slots[...], axis=1), 0, 0)
    )
    early_steps = fold_mid.size // 2 + 1
    fold_mid.pass_on(1, early_steps)
    gh1_across.wait_recv()
    far_spot = gh1.at[2 * (1 - y) + c]
    gh1_on = mail.send(far_spot, far_spot, mate)
    fold_mid.pass_on(early_steps, fold_mid.size + 1)
    rest = [local.fetch(mid_parts.at[view_at], mid_slots.at[fold_mid.outer])]
    gh1_beside.wait_recv()
    gh1_on.wait_recv()
    rest.append(local.fetch(gh1, gh1_out))
    x_here.wait()
    fold_last.end()
    first_parts = last_parts
    total = None
    for q in range(4):
        term = dot_tn(x[q], gh1[q])
        total = term if total is None else total + term
    low = total.astype(first_parts.dtype)
    for to in range(views):
        first_parts[to] = low[to * share_rows : (to + 1) * share_rows]
    fold_first = Fold(first_parts, last_in, first_slots, fold_sems(2), views)
    fold_first.start()

    scatter_end(hl_parts, hl_slots, group_sends.at[0], group_recvs.at[0], group)
    if hid_split == 4:
        head_last_out[chan_at] = add_slots(hl_slots, views)
        gather_start(head_last_out.at[chan_at], head_last_out, chan_sends.at[2], chan_recvs.at[2], chans)
    else:
        head_last_out[0] = add_slots(hl_slots, views)

    def blocks(kind, summed):
        wide = summed.shape[1] // 4
        for to in range(4):
            pair_parts[to, kind] = summed[:, to * wide : (to + 1) * wide]

    def summed_slots(slots):
        def add(at, total):
            return total + slots[at].astype(F32)

        return lax.fori_loop(1, slots.shape[0], add, slots[0].astype(F32))

    blocks(1, summed_slots(last_slots))
    fold_first.pass_on(1, fold_first.size + 1)
    fold_first.end()
    blocks(0, summed_slots(first_slots))
    row_views = views // 4
    to_view = chan_at * row_views + lax.div(view_at, 4)
    slot = lax.rem(view_at, 4)

    def pair_copy(to):
        return pltpu.make_async_remote_copy(
            src_ref=pair_parts.at[to],
            dst_ref=pair_out.at[slot],
            send_sem=pair_sends.at[to],
            recv_sem=pair_recvs.at[slot],
            device_id=(to_view, to),
            device_id_type=MESH,
        )

    def pair_arrival(origin):
        return pltpu.make_async_remote_copy(
            src_ref=pair_parts.at[0],
            dst_ref=pair_out.at[origin],
            send_sem=pair_sends.at[0],
            recv_sem=pair_recvs.at[origin],
            device_id=(from_view + origin, from_chan),
            device_id_type=MESH,
        )

    from_view, from_chan = 4 * lax.rem(view_at, row_views), lax.div(view_at, row_views)
    for to in range(4):
        own = jnp.logical_and(to_view == view_at, chan_at == to)

        @pl.when(own)
        def _():
            pair_out[slot] = pair_parts[to]

        @pl.when(jnp.logical_not(own))
        def _():
            pair_copy(to).start()

    for origin in range(4):
        own = jnp.logical_and(from_view + origin == view_at, chan_at == from_chan)

        @pl.when(jnp.logical_not(own))
        def _():
            pair_arrival(origin).wait_recv()

    for to in range(4):
        own = jnp.logical_and(to_view == view_at, chan_at == to)

        @pl.when(jnp.logical_not(own))
        def _():
            pair_copy(to).wait_send()

    if hid_split == 4:
        share_end(head_last_out.at[chan_at], head_last_out, chan_sends.at[2], chan_recvs.at[2], chans)
    fold_mid.end()
    for copy in rest:
        copy.wait()
    for copy in mail.copies[3:]:
        copy.wait_send()


def back_stage(views, head_outs, forward_outs, x, gain_last, perm, unperm, expand):
    (h3, slope, pooled_all, w2_late, h2q, stat3, grad_shift_last, grad_gain_last, _, _,
     grad_pooled, act4, grad_embed, grad_p1, _, stats2, pooled_means) = head_outs
    pad, h1q, w2, w2_early, w3, act, _, stat1, _, _, smalls = forward_outs
    quarter, width = h3.shape[1], h3.shape[2]
    block = quarter // PIX
    own = 4 * block
    mid = pad.shape[4]
    half = mid // 2
    hid, emb = 2 * act4.shape[2], grad_embed.shape[1]
    taps = w2.shape[1]
    hid_split = 4 if hid // views % 32 == 0 else 1
    hid_block = hid // views // hid_split
    mid_kind, row_kind = link_kind(taps // views), link_kind(width // views)
    vm = pltpu.VMEM
    return call(
        functools.partial(back_body, views),
        "back",
        (
            shape(4, quarter, mid, kind=BF16),
            shape(views // 2, taps // views, half // 2, kind=mid_kind),
            shape(4, 2, width // views, mid // 4),
            shape(hid_split, hid_block, emb),
            shape(width, hid // views),
            *[shape(1, half // 2)] * 4,
        ),
        27,
        [
            vm((4, quarter, width), BF16),
            vm((4, quarter, width), BF16),
            vm(w3.shape, BF16),
            vm(h2q.shape, BF16),
            vm((4, quarter, mid), BF16),
            vm((4, quarter, width), BF16),
            vm((2, quarter, width), BF16),
            vm((quarter, mid), BF16),
            vm((quarter, mid), BF16),
            vm((quarter, mid), F32),
            vm((2, quarter, half), BF16),
            vm((quarter, half), BF16),
            vm((2, PAD, PAD, block, half), BF16),
            vm((quarter, mid), F32),
            vm((2, 2, half), F32),
            vm((2, 4, 2, 2, half), F32),
            vm((2, views, 2, 2, half), F32),
            vm(unperm.shape, BF16),
            vm(pad.shape, BF16),
            vm(h1q.shape, F32),
            vm(w2.shape, BF16),
            vm(w2.shape, BF16),
            vm(act.shape, BF16),
            vm((min(views, 8), own, width), BF16),
            vm((2, taps, half // 2), F32),
            vm((taps if mid_kind == BF16 else 16, half // 2), BF16),
            vm((views, taps // views, half // 2), mid_kind),
            vm((views // 2, taps // views, half // 2), mid_kind),
            vm((views, width // views, mid), row_kind),
            vm((views // 2, width // views, mid), row_kind),
            vm((views // 2, width // views, mid), row_kind),
            vm((views // 2, width // views, mid), row_kind),
            vm((4, 2, width // views, mid // 4), F32),
            vm((views, hid_block, emb), F32),
            vm((views, hid_block, emb), F32),
            vm((views, own, hid // views), F32),
            vm((views, own, hid // views), F32),
            dma(10),
            dma(10),
            dma(3, 4),
            dma(3, 4),
            dma(7, views),
            dma(7, views),
            dma(4),
            dma(4),
            *[dma(3, views // 2)] * 4,
            dma(30),
        ],
        collective=4,
        any_ins=range(13, 27),
        any_outs=range(2),
    )(
        stat3, grad_shift_last, grad_gain_last, grad_pooled, gain_last, expand,
        stats2, smalls, stat1, act4, grad_embed, grad_p1, pooled_means,
        h3, slope, w3, h2q, perm, unperm, pad, h1q, w2, w2_early, w2_late, act,
        x.reshape(4, quarter, width), pooled_all,
    )


def last_body(
    gh1, w1_own, slope, grad_pooled, expand, mid_slots, pair_out, head_last_in, head_first_in, *more
):
    small_ins, small_outs = more[: len(more) // 2 - 3], more[len(more) // 2 + 3 :]
    grad_input, grad_mid, grad_first, grad_last, grad_head_last, grad_head_first = more[
        len(small_ins) : len(small_ins) + 6
    ]
    at = pl.program_id(0)
    high, low = split_pair(grad_pooled[...])
    spread = dot(expand[...], jnp.concatenate([high, low], axis=0))
    grad_input[...] = dot_nt(gh1[...], w1_own[...]) + spread * slope[...].astype(F32)

    @pl.when(at == 0)
    def _():
        views = mid_slots.shape[0]

        def add(slot, total):
            return total + mid_slots[slot].astype(F32)

        grad_mid[...] = lax.fori_loop(1, views, add, mid_slots[0].astype(F32))
        rows = pair_out.shape[2]
        for origin in range(4):
            grad_first[origin * rows : (origin + 1) * rows] = pair_out[origin, 0]
            grad_last[origin * rows : (origin + 1) * rows] = pair_out[origin, 1]
        for source, target in zip(small_ins, small_outs):
            target[...] = source[...]
        grad_head_first[...] = head_first_in[...]
        rows = head_last_in.shape[1]
        for origin in range(head_last_in.shape[0]):
            grad_head_last[origin * rows : (origin + 1) * rows] = head_last_in[origin]


def last_stage(
    gh1, w1_own, slope, grad_pooled, expand, mid_slots, pair_out, head_last_in, head_first_in, small
):
    quarter, mid, width = gh1.shape[1], gh1.shape[2], slope.shape[2]
    block = quarter // PIX

    def whole(array):
        dims = array.shape
        return pl.BlockSpec(dims, lambda q: (0,) * len(dims))

    def part(rows, columns):
        return pl.BlockSpec((rows, columns), lambda q: (q, 0))

    outs = (
        shape(4 * quarter, width),
        shape(*mid_slots.shape[1:]),
        shape(4 * pair_out.shape[2], pair_out.shape[3]),
        shape(4 * pair_out.shape[2], pair_out.shape[3]),
        shape(head_last_in.shape[0] * head_last_in.shape[1], head_last_in.shape[2]),
        shape(*head_first_in.shape),
        *[shape(*array.shape) for array in small],
    )
    return pl.pallas_call(
        last_body,
        grid=(4,),
        out_shape=outs,
        in_specs=[
            part(quarter, mid), whole(w1_own), part(quarter, width), part(block, width), whole(expand),
            whole(mid_slots), whole(pair_out), whole(head_last_in), whole(head_first_in),
            *[whole(array) for array in small],
        ],
        out_specs=(part(quarter, width), *(whole(out) for out in outs[1:])),
        name="results",
        compiler_params=pltpu.CompilerParams(
            vmem_limit_bytes=VMEM_BYTES, dimension_semantics=("arbitrary",)
        ),
    )(
        gh1.reshape(4 * quarter, mid), w1_own, slope.reshape(4 * quarter, width), grad_pooled, expand,
        mid_slots, pair_out, head_last_in, head_first_in, *small,
    )


def per_device(
    views,
    block_input,
    conv_first,
    conv_mid,
    conv_last,
    gain_first,
    shift_first,
    gain_mid,
    shift_mid,
    gain_last,
    shift_last,
    head_first,
    gain_head,
    shift_head,
    head_last,
    image_of,
    partner,
    sub_of,
):
    rows, width = block_input.shape
    quarter = rows // 4
    block = quarter // PIX
    perm, unperm = orders(quarter)
    at_row = np.arange(quarter)
    twice = np.arange(2 * block) % block
    expand = jnp.asarray((at_row[:, None] // PIX == twice[None, :]).astype(BF16))

    def line(vector):
        return vector.reshape(1, -1)

    forward_outs = forward_stage(
        views, block_input, conv_first, conv_mid, conv_last,
        [line(v) for v in (gain_first, shift_first, gain_mid, shift_mid)], perm, unperm,
    )
    w3, act, h2, stat2, w1_own = (forward_outs[at] for at in (4, 5, 6, 8, 9))
    head_outs = head_stage(
        views, [line(v) for v in (gain_last, shift_last, gain_head, shift_head)],
        [line(v) for v in (sub_of, image_of, partner)], stat2,
        act, w3, block_input, head_first, head_last, conv_mid, h2,
    )
    slope, grad_pooled, loss = head_outs[1], head_outs[10], head_outs[14]
    (gh1, mid_slots, pair_out, head_last_in, head_first_in,
     grad_shift_mid, grad_gain_mid, grad_shift_first, grad_gain_first) = back_stage(
        views, head_outs, forward_outs, block_input, line(gain_last), perm, unperm, expand
    )
    small = [
        grad_gain_first, grad_shift_first, grad_gain_mid, grad_shift_mid,
        head_outs[7], head_outs[6], head_outs[9], head_outs[8], loss,
    ]
    grad_input, grad_mid, grad_first, grad_last, grad_head_last, grad_head_first, *small = last_stage(
        gh1, w1_own, slope, grad_pooled, expand, mid_slots, pair_out, head_last_in, head_first_in, small
    )
    return (
        small[8].reshape(()),
        grad_input,
        grad_first,
        grad_mid,
        grad_last,
        grad_head_first,
        grad_head_last,
        *[vector.reshape(-1) for vector in small[:8]],
    )


def solution(mesh):
    views = mesh.shape["views"]
    return jax.shard_map(
        functools.partial(per_device, views),
        mesh=mesh,
        in_specs=(
            P("views", "chan"),
            P(None, "chan"),
            P(None, "chan"),
            P(None, "chan"),
            P("chan"),
            P("chan"),
            P("chan"),
            P("chan"),
            P("chan"),
            P("chan"),
            P("chan", None),
            P(),
            P(),
            P(),
            P(),
            P(),
            P(),
        ),
        out_specs=(
            P(),
            P("views", "chan"),
            P("views", "chan"),
            P("views", "chan"),
            P("views", "chan"),
            P("chan", "views"),
            P("views", None),
            P("chan"),
            P("chan"),
            P("chan"),
            P("chan"),
            P("chan"),
            P("chan"),
            P(),
            P(),
        ),
        check_vma=False,
    )
```

```python
import functools

import jax
import jax.numpy as jnp
import numpy as np
from jax import lax
from jax.experimental import pallas as pl
from jax.experimental.pallas import tpu as pltpu
from jax.sharding import PartitionSpec as P

SIDE = 7
PIX = SIDE * SIDE
PAD = SIDE + 2
SUB = 256
EPS = 1e-05
RIDGE = 0.5
MESH = pl.DeviceIdType.MESH
BF16 = jnp.bfloat16
F32 = jnp.float32
VMEM_BYTES = 60 << 20


def place():
    view_at, chan_at = lax.axis_index("views"), lax.axis_index("chan")
    return view_at, chan_at, lax.div(chan_at, 2), lax.rem(chan_at, 2)


def greet(peers, groups=()):
    barrier = pltpu.get_barrier_semaphore()
    total = len(peers)
    for peer in peers:
        pl.semaphore_signal(barrier, inc=1, device_id=peer, device_id_type=MESH)
    for size, own, device in groups:

        def tell(step, carry, size=size, own=own, device=device):
            pl.semaphore_signal(
                barrier, inc=1, device_id=device(lax.rem(own + step, size)), device_id_type=MESH
            )
            return carry

        lax.fori_loop(1, size, tell, 0)
        total += size - 1
    return lambda: pl.semaphore_wait(barrier, total)


class Mail:
    def __init__(self, send_sems, recv_sems):
        self.send_sems, self.recv_sems, self.copies = send_sems, recv_sems, []

    def send(self, source, target, peer):
        spot = len(self.copies)
        copy = pltpu.make_async_remote_copy(
            src_ref=source,
            dst_ref=target,
            send_sem=self.send_sems.at[spot],
            recv_sem=self.recv_sems.at[spot],
            device_id=peer,
            device_id_type=MESH,
        )
        copy.start()
        self.copies.append(copy)
        return copy

    def finish(self):
        for copy in self.copies:
            copy.wait_send()


class Local:
    def __init__(self, sems):
        self.sems, self.used = sems, 0

    def fetch(self, source, target):
        copy = pltpu.make_async_copy(source, target, self.sems.at[self.used])
        copy.start()
        self.used += 1
        return copy


def group_copy(source, slots, sends, recvs, size, own, device, step):
    to = lax.rem(own + step, size)
    return pltpu.make_async_remote_copy(
        src_ref=source,
        dst_ref=slots.at[own],
        send_sem=sends.at[step],
        recv_sem=recvs.at[own],
        device_id=device(to),
        device_id_type=MESH,
    )


def group_arrival(source, slots, sends, recvs, size, own, device, step):
    origin = lax.rem(own + step, size)
    return pltpu.make_async_remote_copy(
        src_ref=source,
        dst_ref=slots.at[origin],
        send_sem=sends.at[step],
        recv_sem=recvs.at[origin],
        device_id=device(origin),
        device_id_type=MESH,
    )


def share_start(source, slots, sends, recvs, group):
    def start(step, carry):
        group_copy(source, slots, sends, recvs, *group, step).start()
        return carry

    lax.fori_loop(1, group[0], start, 0)
    slots[group[1]] = source[...]


def share_end(source, slots, sends, recvs, group):
    def end(step, carry):
        group_arrival(source, slots, sends, recvs, *group, step).wait_recv()
        group_copy(source, slots, sends, recvs, *group, step).wait_send()
        return carry

    lax.fori_loop(1, group[0], end, 0)


def add_slots(slots, size):
    def add(at, total):
        return total + slots[at]

    return lax.fori_loop(1, size, add, slots[0])


def share(source, slots, sends, recvs, group):
    share_start(source, slots, sends, recvs, group)
    share_end(source, slots, sends, recvs, group)
    return add_slots(slots, group[0])


def gather_start(source, slots, sends, recvs, group):
    def start(step, carry):
        group_copy(source, slots, sends, recvs, *group, step).start()
        return carry

    lax.fori_loop(1, group[0], start, 0)


def scatter_start(parts, slots, sends, recvs, group, keep=True):
    size, own, device = group

    def start(step, carry):
        to = lax.rem(own + step, size)
        group_copy(parts.at[to], slots, sends, recvs, *group, step).start()
        return carry

    lax.fori_loop(1, size, start, 0)
    if keep:
        slots[own] = parts[own]


def scatter_end(parts, slots, sends, recvs, group):
    share_end(parts.at[group[1]], slots, sends, recvs, group)


class Fold:
    def __init__(self, parts, fold_in, slots, sems, views, keep=True):
        view_at, chan_at, _, _ = place()
        self.parts, self.fold_in, self.slots, self.sems, self.keep = parts, fold_in, slots, sems, keep
        self.size, self.outer, self.inner = views // 2, lax.div(view_at, 2), lax.rem(view_at, 2)
        self.pair = (2 * self.outer + 1 - self.inner, chan_at)
        self.chan_at = chan_at

    def block(self, step):
        return lax.rem(self.outer + step, self.size)

    def pair_copy(self, step):
        at = self.block(step)
        return pltpu.make_async_remote_copy(
            src_ref=self.parts.at[2 * at + 1 - self.inner],
            dst_ref=self.fold_in.at[at],
            send_sem=self.sems[0].at[at],
            recv_sem=self.sems[1].at[at],
            device_id=self.pair,
            device_id_type=MESH,
        )

    def out_copy(self, step, slot):
        at = self.block(step)
        return pltpu.make_async_remote_copy(
            src_ref=self.parts.at[2 * at + self.inner],
            dst_ref=self.slots.at[slot],
            send_sem=self.sems[2].at[at],
            recv_sem=self.sems[3].at[slot],
            device_id=(2 * at + self.inner, self.chan_at),
            device_id_type=MESH,
        )

    def start(self):
        def one(step, carry):
            self.pair_copy(step).start()
            return carry

        lax.fori_loop(1, self.size + 1, one, 0)

    def add(self, step):
        self.pair_copy(step).wait_recv()
        at, mine = self.block(step), 2 * self.block(step) + self.inner
        total = self.parts[mine].astype(F32) + self.fold_in[at].astype(F32)
        self.parts[mine] = total.astype(self.parts.dtype)

    def pass_on(self, first, last):
        def one(step, carry):
            self.add(step)
            self.out_copy(step, self.outer).start()
            return carry

        lax.fori_loop(first, min(last, self.size), one, 0)
        if last > self.size:
            self.add(self.size)
            if self.keep:
                self.slots[self.outer] = self.parts[2 * self.outer + self.inner]

    def end(self):
        def one(step, carry):
            self.out_copy(step, self.block(step)).wait_recv()
            self.out_copy(step, self.outer).wait_send()
            return carry

        lax.fori_loop(1, self.size, one, 0)

        def sent(step, carry):
            self.pair_copy(step).wait_send()
            return carry

        lax.fori_loop(1, self.size + 1, sent, 0)


def chan_group():
    view_at, chan_at, y, c = place()
    return (4, chan_at, lambda at: (view_at, at))


def half_group(views):
    view_at, chan_at, y, c = place()
    return (
        2 * views,
        2 * view_at + c,
        lambda at: (lax.div(at, 2), 2 * y + lax.rem(at, 2)),
    )


def view_group(views):
    view_at, chan_at, y, c = place()
    return (views, view_at, lambda at: (at, chan_at))


def all_group(views):
    view_at, chan_at, y, c = place()
    return (4 * views, 4 * view_at + chan_at, lambda at: (lax.div(at, 4), lax.rem(at, 4)))


def dot(left, right):
    return jnp.dot(left, right, preferred_element_type=F32)


def dot_nt(left, right):
    return lax.dot_general(left, right, (((1,), (1,)), ((), ())), preferred_element_type=F32)


def dot_tn(left, right):
    return lax.dot_general(left, right, (((0,), (0,)), ((), ())), preferred_element_type=F32)


def gate(level):
    return 0.5 + 0.5 * jnp.tanh(0.5 * level)


def silu_slope(level):
    open_part = gate(level)
    return open_part * (1.0 + level * (1.0 - open_part))


def call(body, name, outs, ins, scratch, collective, any_ins=(), any_outs=()):
    def spec(at, places):
        return pl.BlockSpec(memory_space=pl.ANY if at in places else pltpu.VMEM)

    return pl.pallas_call(
        body,
        out_shape=outs,
        in_specs=[spec(at, any_ins) for at in range(ins)],
        out_specs=tuple(spec(at, any_outs) for at in range(len(outs))),
        scratch_shapes=scratch,
        name=name,
        compiler_params=pltpu.CompilerParams(
            collective_id=collective,
            has_side_effects=collective is not None,
            vmem_limit_bytes=VMEM_BYTES,
        ),
    )


def shape(*dims, kind=F32):
    return jax.ShapeDtypeStruct(dims, kind)


def dma(*dims):
    return pltpu.SemaphoreType.DMA(dims)


def split_rows(value):
    high = value.astype(BF16)
    rest = value - high.astype(F32)
    middle = rest.astype(BF16)
    low = (rest - middle.astype(F32)).astype(BF16)
    return jnp.concatenate([high, middle, low], axis=0)


def join_rows(stacked):
    rows = stacked.shape[0] // 3
    return stacked[2 * rows :] + stacked[rows : 2 * rows] + stacked[:rows]


def split_pair(value):
    high = value.astype(BF16)
    return high, (value - high.astype(F32)).astype(BF16)


def exact(left, right, left_dim, right_dim):
    return lax.dot_general(
        left,
        right,
        (((left_dim,), (right_dim,)), ((), ())),
        precision=lax.Precision.HIGHEST,
        preferred_element_type=F32,
    )


def over(count, body, start):
    return body(0, start) if count == 1 else lax.fori_loop(0, count, body, start)


def split_three(value):
    high = value.astype(BF16)
    rest = value - high.astype(F32)
    middle = rest.astype(BF16)
    return high, middle, (rest - middle.astype(F32)).astype(BF16)


def short_product(left, right):
    lh, lm, ll = split_three(left)
    rh, rm, rl = split_three(right)
    return dot_tn(
        jnp.concatenate([lh, lh, lm, lh, lm, ll], axis=0),
        jnp.concatenate([rh, rm, rh, rl, rm, rh], axis=0),
    )


def outer_product(left, right):
    def rows(value, high_at, middle_at, low_at):
        parts = [part.astype(F32) for part in split_three(value)]
        row = lax.broadcasted_iota(jnp.int32, (16, value.shape[1]), 0)
        total = jnp.zeros((16, value.shape[1]), F32)
        for part, places in zip(parts, (high_at, middle_at, low_at)):
            for place_at in places:
                total = jnp.where(row == place_at, part, total)
        return total.astype(BF16)

    return dot_tn(rows(left, (0, 1, 3), (2, 4), (5,)), rows(right, (0, 2, 5), (1, 4), (3,)))


def factor_inverse(work, inverse, subs, width):
    panel = 16
    row = lax.broadcasted_iota(jnp.int32, (panel, width), 0)

    def wide(part):
        return jnp.broadcast_to(part, (panel, width))

    def eliminate(s, first):
        rows = work[s, first : first + panel]
        columns = [wide(rows[:, first + j : first + j + 1]) for j in range(panel)]
        diagonal = jnp.zeros((panel, width), F32)
        for j in range(panel):
            pivot = wide(columns[j][j : j + 1])
            diagonal = jnp.where(row == j, pivot, diagonal)
            if j == panel - 1:
                break
            ratio = jnp.where(row > j, columns[j] * (1.0 / pivot), 0.0)
            for k in range(j + 1, panel):
                columns[k] = columns[k] - ratio * wide(columns[k][j : j + 1])
            rows = rows - jnp.concatenate([ratio, ratio], axis=1) * rows[j : j + 1]
        inverse[s, first : first + panel] = rows[:, width:] * lax.rsqrt(diagonal)
        if first + panel < width:
            scaled = rows[:, :width] / diagonal
            work[s, first + panel :] -= short_product(scaled, rows)[first + panel :]

    def some(at, carry):
        for first in range(0, width, panel):
            for k in range(2):
                eliminate(2 * at + k, first)
        return carry

    over(subs // 2, some, 0)


def view_sums(value, block):
    return jnp.concatenate(
        [jnp.sum(value[PIX * v : PIX * (v + 1)], axis=0, keepdims=True) for v in range(block)], axis=0
    )


def columns_of(row, column):
    tile = column.shape[1]

    def one(at, carry):
        cols = pl.ds(pl.multiple_of(at * tile, tile), tile)
        column[cols] = jnp.broadcast_to(row[:, cols].astype(F32), (tile, tile)).T
        return carry

    lax.fori_loop(0, row.shape[1] // tile, one, 0)


def whiten(embed, sub_col, image_col, image_row, partner_col, partner_row, refs, own_rows):
    work, inverse, white, unit, unit_parts, back = refs
    total, width = embed.shape
    subs = inverse.shape[0]
    eye = (
        lax.broadcasted_iota(jnp.int32, (width, width), 0)
        == lax.broadcasted_iota(jnp.int32, (width, width), 1)
    ).astype(F32)
    size = min(total, 512)
    pieces = total // size

    def rows_at(at):
        return pl.ds(pl.multiple_of(at * size, size), size)

    means = []

    def masks(rows, s):
        column = sub_col[rows]
        return (column == float(s)).astype(F32), (column == float(s + 1)).astype(F32)

    for s in range(0, subs, 2):

        def moments(at, sums, s=s):
            rows = rows_at(at)
            value = embed[rows]
            picked = jnp.concatenate([value * mask for mask in masks(rows, s)], axis=1)
            first = sums[0] + jnp.sum(picked, axis=0, keepdims=True)
            return first, sums[1] + exact(picked, value, 0, 0)

        first, second = over(
            pieces, moments, (jnp.zeros((1, 2 * width), F32), jnp.zeros((2 * width, width), F32))
        )
        for k in range(2):
            mean = first[:, k * width : (k + 1) * width] / SUB
            cov = second[k * width : (k + 1) * width] / SUB - exact(mean, mean, 0, 0)
            work[s + k, :, :width] = cov + RIDGE * eye
            work[s + k, :, width:] = eye
            means.append(mean)
    factor_inverse(work, inverse, subs, width)

    def whitening(at, carry):
        rows = rows_at(at)
        value = None
        for s in range(0, subs, 2):
            centred = jnp.concatenate(
                [(embed[rows] - means[s + k]) * mask for k, mask in enumerate(masks(rows, s))], axis=1
            )
            term = exact(centred, jnp.concatenate([inverse[s], inverse[s + 1]], axis=1), 1, 1)
            value = term if value is None else value + term
        white[rows] = value
        value = value * lax.rsqrt(jnp.sum(value * value, axis=1, keepdims=True) + EPS)
        unit[rows] = value
        high = value.astype(BF16)
        rest = value - high.astype(F32)
        middle = rest.astype(BF16)
        unit_parts[rows] = jnp.concatenate(
            [high, middle, (rest - middle.astype(F32)).astype(BF16)], axis=1
        )
        return carry

    over(pieces, whitening, 0)
    chunk = min(total, 262144 // total)

    def pairs(at, loss):
        rows = pl.ds(pl.multiple_of(at * chunk, chunk), chunk)
        across = lax.broadcasted_iota(jnp.int32, (chunk, total), 1).astype(F32)
        down = lax.broadcasted_iota(jnp.int32, (chunk, total), 0) + at * chunk

        def pick(hot):
            found = dot(hot.astype(F32).astype(BF16), unit_parts[...])
            return found[:, 2 * width :] + found[:, width : 2 * width] + found[:, :width]

        mine = unit[rows]
        ahead = pick(partner_col[rows][:, :1] == across)
        behind = pick(partner_row[...] == down)
        members = jnp.sum(
            (image_col[rows][:, :1] == image_row[...].astype(F32)).astype(F32), axis=1, keepdims=True
        )
        weight = 1.0 / members
        apart = mine - ahead
        grad = (4.0 / total) * weight * (2.0 * mine - ahead - behind)
        length = lax.rsqrt(jnp.sum(white[rows] * white[rows], axis=1, keepdims=True) + EPS)
        back[rows] = length * (grad - mine * jnp.sum(mine * grad, axis=1, keepdims=True))
        per_view = jnp.sum(apart * apart, axis=1, keepdims=True) * weight
        return loss + jnp.sum(per_view, axis=0, keepdims=True)

    loss = over(total // chunk, pairs, jnp.zeros((1, 1), F32)) * (2.0 / total)
    lower = lax.broadcasted_iota(jnp.int32, (width, width), 0) >= lax.broadcasted_iota(
        jnp.int32, (width, width), 1
    )
    own_white, own_back = white[own_rows], back[own_rows]
    gradient = jnp.zeros(own_white.shape, F32)
    for s in range(0, subs, 2):

        def pulled(at, sums, s=s):
            rows = rows_at(at)
            picked = jnp.concatenate([back[rows] * mask for mask in masks(rows, s)], axis=1)
            spread = sums[0] + jnp.sum(picked, axis=0, keepdims=True)
            return spread, sums[1] + exact(picked, white[rows], 0, 0)

        spread, sums = over(
            pieces, pulled, (jnp.zeros((1, 2 * width), F32), jnp.zeros((2 * width, width), F32))
        )
        for k, own_mask in enumerate(masks(own_rows, s)):
            cols = slice(k * width, (k + 1) * width)
            low_part = jnp.where(lower, sums[cols], 0.0)
            mirrored = low_part + low_part.T - sums[cols] * eye
            moved = own_back - (exact(own_white, mirrored, 1, 0) + spread[:, cols]) / SUB
            gradient = gradient + own_mask * exact(moved, inverse[s + k], 1, 0)
    return loss, gradient


EARLY_TAPS = 3


def orders(quarter):
    block = quarter // PIX
    row = np.arange(quarter)
    source = (row % block) * PIX + row // block
    hot = (source[:, None] == row[None, :]).astype(BF16)
    return jnp.asarray(hot), jnp.asarray(hot.T)


def front_body(
    views, g1, b1, g2, b2, gain_last, shift_last, gain_head, shift_head, sub_row, image_row, partner_row,
    x_any, w1in, w2in, w3in, perm_any, unperm_any, head_first_any, head_last_any,
    pad_out, h1_out, w2_out, w2_far, w3_out, act_out, h3_out, slope_out, pooled_all, h2q,
    stat, w1_own, smalls, stat3, grad_shift_last, grad_gain_last, grad_shift_head, grad_gain_head,
    grad_pooled_out, act4, grad_embed_out, grad_p1, loss_out, stats2, pooled_means, rows_sum,
    x, w1, act, h3, h1, st, slots, st2, slots2, perm, unperm, pad, w2, w3, hidden, h2, small,
    head_first, head_last, slope, pooled_own, pooled_low, sub_col, image_col, partner_col,
    embed_all, part, part_in, mean_sums, slope_sums, st3, slots3, st4, slots4, bk4, bslots4, bk3, bslots3, embed_own,
    work, inverse, white, unit, unit_parts, back,
    sends, recvs, part_sends, part_recvs, half_sends, half_recvs, group_sends, group_recvs, local_sems,
):
    view_at, chan_at, y, c = place()
    mate, opposite = (view_at, 2 * y + 1 - c), (view_at, 2 * (1 - y) + c)
    diagonal = (view_at, 2 * (1 - y) + 1 - c)
    half_peers, group = half_group(views), view_group(views)
    quarter, depth = x.shape[1], x.shape[2]
    width = h3.shape[2]
    block = quarter // PIX
    views_own = 4 * block
    parts = act.reshape(2, 2, 2, quarter, act.shape[3])
    out_part, in_part = parts.at[0], parts.at[1]
    xm = h3.at[pl.ds(0, 2)]
    near, far = 2 * y + c, 2 * (1 - y) + c
    near_rows = pl.ds(pl.multiple_of(2 * depth * y, 2 * depth), 2 * depth)
    far_rows = pl.ds(pl.multiple_of(2 * depth * (1 - y), 2 * depth), 2 * depth)
    met = greet([opposite, diagonal], [half_peers])
    local = Local(local_sems)
    w1_here = local.fetch(w1in.at[near_rows], w1.at[near])
    perm_here = local.fetch(perm_any, perm)
    x_own = [local.fetch(x_any.at[2 * q + c], x.at[2 * q + c]) for q in range(2)]
    w2_here = local.fetch(w2in, w2.at[c])
    unperm_here = local.fetch(unperm_any, unperm)
    rest = [local.fetch(w3in.at[near_rows], w3.at[near])]
    for at, vector in enumerate((g1, b1, g2, b2)):
        small[at : at + 1] = vector[...]
        small[4 + at : 5 + at] = vector[...]
    smalls[chan_at] = small[...]
    pad[...] = jnp.zeros(pad.shape, pad.dtype)
    met()
    mail = Mail(sends, recvs)
    w1_mate = mail.send(w1in.at[near_rows], w1.at[near], mate)
    x_mate = [mail.send(x_any.at[1 - c], xm.at[0], mate)]
    w1_far = mail.send(w1in.at[far_rows], w1.at[near], opposite)
    x_mate.append(mail.send(x_any.at[3 - c], xm.at[1], mate))
    small_copies = [mail.send(small, smalls.at[chan_at], to) for to in (mate, opposite, diagonal)]
    w2_mate = mail.send(w2in, w2.at[c], mate)
    w3_mate = mail.send(w3in.at[near_rows], w3.at[near], mate)

    def part_copy(half, q):
        return pltpu.make_async_remote_copy(
            src_ref=out_part.at[half, q],
            dst_ref=in_part.at[half, q],
            send_sem=part_sends.at[half, q],
            recv_sem=part_recvs.at[half, q],
            device_id=opposite,
            device_id_type=MESH,
        )

    own_in, mate_in = (
        pl.ds(pl.multiple_of(depth * k, depth), depth) for k in (c, 1 - c)
    )

    def send_part(half, q):
        def weight(rows):
            return jnp.concatenate([w1[2 * half, rows], w1[2 * half + 1, rows]], axis=1)

        value = dot(x[2 * q + c], weight(own_in)) + dot(xm[q], weight(mate_in))
        out_part[half, q] = dot(perm[...], value.astype(BF16)).astype(BF16)
        part_copy(half, q).start()

    w1_here.wait()
    w1_mate.wait_recv()
    perm_here.wait()
    for q in range(2):
        x_own[q].wait()
        x_mate[q].wait_recv()
        send_part(y, q)
    w1_far.wait_recv()
    w1_on = mail.send(w1.at[far], w1.at[far], mate)
    w1_on.wait_recv()
    for q in range(2):
        send_part(1 - y, q)
    x_rest = [local.fetch(x_any.at[2 * q + 1 - c], x.at[2 * q + 1 - c]) for q in range(2)]
    w2_here.wait()
    w2_mate.wait_recv()
    rest.append(local.fetch(w2, w2_out))
    own_rows = pl.ds(pl.multiple_of(depth * c, depth), depth)
    w1_own[...] = jnp.concatenate([w1[k, own_rows] for k in range(4)], axis=1)
    st[...] = jnp.zeros(st.shape, st.dtype)
    step_rows = quarter // SIDE

    def sums(half):
        def one(q, carry):
            part_copy(half, q).wait_recv()

            def rows_of(at, inner):
                rows = pl.ds(at * step_rows, step_rows)
                value = out_part[half, q, rows].astype(F32) + in_part[half, q, rows].astype(F32)
                h1[half, q, rows] = value
                st[half, 0:1] += jnp.sum(value, axis=0, keepdims=True)
                st[half, 1:2] += jnp.sum(value * value, axis=0, keepdims=True)
                return inner

            return lax.fori_loop(0, SIDE, rows_of, carry)

        lax.fori_loop(0, 2, one, 0)

    sums(1 - y)
    sums(y)
    for half in range(2):
        for q in range(2):
            part_copy(half, q).wait_send()
    share_start(st, slots, half_sends.at[0], half_recvs.at[0], half_peers)
    w3_far = mail.send(w3in.at[far_rows], w3.at[near], opposite)
    channels = pad.shape[4]
    early_taps = []
    for tap in range(EARLY_TAPS):
        rows = pl.ds(tap * channels, channels)
        early_taps.append(mail.send(w2in.at[rows], w2_far.at[c, rows], opposite))
    share_end(st, slots, half_sends.at[0], half_recvs.at[0], half_peers)
    totals = add_slots(slots, half_peers[0])
    count = float(views * 4 * quarter)
    for copy in small_copies:
        copy.wait_recv()
    mean = totals[:, 0:1] / count
    rstd = lax.rsqrt(totals[:, 1:2] / count - mean * mean + EPS)
    stat[...] = jnp.concatenate([mean, rstd], axis=1)
    for half in range(2):
        gains = jnp.concatenate([smalls[2 * half], smalls[2 * half + 1]], axis=1)
        scale = rstd[half] * gains[0:1]
        bias = gains[1:2] - mean[half] * scale

        def act_rows(at, carry, half=half, scale=scale, bias=bias):
            q, i = lax.div(at, SIDE), lax.rem(at, SIDE)
            level = h1[half, q, pl.ds(i * step_rows, step_rows)] * scale + bias
            value = (level * gate(level)).astype(BF16)
            pad[q, i + 1, 1 : SIDE + 1, :, 256 * half : 256 * half + 256] = value.reshape(
                SIDE, step_rows // SIDE, 256
            )
            return carry

        lax.fori_loop(0, 2 * SIDE, act_rows, 0)
    rest.append(local.fetch(pad, pad_out))
    rest += [local.fetch(h1.at[half, y], h1_out.at[half]) for half in range(2)]
    w3_far.wait_recv()
    w3_on = mail.send(w3.at[far], w3.at[far], mate)
    st2[...] = jnp.zeros(st2.shape, F32)

    def convolve(q, carry):
        for tap in range(9):
            a, b = tap // 3, tap % 3
            window = pad[q, a : a + SIDE, b : b + SIDE].reshape(quarter, channels)
            taps = slice(tap * channels, (tap + 1) * channels)
            term = dot(window, jnp.concatenate([w2[0, taps], w2[1, taps]], axis=1))
            if tap == 0:
                hidden[q] = term
            else:
                hidden[q] += term
        value = hidden[q]
        h2[q] = value.astype(BF16)
        st2[0:1] += jnp.sum(value, axis=0, keepdims=True)
        st2[1:2] += jnp.sum(value * value, axis=0, keepdims=True)
        return carry

    lax.fori_loop(0, 2, convolve, 0)
    share_start(st2, slots2, half_sends.at[1], half_recvs.at[1], half_peers)
    rest.append(local.fetch(h2.at[y], h2q.at[y]))
    w2_on = []

    def pass_on(taps):
        for tap in taps:
            early_taps[tap].wait_recv()
            rows = pl.ds(tap * channels, channels)
            w2_on.append(mail.send(w2_far.at[c, rows], w2_far.at[c, rows], mate))

    pass_on(range(EARLY_TAPS - 1))
    share_end(st2, slots2, half_sends.at[1], half_recvs.at[1], half_peers)
    totals2 = add_slots(slots2, half_peers[0])
    mean2 = totals2[0:1] / count
    rstd2 = lax.rsqrt(totals2[1:2] / count - mean2 * mean2 + EPS)
    stats2[y] = jnp.concatenate([mean2, rstd2], axis=0)
    gains = jnp.concatenate([smalls[2 * y], smalls[2 * y + 1]], axis=1)
    scale2 = rstd2 * gains[2:3]
    bias2 = gains[3:4] - mean2 * scale2
    across, beside = [], []
    unperm_here.wait()
    for q in range(2):
        level = hidden[q] * scale2 + bias2
        value = (level * gate(level)).astype(BF16)
        act[y, 2 * q + c] = dot(unperm[...], value).astype(BF16)
        spot = act.at[y, 2 * q + c]
        across.append(mail.send(spot, spot, opposite))
        beside.append(mail.send(spot, spot, mate))
    pass_on(range(EARLY_TAPS - 1, EARLY_TAPS))
    stat2_far = mail.send(stats2.at[y], stats2.at[y], opposite)

    own_out = pl.ds(pl.multiple_of(width * c, width), width)
    st3[...] = jnp.zeros(st3.shape, F32)
    head_first_here = local.fetch(head_first_any, head_first)
    head_last_here = local.fetch(head_last_any, head_last)
    for copy in (w3_mate, w3_on):
        copy.wait_recv()
    rest[0].wait()
    w3_kept = local.fetch(w3, w3_out)

    def last_conv(q):
        total = None
        for half in range(2):
            weight = jnp.concatenate([w3[2 * half, own_out], w3[2 * half + 1, own_out]], axis=1)
            term = dot_nt(act[half, q], weight)
            total = term if total is None else total + term
        low = total.astype(BF16)
        h3[q] = low
        value = low.astype(F32)
        st3[0:1] += jnp.sum(value, axis=0, keepdims=True)
        st3[1:2] += jnp.sum(value * value, axis=0, keepdims=True)

    for row, column in ((sub_row, sub_col), (image_row, image_col), (partner_row, partner_col)):
        columns_of(row, column)
    for q in range(2):
        across[q].wait_recv()
        spot = act.at[1 - y, 2 * q + c]
        passed = mail.send(spot, spot, mate)
        last_conv(2 * q + c)
        beside[q].wait_recv()
        passed.wait_recv()
        last_conv(2 * q + 1 - c)
    for copy in w2_on:
        copy.wait_recv()
    act_kept = local.fetch(act, act_out)
    share_start(st3, slots3, group_sends.at[0], group_recvs.at[0], group)
    rest.append(local.fetch(h3, h3_out))
    share_end(st3, slots3, group_sends.at[0], group_recvs.at[0], group)
    totals = add_slots(slots3, views)
    count = float(views * 4 * quarter)
    mean = totals[0:1] / count
    rstd = lax.rsqrt(totals[1:2] / count - mean * mean + EPS)
    stat3[...] = jnp.concatenate([mean, rstd], axis=0)
    scale = rstd * gain_last[...]
    bias = shift_last[...] - mean * scale
    for copy in x_rest:
        copy.wait()

    def pool_block(q, carry):
        before = x[q].astype(F32) + (h3[q].astype(F32) * scale + bias)
        sums = view_sums(before * gate(before), block)
        pooled_own[pl.ds(pl.multiple_of(q * block, block), block)] = sums * (1.0 / PIX)
        return carry

    lax.fori_loop(0, 4, pool_block, 0)
    head_first_here.wait()
    hidden = join_rows(dot(split_rows(pooled_own[...]), head_first[...]))
    wide = hidden.shape[1] // 2
    part[0] = hidden[:, :wide]
    part[1] = hidden[:, wide:]
    swap = mail.send(part, part_in.at[pl.ds(0, 2)], mate)

    def slope_block(q, carry):
        level3 = h3[q].astype(F32)
        before = x[q].astype(F32) + (level3 * scale + bias)
        low = silu_slope(before).astype(BF16)
        slope[q] = low
        normed = (level3 - mean) * rstd
        kept = low.astype(F32)
        rows = pl.ds(pl.multiple_of(q * block, block), block)
        slope_sums[0, rows] = view_sums(kept, block)
        slope_sums[1, rows] = view_sums(kept * normed, block)
        return carry

    swap.wait()
    mean_sums[...] = part[...] + part_in[0:2]
    across_p1 = mail.send(mean_sums.at[c], part_in.at[2], opposite)
    lax.fori_loop(0, 2, slope_block, 0)
    across_p1.wait_recv()
    part_in[4 + c] = mean_sums[c] + part_in[2]
    gathered = mail.send(part_in.at[4 + c], part_in.at[4 + c], mate)
    h2_far = mail.send(h2.at[1 - y], h2q.at[y], opposite)
    late_rows = pl.ds(EARLY_TAPS * channels, w2in.shape[0] - EARLY_TAPS * channels)
    w2_over = mail.send(w2in.at[late_rows], w2_far.at[c, late_rows], opposite)
    gathered.wait_recv()
    p1 = part_in[4:6]
    st4[0:2] = jnp.sum(p1, axis=1)
    st4[2:4] = jnp.sum(p1 * p1, axis=1)
    share_start(st4, slots4, group_sends.at[1], group_recvs.at[1], group)
    lax.fori_loop(2, 4, slope_block, 0)
    rest.append(local.fetch(slope, slope_out))
    share_end(st4, slots4, group_sends.at[1], group_recvs.at[1], group)
    totals4 = add_slots(slots4, views)
    count4 = float(views * views_own)
    mean4 = totals4[0:2] / count4
    rstd4 = lax.rsqrt(totals4[2:4] / count4 - mean4 * mean4 + EPS)
    head_last_here.wait()

    def level4(half):
        cols = slice(half * wide, (half + 1) * wide)
        normed = (part_in[4 + half] - mean4[half : half + 1]) * rstd4[half : half + 1]
        return normed, normed * gain_head[:, cols] + shift_head[:, cols]

    embed = None
    for half in range(2):
        normed, level = level4(half)
        value = level * gate(level)
        act4[half] = value
        term = join_rows(dot(split_rows(value), head_last[half * wide : (half + 1) * wide]))
        embed = term if embed is None else embed + term
    embed_own[...] = embed
    share_start(embed_own, embed_all, group_sends.at[2], group_recvs.at[2], group)
    share_end(embed_own, embed_all, group_sends.at[2], group_recvs.at[2], group)
    pooled_mean = jnp.sum(pooled_own[...], axis=0, keepdims=True) / views_own
    bk3[2:3] = pooled_mean
    pooled_low[...] = (pooled_own[...] - pooled_mean).astype(BF16)
    gather_start(pooled_low, pooled_all, group_sends.at[5], group_recvs.at[5], group)
    rest.append(local.fetch(pooled_low, pooled_all.at[view_at]))
    own_rows = pl.ds(pl.multiple_of(view_at * views_own, views_own), views_own)
    every = embed_all.reshape(views * views_own, embed.shape[1])
    loss, grad_embed = whiten(
        every, sub_col, image_col, image_row, partner_col, partner_row,
        (work, inverse, white, unit, unit_parts, back), own_rows,
    )
    loss_out[...] = loss
    grad_embed_out[...] = grad_embed
    stacked = split_rows(grad_embed)
    for half in range(2):
        normed, level = level4(half)
        grad = join_rows(dot_nt(stacked, head_last[half * wide : (half + 1) * wide]))
        grad = grad * silu_slope(level)
        part[half] = grad
        bk4[half : half + 1] = jnp.sum(grad, axis=0, keepdims=True)
        bk4[2 + half : 3 + half] = jnp.sum(grad * normed, axis=0, keepdims=True)
    tot4 = share(bk4, bslots4, group_sends.at[3], group_recvs.at[3], group)
    grad_pooled = None
    for half in range(2):
        cols = slice(half * wide, (half + 1) * wide)
        normed, level = level4(half)
        shift_sum, gain_sum = tot4[half : half + 1], tot4[2 + half : 3 + half]
        grad_shift_head[:, cols] = shift_sum
        grad_gain_head[:, cols] = gain_sum
        grad = (
            gain_head[:, cols]
            * rstd4[half : half + 1]
            * (part[half] - shift_sum / count4 - normed * (gain_sum / count4))
        )
        grad_p1[half] = grad
        term = join_rows(dot_nt(split_rows(grad), head_first[:, cols]))
        grad_pooled = term if grad_pooled is None else grad_pooled + term
    grad_pooled = grad_pooled * (1.0 / PIX)
    grad_pooled_out[...] = grad_pooled
    bk3[0:1] = jnp.sum(grad_pooled * slope_sums[0], axis=0, keepdims=True)
    bk3[1:2] = jnp.sum(grad_pooled * slope_sums[1], axis=0, keepdims=True)
    share_start(bk3, bslots3, group_sends.at[4], group_recvs.at[4], group)
    w2_over.wait_recv()
    w2_last = mail.send(w2_far.at[c, late_rows], w2_far.at[c, late_rows], mate)
    share_end(bk3, bslots3, group_sends.at[4], group_recvs.at[4], group)
    tot3 = add_slots(bslots3, views)
    grad_shift_last[...] = tot3[0:1]
    grad_gain_last[...] = tot3[1:2]
    own_count = float(4 * quarter)
    normed_sum = (st3[0:1] - own_count * mean) * rstd
    rows_sum[...] = scale * (
        bk3[0:1] - tot3[0:1] * (own_count / count) - normed_sum * (tot3[1:2] / count)
    )
    pooled_means[...] = bslots3[:, 2]
    h2_far.wait_recv()
    stat2_far.wait_recv()
    w2_last.wait_recv()
    share_end(pooled_low, pooled_all, group_sends.at[5], group_recvs.at[5], group)
    for copy in [*rest[1:], w3_kept, act_kept]:
        copy.wait()
    for copy in mail.copies:
        if copy is not swap:
            copy.wait_send()


def front_stage(views, x, weights, vectors, tables, perm, unperm):
    conv_first, conv_mid, conv_last, head_first, head_last = weights
    quarter, depth = x.shape[0] // 4, x.shape[1]
    width = depth
    mid = conv_mid.shape[1] * 4
    half = mid // 2
    block = quarter // PIX
    own = 4 * block
    total = views * own
    hid, emb = head_last.shape
    wide = hid // 2
    subs = total // SUB
    peers = 2 * views
    vm = pltpu.VMEM
    wide_rows = (4, quarter, width)
    return call(
        functools.partial(front_body, views),
        "front",
        (
            shape(2, PAD, PAD, block, mid, kind=BF16),
            shape(2, quarter, half),
            shape(2, *conv_mid.shape, kind=BF16),
            shape(2, *conv_mid.shape, kind=BF16),
            shape(4, 2 * depth, mid // 4, kind=BF16),
            shape(2, 4, quarter, half, kind=BF16),
            shape(*wide_rows, kind=BF16),
            shape(*wide_rows, kind=BF16),
            shape(views, own, width, kind=BF16),
            shape(2, quarter, half, kind=BF16),
            shape(2, 2, half),
            shape(depth, mid, kind=BF16),
            shape(4, 8, mid // 4),
            shape(2, width),
            shape(1, width),
            shape(1, width),
            shape(1, hid),
            shape(1, hid),
            shape(own, width),
            shape(2, own, wide),
            shape(own, emb),
            shape(2, own, wide),
            shape(1, 1),
            shape(2, 2, half),
            shape(views, width),
            shape(1, width),
        ),
        19,
        [
            vm(wide_rows, BF16),
            vm((4, 2 * depth, mid // 4), BF16),
            vm((2, 4, quarter, half), BF16),
            vm(wide_rows, BF16),
            vm((2, 2, quarter, half), F32),
            vm((2, 2, half), F32),
            vm((peers, 2, 2, half), F32),
            vm((2, half), F32),
            vm((peers, 2, half), F32),
            vm((quarter, quarter), BF16),
            vm((quarter, quarter), BF16),
            vm((2, PAD, PAD, block, mid), BF16),
            vm((2, *conv_mid.shape), BF16),
            vm((4, 2 * depth, mid // 4), BF16),
            vm((2, quarter, half), F32),
            vm((2, quarter, half), BF16),
            vm((8, mid // 4), F32),
            vm(head_first.shape, BF16),
            vm(head_last.shape, BF16),
            vm(wide_rows, BF16),
            vm((own, width), F32),
            vm((own, width), BF16),
            vm((total, 128), F32),
            vm((total, 128), F32),
            vm((total, 128), F32),
            vm((views, own, emb), F32),
            vm((2, own, wide), F32),
            vm((6, own, wide), F32),
            vm((2, own, wide), F32),
            vm((2, own, width), F32),
            vm((2, width), F32),
            vm((views, 2, width), F32),
            vm((4, wide), F32),
            vm((views, 4, wide), F32),
            vm((4, wide), F32),
            vm((views, 4, wide), F32),
            vm((3, width), F32),
            vm((views, 3, width), F32),
            vm((own, emb), F32),
            vm((subs, emb, 2 * emb), F32),
            vm((subs, emb, emb), F32),
            vm((total, emb), F32),
            vm((total, emb), F32),
            vm((total, 3 * emb), BF16),
            vm((total, emb), F32),
            dma(40),
            dma(40),
            dma(2, 2),
            dma(2, 2),
            dma(2, peers),
            dma(2, peers),
            dma(6, views),
            dma(6, views),
            dma(32),
        ],
        collective=1,
        any_ins=range(11, 19),
        any_outs=range(10),
    )(
        *vectors, *tables, x.reshape(wide_rows), conv_first, conv_mid, conv_last, perm, unperm,
        head_first, head_last,
    )


def link_kind(rows):
    return BF16 if rows % 16 == 0 else F32


def back_body(
    views, stat3, grad_shift_last, grad_gain_last, grad_pooled, gain_last, expand,
    stats2, smalls, stat1, act4, grad_embed, grad_p1, pooled_means, rows_sum,
    h3_any, slope_any, w3_any, h2q_any, perm_any, unperm_any, pad_any, h1q_any, w2_any,
    w2_far_any, act_any, x_any, pooled_any,
    gh1_out, mid_slots, pair_out, head_last_out, head_first_out,
    grad_shift_mid, grad_gain_mid, grad_shift_first, grad_gain_first,
    h3, slope, w3, h2q, gh1, gh3, gh3_mate, out_part, in_part, ga2, gh2, gh2_far, gpad, ga1, st, chan_slots, view_slots,
    order, pad, h1q, w2, w2_far, act, pooled,
    wsum, wsend, mid_parts, mid_in, last_parts, last_in, last_slots, first_parts, first_in, first_slots, means, mean_slots, pair_parts,
    hl_parts, hl_slots, p1_parts, p1_slots,
    sends, recvs, chan_sends, chan_recvs, group_sends, group_recvs, pair_sends, pair_recvs,
    pair1_sends, pair1_recvs, pair2_sends, pair2_recvs, local_sems,
):
    view_at, chan_at, y, c = place()
    mate, opposite = (view_at, 2 * y + 1 - c), (view_at, 2 * (1 - y) + c)
    group, chans, everyone = view_group(views), chan_group(), all_group(views)
    quarter, width = h3.shape[1], h3.shape[2]
    block = quarter // PIX
    half_width = h2q.shape[2]
    met = greet([], [everyone])
    local = Local(local_sems)
    near_half, own_half = [2 * i + 1 - c for i in (1 - y, y)], [2 * i + c for i in (1 - y, y)]
    rows_here = []

    def fetch_rows(q):
        rows_here.append((local.fetch(h3_any.at[q], h3.at[q]), local.fetch(slope_any.at[q], slope.at[q])))

    for q in near_half:
        fetch_rows(q)
    count = float(views * 4 * quarter)
    mean, rstd = stat3[0:1], stat3[1:2]
    scale = rstd * gain_last[...]
    shift_part, gain_part = grad_shift_last[...] / count, grad_gain_last[...] / count

    def grad_rows(q):
        rows = pl.ds(pl.multiple_of(q * block, block), block)
        high, low = split_pair(grad_pooled[rows])
        spread = dot(expand[...], jnp.concatenate([high, low], axis=0))
        grad = spread * slope[q].astype(F32)
        normed = (h3[q].astype(F32) - mean) * rstd
        gh3[q] = (scale * (grad - shift_part - normed * gain_part)).astype(BF16)

    mate_out = pl.ds(pl.multiple_of(width * (1 - c), width), width)
    own_out = pl.ds(pl.multiple_of(width * c, width), width)

    def part_of(i):
        def weight(rows):
            return jnp.concatenate([w3[k, rows] for k in range(4)], axis=1)

        value = dot(gh3[2 * i + c], weight(own_out)) + dot(gh3_mate[i], weight(mate_out))
        return dot(order[...], value.astype(BF16))

    mail = Mail(sends, recvs)
    beside = []
    for at, i in enumerate((1 - y, y)):
        for copy in rows_here[at]:
            copy.wait()
        grad_rows(2 * i + 1 - c)
        if at == 0:
            met()
        beside.append(mail.send(gh3.at[2 * i + 1 - c], gh3_mate.at[i], mate))
        if at == 0:
            for q in own_half:
                fetch_rows(q)
            w3_here = local.fetch(w3_any, w3)
            perm_here = local.fetch(perm_any, order)
    for at, i in enumerate((1 - y, y)):
        for copy in rows_here[2 + at]:
            copy.wait()
        grad_rows(2 * i + c)
        if at == 0:
            w3_here.wait()
            perm_here.wait()
            beside[0].wait_recv()
            value = part_of(1 - y).astype(BF16)
            for half in range(2):
                out_part[half] = value[:, half * half_width : (half + 1) * half_width]
            across = [mail.send(out_part.at[half], in_part.at[half], opposite) for half in range(2)]
            act_here = local.fetch(act_any, act)
            h2q_here = local.fetch(h2q_any, h2q)
            w2_here = local.fetch(w2_any, w2)
            w2_far_here = local.fetch(w2_far_any, w2_far)
            h1q_here = local.fetch(h1q_any, h1q)
            pad_here = local.fetch(pad_any, pad)
    beside[1].wait_recv()
    ga2[...] = part_of(y)
    unperm_here = local.fetch(unperm_any, order)

    def fold_sems(at):
        return [sems.at[at] for sems in (pair1_sends, pair1_recvs, pair2_sends, pair2_recvs)]

    hid_block, hid_split = hl_parts.shape[1], head_last_out.shape[0]
    for half in range(2):
        product = exact(act4[half], grad_embed[...], 0, 0)
        ga1[: product.shape[0], : product.shape[1]] = product
        per_half = views // 2

        def spread_hidden(to, carry, half=half, per_half=per_half):
            spot = (4 * to + chan_at) * hid_block if hid_split == 4 else to * hid_block
            rows = pl.ds(pl.multiple_of(spot, hid_block), hid_block)
            hl_parts[half * per_half + to] = ga1[rows, : hl_parts.shape[2]]
            return carry

        lax.fori_loop(0, per_half, spread_hidden, 0)
        wide = grad_p1.shape[2] // per_half
        for to in range(per_half):
            p1_parts[half * per_half + to] = grad_p1[half, :, to * wide : (to + 1) * wide]
    scatter_start(hl_parts, hl_slots, group_sends.at[0], group_recvs.at[0], group)
    scatter_start(p1_parts, p1_slots, group_sends.at[1], group_recvs.at[1], group)
    act_here.wait()
    share_rows = last_parts.shape[1]
    means[0:1] = rows_sum[...]
    few_rows = quarter // SIDE
    for half in range(2):
        cols = slice(half * half_width, (half + 1) * half_width)
        sampled = [jnp.sum(act[half, q, :few_rows].astype(F32), axis=0, keepdims=True) for q in range(4)]
        means[1:2, cols] = sum(sampled) / (4 * few_rows)
    share_start(means, mean_slots, group_sends.at[2], group_recvs.at[2], group)
    for half in range(2):
        cols = slice(half * half_width, (half + 1) * half_width)
        total = None
        for q in range(4):
            term = dot_tn(gh3[q], act[half, q])
            total = term if total is None else total + term
        ga1[:width, :half_width] = total
        low = (
            ga1[:width, :half_width] - outer_product(means[0:1], means[1:2, cols])
        ).astype(last_parts.dtype)
        for to in range(views):
            last_parts[to, :, half * half_width : (half + 1) * half_width] = low[
                to * share_rows : (to + 1) * share_rows
            ]
    fold_last = Fold(last_parts, last_in, last_slots, fold_sems(0), views)
    fold_last.start()
    for copy in beside:
        copy.wait_send()
    x = gh3
    x_here = local.fetch(x_any, x)
    h2q_here.wait()

    def sums_everywhere(at):
        return share(
            share_value(st, chan_slots.at[at], chan_sends.at[at], chan_recvs.at[at], chans),
            view_slots.at[at], group_sends.at[3 + at], group_recvs.at[3 + at], group,
        )

    def share_value(source, slots, send, recv, who):
        source[...] = share(source, slots, send, recv, who)
        return source

    gpad[...] = jnp.zeros(gpad.shape, gpad.dtype)
    for half in range(2):
        across[half].wait()
        cols = slice(half * half_width, (half + 1) * half_width)
        ga2[:, cols] += in_part[half].astype(F32)
    halves = (y, 1 - y)

    def mid_norm(near):
        half = halves[near]
        gains = jnp.concatenate([smalls[2 * half], smalls[2 * half + 1]], axis=1)
        mean2, rstd2 = stats2[half, 0:1], stats2[half, 1:2]
        return mean2, rstd2, gains[2:3], gains[3:4]

    def half_cols(ref, near):
        low, high = ref[:, :half_width], ref[:, half_width:]
        return jnp.where(halves[near] == 0, low, high)

    for near in range(2):
        mean2, rstd2, gain2, shift2 = mid_norm(near)
        normed = (h2q[halves[near]].astype(F32) - mean2) * rstd2
        grad = half_cols(ga2, near) * silu_slope(normed * gain2 + shift2)
        ga1[:, near * half_width : (near + 1) * half_width] = grad
        st[halves[near], 0:1] = jnp.sum(grad, axis=0, keepdims=True)
        st[halves[near], 1:2] = jnp.sum(grad * normed, axis=0, keepdims=True)
    totals2 = sums_everywhere(0)
    view_slots[0, 0] = totals2
    for near in range(2):
        mean2, rstd2, gain2, shift2 = mid_norm(near)
        tot = view_slots[0, 0, halves[near]]
        normed = (h2q[halves[near]].astype(F32) - mean2) * rstd2
        grad = ga1[:, near * half_width : (near + 1) * half_width]
        low = (gain2 * rstd2 * (grad - tot[0:1] / count - normed * (tot[1:2] / count))).astype(BF16)
        gh2[near] = low
        gpad[near, 1 : SIDE + 1, 1 : SIDE + 1] = low.reshape(SIDE, SIDE, block, half_width)
    tot = view_slots[0, 0, y]
    own_cols = jnp.where(c == 0, tot[:, : half_width // 2], tot[:, half_width // 2 :])
    grad_shift_mid[...] = own_cols[0:1]
    grad_gain_mid[...] = own_cols[1:2]
    cut = quarter // 32 * 16
    far_pieces = [pl.ds(0, cut), pl.ds(cut, quarter - cut)]
    far_copies = [mail.send(gh2.at[1, far_pieces[0]], gh2_far.at[far_pieces[0]], opposite)]
    fold_last.pass_on(1, fold_last.size + 1)
    w2_here.wait()
    w2_far_here.wait()
    channels = w2.shape[1] // 9
    for tap in range(9):
        a, b = 2 - tap // 3, 2 - tap % 3
        taps = slice(tap * channels, (tap + 1) * channels)
        term = None
        for near, weight in enumerate((w2, w2_far)):
            window = gpad[near, a : a + SIDE, b : b + SIDE].reshape(quarter, half_width)
            both = jnp.concatenate([weight[0, taps], weight[1, taps]], axis=1)
            piece = dot_nt(window, both)
            term = piece if term is None else term + piece
        if tap == 0:
            ga1[...] = term
        else:
            ga1[...] += term
    h1q_here.wait()
    for half in range(2):
        gains = jnp.concatenate([smalls[2 * half], smalls[2 * half + 1]], axis=1)
        normed = (h1q[half] - stat1[half, 0:1]) * stat1[half, 1:2]
        cols = slice(half * half_width, (half + 1) * half_width)
        grad = ga1[:, cols] * silu_slope(normed * gains[0:1] + gains[1:2])
        ga2[:, cols] = grad
        st[half, 0:1] = jnp.sum(grad, axis=0, keepdims=True)
        st[half, 1:2] = jnp.sum(grad * normed, axis=0, keepdims=True)
    share_value(st, chan_slots.at[1], chan_sends.at[1], chan_recvs.at[1], chans)
    far_copies.append(mail.send(gh2.at[1, far_pieces[1]], gh2_far.at[far_pieces[1]], opposite))
    share_start(st, view_slots.at[1], group_sends.at[4], group_recvs.at[4], group)

    pad_here.wait()

    def tap_term(at, tap, grads):
        a, b = tap // 3, tap % 3
        window = pad[at, a : a + SIDE, b : b + SIDE].reshape(quarter, channels)
        return dot_tn(window, grads)

    for tap in range(9):
        total = tap_term(y, tap, gh2[0])
        taps = slice(tap * channels, (tap + 1) * channels)
        wsum[0, taps] = total[:, : half_width // 2]
        wsum[1, taps] = total[:, half_width // 2 :]
    share_end(st, view_slots.at[1], group_sends.at[4], group_recvs.at[4], group)
    totals1 = add_slots(view_slots.at[1], views)
    view_slots[1, 0] = totals1
    tot = view_slots[1, 0, y]
    own_cols = jnp.where(c == 0, tot[:, : half_width // 2], tot[:, half_width // 2 :])
    grad_shift_first[...] = own_cols[0:1]
    grad_gain_first[...] = own_cols[1:2]
    unperm_here.wait()
    gh1_across, gh1_beside = [], []
    for half in range(2):
        gains = jnp.concatenate([smalls[2 * half], smalls[2 * half + 1]], axis=1)
        normed = (h1q[half] - stat1[half, 0:1]) * stat1[half, 1:2]
        cols = slice(half * half_width, (half + 1) * half_width)
        tot = totals1[half]
        low = (
            gains[0:1]
            * stat1[half, 1:2]
            * (ga2[:, cols] - tot[0:1] / count - normed * (tot[1:2] / count))
        ).astype(BF16)
        gh1[half, chan_at] = dot(order[...], low).astype(BF16)
        spot = gh1.at[half, chan_at]
        gh1_across.append(mail.send(spot, spot, opposite))
        gh1_beside.append(mail.send(spot, spot, mate))

    for copy in far_copies:
        copy.wait_recv()
    for tap in range(9):
        total = tap_term(1 - y, tap, gh2_far[...])
        taps = slice(tap * channels, (tap + 1) * channels)
        wsum[0, taps] += total[:, : half_width // 2]
        wsum[1, taps] += total[:, half_width // 2 :]
    mid_rows = mid_parts.shape[1]
    mid_flat = mid_parts.reshape(views * mid_rows, mid_parts.shape[2])
    if mid_parts.dtype == F32:
        mid_mate = mail.send(wsum.at[1 - c], mid_flat, mate)
    else:
        wsend[...] = wsum[1 - c].astype(wsend.dtype)
        mid_mate = mail.send(wsend, mid_flat, mate)
    mid_mate.wait_recv()

    def mid_block(to, carry):
        rows = pl.ds(pl.multiple_of(to * mid_rows, mid_rows), mid_rows)
        mid_parts[to] = (wsum[c, rows] + mid_parts[to].astype(F32)).astype(mid_parts.dtype)
        return carry

    lax.fori_loop(0, views, mid_block, 0)
    fold_mid = Fold(mid_parts, mid_in, mid_slots, fold_sems(1), views, False)
    fold_mid.start()
    scatter_end(p1_parts, p1_slots, group_sends.at[1], group_recvs.at[1], group)
    few = pooled.shape[0]

    def head_first_term(at, total):
        views_at = pl.ds(at * few, few)
        copy = pltpu.make_async_copy(pooled_any.at[views_at], pooled, local_sems.at[29])
        copy.start()
        copy.wait()
        rows = pooled[...].astype(F32).reshape(-1, width)
        return total + exact(rows, p1_slots[views_at].reshape(rows.shape[0], -1), 0, 0)

    head_first_out[...] = over(
        views // few, head_first_term, exact(pooled_means[...], jnp.sum(p1_slots[...], axis=1), 0, 0)
    )
    share_end(means, mean_slots, group_sends.at[2], group_recvs.at[2], group)
    fold_last.end()
    rest, folds = [], []
    cuts = [1 + fold_mid.size * k // 4 for k in range(4)] + [fold_mid.size + 1]
    x_here.wait()
    for half in range(2):
        gh1_across[half].wait_recv()
        far_spot = gh1.at[half, 2 * (1 - y) + c]
        gh1_on = mail.send(far_spot, far_spot, mate)
        fold_mid.pass_on(cuts[2 * half], cuts[2 * half + 1])
        gh1_beside[half].wait_recv()
        gh1_on.wait_recv()
        rest.append(local.fetch(gh1.at[half], gh1_out.at[half]))
        total = None
        for q in range(4):
            term = dot_tn(x[q], gh1[half, q])
            total = term if total is None else total + term
        low = total.astype(first_parts.dtype)
        for to in range(views):
            first_parts[half, to] = low[to * share_rows : (to + 1) * share_rows]
        folds.append(Fold(first_parts.at[half], first_in.at[half], first_slots.at[half], fold_sems(2 + half), views))
        folds[half].start()
        fold_mid.pass_on(cuts[2 * half + 1], cuts[2 * half + 2])
    rest.append(local.fetch(mid_parts.at[view_at], mid_slots.at[fold_mid.outer]))

    scatter_end(hl_parts, hl_slots, group_sends.at[0], group_recvs.at[0], group)
    if hid_split == 4:
        head_last_out[chan_at] = add_slots(hl_slots, views)
        gather_start(head_last_out.at[chan_at], head_last_out, chan_sends.at[2], chan_recvs.at[2], chans)
    else:
        head_last_out[0] = add_slots(hl_slots, views)

    def blocks(kind, summed):
        wide = summed.shape[1] // 4
        for to in range(4):
            pair_parts[to, kind] = summed[:, to * wide : (to + 1) * wide]

    def summed_slots(slots):
        def add(at, total):
            return total + slots[at].astype(F32)

        return lax.fori_loop(1, slots.shape[0], add, slots[0].astype(F32))

    everywhere = short_product(mean_slots[:, 0], mean_slots[:, 1])
    ga1[: everywhere.shape[0]] = everywhere
    own_block = pl.ds(pl.multiple_of(view_at * share_rows, share_rows), share_rows)
    blocks(1, summed_slots(last_slots) + ga1[own_block])
    for fold in folds:
        fold.pass_on(1, fold.size + 1)
    for fold in folds:
        fold.end()
    blocks(0, jnp.concatenate([summed_slots(first_slots.at[half]) for half in range(2)], axis=1))
    row_views = views // 4
    to_view = chan_at * row_views + lax.div(view_at, 4)
    slot = lax.rem(view_at, 4)

    def pair_copy(to):
        return pltpu.make_async_remote_copy(
            src_ref=pair_parts.at[to],
            dst_ref=pair_out.at[slot],
            send_sem=pair_sends.at[to],
            recv_sem=pair_recvs.at[slot],
            device_id=(to_view, to),
            device_id_type=MESH,
        )

    def pair_arrival(origin):
        return pltpu.make_async_remote_copy(
            src_ref=pair_parts.at[0],
            dst_ref=pair_out.at[origin],
            send_sem=pair_sends.at[0],
            recv_sem=pair_recvs.at[origin],
            device_id=(from_view + origin, from_chan),
            device_id_type=MESH,
        )

    from_view, from_chan = 4 * lax.rem(view_at, row_views), lax.div(view_at, row_views)
    for to in range(4):
        own = jnp.logical_and(to_view == view_at, chan_at == to)

        @pl.when(own)
        def _():
            pair_out[slot] = pair_parts[to]

        @pl.when(jnp.logical_not(own))
        def _():
            pair_copy(to).start()

    for origin in range(4):
        own = jnp.logical_and(from_view + origin == view_at, chan_at == from_chan)

        @pl.when(jnp.logical_not(own))
        def _():
            pair_arrival(origin).wait_recv()

    for to in range(4):
        own = jnp.logical_and(to_view == view_at, chan_at == to)

        @pl.when(jnp.logical_not(own))
        def _():
            pair_copy(to).wait_send()

    if hid_split == 4:
        share_end(head_last_out.at[chan_at], head_last_out, chan_sends.at[2], chan_recvs.at[2], chans)
    fold_mid.end()
    for copy in rest:
        copy.wait()
    for copy in mail.copies[4:]:
        copy.wait_send()


def back_stage(views, front_outs, x, gain_last, perm, unperm, expand):
    (pad, h1q, w2, w2_far, w3, act, h3, slope, pooled_all, h2q, stat1, _, smalls, stat3,
     grad_shift_last, grad_gain_last, _, _, grad_pooled, act4, grad_embed, grad_p1, _,
     stats2, pooled_means, rows_sum) = front_outs
    quarter, width = h3.shape[1], h3.shape[2]
    block = quarter // PIX
    own = 4 * block
    mid = pad.shape[4]
    half = mid // 2
    hid, emb = 2 * act4.shape[2], grad_embed.shape[1]
    taps = w2.shape[1]
    hid_split = 4 if hid // views % 32 == 0 else 1
    hid_block = hid // views // hid_split
    mid_kind, row_kind = link_kind(taps // views), link_kind(width // views)
    vm = pltpu.VMEM
    return call(
        functools.partial(back_body, views),
        "back",
        (
            shape(2, 4, quarter, half, kind=BF16),
            shape(views // 2, taps // views, half // 2, kind=mid_kind),
            shape(4, 2, width // views, mid // 4),
            shape(hid_split, hid_block, emb),
            shape(width, hid // views),
            *[shape(1, half // 2)] * 4,
        ),
        27,
        [
            vm((4, quarter, width), BF16),
            vm((4, quarter, width), BF16),
            vm(w3.shape, BF16),
            vm(h2q.shape, BF16),
            vm((2, 4, quarter, half), BF16),
            vm((4, quarter, width), BF16),
            vm((2, quarter, width), BF16),
            vm((2, quarter, half), BF16),
            vm((2, quarter, half), BF16),
            vm((quarter, mid), F32),
            vm((2, quarter, half), BF16),
            vm((quarter, half), BF16),
            vm((2, PAD, PAD, block, half), BF16),
            vm((quarter, mid), F32),
            vm((2, 2, half), F32),
            vm((2, 4, 2, 2, half), F32),
            vm((2, views, 2, 2, half), F32),
            vm(unperm.shape, BF16),
            vm(pad.shape, BF16),
            vm(h1q.shape, F32),
            vm(w2.shape, BF16),
            vm(w2.shape, BF16),
            vm(act.shape, BF16),
            vm((min(views, 8), own, width), BF16),
            vm((2, taps, half // 2), F32),
            vm((taps if mid_kind == BF16 else 16, half // 2), BF16),
            vm((views, taps // views, half // 2), mid_kind),
            vm((views // 2, taps // views, half // 2), mid_kind),
            vm((views, width // views, mid), row_kind),
            vm((views // 2, width // views, mid), row_kind),
            vm((views // 2, width // views, mid), row_kind),
            vm((2, views, width // views, half), row_kind),
            vm((2, views // 2, width // views, half), row_kind),
            vm((2, views // 2, width // views, half), row_kind),
            vm((2, width), F32),
            vm((views, 2, width), F32),
            vm((4, 2, width // views, mid // 4), F32),
            vm((views, hid_block, emb), F32),
            vm((views, hid_block, emb), F32),
            vm((views, own, hid // views), F32),
            vm((views, own, hid // views), F32),
            dma(20),
            dma(20),
            dma(3, 4),
            dma(3, 4),
            dma(7, views),
            dma(7, views),
            dma(4),
            dma(4),
            *[dma(4, views // 2)] * 4,
            dma(30),
        ],
        collective=4,
        any_ins=range(14, 27),
        any_outs=range(2),
    )(
        stat3, grad_shift_last, grad_gain_last, grad_pooled, gain_last, expand,
        stats2, smalls, stat1, act4, grad_embed, grad_p1, pooled_means, rows_sum,
        h3, slope, w3, h2q, perm, unperm, pad, h1q, w2, w2_far, act,
        x.reshape(4, quarter, width), pooled_all,
    )


def last_body(
    small_count, w1_any, grad_pooled, expand, gh1_any, slope_any, mid_any, pair_out, head_last_in, head_first_in, *more
):
    small_ins, outs = more[:small_count], more[small_count : 2 * small_count + 6]
    gh1, w1_own, slope, term, mid_slots, sems = more[2 * small_count + 6 :]
    grad_input, grad_mid, grad_first, grad_last, grad_head_last, grad_head_first, *small_outs = outs
    local = Local(sems)
    quarters, quarter, half = gh1.shape[1], gh1.shape[2], gh1.shape[3]
    w1_here = local.fetch(w1_any, w1_own)
    rows_here = [
        (local.fetch(gh1_any.at[:, q], gh1.at[:, q]), local.fetch(slope_any.at[q], slope.at[q]))
        for q in range(quarters)
    ]
    mid_here = local.fetch(mid_any, mid_slots)
    rest = []
    w1_here.wait()
    block = quarter // PIX
    for q in range(quarters):
        for copy in rows_here[q]:
            copy.wait()
        high, low = split_pair(grad_pooled[q * block : (q + 1) * block])
        spread = dot(expand[...], jnp.concatenate([high, low], axis=0))
        value = dot_nt(gh1[0, q], w1_own[:, :half]) + dot_nt(gh1[1, q], w1_own[:, half:])
        term[q] = value + spread * slope[q].astype(F32)
        rest.append(local.fetch(term.at[q], grad_input.at[q]))
    mid_here.wait()

    def add(slot, total):
        return total + mid_slots[slot].astype(F32)

    grad_mid[...] = lax.fori_loop(1, mid_slots.shape[0], add, mid_slots[0].astype(F32))
    grad_head_first[...] = head_first_in[...]
    for source, target in zip(small_ins, small_outs):
        target[...] = source[...]
    rows = pair_out.shape[2]
    for origin in range(4):
        grad_first[origin * rows : (origin + 1) * rows] = pair_out[origin, 0]
        grad_last[origin * rows : (origin + 1) * rows] = pair_out[origin, 1]
    rows = head_last_in.shape[1]
    for origin in range(head_last_in.shape[0]):
        grad_head_last[origin * rows : (origin + 1) * rows] = head_last_in[origin]
    for copy in rest:
        copy.wait()


def last_stage(
    gh1, w1_own, slope, grad_pooled, expand, mid_slots, pair_out, head_last_in, head_first_in, small
):
    quarter, half, width = gh1.shape[2], gh1.shape[3], slope.shape[2]
    outs = (
        shape(4, quarter, width),
        shape(*mid_slots.shape[1:]),
        shape(4 * pair_out.shape[2], pair_out.shape[3]),
        shape(4 * pair_out.shape[2], pair_out.shape[3]),
        shape(head_last_in.shape[0] * head_last_in.shape[1], head_last_in.shape[2]),
        shape(*head_first_in.shape),
        *[shape(*array.shape) for array in small],
    )
    ins = 9 + len(small)
    return call(
        functools.partial(last_body, len(small)),
        "results",
        outs,
        ins,
        [
            pltpu.VMEM(gh1.shape, BF16),
            pltpu.VMEM(w1_own.shape, BF16),
            pltpu.VMEM(slope.shape, BF16),
            pltpu.VMEM(slope.shape, F32),
            pltpu.VMEM(mid_slots.shape, mid_slots.dtype),
            dma(20),
        ],
        collective=None,
        any_ins=(0, 3, 4, 5),
        any_outs=(0,),
    )(w1_own, grad_pooled, expand, gh1, slope, mid_slots, pair_out, head_last_in, head_first_in, *small)


def per_device(
    views,
    block_input,
    conv_first,
    conv_mid,
    conv_last,
    gain_first,
    shift_first,
    gain_mid,
    shift_mid,
    gain_last,
    shift_last,
    head_first,
    gain_head,
    shift_head,
    head_last,
    image_of,
    partner,
    sub_of,
):
    rows, width = block_input.shape
    quarter = rows // 4
    block = quarter // PIX
    perm, unperm = orders(quarter)
    at_row = np.arange(quarter)
    twice = np.arange(2 * block) % block
    expand = jnp.asarray((at_row[:, None] // PIX == twice[None, :]).astype(BF16))

    def line(vector):
        return vector.reshape(1, -1)

    front_outs = front_stage(
        views, block_input, (conv_first, conv_mid, conv_last, head_first, head_last),
        [line(v) for v in (gain_first, shift_first, gain_mid, shift_mid, gain_last, shift_last, gain_head, shift_head)],
        [line(v) for v in (sub_of, image_of, partner)], perm, unperm,
    )
    slope, w1_own, grad_pooled, loss = (front_outs[at] for at in (7, 11, 18, 22))
    (gh1, mid_slots, pair_out, head_last_in, head_first_in,
     grad_shift_mid, grad_gain_mid, grad_shift_first, grad_gain_first) = back_stage(
        views, front_outs, block_input, line(gain_last), perm, unperm, expand
    )
    small = [
        grad_gain_first, grad_shift_first, grad_gain_mid, grad_shift_mid,
        front_outs[15], front_outs[14], front_outs[17], front_outs[16], loss,
    ]
    grad_input, grad_mid, grad_first, grad_last, grad_head_last, grad_head_first, *small = last_stage(
        gh1, w1_own, slope, grad_pooled, expand, mid_slots, pair_out, head_last_in, head_first_in, small
    )
    return (
        small[8].reshape(()),
        grad_input.reshape(rows, width),
        grad_first,
        grad_mid,
        grad_last,
        grad_head_first,
        grad_head_last,
        *[vector.reshape(-1) for vector in small[:8]],
    )


def solution(mesh):
    views = mesh.shape["views"]
    return jax.shard_map(
        functools.partial(per_device, views),
        mesh=mesh,
        in_specs=(
            P("views", "chan"),
            P(None, "chan"),
            P(None, "chan"),
            P(None, "chan"),
            P("chan"),
            P("chan"),
            P("chan"),
            P("chan"),
            P("chan"),
            P("chan"),
            P("chan", None),
            P(),
            P(),
            P(),
            P(),
            P(),
            P(),
        ),
        out_specs=(
            P(),
            P("views", "chan"),
            P("views", "chan"),
            P("views", "chan"),
            P("views", "chan"),
            P("chan", "views"),
            P("views", None),
            P("chan"),
            P("chan"),
            P("chan"),
            P("chan"),
            P("chan"),
            P("chan"),
            P(),
            P(),
        ),
        check_vma=False,
    )
```

```python
import functools

import jax
import jax.numpy as jnp
import numpy as np
from jax import lax
from jax.experimental import pallas as pl
from jax.experimental.pallas import tpu as pltpu
from jax.sharding import PartitionSpec as P

SIDE = 7
PIX = SIDE * SIDE
PAD = SIDE + 2
SUB = 256
EPS = 1e-05
RIDGE = 0.5
MESH = pl.DeviceIdType.MESH
BF16 = jnp.bfloat16
F32 = jnp.float32
VMEM_BYTES = 60 << 20


def place():
    view_at, chan_at = lax.axis_index("views"), lax.axis_index("chan")
    return view_at, chan_at, lax.div(chan_at, 2), lax.rem(chan_at, 2)


def greet(peers, groups=()):
    barrier = pltpu.get_barrier_semaphore()
    total = len(peers)
    for peer in peers:
        pl.semaphore_signal(barrier, inc=1, device_id=peer, device_id_type=MESH)
    for size, own, device in groups:

        def tell(step, carry, size=size, own=own, device=device):
            pl.semaphore_signal(
                barrier, inc=1, device_id=device(lax.rem(own + step, size)), device_id_type=MESH
            )
            return carry

        lax.fori_loop(1, size, tell, 0)
        total += size - 1
    return lambda: pl.semaphore_wait(barrier, total)


class Mail:
    def __init__(self, send_sems, recv_sems):
        self.send_sems, self.recv_sems, self.copies = send_sems, recv_sems, []

    def send(self, source, target, peer):
        spot = len(self.copies)
        copy = pltpu.make_async_remote_copy(
            src_ref=source,
            dst_ref=target,
            send_sem=self.send_sems.at[spot],
            recv_sem=self.recv_sems.at[spot],
            device_id=peer,
            device_id_type=MESH,
        )
        copy.start()
        self.copies.append(copy)
        return copy

    def finish(self):
        for copy in self.copies:
            copy.wait_send()


class Local:
    def __init__(self, sems):
        self.sems, self.used = sems, 0

    def fetch(self, source, target):
        copy = pltpu.make_async_copy(source, target, self.sems.at[self.used])
        copy.start()
        self.used += 1
        return copy


def group_copy(source, slots, sends, recvs, size, own, device, step):
    to = lax.rem(own + step, size)
    return pltpu.make_async_remote_copy(
        src_ref=source,
        dst_ref=slots.at[own],
        send_sem=sends.at[step],
        recv_sem=recvs.at[own],
        device_id=device(to),
        device_id_type=MESH,
    )


def group_arrival(source, slots, sends, recvs, size, own, device, step):
    origin = lax.rem(own + step, size)
    return pltpu.make_async_remote_copy(
        src_ref=source,
        dst_ref=slots.at[origin],
        send_sem=sends.at[step],
        recv_sem=recvs.at[origin],
        device_id=device(origin),
        device_id_type=MESH,
    )


def share_start(source, slots, sends, recvs, group):
    def start(step, carry):
        group_copy(source, slots, sends, recvs, *group, step).start()
        return carry

    lax.fori_loop(1, group[0], start, 0)
    slots[group[1]] = source[...]


def share_end(source, slots, sends, recvs, group):
    def end(step, carry):
        group_arrival(source, slots, sends, recvs, *group, step).wait_recv()
        group_copy(source, slots, sends, recvs, *group, step).wait_send()
        return carry

    lax.fori_loop(1, group[0], end, 0)


def add_slots(slots, size):
    def add(at, total):
        return total + slots[at]

    return lax.fori_loop(1, size, add, slots[0])


def share(source, slots, sends, recvs, group):
    share_start(source, slots, sends, recvs, group)
    share_end(source, slots, sends, recvs, group)
    return add_slots(slots, group[0])


def gather_start(source, slots, sends, recvs, group):
    def start(step, carry):
        group_copy(source, slots, sends, recvs, *group, step).start()
        return carry

    lax.fori_loop(1, group[0], start, 0)


def scatter_start(parts, slots, sends, recvs, group, keep=True):
    size, own, device = group

    def start(step, carry):
        to = lax.rem(own + step, size)
        group_copy(parts.at[to], slots, sends, recvs, *group, step).start()
        return carry

    lax.fori_loop(1, size, start, 0)
    if keep:
        slots[own] = parts[own]


def scatter_end(parts, slots, sends, recvs, group):
    share_end(parts.at[group[1]], slots, sends, recvs, group)


class Fold:
    def __init__(self, parts, fold_in, slots, sems, views, keep=True):
        view_at, chan_at, _, _ = place()
        self.parts, self.fold_in, self.slots, self.sems, self.keep = parts, fold_in, slots, sems, keep
        self.size, self.outer, self.inner = views // 2, lax.div(view_at, 2), lax.rem(view_at, 2)
        self.pair = (2 * self.outer + 1 - self.inner, chan_at)
        self.chan_at = chan_at

    def block(self, step):
        return lax.rem(self.outer + step, self.size)

    def pair_copy(self, step):
        at = self.block(step)
        return pltpu.make_async_remote_copy(
            src_ref=self.parts.at[2 * at + 1 - self.inner],
            dst_ref=self.fold_in.at[at],
            send_sem=self.sems[0].at[at],
            recv_sem=self.sems[1].at[at],
            device_id=self.pair,
            device_id_type=MESH,
        )

    def out_copy(self, step, slot):
        at = self.block(step)
        return pltpu.make_async_remote_copy(
            src_ref=self.parts.at[2 * at + self.inner],
            dst_ref=self.slots.at[slot],
            send_sem=self.sems[2].at[at],
            recv_sem=self.sems[3].at[slot],
            device_id=(2 * at + self.inner, self.chan_at),
            device_id_type=MESH,
        )

    def start(self):
        def one(step, carry):
            self.pair_copy(step).start()
            return carry

        lax.fori_loop(1, self.size + 1, one, 0)

    def add(self, step):
        self.pair_copy(step).wait_recv()
        at, mine = self.block(step), 2 * self.block(step) + self.inner
        total = self.parts[mine].astype(F32) + self.fold_in[at].astype(F32)
        self.parts[mine] = total.astype(self.parts.dtype)

    def pass_on(self, first, last):
        def one(step, carry):
            self.add(step)
            self.out_copy(step, self.outer).start()
            return carry

        lax.fori_loop(first, min(last, self.size), one, 0)
        if last > self.size:
            self.add(self.size)
            if self.keep:
                self.slots[self.outer] = self.parts[2 * self.outer + self.inner]

    def end(self):
        def one(step, carry):
            self.out_copy(step, self.block(step)).wait_recv()
            self.out_copy(step, self.outer).wait_send()
            return carry

        lax.fori_loop(1, self.size, one, 0)

        def sent(step, carry):
            self.pair_copy(step).wait_send()
            return carry

        lax.fori_loop(1, self.size + 1, sent, 0)


def chan_group():
    view_at, chan_at, y, c = place()
    return (4, chan_at, lambda at: (view_at, at))


def half_group(views):
    view_at, chan_at, y, c = place()
    return (
        2 * views,
        2 * view_at + c,
        lambda at: (lax.div(at, 2), 2 * y + lax.rem(at, 2)),
    )


def view_group(views):
    view_at, chan_at, y, c = place()
    return (views, view_at, lambda at: (at, chan_at))


def all_group(views):
    view_at, chan_at, y, c = place()
    return (4 * views, 4 * view_at + chan_at, lambda at: (lax.div(at, 4), lax.rem(at, 4)))


def dot(left, right):
    return jnp.dot(left, right, preferred_element_type=F32)


def dot_nt(left, right):
    return lax.dot_general(left, right, (((1,), (1,)), ((), ())), preferred_element_type=F32)


def dot_tn(left, right):
    return lax.dot_general(left, right, (((0,), (0,)), ((), ())), preferred_element_type=F32)


def gate(level):
    return 0.5 + 0.5 * jnp.tanh(0.5 * level)


def silu_slope(level):
    open_part = gate(level)
    return open_part * (1.0 + level * (1.0 - open_part))


def call(body, name, outs, ins, scratch, collective, any_ins=(), any_outs=()):
    def spec(at, places):
        return pl.BlockSpec(memory_space=pl.ANY if at in places else pltpu.VMEM)

    return pl.pallas_call(
        body,
        out_shape=outs,
        in_specs=[spec(at, any_ins) for at in range(ins)],
        out_specs=tuple(spec(at, any_outs) for at in range(len(outs))),
        scratch_shapes=scratch,
        name=name,
        compiler_params=pltpu.CompilerParams(
            collective_id=collective,
            has_side_effects=collective is not None,
            vmem_limit_bytes=VMEM_BYTES,
        ),
    )


def shape(*dims, kind=F32):
    return jax.ShapeDtypeStruct(dims, kind)


def dma(*dims):
    return pltpu.SemaphoreType.DMA(dims)


def split_rows(value):
    high = value.astype(BF16)
    rest = value - high.astype(F32)
    middle = rest.astype(BF16)
    low = (rest - middle.astype(F32)).astype(BF16)
    return jnp.concatenate([high, middle, low], axis=0)


def join_rows(stacked):
    rows = stacked.shape[0] // 3
    return stacked[2 * rows :] + stacked[rows : 2 * rows] + stacked[:rows]


def split_pair(value):
    high = value.astype(BF16)
    return high, (value - high.astype(F32)).astype(BF16)


def exact(left, right, left_dim, right_dim):
    return lax.dot_general(
        left,
        right,
        (((left_dim,), (right_dim,)), ((), ())),
        precision=lax.Precision.HIGHEST,
        preferred_element_type=F32,
    )


def over(count, body, start):
    return body(0, start) if count == 1 else lax.fori_loop(0, count, body, start)


def split_three(value):
    high = value.astype(BF16)
    rest = value - high.astype(F32)
    middle = rest.astype(BF16)
    return high, middle, (rest - middle.astype(F32)).astype(BF16)


def short_product(left, right):
    lh, lm, ll = split_three(left)
    rh, rm, rl = split_three(right)
    return dot_tn(
        jnp.concatenate([lh, lh, lm, lh, lm, ll], axis=0),
        jnp.concatenate([rh, rm, rh, rl, rm, rh], axis=0),
    )


def outer_product(left, right):
    def rows(value, high_at, middle_at, low_at):
        parts = [part.astype(F32) for part in split_three(value)]
        row = lax.broadcasted_iota(jnp.int32, (16, value.shape[1]), 0)
        total = jnp.zeros((16, value.shape[1]), F32)
        for part, places in zip(parts, (high_at, middle_at, low_at)):
            for place_at in places:
                total = jnp.where(row == place_at, part, total)
        return total.astype(BF16)

    return dot_tn(rows(left, (0, 1, 3), (2, 4), (5,)), rows(right, (0, 2, 5), (1, 4), (3,)))


def factor_inverse(work, inverse, subs, width):
    panel = 16
    row = lax.broadcasted_iota(jnp.int32, (panel, width), 0)

    def wide(part):
        return jnp.broadcast_to(part, (panel, width))

    def eliminate(s, first):
        rows = work[s, first : first + panel]
        columns = [wide(rows[:, first + j : first + j + 1]) for j in range(panel)]
        diagonal = jnp.zeros((panel, width), F32)
        for j in range(panel):
            pivot = wide(columns[j][j : j + 1])
            diagonal = jnp.where(row == j, pivot, diagonal)
            if j == panel - 1:
                break
            ratio = jnp.where(row > j, columns[j] * (1.0 / pivot), 0.0)
            for k in range(j + 1, panel):
                columns[k] = columns[k] - ratio * wide(columns[k][j : j + 1])
            rows = rows - jnp.concatenate([ratio, ratio], axis=1) * rows[j : j + 1]
        inverse[s, first : first + panel] = rows[:, width:] * lax.rsqrt(diagonal)
        if first + panel < width:
            scaled = rows[:, :width] / diagonal
            work[s, first + panel :] -= short_product(scaled, rows)[first + panel :]

    def some(at, carry):
        for first in range(0, width, panel):
            for k in range(2):
                eliminate(2 * at + k, first)
        return carry

    over(subs // 2, some, 0)


def view_sums(value, block):
    return jnp.concatenate(
        [jnp.sum(value[PIX * v : PIX * (v + 1)], axis=0, keepdims=True) for v in range(block)], axis=0
    )


def columns_of(row, column):
    tile = column.shape[1]

    def one(at, carry):
        cols = pl.ds(pl.multiple_of(at * tile, tile), tile)
        column[cols] = jnp.broadcast_to(row[:, cols].astype(F32), (tile, tile)).T
        return carry

    lax.fori_loop(0, row.shape[1] // tile, one, 0)


def whiten(embed, sub_col, image_col, image_row, partner_col, partner_row, refs, own_rows):
    work, inverse, white, unit, unit_parts, back = refs
    total, width = embed.shape
    subs = inverse.shape[0]
    eye = (
        lax.broadcasted_iota(jnp.int32, (width, width), 0)
        == lax.broadcasted_iota(jnp.int32, (width, width), 1)
    ).astype(F32)
    size = min(total, 512)
    pieces = total // size

    def rows_at(at):
        return pl.ds(pl.multiple_of(at * size, size), size)

    means = []

    def masks(rows, s):
        column = sub_col[rows]
        return (column == float(s)).astype(F32), (column == float(s + 1)).astype(F32)

    for s in range(0, subs, 2):

        def moments(at, sums, s=s):
            rows = rows_at(at)
            value = embed[rows]
            picked = jnp.concatenate([value * mask for mask in masks(rows, s)], axis=1)
            first = sums[0] + jnp.sum(picked, axis=0, keepdims=True)
            return first, sums[1] + exact(picked, value, 0, 0)

        first, second = over(
            pieces, moments, (jnp.zeros((1, 2 * width), F32), jnp.zeros((2 * width, width), F32))
        )
        for k in range(2):
            mean = first[:, k * width : (k + 1) * width] / SUB
            cov = second[k * width : (k + 1) * width] / SUB - exact(mean, mean, 0, 0)
            work[s + k, :, :width] = cov + RIDGE * eye
            work[s + k, :, width:] = eye
            means.append(mean)
    factor_inverse(work, inverse, subs, width)

    def whitening(at, carry):
        rows = rows_at(at)
        value = None
        for s in range(0, subs, 2):
            centred = jnp.concatenate(
                [(embed[rows] - means[s + k]) * mask for k, mask in enumerate(masks(rows, s))], axis=1
            )
            term = exact(centred, jnp.concatenate([inverse[s], inverse[s + 1]], axis=1), 1, 1)
            value = term if value is None else value + term
        white[rows] = value
        value = value * lax.rsqrt(jnp.sum(value * value, axis=1, keepdims=True) + EPS)
        unit[rows] = value
        high = value.astype(BF16)
        rest = value - high.astype(F32)
        middle = rest.astype(BF16)
        unit_parts[rows] = jnp.concatenate(
            [high, middle, (rest - middle.astype(F32)).astype(BF16)], axis=1
        )
        return carry

    over(pieces, whitening, 0)
    chunk = min(total, 262144 // total)

    def pairs(at, loss):
        rows = pl.ds(pl.multiple_of(at * chunk, chunk), chunk)
        across = lax.broadcasted_iota(jnp.int32, (chunk, total), 1).astype(F32)
        down = lax.broadcasted_iota(jnp.int32, (chunk, total), 0) + at * chunk

        def pick(hot):
            found = dot(hot.astype(F32).astype(BF16), unit_parts[...])
            return found[:, 2 * width :] + found[:, width : 2 * width] + found[:, :width]

        mine = unit[rows]
        ahead = pick(partner_col[rows][:, :1] == across)
        behind = pick(partner_row[...] == down)
        members = jnp.sum(
            (image_col[rows][:, :1] == image_row[...].astype(F32)).astype(F32), axis=1, keepdims=True
        )
        weight = 1.0 / members
        apart = mine - ahead
        grad = (4.0 / total) * weight * (2.0 * mine - ahead - behind)
        length = lax.rsqrt(jnp.sum(white[rows] * white[rows], axis=1, keepdims=True) + EPS)
        back[rows] = length * (grad - mine * jnp.sum(mine * grad, axis=1, keepdims=True))
        per_view = jnp.sum(apart * apart, axis=1, keepdims=True) * weight
        return loss + jnp.sum(per_view, axis=0, keepdims=True)

    loss = over(total // chunk, pairs, jnp.zeros((1, 1), F32)) * (2.0 / total)
    lower = lax.broadcasted_iota(jnp.int32, (width, width), 0) >= lax.broadcasted_iota(
        jnp.int32, (width, width), 1
    )
    own_white, own_back = white[own_rows], back[own_rows]
    gradient = jnp.zeros(own_white.shape, F32)
    for s in range(0, subs, 2):

        def pulled(at, sums, s=s):
            rows = rows_at(at)
            picked = jnp.concatenate([back[rows] * mask for mask in masks(rows, s)], axis=1)
            spread = sums[0] + jnp.sum(picked, axis=0, keepdims=True)
            return spread, sums[1] + exact(picked, white[rows], 0, 0)

        spread, sums = over(
            pieces, pulled, (jnp.zeros((1, 2 * width), F32), jnp.zeros((2 * width, width), F32))
        )
        for k, own_mask in enumerate(masks(own_rows, s)):
            cols = slice(k * width, (k + 1) * width)
            low_part = jnp.where(lower, sums[cols], 0.0)
            mirrored = low_part + low_part.T - sums[cols] * eye
            moved = own_back - (exact(own_white, mirrored, 1, 0) + spread[:, cols]) / SUB
            gradient = gradient + own_mask * exact(moved, inverse[s + k], 1, 0)
    return loss, gradient


MIDDLE_TAPS = 3
EARLY_TAPS = 3


def orders(quarter):
    block = quarter // PIX
    row = np.arange(quarter)
    source = (row % block) * PIX + row // block
    hot = (source[:, None] == row[None, :]).astype(BF16)
    return jnp.asarray(hot), jnp.asarray(hot.T)


def front_body(
    views, g1, b1, g2, b2, gain_last, shift_last, gain_head, shift_head, sub_row, image_row, partner_row,
    x_any, w1in, w2in, w3in, perm_any, unperm_any, head_first_any, head_last_any,
    pad_out, h1_out, w2_out, w2_far, w3_out, act_out, h3_out, slope_out, pooled_all, h2_near, h2_far,
    stat, w1_own, smalls, stat3, grad_shift_last, grad_gain_last, grad_shift_head, grad_gain_head,
    grad_pooled_out, act4, grad_embed_out, grad_p1, loss_out, stats2, pooled_means, rows_sum,
    x, w1, act, h3, h1, st, slots, st2, slots2, perm, unperm, pad, w2, w3, hidden, h2, small,
    head_first, head_last, slope, pooled_own, pooled_low, sub_col, image_col, partner_col,
    embed_all, part, part_in, mean_sums, slope_sums, st3, slots3, st4, slots4, bk4, bslots4, bk3, bslots3, embed_own,
    work, inverse, white, unit, unit_parts, back,
    sends, recvs, part_sends, part_recvs, half_sends, half_recvs, group_sends, group_recvs, local_sems,
):
    view_at, chan_at, y, c = place()
    mate, opposite = (view_at, 2 * y + 1 - c), (view_at, 2 * (1 - y) + c)
    diagonal = (view_at, 2 * (1 - y) + 1 - c)
    half_peers, group = half_group(views), view_group(views)
    quarter, depth = x.shape[1], x.shape[2]
    width = h3.shape[2]
    block = quarter // PIX
    views_own = 4 * block
    parts = act.reshape(2, 2, 2, quarter, act.shape[3])
    out_part, in_part = parts.at[0], parts.at[1]
    xm = h3.at[pl.ds(0, 2)]
    near, far = 2 * y + c, 2 * (1 - y) + c
    near_rows = pl.ds(pl.multiple_of(2 * depth * y, 2 * depth), 2 * depth)
    far_rows = pl.ds(pl.multiple_of(2 * depth * (1 - y), 2 * depth), 2 * depth)
    met = greet([opposite, diagonal], [half_peers])
    local = Local(local_sems)
    w1_here = local.fetch(w1in.at[near_rows], w1.at[near])
    perm_here = local.fetch(perm_any, perm)
    x_own = [local.fetch(x_any.at[2 * q + c], x.at[2 * q + c]) for q in range(2)]
    w2_here = local.fetch(w2in, w2.at[c])
    unperm_here = local.fetch(unperm_any, unperm)
    rest = [local.fetch(w3in.at[near_rows], w3.at[near])]
    for at, vector in enumerate((g1, b1, g2, b2)):
        small[at : at + 1] = vector[...]
        small[4 + at : 5 + at] = vector[...]
    smalls[chan_at] = small[...]
    pad[...] = jnp.zeros(pad.shape, pad.dtype)
    met()
    mail = Mail(sends, recvs)
    w1_mate = mail.send(w1in.at[near_rows], w1.at[near], mate)
    x_mate = [mail.send(x_any.at[1 - c], xm.at[0], mate)]
    w1_far = mail.send(w1in.at[far_rows], w1.at[near], opposite)
    x_mate.append(mail.send(x_any.at[3 - c], xm.at[1], mate))
    small_copies = [mail.send(small, smalls.at[chan_at], to) for to in (mate, opposite, diagonal)]
    w2_mate = mail.send(w2in, w2.at[c], mate)
    w3_mate = mail.send(w3in.at[near_rows], w3.at[near], mate)

    def part_copy(half, q):
        return pltpu.make_async_remote_copy(
            src_ref=out_part.at[half, q],
            dst_ref=in_part.at[half, q],
            send_sem=part_sends.at[half, q],
            recv_sem=part_recvs.at[half, q],
            device_id=opposite,
            device_id_type=MESH,
        )

    own_in, mate_in = (
        pl.ds(pl.multiple_of(depth * k, depth), depth) for k in (c, 1 - c)
    )

    def send_part(half, q):
        def weight(rows):
            return jnp.concatenate([w1[2 * half, rows], w1[2 * half + 1, rows]], axis=1)

        value = dot(x[2 * q + c], weight(own_in)) + dot(xm[q], weight(mate_in))
        out_part[half, q] = dot(perm[...], value.astype(BF16)).astype(BF16)
        part_copy(half, q).start()

    w1_here.wait()
    w1_mate.wait_recv()
    perm_here.wait()
    for q in range(2):
        x_own[q].wait()
        x_mate[q].wait_recv()
        send_part(y, q)
    w1_far.wait_recv()
    w1_on = mail.send(w1.at[far], w1.at[far], mate)
    w1_on.wait_recv()
    for q in range(2):
        send_part(1 - y, q)
    x_rest = [local.fetch(x_any.at[2 * q + 1 - c], x.at[2 * q + 1 - c]) for q in range(2)]
    w2_here.wait()
    w2_mate.wait_recv()
    rest.append(local.fetch(w2, w2_out))
    own_rows = pl.ds(pl.multiple_of(depth * c, depth), depth)
    w1_own[...] = jnp.concatenate([w1[k, own_rows] for k in range(4)], axis=1)
    st[...] = jnp.zeros(st.shape, st.dtype)
    step_rows = quarter // SIDE

    def sums(half):
        def one(q, carry):
            part_copy(half, q).wait_recv()

            def rows_of(at, inner):
                rows = pl.ds(at * step_rows, step_rows)
                value = out_part[half, q, rows].astype(F32) + in_part[half, q, rows].astype(F32)
                h1[half, q, rows] = value
                st[half, 0:1] += jnp.sum(value, axis=0, keepdims=True)
                st[half, 1:2] += jnp.sum(value * value, axis=0, keepdims=True)
                return inner

            return lax.fori_loop(0, SIDE, rows_of, carry)

        lax.fori_loop(0, 2, one, 0)

    sums(1 - y)
    sums(y)
    for half in range(2):
        for q in range(2):
            part_copy(half, q).wait_send()
    share_start(st, slots, half_sends.at[0], half_recvs.at[0], half_peers)
    w3_far = mail.send(w3in.at[far_rows], w3.at[near], opposite)
    channels = pad.shape[4]
    early_taps = []
    for tap in range(EARLY_TAPS):
        rows = pl.ds(tap * channels, channels)
        early_taps.append(mail.send(w2in.at[rows], w2_far.at[c, rows], opposite))
    share_end(st, slots, half_sends.at[0], half_recvs.at[0], half_peers)
    totals = add_slots(slots, half_peers[0])
    count = float(views * 4 * quarter)
    for copy in small_copies:
        copy.wait_recv()
    mean = totals[:, 0:1] / count
    rstd = lax.rsqrt(totals[:, 1:2] / count - mean * mean + EPS)
    stat[...] = jnp.concatenate([mean, rstd], axis=1)
    for half in range(2):
        gains = jnp.concatenate([smalls[2 * half], smalls[2 * half + 1]], axis=1)
        scale = rstd[half] * gains[0:1]
        bias = gains[1:2] - mean[half] * scale

        def act_rows(at, carry, half=half, scale=scale, bias=bias):
            q, i = lax.div(at, SIDE), lax.rem(at, SIDE)
            level = h1[half, q, pl.ds(i * step_rows, step_rows)] * scale + bias
            value = (level * gate(level)).astype(BF16)
            pad[q, i + 1, 1 : SIDE + 1, :, 256 * half : 256 * half + 256] = value.reshape(
                SIDE, step_rows // SIDE, 256
            )
            return carry

        lax.fori_loop(0, 2 * SIDE, act_rows, 0)
    rest.append(local.fetch(pad, pad_out))
    rest += [local.fetch(h1.at[half, y], h1_out.at[half]) for half in range(2)]
    w3_far.wait_recv()
    w3_on = mail.send(w3.at[far], w3.at[far], mate)
    st2[...] = jnp.zeros(st2.shape, F32)

    def convolve(q, carry):
        for tap in range(9):
            a, b = tap // 3, tap % 3
            window = pad[q, a : a + SIDE, b : b + SIDE].reshape(quarter, channels)
            taps = slice(tap * channels, (tap + 1) * channels)
            term = dot(window, jnp.concatenate([w2[0, taps], w2[1, taps]], axis=1))
            if tap == 0:
                hidden[q] = term
            else:
                hidden[q] += term
        value = hidden[q]
        h2[q] = value.astype(BF16)
        st2[0:1] += jnp.sum(value, axis=0, keepdims=True)
        st2[1:2] += jnp.sum(value * value, axis=0, keepdims=True)
        return carry

    lax.fori_loop(0, 2, convolve, 0)
    share_start(st2, slots2, half_sends.at[1], half_recvs.at[1], half_peers)
    rest.append(local.fetch(h2, h2_near))
    w2_on = []

    def pass_on(taps):
        for tap in taps:
            early_taps[tap].wait_recv()
            rows = pl.ds(tap * channels, channels)
            w2_on.append(mail.send(w2_far.at[c, rows], w2_far.at[c, rows], mate))

    pass_on(range(EARLY_TAPS - 1))
    share_end(st2, slots2, half_sends.at[1], half_recvs.at[1], half_peers)
    totals2 = add_slots(slots2, half_peers[0])
    mean2 = totals2[0:1] / count
    rstd2 = lax.rsqrt(totals2[1:2] / count - mean2 * mean2 + EPS)
    stats2[y] = jnp.concatenate([mean2, rstd2], axis=0)
    gains = jnp.concatenate([smalls[2 * y], smalls[2 * y + 1]], axis=1)
    scale2 = rstd2 * gains[2:3]
    bias2 = gains[3:4] - mean2 * scale2
    across, beside = [], []
    unperm_here.wait()
    for q in range(2):
        level = hidden[q] * scale2 + bias2
        value = (level * gate(level)).astype(BF16)
        act[y, 2 * q + c] = dot(unperm[...], value).astype(BF16)
        spot = act.at[y, 2 * q + c]
        across.append(mail.send(spot, spot, opposite))
        beside.append(mail.send(spot, spot, mate))
    pass_on(range(EARLY_TAPS - 1, EARLY_TAPS))
    stat2_far = mail.send(stats2.at[y], stats2.at[y], opposite)

    own_out = pl.ds(pl.multiple_of(width * c, width), width)
    st3[...] = jnp.zeros(st3.shape, F32)
    head_first_here = local.fetch(head_first_any, head_first)
    head_last_here = local.fetch(head_last_any, head_last)
    for copy in (w3_mate, w3_on):
        copy.wait_recv()
    rest[0].wait()
    w3_kept = local.fetch(w3, w3_out)

    def last_conv(q):
        total = None
        for half in range(2):
            weight = jnp.concatenate([w3[2 * half, own_out], w3[2 * half + 1, own_out]], axis=1)
            term = dot_nt(act[half, q], weight)
            total = term if total is None else total + term
        low = total.astype(BF16)
        h3[q] = low
        value = low.astype(F32)
        st3[0:1] += jnp.sum(value, axis=0, keepdims=True)
        st3[1:2] += jnp.sum(value * value, axis=0, keepdims=True)

    for row, column in ((sub_row, sub_col), (image_row, image_col), (partner_row, partner_col)):
        columns_of(row, column)
    for q in range(2):
        across[q].wait_recv()
        spot = act.at[1 - y, 2 * q + c]
        passed = mail.send(spot, spot, mate)
        last_conv(2 * q + c)
        beside[q].wait_recv()
        passed.wait_recv()
        last_conv(2 * q + 1 - c)
    for copy in w2_on:
        copy.wait_recv()
    act_kept = local.fetch(act, act_out)
    middle_rows = pl.ds(EARLY_TAPS * channels, MIDDLE_TAPS * channels)
    w2_middle = mail.send(w2in.at[middle_rows], w2_far.at[c, middle_rows], opposite)
    share_start(st3, slots3, group_sends.at[0], group_recvs.at[0], group)
    rest.append(local.fetch(h3, h3_out))
    share_end(st3, slots3, group_sends.at[0], group_recvs.at[0], group)
    totals = add_slots(slots3, views)
    count = float(views * 4 * quarter)
    mean = totals[0:1] / count
    rstd = lax.rsqrt(totals[1:2] / count - mean * mean + EPS)
    stat3[...] = jnp.concatenate([mean, rstd], axis=0)
    scale = rstd * gain_last[...]
    bias = shift_last[...] - mean * scale
    for copy in x_rest:
        copy.wait()

    def pool_block(q, carry):
        before = x[q].astype(F32) + (h3[q].astype(F32) * scale + bias)
        sums = view_sums(before * gate(before), block)
        pooled_own[pl.ds(pl.multiple_of(q * block, block), block)] = sums * (1.0 / PIX)
        return carry

    lax.fori_loop(0, 4, pool_block, 0)
    head_first_here.wait()
    hidden = join_rows(dot(split_rows(pooled_own[...]), head_first[...]))
    wide = hidden.shape[1] // 2
    part[0] = hidden[:, :wide]
    part[1] = hidden[:, wide:]
    swap = mail.send(part, part_in.at[pl.ds(0, 2)], mate)

    def slope_block(q, carry):
        level3 = h3[q].astype(F32)
        before = x[q].astype(F32) + (level3 * scale + bias)
        low = silu_slope(before).astype(BF16)
        slope[q] = low
        normed = (level3 - mean) * rstd
        kept = low.astype(F32)
        rows = pl.ds(pl.multiple_of(q * block, block), block)
        slope_sums[0, rows] = view_sums(kept, block)
        slope_sums[1, rows] = view_sums(kept * normed, block)
        return carry

    swap.wait()
    mean_sums[...] = part[...] + part_in[0:2]
    across_p1 = mail.send(mean_sums.at[c], part_in.at[2], opposite)
    lax.fori_loop(0, 2, slope_block, 0)
    across_p1.wait_recv()
    part_in[4 + c] = mean_sums[c] + part_in[2]
    gathered = mail.send(part_in.at[4 + c], part_in.at[4 + c], mate)
    h2_over = mail.send(h2, h2_far, opposite)
    w2_middle.wait_recv()
    w2_middle_on = mail.send(w2_far.at[c, middle_rows], w2_far.at[c, middle_rows], mate)
    before_late = (EARLY_TAPS + MIDDLE_TAPS) * channels
    late_rows = pl.ds(before_late, w2in.shape[0] - before_late)
    w2_over = mail.send(w2in.at[late_rows], w2_far.at[c, late_rows], opposite)
    gathered.wait_recv()
    p1 = part_in[4:6]
    st4[0:2] = jnp.sum(p1, axis=1)
    st4[2:4] = jnp.sum(p1 * p1, axis=1)
    share_start(st4, slots4, group_sends.at[1], group_recvs.at[1], group)
    lax.fori_loop(2, 4, slope_block, 0)
    rest.append(local.fetch(slope, slope_out))
    share_end(st4, slots4, group_sends.at[1], group_recvs.at[1], group)
    totals4 = add_slots(slots4, views)
    count4 = float(views * views_own)
    mean4 = totals4[0:2] / count4
    rstd4 = lax.rsqrt(totals4[2:4] / count4 - mean4 * mean4 + EPS)
    head_last_here.wait()

    def level4(half):
        cols = slice(half * wide, (half + 1) * wide)
        normed = (part_in[4 + half] - mean4[half : half + 1]) * rstd4[half : half + 1]
        return normed, normed * gain_head[:, cols] + shift_head[:, cols]

    embed = None
    for half in range(2):
        normed, level = level4(half)
        value = level * gate(level)
        act4[half] = value
        term = join_rows(dot(split_rows(value), head_last[half * wide : (half + 1) * wide]))
        embed = term if embed is None else embed + term
    embed_own[...] = embed
    share_start(embed_own, embed_all, group_sends.at[2], group_recvs.at[2], group)
    share_end(embed_own, embed_all, group_sends.at[2], group_recvs.at[2], group)
    pooled_mean = jnp.sum(pooled_own[...], axis=0, keepdims=True) / views_own
    bk3[2:3] = pooled_mean
    pooled_low[...] = (pooled_own[...] - pooled_mean).astype(BF16)
    gather_start(pooled_low, pooled_all, group_sends.at[5], group_recvs.at[5], group)
    rest.append(local.fetch(pooled_low, pooled_all.at[view_at]))
    own_rows = pl.ds(pl.multiple_of(view_at * views_own, views_own), views_own)
    every = embed_all.reshape(views * views_own, embed.shape[1])
    loss, grad_embed = whiten(
        every, sub_col, image_col, image_row, partner_col, partner_row,
        (work, inverse, white, unit, unit_parts, back), own_rows,
    )
    loss_out[...] = loss
    grad_embed_out[...] = grad_embed
    stacked = split_rows(grad_embed)
    for half in range(2):
        normed, level = level4(half)
        grad = join_rows(dot_nt(stacked, head_last[half * wide : (half + 1) * wide]))
        grad = grad * silu_slope(level)
        part[half] = grad
        bk4[half : half + 1] = jnp.sum(grad, axis=0, keepdims=True)
        bk4[2 + half : 3 + half] = jnp.sum(grad * normed, axis=0, keepdims=True)
    tot4 = share(bk4, bslots4, group_sends.at[3], group_recvs.at[3], group)
    grad_pooled = None
    for half in range(2):
        cols = slice(half * wide, (half + 1) * wide)
        normed, level = level4(half)
        shift_sum, gain_sum = tot4[half : half + 1], tot4[2 + half : 3 + half]
        grad_shift_head[:, cols] = shift_sum
        grad_gain_head[:, cols] = gain_sum
        grad = (
            gain_head[:, cols]
            * rstd4[half : half + 1]
            * (part[half] - shift_sum / count4 - normed * (gain_sum / count4))
        )
        grad_p1[half] = grad
        term = join_rows(dot_nt(split_rows(grad), head_first[:, cols]))
        grad_pooled = term if grad_pooled is None else grad_pooled + term
    grad_pooled = grad_pooled * (1.0 / PIX)
    grad_pooled_out[...] = grad_pooled
    bk3[0:1] = jnp.sum(grad_pooled * slope_sums[0], axis=0, keepdims=True)
    bk3[1:2] = jnp.sum(grad_pooled * slope_sums[1], axis=0, keepdims=True)
    share_start(bk3, bslots3, group_sends.at[4], group_recvs.at[4], group)
    w2_over.wait_recv()
    w2_last = mail.send(w2_far.at[c, late_rows], w2_far.at[c, late_rows], mate)
    share_end(bk3, bslots3, group_sends.at[4], group_recvs.at[4], group)
    tot3 = add_slots(bslots3, views)
    grad_shift_last[...] = tot3[0:1]
    grad_gain_last[...] = tot3[1:2]
    own_count = float(4 * quarter)
    normed_sum = (st3[0:1] - own_count * mean) * rstd
    rows_sum[...] = scale * (
        bk3[0:1] - tot3[0:1] * (own_count / count) - normed_sum * (tot3[1:2] / count)
    )
    pooled_means[...] = bslots3[:, 2]
    h2_over.wait_recv()
    stat2_far.wait_recv()
    w2_last.wait_recv()
    w2_middle_on.wait_recv()
    share_end(pooled_low, pooled_all, group_sends.at[5], group_recvs.at[5], group)
    for copy in [*rest[1:], w3_kept, act_kept]:
        copy.wait()
    for copy in mail.copies:
        if copy is not swap:
            copy.wait_send()


def front_stage(views, x, weights, vectors, tables, perm, unperm):
    conv_first, conv_mid, conv_last, head_first, head_last = weights
    quarter, depth = x.shape[0] // 4, x.shape[1]
    width = depth
    mid = conv_mid.shape[1] * 4
    half = mid // 2
    block = quarter // PIX
    own = 4 * block
    total = views * own
    hid, emb = head_last.shape
    wide = hid // 2
    subs = total // SUB
    peers = 2 * views
    vm = pltpu.VMEM
    wide_rows = (4, quarter, width)
    return call(
        functools.partial(front_body, views),
        "front",
        (
            shape(2, PAD, PAD, block, mid, kind=BF16),
            shape(2, quarter, half),
            shape(2, *conv_mid.shape, kind=BF16),
            shape(2, *conv_mid.shape, kind=BF16),
            shape(4, 2 * depth, mid // 4, kind=BF16),
            shape(2, 4, quarter, half, kind=BF16),
            shape(*wide_rows, kind=BF16),
            shape(*wide_rows, kind=BF16),
            shape(views, own, width, kind=BF16),
            shape(2, quarter, half, kind=BF16),
            shape(2, quarter, half, kind=BF16),
            shape(2, 2, half),
            shape(depth, mid, kind=BF16),
            shape(4, 8, mid // 4),
            shape(2, width),
            shape(1, width),
            shape(1, width),
            shape(1, hid),
            shape(1, hid),
            shape(own, width),
            shape(2, own, wide),
            shape(own, emb),
            shape(2, own, wide),
            shape(1, 1),
            shape(2, 2, half),
            shape(views, width),
            shape(1, width),
        ),
        19,
        [
            vm(wide_rows, BF16),
            vm((4, 2 * depth, mid // 4), BF16),
            vm((2, 4, quarter, half), BF16),
            vm(wide_rows, BF16),
            vm((2, 2, quarter, half), F32),
            vm((2, 2, half), F32),
            vm((peers, 2, 2, half), F32),
            vm((2, half), F32),
            vm((peers, 2, half), F32),
            vm((quarter, quarter), BF16),
            vm((quarter, quarter), BF16),
            vm((2, PAD, PAD, block, mid), BF16),
            vm((2, *conv_mid.shape), BF16),
            vm((4, 2 * depth, mid // 4), BF16),
            vm((2, quarter, half), F32),
            vm((2, quarter, half), BF16),
            vm((8, mid // 4), F32),
            vm(head_first.shape, BF16),
            vm(head_last.shape, BF16),
            vm(wide_rows, BF16),
            vm((own, width), F32),
            vm((own, width), BF16),
            vm((total, 128), F32),
            vm((total, 128), F32),
            vm((total, 128), F32),
            vm((views, own, emb), F32),
            vm((2, own, wide), F32),
            vm((6, own, wide), F32),
            vm((2, own, wide), F32),
            vm((2, own, width), F32),
            vm((2, width), F32),
            vm((views, 2, width), F32),
            vm((4, wide), F32),
            vm((views, 4, wide), F32),
            vm((4, wide), F32),
            vm((views, 4, wide), F32),
            vm((3, width), F32),
            vm((views, 3, width), F32),
            vm((own, emb), F32),
            vm((subs, emb, 2 * emb), F32),
            vm((subs, emb, emb), F32),
            vm((total, emb), F32),
            vm((total, emb), F32),
            vm((total, 3 * emb), BF16),
            vm((total, emb), F32),
            dma(40),
            dma(40),
            dma(2, 2),
            dma(2, 2),
            dma(2, peers),
            dma(2, peers),
            dma(6, views),
            dma(6, views),
            dma(32),
        ],
        collective=1,
        any_ins=range(11, 19),
        any_outs=range(11),
    )(
        *vectors, *tables, x.reshape(wide_rows), conv_first, conv_mid, conv_last, perm, unperm,
        head_first, head_last,
    )


def link_kind(rows):
    return BF16 if rows % 16 == 0 else F32


def back_body(
    views, stat3, grad_shift_last, grad_gain_last, grad_pooled, gain_last, expand,
    stats2, smalls, stat1, act4, grad_embed, grad_p1, pooled_means, rows_sum,
    h3_any, slope_any, w3_any, h2_near_any, h2_far_any, perm_any, unperm_any, pad_any, h1q_any, w2_any,
    w2_far_any, act_any, x_any, pooled_any,
    gh1_out, mid_slots, pair_out, head_last_out, head_first_out,
    grad_shift_mid, grad_gain_mid, grad_shift_first, grad_gain_first,
    h3, slope, w3, h2_near, h2_far, gh1, gh3, gh3_mate, out_part, in_part, ga2, gh2_far, gpad, ga1, st, sum_parts, chan_slots, view_slots,
    order, pad, h1q, w2, w2_far, act, pooled,
    wsum, wsend, mid_parts, mid_in, last_parts, last_in, last_slots, first_parts, first_in, first_slots, means, mean_slots, pair_parts,
    hl_parts, hl_slots, p1_parts, p1_slots,
    sends, recvs, chan_sends, chan_recvs, group_sends, group_recvs, pair_sends, pair_recvs,
    pair1_sends, pair1_recvs, pair2_sends, pair2_recvs, local_sems,
):
    view_at, chan_at, y, c = place()
    mate, opposite = (view_at, 2 * y + 1 - c), (view_at, 2 * (1 - y) + c)
    group, chans, everyone = view_group(views), chan_group(), all_group(views)
    quarter, width = h3.shape[1], h3.shape[2]
    block = quarter // PIX
    half_width = h2_near.shape[2]
    met = greet([], [everyone])
    local = Local(local_sems)
    near_half, own_half = [2 * i + 1 - c for i in (1 - y, y)], [2 * i + c for i in (1 - y, y)]
    rows_here = []

    def fetch_rows(q):
        rows_here.append((local.fetch(h3_any.at[q], h3.at[q]), local.fetch(slope_any.at[q], slope.at[q])))

    for q in near_half:
        fetch_rows(q)
    count = float(views * 4 * quarter)
    mean, rstd = stat3[0:1], stat3[1:2]
    scale = rstd * gain_last[...]
    shift_part, gain_part = grad_shift_last[...] / count, grad_gain_last[...] / count

    def grad_rows(q):
        rows = pl.ds(pl.multiple_of(q * block, block), block)
        high, low = split_pair(grad_pooled[rows])
        spread = dot(expand[...], jnp.concatenate([high, low], axis=0))
        grad = spread * slope[q].astype(F32)
        normed = (h3[q].astype(F32) - mean) * rstd
        gh3[q] = (scale * (grad - shift_part - normed * gain_part)).astype(BF16)

    mate_out = pl.ds(pl.multiple_of(width * (1 - c), width), width)
    own_out = pl.ds(pl.multiple_of(width * c, width), width)

    def part_of(i):
        def weight(rows):
            return jnp.concatenate([w3[k, rows] for k in range(4)], axis=1)

        value = dot(gh3[2 * i + c], weight(own_out)) + dot(gh3_mate[i], weight(mate_out))
        return dot(order[...], value.astype(BF16))

    mail = Mail(sends, recvs)
    beside = []
    for at, i in enumerate((1 - y, y)):
        for copy in rows_here[at]:
            copy.wait()
        grad_rows(2 * i + 1 - c)
        if at == 0:
            met()
        beside.append(mail.send(gh3.at[2 * i + 1 - c], gh3_mate.at[i], mate))
        if at == 0:
            for q in own_half:
                fetch_rows(q)
            w3_here = local.fetch(w3_any, w3)
            perm_here = local.fetch(perm_any, order)
    for at, i in enumerate((1 - y, y)):
        for copy in rows_here[2 + at]:
            copy.wait()
        grad_rows(2 * i + c)
        if at == 0:
            w3_here.wait()
            perm_here.wait()
            beside[0].wait_recv()
            value = part_of(1 - y).astype(BF16)
            for half in range(2):
                out_part[half] = value[:, half * half_width : (half + 1) * half_width]
            across = [mail.send(out_part.at[half], in_part.at[half], opposite) for half in range(2)]
            h2_here = [local.fetch(h2_near_any, h2_near), local.fetch(h2_far_any, h2_far)]
            act_here = local.fetch(act_any, act)
            w2_here = local.fetch(w2_any, w2)
            w2_far_here = local.fetch(w2_far_any, w2_far)
            h1q_here = local.fetch(h1q_any, h1q)
            pad_here = local.fetch(pad_any, pad)
    beside[1].wait_recv()
    ga2[...] = part_of(y)
    unperm_here = local.fetch(unperm_any, order)

    def fold_sems(at):
        return [sems.at[at] for sems in (pair1_sends, pair1_recvs, pair2_sends, pair2_recvs)]

    halves = (y, 1 - y)

    def mid_norm(near):
        half = halves[near]
        gains = jnp.concatenate([smalls[2 * half], smalls[2 * half + 1]], axis=1)
        mean2, rstd2 = stats2[half, 0:1], stats2[half, 1:2]
        return mean2, rstd2, gains[2:3], gains[3:4]

    def half_cols(ref, near):
        low, high = ref[:, :half_width], ref[:, half_width:]
        return jnp.where(halves[near] == 0, low, high)

    for copy in h2_here:
        copy.wait()
    for near, h2 in enumerate((h2_near, h2_far)):
        mean2, rstd2, gain2, shift2 = mid_norm(near)
        normed = (h2[1 - y].astype(F32) - mean2) * rstd2
        grad = out_part[halves[near]].astype(F32) * silu_slope(normed * gain2 + shift2)
        st[halves[near], 0:1] = jnp.sum(grad, axis=0, keepdims=True)
        st[halves[near], 1:2] = jnp.sum(grad * normed, axis=0, keepdims=True)
        normed = (h2[y].astype(F32) - mean2) * rstd2
        kept = silu_slope(normed * gain2 + shift2)
        ga1[:, near * half_width : (near + 1) * half_width] = kept
        grad = half_cols(ga2, near) * kept
        st[halves[near], 0:1] += jnp.sum(grad, axis=0, keepdims=True)
        st[halves[near], 1:2] += jnp.sum(grad * normed, axis=0, keepdims=True)
    share_start(st, view_slots.at[0], group_sends.at[3], group_recvs.at[3], group)

    hid_block, hid_split = hl_parts.shape[1], head_last_out.shape[0]
    for half in range(2):
        product = exact(act4[half], grad_embed[...], 0, 0)
        wsum[0, : product.shape[0]] = product
        per_half = views // 2

        def spread_hidden(to, carry, half=half, per_half=per_half):
            spot = (4 * to + chan_at) * hid_block if hid_split == 4 else to * hid_block
            rows = pl.ds(pl.multiple_of(spot, hid_block), hid_block)
            hl_parts[half * per_half + to] = wsum[0, rows]
            return carry

        lax.fori_loop(0, per_half, spread_hidden, 0)
        wide = grad_p1.shape[2] // per_half
        for to in range(per_half):
            p1_parts[half * per_half + to] = grad_p1[half, :, to * wide : (to + 1) * wide]
    act_here.wait()
    share_rows = last_parts.shape[1]
    means[0:1] = rows_sum[...]
    few_rows = quarter // SIDE
    for half in range(2):
        cols = slice(half * half_width, (half + 1) * half_width)
        sampled = [jnp.sum(act[half, q, :few_rows].astype(F32), axis=0, keepdims=True) for q in range(4)]
        means[1:2, cols] = sum(sampled) / (4 * few_rows)
    for half in range(2):
        cols = slice(half * half_width, (half + 1) * half_width)
        total = None
        for q in range(4):
            term = dot_tn(gh3[q], act[half, q])
            total = term if total is None else total + term
        wsum[0, :width] = total[:, : half_width // 2]
        wsum[1, :width] = total[:, half_width // 2 :]
        low = (
            jnp.concatenate([wsum[0, :width], wsum[1, :width]], axis=1)
            - outer_product(means[0:1], means[1:2, cols])
        ).astype(last_parts.dtype)
        for to in range(views):
            last_parts[to, :, half * half_width : (half + 1) * half_width] = low[
                to * share_rows : (to + 1) * share_rows
            ]
    share_end(st, view_slots.at[0], group_sends.at[3], group_recvs.at[3], group)
    sum_parts[0] = add_slots(view_slots.at[0], views)
    sums_beside = mail.send(sum_parts.at[0], sum_parts.at[1], mate)
    scatter_start(hl_parts, hl_slots, group_sends.at[0], group_recvs.at[0], group)
    scatter_start(p1_parts, p1_slots, group_sends.at[1], group_recvs.at[1], group)
    share_start(means, mean_slots, group_sends.at[2], group_recvs.at[2], group)
    fold_last = Fold(last_parts, last_in, last_slots, fold_sems(0), views)
    fold_last.start()
    sums_beside.wait_recv()
    sum_parts[2] = sum_parts[0] + sum_parts[1]
    sums_across = mail.send(sum_parts.at[2], sum_parts.at[3], opposite)
    for copy in beside:
        copy.wait_send()
    x = gh3
    x_here = local.fetch(x_any, x)

    def share_value(source, slots, send, recv, who):
        source[...] = share(source, slots, send, recv, who)
        return source

    gpad[...] = jnp.zeros(gpad.shape, gpad.dtype)
    for half in range(2):
        across[half].wait()
        cols = slice(half * half_width, (half + 1) * half_width)
        ga2[:, cols] += in_part[half].astype(F32)
    gh2 = out_part
    sums_across.wait_recv()
    sum_parts[4] = sum_parts[2] + sum_parts[3]
    for near, h2 in enumerate((h2_near, h2_far)):
        mean2, rstd2, gain2, shift2 = mid_norm(near)
        tot = sum_parts[4, halves[near]]
        normed = (h2[y].astype(F32) - mean2) * rstd2
        grad = half_cols(ga2, near) * ga1[:, near * half_width : (near + 1) * half_width]
        low = (gain2 * rstd2 * (grad - tot[0:1] / count - normed * (tot[1:2] / count))).astype(BF16)
        gh2[near] = low
        gpad[near, 1 : SIDE + 1, 1 : SIDE + 1] = low.reshape(SIDE, SIDE, block, half_width)
    tot = sum_parts[4, y]
    own_cols = jnp.where(c == 0, tot[:, : half_width // 2], tot[:, half_width // 2 :])
    grad_shift_mid[...] = own_cols[0:1]
    grad_gain_mid[...] = own_cols[1:2]
    cut = quarter // 32 * 16
    far_pieces = [pl.ds(0, cut), pl.ds(cut, quarter - cut)]
    far_copies = [mail.send(gh2.at[1, far_pieces[0]], gh2_far.at[far_pieces[0]], opposite)]
    fold_last.pass_on(1, fold_last.size + 1)
    w2_here.wait()
    w2_far_here.wait()
    channels = w2.shape[1] // 9
    for tap in range(9):
        a, b = 2 - tap // 3, 2 - tap % 3
        taps = slice(tap * channels, (tap + 1) * channels)
        term = None
        for near, weight in enumerate((w2, w2_far)):
            window = gpad[near, a : a + SIDE, b : b + SIDE].reshape(quarter, half_width)
            both = jnp.concatenate([weight[0, taps], weight[1, taps]], axis=1)
            piece = dot_nt(window, both)
            term = piece if term is None else term + piece
        if tap == 0:
            ga1[...] = term
        else:
            ga1[...] += term
    h1q_here.wait()
    for half in range(2):
        gains = jnp.concatenate([smalls[2 * half], smalls[2 * half + 1]], axis=1)
        normed = (h1q[half] - stat1[half, 0:1]) * stat1[half, 1:2]
        cols = slice(half * half_width, (half + 1) * half_width)
        grad = ga1[:, cols] * silu_slope(normed * gains[0:1] + gains[1:2])
        ga2[:, cols] = grad
        st[half, 0:1] = jnp.sum(grad, axis=0, keepdims=True)
        st[half, 1:2] = jnp.sum(grad * normed, axis=0, keepdims=True)
    share_value(st, chan_slots.at[1], chan_sends.at[1], chan_recvs.at[1], chans)
    far_copies.append(mail.send(gh2.at[1, far_pieces[1]], gh2_far.at[far_pieces[1]], opposite))
    share_start(st, view_slots.at[1], group_sends.at[4], group_recvs.at[4], group)

    pad_here.wait()

    def tap_term(at, tap, grads):
        a, b = tap // 3, tap % 3
        window = pad[at, a : a + SIDE, b : b + SIDE].reshape(quarter, channels)
        return dot_tn(window, grads)

    for tap in range(9):
        total = tap_term(y, tap, gh2[0])
        taps = slice(tap * channels, (tap + 1) * channels)
        wsum[0, taps] = total[:, : half_width // 2]
        wsum[1, taps] = total[:, half_width // 2 :]
    share_end(st, view_slots.at[1], group_sends.at[4], group_recvs.at[4], group)
    totals1 = add_slots(view_slots.at[1], views)
    view_slots[1, 0] = totals1
    tot = view_slots[1, 0, y]
    own_cols = jnp.where(c == 0, tot[:, : half_width // 2], tot[:, half_width // 2 :])
    grad_shift_first[...] = own_cols[0:1]
    grad_gain_first[...] = own_cols[1:2]
    unperm_here.wait()
    gh1_across, gh1_beside = [], []
    for half in range(2):
        gains = jnp.concatenate([smalls[2 * half], smalls[2 * half + 1]], axis=1)
        normed = (h1q[half] - stat1[half, 0:1]) * stat1[half, 1:2]
        cols = slice(half * half_width, (half + 1) * half_width)
        tot = totals1[half]
        low = (
            gains[0:1]
            * stat1[half, 1:2]
            * (ga2[:, cols] - tot[0:1] / count - normed * (tot[1:2] / count))
        ).astype(BF16)
        gh1[half, chan_at] = dot(order[...], low).astype(BF16)
        spot = gh1.at[half, chan_at]
        gh1_across.append(mail.send(spot, spot, opposite))
        gh1_beside.append(mail.send(spot, spot, mate))

    for copy in far_copies:
        copy.wait_recv()
    for tap in range(9):
        total = tap_term(1 - y, tap, gh2_far[...])
        taps = slice(tap * channels, (tap + 1) * channels)
        wsum[0, taps] += total[:, : half_width // 2]
        wsum[1, taps] += total[:, half_width // 2 :]
    mid_rows = mid_parts.shape[1]
    mid_flat = mid_parts.reshape(views * mid_rows, mid_parts.shape[2])
    if mid_parts.dtype == F32:
        mid_mate = mail.send(wsum.at[1 - c], mid_flat, mate)
    else:
        wsend[...] = wsum[1 - c].astype(wsend.dtype)
        mid_mate = mail.send(wsend, mid_flat, mate)
    mid_mate.wait_recv()

    def mid_block(to, carry):
        rows = pl.ds(pl.multiple_of(to * mid_rows, mid_rows), mid_rows)
        mid_parts[to] = (wsum[c, rows] + mid_parts[to].astype(F32)).astype(mid_parts.dtype)
        return carry

    lax.fori_loop(0, views, mid_block, 0)
    fold_mid = Fold(mid_parts, mid_in, mid_slots, fold_sems(1), views, False)
    fold_mid.start()
    scatter_end(p1_parts, p1_slots, group_sends.at[1], group_recvs.at[1], group)
    few = pooled.shape[0]

    def head_first_term(at, total):
        views_at = pl.ds(at * few, few)
        copy = pltpu.make_async_copy(pooled_any.at[views_at], pooled, local_sems.at[29])
        copy.start()
        copy.wait()
        rows = pooled[...].astype(F32).reshape(-1, width)
        return total + exact(rows, p1_slots[views_at].reshape(rows.shape[0], -1), 0, 0)

    head_first_out[...] = over(
        views // few, head_first_term, exact(pooled_means[...], jnp.sum(p1_slots[...], axis=1), 0, 0)
    )
    share_end(means, mean_slots, group_sends.at[2], group_recvs.at[2], group)
    fold_last.end()
    rest, folds = [], []
    cuts = [1 + fold_mid.size * k // 4 for k in range(4)] + [fold_mid.size + 1]
    x_here.wait()
    for half in range(2):
        gh1_across[half].wait_recv()
        far_spot = gh1.at[half, 2 * (1 - y) + c]
        gh1_on = mail.send(far_spot, far_spot, mate)
        fold_mid.pass_on(cuts[2 * half], cuts[2 * half + 1])
        gh1_beside[half].wait_recv()
        gh1_on.wait_recv()
        rest.append(local.fetch(gh1.at[half], gh1_out.at[half]))
        total = None
        for q in range(4):
            term = dot_tn(x[q], gh1[half, q])
            total = term if total is None else total + term
        low = total.astype(first_parts.dtype)
        for to in range(views):
            first_parts[half, to] = low[to * share_rows : (to + 1) * share_rows]
        folds.append(Fold(first_parts.at[half], first_in.at[half], first_slots.at[half], fold_sems(2 + half), views))
        folds[half].start()
        fold_mid.pass_on(cuts[2 * half + 1], cuts[2 * half + 2])
    rest.append(local.fetch(mid_parts.at[view_at], mid_slots.at[fold_mid.outer]))

    scatter_end(hl_parts, hl_slots, group_sends.at[0], group_recvs.at[0], group)
    if hid_split == 4:
        head_last_out[chan_at] = add_slots(hl_slots, views)
        gather_start(head_last_out.at[chan_at], head_last_out, chan_sends.at[2], chan_recvs.at[2], chans)
    else:
        head_last_out[0] = add_slots(hl_slots, views)

    def blocks(kind, summed):
        wide = summed.shape[1] // 4
        for to in range(4):
            pair_parts[to, kind] = summed[:, to * wide : (to + 1) * wide]

    def summed_slots(slots):
        def add(at, total):
            return total + slots[at].astype(F32)

        return lax.fori_loop(1, slots.shape[0], add, slots[0].astype(F32))

    everywhere = short_product(mean_slots[:, 0], mean_slots[:, 1])
    ga1[: everywhere.shape[0]] = everywhere
    own_block = pl.ds(pl.multiple_of(view_at * share_rows, share_rows), share_rows)
    blocks(1, summed_slots(last_slots) + ga1[own_block])
    for fold in folds:
        fold.pass_on(1, fold.size + 1)
    for fold in folds:
        fold.end()
    blocks(0, jnp.concatenate([summed_slots(first_slots.at[half]) for half in range(2)], axis=1))
    row_views = views // 4
    to_view = chan_at * row_views + lax.div(view_at, 4)
    slot = lax.rem(view_at, 4)

    def pair_copy(to):
        return pltpu.make_async_remote_copy(
            src_ref=pair_parts.at[to],
            dst_ref=pair_out.at[slot],
            send_sem=pair_sends.at[to],
            recv_sem=pair_recvs.at[slot],
            device_id=(to_view, to),
            device_id_type=MESH,
        )

    def pair_arrival(origin):
        return pltpu.make_async_remote_copy(
            src_ref=pair_parts.at[0],
            dst_ref=pair_out.at[origin],
            send_sem=pair_sends.at[0],
            recv_sem=pair_recvs.at[origin],
            device_id=(from_view + origin, from_chan),
            device_id_type=MESH,
        )

    from_view, from_chan = 4 * lax.rem(view_at, row_views), lax.div(view_at, row_views)
    for to in range(4):
        own = jnp.logical_and(to_view == view_at, chan_at == to)

        @pl.when(own)
        def _():
            pair_out[slot] = pair_parts[to]

        @pl.when(jnp.logical_not(own))
        def _():
            pair_copy(to).start()

    for origin in range(4):
        own = jnp.logical_and(from_view + origin == view_at, chan_at == from_chan)

        @pl.when(jnp.logical_not(own))
        def _():
            pair_arrival(origin).wait_recv()

    for to in range(4):
        own = jnp.logical_and(to_view == view_at, chan_at == to)

        @pl.when(jnp.logical_not(own))
        def _():
            pair_copy(to).wait_send()

    if hid_split == 4:
        share_end(head_last_out.at[chan_at], head_last_out, chan_sends.at[2], chan_recvs.at[2], chans)
    fold_mid.end()
    for copy in rest:
        copy.wait()
    for copy in mail.copies[4:]:
        copy.wait_send()


def back_stage(views, front_outs, x, gain_last, perm, unperm, expand):
    (pad, h1q, w2, w2_far, w3, act, h3, slope, pooled_all, h2_near, h2_far, stat1, _, smalls, stat3,
     grad_shift_last, grad_gain_last, _, _, grad_pooled, act4, grad_embed, grad_p1, _,
     stats2, pooled_means, rows_sum) = front_outs
    quarter, width = h3.shape[1], h3.shape[2]
    block = quarter // PIX
    own = 4 * block
    mid = pad.shape[4]
    half = mid // 2
    hid, emb = 2 * act4.shape[2], grad_embed.shape[1]
    taps = w2.shape[1]
    hid_split = 4 if hid // views % 32 == 0 else 1
    hid_block = hid // views // hid_split
    mid_kind, row_kind = link_kind(taps // views), link_kind(width // views)
    vm = pltpu.VMEM
    return call(
        functools.partial(back_body, views),
        "back",
        (
            shape(2, 4, quarter, half, kind=BF16),
            shape(views // 2, taps // views, half // 2, kind=mid_kind),
            shape(4, 2, width // views, mid // 4),
            shape(hid_split, hid_block, emb),
            shape(width, hid // views),
            *[shape(1, half // 2)] * 4,
        ),
        28,
        [
            vm((4, quarter, width), BF16),
            vm((4, quarter, width), BF16),
            vm(w3.shape, BF16),
            vm(h2_near.shape, BF16),
            vm(h2_near.shape, BF16),
            vm((2, 4, quarter, half), BF16),
            vm((4, quarter, width), BF16),
            vm((2, quarter, width), BF16),
            vm((2, quarter, half), BF16),
            vm((2, quarter, half), BF16),
            vm((quarter, mid), F32),
            vm((quarter, half), BF16),
            vm((2, PAD, PAD, block, half), BF16),
            vm((quarter, mid), F32),
            vm((2, 2, half), F32),
            vm((5, 2, 2, half), F32),
            vm((2, 4, 2, 2, half), F32),
            vm((2, views, 2, 2, half), F32),
            vm(unperm.shape, BF16),
            vm(pad.shape, BF16),
            vm(h1q.shape, F32),
            vm(w2.shape, BF16),
            vm(w2.shape, BF16),
            vm(act.shape, BF16),
            vm((min(views, 8), own, width), BF16),
            vm((2, taps, half // 2), F32),
            vm((taps if mid_kind == BF16 else 16, half // 2), BF16),
            vm((views, taps // views, half // 2), mid_kind),
            vm((views // 2, taps // views, half // 2), mid_kind),
            vm((views, width // views, mid), row_kind),
            vm((views // 2, width // views, mid), row_kind),
            vm((views // 2, width // views, mid), row_kind),
            vm((2, views, width // views, half), row_kind),
            vm((2, views // 2, width // views, half), row_kind),
            vm((2, views // 2, width // views, half), row_kind),
            vm((2, width), F32),
            vm((views, 2, width), F32),
            vm((4, 2, width // views, mid // 4), F32),
            vm((views, hid_block, emb), F32),
            vm((views, hid_block, emb), F32),
            vm((views, own, hid // views), F32),
            vm((views, own, hid // views), F32),
            dma(20),
            dma(20),
            dma(3, 4),
            dma(3, 4),
            dma(7, views),
            dma(7, views),
            dma(4),
            dma(4),
            *[dma(4, views // 2)] * 4,
            dma(30),
        ],
        collective=4,
        any_ins=range(14, 28),
        any_outs=range(2),
    )(
        stat3, grad_shift_last, grad_gain_last, grad_pooled, gain_last, expand,
        stats2, smalls, stat1, act4, grad_embed, grad_p1, pooled_means, rows_sum,
        h3, slope, w3, h2_near, h2_far, perm, unperm, pad, h1q, w2, w2_far, act,
        x.reshape(4, quarter, width), pooled_all,
    )


def last_body(
    small_count, w1_any, grad_pooled, expand, gh1_any, slope_any, mid_any, pair_out, head_last_in, head_first_in, *more
):
    small_ins, outs = more[:small_count], more[small_count : 2 * small_count + 6]
    gh1, w1_own, slope, term, mid_slots, sems = more[2 * small_count + 6 :]
    grad_input, grad_mid, grad_first, grad_last, grad_head_last, grad_head_first, *small_outs = outs
    local = Local(sems)
    quarters, quarter, half = gh1.shape[1], gh1.shape[2], gh1.shape[3]
    w1_here = local.fetch(w1_any, w1_own)
    rows_here = [
        (local.fetch(gh1_any.at[:, q], gh1.at[:, q]), local.fetch(slope_any.at[q], slope.at[q]))
        for q in range(quarters)
    ]
    mid_here = local.fetch(mid_any, mid_slots)
    rest = []
    w1_here.wait()
    block = quarter // PIX
    for q in range(quarters):
        for copy in rows_here[q]:
            copy.wait()
        high, low = split_pair(grad_pooled[q * block : (q + 1) * block])
        spread = dot(expand[...], jnp.concatenate([high, low], axis=0))
        value = dot_nt(gh1[0, q], w1_own[:, :half]) + dot_nt(gh1[1, q], w1_own[:, half:])
        term[q] = value + spread * slope[q].astype(F32)
        rest.append(local.fetch(term.at[q], grad_input.at[q]))
    mid_here.wait()

    def add(slot, total):
        return total + mid_slots[slot].astype(F32)

    grad_mid[...] = lax.fori_loop(1, mid_slots.shape[0], add, mid_slots[0].astype(F32))
    grad_head_first[...] = head_first_in[...]
    for source, target in zip(small_ins, small_outs):
        target[...] = source[...]
    rows = pair_out.shape[2]
    for origin in range(4):
        grad_first[origin * rows : (origin + 1) * rows] = pair_out[origin, 0]
        grad_last[origin * rows : (origin + 1) * rows] = pair_out[origin, 1]
    rows = head_last_in.shape[1]
    for origin in range(head_last_in.shape[0]):
        grad_head_last[origin * rows : (origin + 1) * rows] = head_last_in[origin]
    for copy in rest:
        copy.wait()


def last_stage(
    gh1, w1_own, slope, grad_pooled, expand, mid_slots, pair_out, head_last_in, head_first_in, small
):
    quarter, half, width = gh1.shape[2], gh1.shape[3], slope.shape[2]
    outs = (
        shape(4, quarter, width),
        shape(*mid_slots.shape[1:]),
        shape(4 * pair_out.shape[2], pair_out.shape[3]),
        shape(4 * pair_out.shape[2], pair_out.shape[3]),
        shape(head_last_in.shape[0] * head_last_in.shape[1], head_last_in.shape[2]),
        shape(*head_first_in.shape),
        *[shape(*array.shape) for array in small],
    )
    ins = 9 + len(small)
    return call(
        functools.partial(last_body, len(small)),
        "results",
        outs,
        ins,
        [
            pltpu.VMEM(gh1.shape, BF16),
            pltpu.VMEM(w1_own.shape, BF16),
            pltpu.VMEM(slope.shape, BF16),
            pltpu.VMEM(slope.shape, F32),
            pltpu.VMEM(mid_slots.shape, mid_slots.dtype),
            dma(20),
        ],
        collective=None,
        any_ins=(0, 3, 4, 5),
        any_outs=(0,),
    )(w1_own, grad_pooled, expand, gh1, slope, mid_slots, pair_out, head_last_in, head_first_in, *small)


def per_device(
    views,
    block_input,
    conv_first,
    conv_mid,
    conv_last,
    gain_first,
    shift_first,
    gain_mid,
    shift_mid,
    gain_last,
    shift_last,
    head_first,
    gain_head,
    shift_head,
    head_last,
    image_of,
    partner,
    sub_of,
):
    rows, width = block_input.shape
    quarter = rows // 4
    block = quarter // PIX
    perm, unperm = orders(quarter)
    at_row = np.arange(quarter)
    twice = np.arange(2 * block) % block
    expand = jnp.asarray((at_row[:, None] // PIX == twice[None, :]).astype(BF16))

    def line(vector):
        return vector.reshape(1, -1)

    front_outs = front_stage(
        views, block_input, (conv_first, conv_mid, conv_last, head_first, head_last),
        [line(v) for v in (gain_first, shift_first, gain_mid, shift_mid, gain_last, shift_last, gain_head, shift_head)],
        [line(v) for v in (sub_of, image_of, partner)], perm, unperm,
    )
    slope, w1_own, grad_pooled, loss = (front_outs[at] for at in (7, 12, 19, 23))
    (gh1, mid_slots, pair_out, head_last_in, head_first_in,
     grad_shift_mid, grad_gain_mid, grad_shift_first, grad_gain_first) = back_stage(
        views, front_outs, block_input, line(gain_last), perm, unperm, expand
    )
    small = [
        grad_gain_first, grad_shift_first, grad_gain_mid, grad_shift_mid,
        front_outs[16], front_outs[15], front_outs[18], front_outs[17], loss,
    ]
    grad_input, grad_mid, grad_first, grad_last, grad_head_last, grad_head_first, *small = last_stage(
        gh1, w1_own, slope, grad_pooled, expand, mid_slots, pair_out, head_last_in, head_first_in, small
    )
    return (
        small[8].reshape(()),
        grad_input.reshape(rows, width),
        grad_first,
        grad_mid,
        grad_last,
        grad_head_first,
        grad_head_last,
        *[vector.reshape(-1) for vector in small[:8]],
    )


def solution(mesh):
    views = mesh.shape["views"]
    return jax.shard_map(
        functools.partial(per_device, views),
        mesh=mesh,
        in_specs=(
            P("views", "chan"),
            P(None, "chan"),
            P(None, "chan"),
            P(None, "chan"),
            P("chan"),
            P("chan"),
            P("chan"),
            P("chan"),
            P("chan"),
            P("chan"),
            P("chan", None),
            P(),
            P(),
            P(),
            P(),
            P(),
            P(),
        ),
        out_specs=(
            P(),
            P("views", "chan"),
            P("views", "chan"),
            P("views", "chan"),
            P("views", "chan"),
            P("chan", "views"),
            P("views", None),
            P("chan"),
            P("chan"),
            P("chan"),
            P("chan"),
            P("chan"),
            P("chan"),
            P(),
            P(),
        ),
        check_vma=False,
    )
```

```python
import functools
import inspect

import jax
import jax.numpy as jnp
import numpy as np
from jax import lax
from jax.experimental import pallas as pl
from jax.experimental.pallas import tpu as pltpu
from jax.sharding import PartitionSpec as P

SIDE = 7
PIX = SIDE * SIDE
PAD = SIDE + 2
SUB = 256
EPS = 1e-05
RIDGE = 0.5
MESH = pl.DeviceIdType.MESH
BF16 = jnp.bfloat16
F32 = jnp.float32
VMEM_BYTES = 60 << 20
JOINED_VIEWS = 8


def place():
    view_at, chan_at = lax.axis_index("views"), lax.axis_index("chan")
    return view_at, chan_at, lax.div(chan_at, 2), lax.rem(chan_at, 2)


def greet(peers, groups=()):
    barrier = pltpu.get_barrier_semaphore()
    total = len(peers)
    for peer in peers:
        pl.semaphore_signal(barrier, inc=1, device_id=peer, device_id_type=MESH)
    for size, own, device in groups:

        def tell(step, carry, size=size, own=own, device=device):
            pl.semaphore_signal(
                barrier, inc=1, device_id=device(lax.rem(own + step, size)), device_id_type=MESH
            )
            return carry

        lax.fori_loop(1, size, tell, 0)
        total += size - 1
    return lambda: pl.semaphore_wait(barrier, total)


class Mail:
    def __init__(self, send_sems, recv_sems):
        self.send_sems, self.recv_sems, self.copies = send_sems, recv_sems, []

    def send(self, source, target, peer):
        spot = len(self.copies)
        copy = pltpu.make_async_remote_copy(
            src_ref=source,
            dst_ref=target,
            send_sem=self.send_sems.at[spot],
            recv_sem=self.recv_sems.at[spot],
            device_id=peer,
            device_id_type=MESH,
        )
        copy.start()
        self.copies.append(copy)
        return copy

    def finish(self):
        for copy in self.copies:
            copy.wait_send()


class Done:
    def wait(self):
        pass


def part_of_ref(ref, *index):
    return None if ref is None else ref.at[index]


class Local:
    def __init__(self, sems):
        self.sems, self.used = sems, 0

    def fetch(self, source, target):
        if target is None or source is target:
            return Done()
        copy = pltpu.make_async_copy(source, target, self.sems.at[self.used])
        copy.start()
        self.used += 1
        return copy


def group_copy(source, slots, sends, recvs, size, own, device, step):
    to = lax.rem(own + step, size)
    return pltpu.make_async_remote_copy(
        src_ref=source,
        dst_ref=slots.at[own],
        send_sem=sends.at[step],
        recv_sem=recvs.at[own],
        device_id=device(to),
        device_id_type=MESH,
    )


def group_arrival(source, slots, sends, recvs, size, own, device, step):
    origin = lax.rem(own + step, size)
    return pltpu.make_async_remote_copy(
        src_ref=source,
        dst_ref=slots.at[origin],
        send_sem=sends.at[step],
        recv_sem=recvs.at[origin],
        device_id=device(origin),
        device_id_type=MESH,
    )


def share_start(source, slots, sends, recvs, group):
    def start(step, carry):
        group_copy(source, slots, sends, recvs, *group, step).start()
        return carry

    lax.fori_loop(1, group[0], start, 0)
    slots[group[1]] = source[...]


def share_end(source, slots, sends, recvs, group):
    def end(step, carry):
        group_arrival(source, slots, sends, recvs, *group, step).wait_recv()
        group_copy(source, slots, sends, recvs, *group, step).wait_send()
        return carry

    lax.fori_loop(1, group[0], end, 0)


def add_slots(slots, size):
    def add(at, total):
        return total + slots[at]

    return lax.fori_loop(1, size, add, slots[0])


def share(source, slots, sends, recvs, group):
    share_start(source, slots, sends, recvs, group)
    share_end(source, slots, sends, recvs, group)
    return add_slots(slots, group[0])


def gather_start(source, slots, sends, recvs, group):
    def start(step, carry):
        group_copy(source, slots, sends, recvs, *group, step).start()
        return carry

    lax.fori_loop(1, group[0], start, 0)


def scatter_start(parts, slots, sends, recvs, group, keep=True):
    size, own, device = group

    def start(step, carry):
        to = lax.rem(own + step, size)
        group_copy(parts.at[to], slots, sends, recvs, *group, step).start()
        return carry

    lax.fori_loop(1, size, start, 0)
    if keep:
        slots[own] = parts[own]


def scatter_end(parts, slots, sends, recvs, group):
    share_end(parts.at[group[1]], slots, sends, recvs, group)


class Fold:
    def __init__(self, parts, fold_in, slots, sems, views, keep=True):
        view_at, chan_at, _, _ = place()
        self.parts, self.fold_in, self.slots, self.sems, self.keep = parts, fold_in, slots, sems, keep
        self.size, self.outer, self.inner = views // 2, lax.div(view_at, 2), lax.rem(view_at, 2)
        self.pair = (2 * self.outer + 1 - self.inner, chan_at)
        self.chan_at = chan_at

    def block(self, step):
        return lax.rem(self.outer + step, self.size)

    def pair_copy(self, step):
        at = self.block(step)
        return pltpu.make_async_remote_copy(
            src_ref=self.parts.at[2 * at + 1 - self.inner],
            dst_ref=self.fold_in.at[at],
            send_sem=self.sems[0].at[at],
            recv_sem=self.sems[1].at[at],
            device_id=self.pair,
            device_id_type=MESH,
        )

    def out_copy(self, step, slot):
        at = self.block(step)
        return pltpu.make_async_remote_copy(
            src_ref=self.parts.at[2 * at + self.inner],
            dst_ref=self.slots.at[slot],
            send_sem=self.sems[2].at[at],
            recv_sem=self.sems[3].at[slot],
            device_id=(2 * at + self.inner, self.chan_at),
            device_id_type=MESH,
        )

    def start(self):
        def one(step, carry):
            self.pair_copy(step).start()
            return carry

        lax.fori_loop(1, self.size + 1, one, 0)

    def add(self, step):
        self.pair_copy(step).wait_recv()
        at, mine = self.block(step), 2 * self.block(step) + self.inner
        total = self.parts[mine].astype(F32) + self.fold_in[at].astype(F32)
        self.parts[mine] = total.astype(self.parts.dtype)

    def pass_on(self, first, last):
        def one(step, carry):
            self.add(step)
            self.out_copy(step, self.outer).start()
            return carry

        lax.fori_loop(first, min(last, self.size), one, 0)
        if last > self.size:
            self.add(self.size)
            if self.keep:
                self.slots[self.outer] = self.parts[2 * self.outer + self.inner]

    def end(self):
        def one(step, carry):
            self.out_copy(step, self.block(step)).wait_recv()
            self.out_copy(step, self.outer).wait_send()
            return carry

        lax.fori_loop(1, self.size, one, 0)

        def sent(step, carry):
            self.pair_copy(step).wait_send()
            return carry

        lax.fori_loop(1, self.size + 1, sent, 0)


def chan_group():
    view_at, chan_at, y, c = place()
    return (4, chan_at, lambda at: (view_at, at))


def half_group(views):
    view_at, chan_at, y, c = place()
    return (
        2 * views,
        2 * view_at + c,
        lambda at: (lax.div(at, 2), 2 * y + lax.rem(at, 2)),
    )


def view_group(views):
    view_at, chan_at, y, c = place()
    return (views, view_at, lambda at: (at, chan_at))


def all_group(views):
    view_at, chan_at, y, c = place()
    return (4 * views, 4 * view_at + chan_at, lambda at: (lax.div(at, 4), lax.rem(at, 4)))


def dot(left, right):
    return jnp.dot(left, right, preferred_element_type=F32)


def dot_nt(left, right):
    return lax.dot_general(left, right, (((1,), (1,)), ((), ())), preferred_element_type=F32)


def dot_tn(left, right):
    return lax.dot_general(left, right, (((0,), (0,)), ((), ())), preferred_element_type=F32)


def gate(level):
    return 0.5 + 0.5 * jnp.tanh(0.5 * level)


def silu_slope(level):
    open_part = gate(level)
    return open_part * (1.0 + level * (1.0 - open_part))


def call(body, name, outs, ins, scratch, collective, any_ins=(), any_outs=()):
    def spec(at, places):
        return pl.BlockSpec(memory_space=pl.ANY if at in places else pltpu.VMEM)

    return pl.pallas_call(
        body,
        out_shape=outs,
        in_specs=[spec(at, any_ins) for at in range(ins)],
        out_specs=tuple(spec(at, any_outs) for at in range(len(outs))),
        scratch_shapes=scratch,
        name=name,
        compiler_params=pltpu.CompilerParams(
            collective_id=collective,
            has_side_effects=collective is not None,
            vmem_limit_bytes=VMEM_BYTES,
        ),
    )


def shape(*dims, kind=F32):
    return jax.ShapeDtypeStruct(dims, kind)


def dma(*dims):
    return pltpu.SemaphoreType.DMA(dims)


def split_rows(value):
    high = value.astype(BF16)
    rest = value - high.astype(F32)
    middle = rest.astype(BF16)
    low = (rest - middle.astype(F32)).astype(BF16)
    return jnp.concatenate([high, middle, low], axis=0)


def join_rows(stacked):
    rows = stacked.shape[0] // 3
    return stacked[2 * rows :] + stacked[rows : 2 * rows] + stacked[:rows]


def split_pair(value):
    high = value.astype(BF16)
    return high, (value - high.astype(F32)).astype(BF16)


def exact(left, right, left_dim, right_dim):
    return lax.dot_general(
        left,
        right,
        (((left_dim,), (right_dim,)), ((), ())),
        precision=lax.Precision.HIGHEST,
        preferred_element_type=F32,
    )


def over(count, body, start):
    return body(0, start) if count == 1 else lax.fori_loop(0, count, body, start)


def split_three(value):
    high = value.astype(BF16)
    rest = value - high.astype(F32)
    middle = rest.astype(BF16)
    return high, middle, (rest - middle.astype(F32)).astype(BF16)


def short_product(left, right):
    lh, lm, ll = split_three(left)
    rh, rm, rl = split_three(right)
    return dot_tn(
        jnp.concatenate([lh, lh, lm, lh, lm, ll], axis=0),
        jnp.concatenate([rh, rm, rh, rl, rm, rh], axis=0),
    )


def outer_product(left, right):
    def rows(value, high_at, middle_at, low_at):
        parts = [part.astype(F32) for part in split_three(value)]
        row = lax.broadcasted_iota(jnp.int32, (16, value.shape[1]), 0)
        total = jnp.zeros((16, value.shape[1]), F32)
        for part, places in zip(parts, (high_at, middle_at, low_at)):
            for place_at in places:
                total = jnp.where(row == place_at, part, total)
        return total.astype(BF16)

    return dot_tn(rows(left, (0, 1, 3), (2, 4), (5,)), rows(right, (0, 2, 5), (1, 4), (3,)))


def factor_inverse(work, inverse, subs, width):
    panel = 16
    row = lax.broadcasted_iota(jnp.int32, (panel, width), 0)

    def wide(part):
        return jnp.broadcast_to(part, (panel, width))

    def eliminate(s, first):
        rows = work[s, first : first + panel]
        columns = [wide(rows[:, first + j : first + j + 1]) for j in range(panel)]
        diagonal = jnp.zeros((panel, width), F32)
        for j in range(panel):
            pivot = wide(columns[j][j : j + 1])
            diagonal = jnp.where(row == j, pivot, diagonal)
            if j == panel - 1:
                break
            ratio = jnp.where(row > j, columns[j] * (1.0 / pivot), 0.0)
            for k in range(j + 1, panel):
                columns[k] = columns[k] - ratio * wide(columns[k][j : j + 1])
            rows = rows - jnp.concatenate([ratio, ratio], axis=1) * rows[j : j + 1]
        inverse[s, first : first + panel] = rows[:, width:] * lax.rsqrt(diagonal)
        if first + panel < width:
            scaled = rows[:, :width] / diagonal
            work[s, first + panel :] -= short_product(scaled, rows)[first + panel :]

    def some(at, carry):
        for first in range(0, width, panel):
            for k in range(2):
                eliminate(2 * at + k, first)
        return carry

    over(subs // 2, some, 0)


def view_sums(value, block):
    return jnp.concatenate(
        [jnp.sum(value[PIX * v : PIX * (v + 1)], axis=0, keepdims=True) for v in range(block)], axis=0
    )


def columns_of(row, column):
    tile = column.shape[1]

    def one(at, carry):
        cols = pl.ds(pl.multiple_of(at * tile, tile), tile)
        column[cols] = jnp.broadcast_to(row[:, cols].astype(F32), (tile, tile)).T
        return carry

    lax.fori_loop(0, row.shape[1] // tile, one, 0)


def whiten(embed, sub_col, image_col, image_row, partner_col, partner_row, refs, own_rows):
    work, inverse, white, unit, unit_parts, back = refs
    total, width = embed.shape
    subs = inverse.shape[0]
    eye = (
        lax.broadcasted_iota(jnp.int32, (width, width), 0)
        == lax.broadcasted_iota(jnp.int32, (width, width), 1)
    ).astype(F32)
    size = min(total, 512)
    pieces = total // size

    def rows_at(at):
        return pl.ds(pl.multiple_of(at * size, size), size)

    means = []

    def masks(rows, s):
        column = sub_col[rows]
        return (column == float(s)).astype(F32), (column == float(s + 1)).astype(F32)

    for s in range(0, subs, 2):

        def moments(at, sums, s=s):
            rows = rows_at(at)
            value = embed[rows]
            picked = jnp.concatenate([value * mask for mask in masks(rows, s)], axis=1)
            first = sums[0] + jnp.sum(picked, axis=0, keepdims=True)
            return first, sums[1] + exact(picked, value, 0, 0)

        first, second = over(
            pieces, moments, (jnp.zeros((1, 2 * width), F32), jnp.zeros((2 * width, width), F32))
        )
        for k in range(2):
            mean = first[:, k * width : (k + 1) * width] / SUB
            cov = second[k * width : (k + 1) * width] / SUB - exact(mean, mean, 0, 0)
            work[s + k, :, :width] = cov + RIDGE * eye
            work[s + k, :, width:] = eye
            means.append(mean)
    factor_inverse(work, inverse, subs, width)

    def whitening(at, carry):
        rows = rows_at(at)
        value = None
        for s in range(0, subs, 2):
            centred = jnp.concatenate(
                [(embed[rows] - means[s + k]) * mask for k, mask in enumerate(masks(rows, s))], axis=1
            )
            term = exact(centred, jnp.concatenate([inverse[s], inverse[s + 1]], axis=1), 1, 1)
            value = term if value is None else value + term
        white[rows] = value
        value = value * lax.rsqrt(jnp.sum(value * value, axis=1, keepdims=True) + EPS)
        unit[rows] = value
        high = value.astype(BF16)
        rest = value - high.astype(F32)
        middle = rest.astype(BF16)
        unit_parts[rows] = jnp.concatenate(
            [high, middle, (rest - middle.astype(F32)).astype(BF16)], axis=1
        )
        return carry

    over(pieces, whitening, 0)
    chunk = min(total, 262144 // total)

    def pairs(at, loss):
        rows = pl.ds(pl.multiple_of(at * chunk, chunk), chunk)
        across = lax.broadcasted_iota(jnp.int32, (chunk, total), 1).astype(F32)
        down = lax.broadcasted_iota(jnp.int32, (chunk, total), 0) + at * chunk

        def pick(hot):
            found = dot(hot.astype(F32).astype(BF16), unit_parts[...])
            return found[:, 2 * width :] + found[:, width : 2 * width] + found[:, :width]

        mine = unit[rows]
        ahead = pick(partner_col[rows][:, :1] == across)
        behind = pick(partner_row[...] == down)
        members = jnp.sum(
            (image_col[rows][:, :1] == image_row[...].astype(F32)).astype(F32), axis=1, keepdims=True
        )
        weight = 1.0 / members
        apart = mine - ahead
        grad = (4.0 / total) * weight * (2.0 * mine - ahead - behind)
        length = lax.rsqrt(jnp.sum(white[rows] * white[rows], axis=1, keepdims=True) + EPS)
        back[rows] = length * (grad - mine * jnp.sum(mine * grad, axis=1, keepdims=True))
        per_view = jnp.sum(apart * apart, axis=1, keepdims=True) * weight
        return loss + jnp.sum(per_view, axis=0, keepdims=True)

    loss = over(total // chunk, pairs, jnp.zeros((1, 1), F32)) * (2.0 / total)
    lower = lax.broadcasted_iota(jnp.int32, (width, width), 0) >= lax.broadcasted_iota(
        jnp.int32, (width, width), 1
    )
    own_white, own_back = white[own_rows], back[own_rows]
    gradient = jnp.zeros(own_white.shape, F32)
    for s in range(0, subs, 2):

        def pulled(at, sums, s=s):
            rows = rows_at(at)
            picked = jnp.concatenate([back[rows] * mask for mask in masks(rows, s)], axis=1)
            spread = sums[0] + jnp.sum(picked, axis=0, keepdims=True)
            return spread, sums[1] + exact(picked, white[rows], 0, 0)

        spread, sums = over(
            pieces, pulled, (jnp.zeros((1, 2 * width), F32), jnp.zeros((2 * width, width), F32))
        )
        for k, own_mask in enumerate(masks(own_rows, s)):
            cols = slice(k * width, (k + 1) * width)
            low_part = jnp.where(lower, sums[cols], 0.0)
            mirrored = low_part + low_part.T - sums[cols] * eye
            moved = own_back - (exact(own_white, mirrored, 1, 0) + spread[:, cols]) / SUB
            gradient = gradient + own_mask * exact(moved, inverse[s + k], 1, 0)
    return loss, gradient


MIDDLE_TAPS = 3
EARLY_TAPS = 3


def orders(quarter):
    block = quarter // PIX
    row = np.arange(quarter)
    source = (row % block) * PIX + row // block
    hot = (source[:, None] == row[None, :]).astype(BF16)
    return jnp.asarray(hot), jnp.asarray(hot.T)


def front_body(
    views, g1, b1, g2, b2, gain_last, shift_last, gain_head, shift_head, sub_row, image_row, partner_row,
    x_any, w1in, w2in, w3in, perm_any, unperm_any, head_first_any, head_last_any,
    pad_out, h1_out, w2_out, w2_far, w3_out, act_out, h3_out, slope_out, pooled_all, h2_near, h2_far,
    stat, w1_own, smalls, stat3, grad_shift_last, grad_gain_last, grad_shift_head, grad_gain_head,
    grad_pooled_out, act4, grad_embed_out, grad_p1, loss_out, stats2, pooled_means, rows_sum,
    x, w1, act, h3, h1, st, slots, st2, slots2, perm, unperm, pad, w2, w3, hidden, h2, small,
    head_first, head_last, slope, pooled_own, pooled_low, sub_col, image_col, partner_col,
    embed_all, part, part_in, mean_sums, slope_sums, st3, slots3, st4, slots4, bk4, bslots4, bk3, bslots3, embed_own,
    work, inverse, white, unit, unit_parts, back,
    sends, recvs, part_sends, part_recvs, half_sends, half_recvs, group_sends, group_recvs, local_sems,
    everyone=False,
):
    view_at, chan_at, y, c = place()
    mate, opposite = (view_at, 2 * y + 1 - c), (view_at, 2 * (1 - y) + c)
    diagonal = (view_at, 2 * (1 - y) + 1 - c)
    half_peers, group = half_group(views), view_group(views)
    quarter, depth = x.shape[1], x.shape[2]
    width = h3.shape[2]
    block = quarter // PIX
    views_own = 4 * block
    parts = act.reshape(2, 2, 2, quarter, act.shape[3])
    out_part, in_part = parts.at[0], parts.at[1]
    xm = h3.at[pl.ds(0, 2)]
    near, far = 2 * y + c, 2 * (1 - y) + c
    near_rows = pl.ds(pl.multiple_of(2 * depth * y, 2 * depth), 2 * depth)
    far_rows = pl.ds(pl.multiple_of(2 * depth * (1 - y), 2 * depth), 2 * depth)
    met = greet([], [all_group(views)]) if everyone else greet([opposite, diagonal], [half_peers])
    local = Local(local_sems)
    w1_here = local.fetch(w1in.at[near_rows], w1.at[near])
    perm_here = local.fetch(perm_any, perm)
    x_own = [local.fetch(x_any.at[2 * q + c], x.at[2 * q + c]) for q in range(2)]
    w2_here = local.fetch(w2in, w2.at[c])
    unperm_here = local.fetch(unperm_any, unperm)
    rest = [local.fetch(w3in.at[near_rows], w3.at[near])]
    for at, vector in enumerate((g1, b1, g2, b2)):
        small[at : at + 1] = vector[...]
        small[4 + at : 5 + at] = vector[...]
    smalls[chan_at] = small[...]
    pad[...] = jnp.zeros(pad.shape, pad.dtype)
    met()
    mail = Mail(sends, recvs)
    w1_mate = mail.send(w1in.at[near_rows], w1.at[near], mate)
    x_mate = [mail.send(x_any.at[1 - c], xm.at[0], mate)]
    w1_far = mail.send(w1in.at[far_rows], w1.at[near], opposite)
    x_mate.append(mail.send(x_any.at[3 - c], xm.at[1], mate))
    small_copies = [mail.send(small, smalls.at[chan_at], to) for to in (mate, opposite, diagonal)]
    w2_mate = mail.send(w2in, w2.at[c], mate)
    w3_mate = mail.send(w3in.at[near_rows], w3.at[near], mate)

    def part_copy(half, q):
        return pltpu.make_async_remote_copy(
            src_ref=out_part.at[half, q],
            dst_ref=in_part.at[half, q],
            send_sem=part_sends.at[half, q],
            recv_sem=part_recvs.at[half, q],
            device_id=opposite,
            device_id_type=MESH,
        )

    own_in, mate_in = (
        pl.ds(pl.multiple_of(depth * k, depth), depth) for k in (c, 1 - c)
    )

    def send_part(half, q):
        def weight(rows):
            return jnp.concatenate([w1[2 * half, rows], w1[2 * half + 1, rows]], axis=1)

        value = dot(x[2 * q + c], weight(own_in)) + dot(xm[q], weight(mate_in))
        out_part[half, q] = dot(perm[...], value.astype(BF16)).astype(BF16)
        part_copy(half, q).start()

    w1_here.wait()
    w1_mate.wait_recv()
    perm_here.wait()
    for q in range(2):
        x_own[q].wait()
        x_mate[q].wait_recv()
        send_part(y, q)
    w1_far.wait_recv()
    w1_on = mail.send(w1.at[far], w1.at[far], mate)
    w1_on.wait_recv()
    for q in range(2):
        send_part(1 - y, q)
    x_rest = [local.fetch(x_any.at[2 * q + 1 - c], x.at[2 * q + 1 - c]) for q in range(2)]
    w2_here.wait()
    w2_mate.wait_recv()
    rest.append(local.fetch(w2, w2_out))
    own_rows = pl.ds(pl.multiple_of(depth * c, depth), depth)
    w1_own[...] = jnp.concatenate([w1[k, own_rows] for k in range(4)], axis=1)
    st[...] = jnp.zeros(st.shape, st.dtype)
    step_rows = quarter // SIDE

    def sums(half):
        def one(q, carry):
            part_copy(half, q).wait_recv()

            def rows_of(at, inner):
                rows = pl.ds(at * step_rows, step_rows)
                value = out_part[half, q, rows].astype(F32) + in_part[half, q, rows].astype(F32)
                h1[half, q, rows] = value
                st[half, 0:1] += jnp.sum(value, axis=0, keepdims=True)
                st[half, 1:2] += jnp.sum(value * value, axis=0, keepdims=True)
                return inner

            return lax.fori_loop(0, SIDE, rows_of, carry)

        lax.fori_loop(0, 2, one, 0)

    sums(1 - y)
    sums(y)
    for half in range(2):
        for q in range(2):
            part_copy(half, q).wait_send()
    share_start(st, slots, half_sends.at[0], half_recvs.at[0], half_peers)
    w3_far = mail.send(w3in.at[far_rows], w3.at[near], opposite)
    channels = pad.shape[4]
    early_taps = []
    for tap in range(EARLY_TAPS):
        rows = pl.ds(tap * channels, channels)
        early_taps.append(mail.send(w2in.at[rows], w2_far.at[c, rows], opposite))
    share_end(st, slots, half_sends.at[0], half_recvs.at[0], half_peers)
    totals = add_slots(slots, half_peers[0])
    count = float(views * 4 * quarter)
    for copy in small_copies:
        copy.wait_recv()
    mean = totals[:, 0:1] / count
    rstd = lax.rsqrt(totals[:, 1:2] / count - mean * mean + EPS)
    stat[...] = jnp.concatenate([mean, rstd], axis=1)
    for half in range(2):
        gains = jnp.concatenate([smalls[2 * half], smalls[2 * half + 1]], axis=1)
        scale = rstd[half] * gains[0:1]
        bias = gains[1:2] - mean[half] * scale

        def act_rows(at, carry, half=half, scale=scale, bias=bias):
            q, i = lax.div(at, SIDE), lax.rem(at, SIDE)
            level = h1[half, q, pl.ds(i * step_rows, step_rows)] * scale + bias
            value = (level * gate(level)).astype(BF16)
            pad[q, i + 1, 1 : SIDE + 1, :, 256 * half : 256 * half + 256] = value.reshape(
                SIDE, step_rows // SIDE, 256
            )
            return carry

        lax.fori_loop(0, 2 * SIDE, act_rows, 0)
    rest.append(local.fetch(pad, pad_out))
    rest += [local.fetch(h1.at[half, y], part_of_ref(h1_out, half)) for half in range(2)]
    w3_far.wait_recv()
    w3_on = mail.send(w3.at[far], w3.at[far], mate)
    st2[...] = jnp.zeros(st2.shape, F32)

    def convolve(q, carry):
        for tap in range(9):
            a, b = tap // 3, tap % 3
            window = pad[q, a : a + SIDE, b : b + SIDE].reshape(quarter, channels)
            taps = slice(tap * channels, (tap + 1) * channels)
            term = dot(window, jnp.concatenate([w2[0, taps], w2[1, taps]], axis=1))
            if tap == 0:
                hidden[q] = term
            else:
                hidden[q] += term
        value = hidden[q]
        h2[q] = value.astype(BF16)
        st2[0:1] += jnp.sum(value, axis=0, keepdims=True)
        st2[1:2] += jnp.sum(value * value, axis=0, keepdims=True)
        return carry

    lax.fori_loop(0, 2, convolve, 0)
    share_start(st2, slots2, half_sends.at[1], half_recvs.at[1], half_peers)
    rest.append(local.fetch(h2, h2_near))
    w2_on = []

    def pass_on(taps):
        for tap in taps:
            early_taps[tap].wait_recv()
            rows = pl.ds(tap * channels, channels)
            w2_on.append(mail.send(w2_far.at[c, rows], w2_far.at[c, rows], mate))

    pass_on(range(EARLY_TAPS - 1))
    share_end(st2, slots2, half_sends.at[1], half_recvs.at[1], half_peers)
    totals2 = add_slots(slots2, half_peers[0])
    mean2 = totals2[0:1] / count
    rstd2 = lax.rsqrt(totals2[1:2] / count - mean2 * mean2 + EPS)
    stats2[y] = jnp.concatenate([mean2, rstd2], axis=0)
    gains = jnp.concatenate([smalls[2 * y], smalls[2 * y + 1]], axis=1)
    scale2 = rstd2 * gains[2:3]
    bias2 = gains[3:4] - mean2 * scale2
    across, beside = [], []
    unperm_here.wait()
    for q in range(2):
        level = hidden[q] * scale2 + bias2
        value = (level * gate(level)).astype(BF16)
        act[y, 2 * q + c] = dot(unperm[...], value).astype(BF16)
        spot = act.at[y, 2 * q + c]
        across.append(mail.send(spot, spot, opposite))
        beside.append(mail.send(spot, spot, mate))
    pass_on(range(EARLY_TAPS - 1, EARLY_TAPS))
    stat2_far = mail.send(stats2.at[y], stats2.at[y], opposite)

    own_out = pl.ds(pl.multiple_of(width * c, width), width)
    st3[...] = jnp.zeros(st3.shape, F32)
    head_first_here = local.fetch(head_first_any, head_first)
    head_last_here = local.fetch(head_last_any, head_last)
    for copy in (w3_mate, w3_on):
        copy.wait_recv()
    rest[0].wait()
    w3_kept = local.fetch(w3, w3_out)

    def last_conv(q):
        total = None
        for half in range(2):
            weight = jnp.concatenate([w3[2 * half, own_out], w3[2 * half + 1, own_out]], axis=1)
            term = dot_nt(act[half, q], weight)
            total = term if total is None else total + term
        low = total.astype(BF16)
        h3[q] = low
        value = low.astype(F32)
        st3[0:1] += jnp.sum(value, axis=0, keepdims=True)
        st3[1:2] += jnp.sum(value * value, axis=0, keepdims=True)

    for row, column in ((sub_row, sub_col), (image_row, image_col), (partner_row, partner_col)):
        columns_of(row, column)
    for q in range(2):
        across[q].wait_recv()
        spot = act.at[1 - y, 2 * q + c]
        passed = mail.send(spot, spot, mate)
        last_conv(2 * q + c)
        beside[q].wait_recv()
        passed.wait_recv()
        last_conv(2 * q + 1 - c)
    for copy in w2_on:
        copy.wait_recv()
    act_kept = local.fetch(act, act_out)
    middle_rows = pl.ds(EARLY_TAPS * channels, MIDDLE_TAPS * channels)
    w2_middle = mail.send(w2in.at[middle_rows], w2_far.at[c, middle_rows], opposite)
    share_start(st3, slots3, group_sends.at[0], group_recvs.at[0], group)
    rest.append(local.fetch(h3, h3_out))
    share_end(st3, slots3, group_sends.at[0], group_recvs.at[0], group)
    totals = add_slots(slots3, views)
    count = float(views * 4 * quarter)
    mean = totals[0:1] / count
    rstd = lax.rsqrt(totals[1:2] / count - mean * mean + EPS)
    stat3[...] = jnp.concatenate([mean, rstd], axis=0)
    scale = rstd * gain_last[...]
    bias = shift_last[...] - mean * scale
    for copy in x_rest:
        copy.wait()

    def pool_block(q, carry):
        before = x[q].astype(F32) + (h3[q].astype(F32) * scale + bias)
        sums = view_sums(before * gate(before), block)
        pooled_own[pl.ds(pl.multiple_of(q * block, block), block)] = sums * (1.0 / PIX)
        return carry

    lax.fori_loop(0, 4, pool_block, 0)
    head_first_here.wait()
    hidden = join_rows(dot(split_rows(pooled_own[...]), head_first[...]))
    wide = hidden.shape[1] // 2
    part[0] = hidden[:, :wide]
    part[1] = hidden[:, wide:]
    swap = mail.send(part, part_in.at[pl.ds(0, 2)], mate)

    def slope_block(q, carry):
        level3 = h3[q].astype(F32)
        before = x[q].astype(F32) + (level3 * scale + bias)
        low = silu_slope(before).astype(BF16)
        slope[q] = low
        normed = (level3 - mean) * rstd
        kept = low.astype(F32)
        rows = pl.ds(pl.multiple_of(q * block, block), block)
        slope_sums[0, rows] = view_sums(kept, block)
        slope_sums[1, rows] = view_sums(kept * normed, block)
        return carry

    swap.wait()
    mean_sums[...] = part[...] + part_in[0:2]
    across_p1 = mail.send(mean_sums.at[c], part_in.at[2], opposite)
    lax.fori_loop(0, 2, slope_block, 0)
    across_p1.wait_recv()
    part_in[4 + c] = mean_sums[c] + part_in[2]
    gathered = mail.send(part_in.at[4 + c], part_in.at[4 + c], mate)
    h2_over = mail.send(h2, h2_far, opposite)
    w2_middle.wait_recv()
    w2_middle_on = mail.send(w2_far.at[c, middle_rows], w2_far.at[c, middle_rows], mate)
    before_late = (EARLY_TAPS + MIDDLE_TAPS) * channels
    late_rows = pl.ds(before_late, w2in.shape[0] - before_late)
    w2_over = mail.send(w2in.at[late_rows], w2_far.at[c, late_rows], opposite)
    gathered.wait_recv()
    p1 = part_in[4:6]
    st4[0:2] = jnp.sum(p1, axis=1)
    st4[2:4] = jnp.sum(p1 * p1, axis=1)
    share_start(st4, slots4, group_sends.at[1], group_recvs.at[1], group)
    lax.fori_loop(2, 4, slope_block, 0)
    rest.append(local.fetch(slope, slope_out))
    share_end(st4, slots4, group_sends.at[1], group_recvs.at[1], group)
    totals4 = add_slots(slots4, views)
    count4 = float(views * views_own)
    mean4 = totals4[0:2] / count4
    rstd4 = lax.rsqrt(totals4[2:4] / count4 - mean4 * mean4 + EPS)
    head_last_here.wait()

    def level4(half):
        cols = slice(half * wide, (half + 1) * wide)
        normed = (part_in[4 + half] - mean4[half : half + 1]) * rstd4[half : half + 1]
        return normed, normed * gain_head[:, cols] + shift_head[:, cols]

    embed = None
    for half in range(2):
        normed, level = level4(half)
        value = level * gate(level)
        act4[half] = value
        term = join_rows(dot(split_rows(value), head_last[half * wide : (half + 1) * wide]))
        embed = term if embed is None else embed + term
    embed_own[...] = embed
    share_start(embed_own, embed_all, group_sends.at[2], group_recvs.at[2], group)
    share_end(embed_own, embed_all, group_sends.at[2], group_recvs.at[2], group)
    pooled_mean = jnp.sum(pooled_own[...], axis=0, keepdims=True) / views_own
    bk3[2:3] = pooled_mean
    pooled_low[...] = (pooled_own[...] - pooled_mean).astype(BF16)
    gather_start(pooled_low, pooled_all, group_sends.at[5], group_recvs.at[5], group)
    rest.append(local.fetch(pooled_low, pooled_all.at[view_at]))
    own_rows = pl.ds(pl.multiple_of(view_at * views_own, views_own), views_own)
    every = embed_all.reshape(views * views_own, embed.shape[1])
    loss, grad_embed = whiten(
        every, sub_col, image_col, image_row, partner_col, partner_row,
        (work, inverse, white, unit, unit_parts, back), own_rows,
    )
    loss_out[...] = loss
    grad_embed_out[...] = grad_embed
    stacked = split_rows(grad_embed)
    for half in range(2):
        normed, level = level4(half)
        grad = join_rows(dot_nt(stacked, head_last[half * wide : (half + 1) * wide]))
        grad = grad * silu_slope(level)
        part[half] = grad
        bk4[half : half + 1] = jnp.sum(grad, axis=0, keepdims=True)
        bk4[2 + half : 3 + half] = jnp.sum(grad * normed, axis=0, keepdims=True)
    tot4 = share(bk4, bslots4, group_sends.at[3], group_recvs.at[3], group)
    grad_pooled = None
    for half in range(2):
        cols = slice(half * wide, (half + 1) * wide)
        normed, level = level4(half)
        shift_sum, gain_sum = tot4[half : half + 1], tot4[2 + half : 3 + half]
        grad_shift_head[:, cols] = shift_sum
        grad_gain_head[:, cols] = gain_sum
        grad = (
            gain_head[:, cols]
            * rstd4[half : half + 1]
            * (part[half] - shift_sum / count4 - normed * (gain_sum / count4))
        )
        grad_p1[half] = grad
        term = join_rows(dot_nt(split_rows(grad), head_first[:, cols]))
        grad_pooled = term if grad_pooled is None else grad_pooled + term
    grad_pooled = grad_pooled * (1.0 / PIX)
    grad_pooled_out[...] = grad_pooled
    bk3[0:1] = jnp.sum(grad_pooled * slope_sums[0], axis=0, keepdims=True)
    bk3[1:2] = jnp.sum(grad_pooled * slope_sums[1], axis=0, keepdims=True)
    share_start(bk3, bslots3, group_sends.at[4], group_recvs.at[4], group)
    w2_over.wait_recv()
    w2_last = mail.send(w2_far.at[c, late_rows], w2_far.at[c, late_rows], mate)
    share_end(bk3, bslots3, group_sends.at[4], group_recvs.at[4], group)
    tot3 = add_slots(bslots3, views)
    grad_shift_last[...] = tot3[0:1]
    grad_gain_last[...] = tot3[1:2]
    own_count = float(4 * quarter)
    normed_sum = (st3[0:1] - own_count * mean) * rstd
    rows_sum[...] = scale * (
        bk3[0:1] - tot3[0:1] * (own_count / count) - normed_sum * (tot3[1:2] / count)
    )
    pooled_means[...] = bslots3[:, 2]
    h2_over.wait_recv()
    stat2_far.wait_recv()
    w2_last.wait_recv()
    w2_middle_on.wait_recv()
    share_end(pooled_low, pooled_all, group_sends.at[5], group_recvs.at[5], group)
    for copy in [*rest[1:], w3_kept, act_kept]:
        copy.wait()
    for copy in mail.copies:
        if copy is not swap:
            copy.wait_send()


def front_specs(views, x, weights):
    conv_mid, head_first, head_last = weights[1], weights[3], weights[4]
    quarter, depth = x.shape[0] // 4, x.shape[1]
    width = depth
    mid = conv_mid.shape[1] * 4
    half = mid // 2
    block = quarter // PIX
    own = 4 * block
    total = views * own
    hid, emb = head_last.shape
    wide = hid // 2
    subs = total // SUB
    peers = 2 * views
    vm = pltpu.VMEM
    wide_rows = (4, quarter, width)
    outs = (
        shape(2, PAD, PAD, block, mid, kind=BF16),
        shape(2, quarter, half),
        shape(2, *conv_mid.shape, kind=BF16),
        shape(2, *conv_mid.shape, kind=BF16),
        shape(4, 2 * depth, mid // 4, kind=BF16),
        shape(2, 4, quarter, half, kind=BF16),
        shape(*wide_rows, kind=BF16),
        shape(*wide_rows, kind=BF16),
        shape(views, own, width, kind=BF16),
        shape(2, quarter, half, kind=BF16),
        shape(2, quarter, half, kind=BF16),
        shape(2, 2, half),
        shape(depth, mid, kind=BF16),
        shape(4, 8, mid // 4),
        shape(2, width),
        shape(1, width),
        shape(1, width),
        shape(1, hid),
        shape(1, hid),
        shape(own, width),
        shape(2, own, wide),
        shape(own, emb),
        shape(2, own, wide),
        shape(1, 1),
        shape(2, 2, half),
        shape(views, width),
        shape(1, width),
    )
    scratch = [
        vm(wide_rows, BF16),
        vm((4, 2 * depth, mid // 4), BF16),
        vm((2, 4, quarter, half), BF16),
        vm(wide_rows, BF16),
        vm((2, 2, quarter, half), F32),
        vm((2, 2, half), F32),
        vm((peers, 2, 2, half), F32),
        vm((2, half), F32),
        vm((peers, 2, half), F32),
        vm((quarter, quarter), BF16),
        vm((quarter, quarter), BF16),
        vm((2, PAD, PAD, block, mid), BF16),
        vm((2, *conv_mid.shape), BF16),
        vm((4, 2 * depth, mid // 4), BF16),
        vm((2, quarter, half), F32),
        vm((2, quarter, half), BF16),
        vm((8, mid // 4), F32),
        vm(head_first.shape, BF16),
        vm(head_last.shape, BF16),
        vm(wide_rows, BF16),
        vm((own, width), F32),
        vm((own, width), BF16),
        vm((total, 128), F32),
        vm((total, 128), F32),
        vm((total, 128), F32),
        vm((views, own, emb), F32),
        vm((2, own, wide), F32),
        vm((6, own, wide), F32),
        vm((2, own, wide), F32),
        vm((2, own, width), F32),
        vm((2, width), F32),
        vm((views, 2, width), F32),
        vm((4, wide), F32),
        vm((views, 4, wide), F32),
        vm((4, wide), F32),
        vm((views, 4, wide), F32),
        vm((3, width), F32),
        vm((views, 3, width), F32),
        vm((own, emb), F32),
        vm((subs, emb, 2 * emb), F32),
        vm((subs, emb, emb), F32),
        vm((total, emb), F32),
        vm((total, emb), F32),
        vm((total, 3 * emb), BF16),
        vm((total, emb), F32),
        dma(40),
        dma(40),
        dma(2, 2),
        dma(2, 2),
        dma(2, peers),
        dma(2, peers),
        dma(6, views),
        dma(6, views),
        dma(32),
    ]
    return outs, scratch


def front_stage(views, x, weights, vectors, tables, perm, unperm):
    conv_first, conv_mid, conv_last, head_first, head_last = weights
    outs, scratch = front_specs(views, x, weights)
    return call(
        functools.partial(front_body, views),
        "front",
        outs,
        19,
        scratch,
        collective=1,
        any_ins=range(11, 19),
        any_outs=range(11),
    )(
        *vectors, *tables, x.reshape(4, x.shape[0] // 4, x.shape[1]), conv_first, conv_mid, conv_last,
        perm, unperm, head_first, head_last,
    )


def link_kind(rows):
    return BF16 if rows % 16 == 0 else F32


def back_body(
    views, stat3, grad_shift_last, grad_gain_last, grad_pooled, gain_last, expand,
    stats2, smalls, stat1, act4, grad_embed, grad_p1, pooled_means, rows_sum,
    h3_any, slope_any, w3_any, h2_near_any, h2_far_any, perm_any, unperm_any, pad_any, h1q_any, w2_any,
    w2_far_any, act_any, x_any, pooled_any,
    gh1_out, mid_slots, pair_out, head_last_out, head_first_out,
    grad_shift_mid, grad_gain_mid, grad_shift_first, grad_gain_first,
    h3, slope, w3, h2_near, h2_far, gh1, gh3, gh3_mate, out_part, in_part, ga2, gh2_far, gpad, ga1, st, sum_parts, chan_slots, view_slots,
    order, pad, h1q, w2, w2_far, act, pooled,
    wsum, mid_parts, mid_in, last_parts, last_in, last_slots, first_parts, first_in, first_slots, means, mean_slots, pair_parts,
    hl_parts, hl_slots, p1_parts, p1_slots,
    sends, recvs, chan_sends, chan_recvs, group_sends, group_recvs, pair_sends, pair_recvs,
    pair1_sends, pair1_recvs, pair2_sends, pair2_recvs, local_sems,
    resident=False,
):
    view_at, chan_at, y, c = place()
    mate, opposite = (view_at, 2 * y + 1 - c), (view_at, 2 * (1 - y) + c)
    group, chans, everyone = view_group(views), chan_group(), all_group(views)
    quarter, width = h3.shape[1], h3.shape[2]
    block = quarter // PIX
    half_width = h2_near.shape[2]
    met = (lambda: None) if resident else greet([], [everyone])
    to_pixels, to_views = (perm_any, unperm_any) if resident else (order, order)
    local = Local(local_sems)
    near_half, own_half = [2 * i + 1 - c for i in (1 - y, y)], [2 * i + c for i in (1 - y, y)]
    rows_here = []

    def fetch_rows(q):
        if not resident:
            rows_here.append((local.fetch(h3_any.at[q], h3.at[q]), local.fetch(slope_any.at[q], slope.at[q])))
        else:
            rows_here.append(())

    for q in near_half:
        fetch_rows(q)
    count = float(views * 4 * quarter)
    mean, rstd = stat3[0:1], stat3[1:2]
    scale = rstd * gain_last[...]
    shift_part, gain_part = grad_shift_last[...] / count, grad_gain_last[...] / count

    def grad_rows(q):
        rows = pl.ds(pl.multiple_of(q * block, block), block)
        high, low = split_pair(grad_pooled[rows])
        spread = dot(expand[...], jnp.concatenate([high, low], axis=0))
        grad = spread * slope[q].astype(F32)
        normed = (h3[q].astype(F32) - mean) * rstd
        gh3[q] = (scale * (grad - shift_part - normed * gain_part)).astype(BF16)

    mate_out = pl.ds(pl.multiple_of(width * (1 - c), width), width)
    own_out = pl.ds(pl.multiple_of(width * c, width), width)

    def part_of(i):
        def weight(rows):
            return jnp.concatenate([w3[k, rows] for k in range(4)], axis=1)

        value = dot(gh3[2 * i + c], weight(own_out)) + dot(gh3_mate[i], weight(mate_out))
        return dot(to_pixels[...], value.astype(BF16))

    mail = Mail(sends, recvs)
    beside = []
    for at, i in enumerate((1 - y, y)):
        for copy in rows_here[at]:
            copy.wait()
        grad_rows(2 * i + 1 - c)
        if at == 0:
            met()
        beside.append(mail.send(gh3.at[2 * i + 1 - c], gh3_mate.at[i], mate))
        if at == 0:
            for q in own_half:
                fetch_rows(q)
            w3_here = local.fetch(w3_any, w3)
            perm_here = local.fetch(perm_any, order)
    for at, i in enumerate((1 - y, y)):
        for copy in rows_here[2 + at]:
            copy.wait()
        grad_rows(2 * i + c)
        if at == 0:
            w3_here.wait()
            perm_here.wait()
            beside[0].wait_recv()
            value = part_of(1 - y).astype(BF16)
            for half in range(2):
                out_part[half] = value[:, half * half_width : (half + 1) * half_width]
            across = [mail.send(out_part.at[half], in_part.at[half], opposite) for half in range(2)]
            h2_here = [local.fetch(h2_near_any, h2_near), local.fetch(h2_far_any, h2_far)]
            act_here = local.fetch(act_any, act)
            w2_here = local.fetch(w2_any, w2)
            w2_far_here = local.fetch(w2_far_any, w2_far)
            h1q_here = local.fetch(h1q_any, h1q)
            pad_here = local.fetch(pad_any, pad)
    beside[1].wait_recv()
    ga2[...] = part_of(y)
    unperm_here = local.fetch(unperm_any, order)

    def fold_sems(at):
        return [sems.at[at] for sems in (pair1_sends, pair1_recvs, pair2_sends, pair2_recvs)]

    halves = (y, 1 - y)

    def mid_norm(near):
        half = halves[near]
        gains = jnp.concatenate([smalls[2 * half], smalls[2 * half + 1]], axis=1)
        mean2, rstd2 = stats2[half, 0:1], stats2[half, 1:2]
        return mean2, rstd2, gains[2:3], gains[3:4]

    def half_cols(ref, near):
        low, high = ref[:, :half_width], ref[:, half_width:]
        return jnp.where(halves[near] == 0, low, high)

    for copy in h2_here:
        copy.wait()
    for near, h2 in enumerate((h2_near, h2_far)):
        mean2, rstd2, gain2, shift2 = mid_norm(near)
        normed = (h2[1 - y].astype(F32) - mean2) * rstd2
        grad = out_part[halves[near]].astype(F32) * silu_slope(normed * gain2 + shift2)
        st[halves[near], 0:1] = jnp.sum(grad, axis=0, keepdims=True)
        st[halves[near], 1:2] = jnp.sum(grad * normed, axis=0, keepdims=True)
        normed = (h2[y].astype(F32) - mean2) * rstd2
        kept = silu_slope(normed * gain2 + shift2)
        ga1[:, near * half_width : (near + 1) * half_width] = kept
        grad = half_cols(ga2, near) * kept
        st[halves[near], 0:1] += jnp.sum(grad, axis=0, keepdims=True)
        st[halves[near], 1:2] += jnp.sum(grad * normed, axis=0, keepdims=True)
    share_start(st, view_slots.at[0], group_sends.at[3], group_recvs.at[3], group)

    hid_block, hid_split = hl_parts.shape[1], head_last_out.shape[0]
    for half in range(2):
        product = exact(act4[half], grad_embed[...], 0, 0)
        wsum[0, : product.shape[0]] = product
        per_half = views // 2

        def spread_hidden(to, carry, half=half, per_half=per_half):
            spot = (4 * to + chan_at) * hid_block if hid_split == 4 else to * hid_block
            rows = pl.ds(pl.multiple_of(spot, hid_block), hid_block)
            hl_parts[half * per_half + to] = wsum[0, rows]
            return carry

        lax.fori_loop(0, per_half, spread_hidden, 0)
        wide = grad_p1.shape[2] // per_half
        for to in range(per_half):
            p1_parts[half * per_half + to] = grad_p1[half, :, to * wide : (to + 1) * wide]
    act_here.wait()
    share_rows = last_parts.shape[1]
    means[0:1] = rows_sum[...]
    few_rows = quarter // SIDE
    for half in range(2):
        cols = slice(half * half_width, (half + 1) * half_width)
        sampled = [jnp.sum(act[half, q, :few_rows].astype(F32), axis=0, keepdims=True) for q in range(4)]
        means[1:2, cols] = sum(sampled) / (4 * few_rows)
    for half in range(2):
        cols = slice(half * half_width, (half + 1) * half_width)
        total = None
        for q in range(4):
            term = dot_tn(gh3[q], act[half, q])
            total = term if total is None else total + term
        wsum[0, :width] = total[:, : half_width // 2]
        wsum[1, :width] = total[:, half_width // 2 :]
        low = (
            jnp.concatenate([wsum[0, :width], wsum[1, :width]], axis=1)
            - outer_product(means[0:1], means[1:2, cols])
        ).astype(last_parts.dtype)
        for to in range(views):
            last_parts[to, :, half * half_width : (half + 1) * half_width] = low[
                to * share_rows : (to + 1) * share_rows
            ]
    share_end(st, view_slots.at[0], group_sends.at[3], group_recvs.at[3], group)
    sum_parts[0] = add_slots(view_slots.at[0], views)
    sums_beside = mail.send(sum_parts.at[0], sum_parts.at[1], mate)
    scatter_start(hl_parts, hl_slots, group_sends.at[0], group_recvs.at[0], group)
    scatter_start(p1_parts, p1_slots, group_sends.at[1], group_recvs.at[1], group)
    share_start(means, mean_slots, group_sends.at[2], group_recvs.at[2], group)
    fold_last = Fold(last_parts, last_in, last_slots, fold_sems(0), views)
    fold_last.start()
    sums_beside.wait_recv()
    sum_parts[2] = sum_parts[0] + sum_parts[1]
    sums_across = mail.send(sum_parts.at[2], sum_parts.at[3], opposite)
    for copy in beside:
        copy.wait_send()
    x = x_any if resident else gh3
    x_here = local.fetch(x_any, x)

    def share_value(source, slots, send, recv, who):
        source[...] = share(source, slots, send, recv, who)
        return source

    gpad[...] = jnp.zeros(gpad.shape, gpad.dtype)
    for half in range(2):
        across[half].wait()
        cols = slice(half * half_width, (half + 1) * half_width)
        ga2[:, cols] += in_part[half].astype(F32)
    gh2 = out_part
    sums_across.wait_recv()
    sum_parts[4] = sum_parts[2] + sum_parts[3]
    for near, h2 in enumerate((h2_near, h2_far)):
        mean2, rstd2, gain2, shift2 = mid_norm(near)
        tot = sum_parts[4, halves[near]]
        normed = (h2[y].astype(F32) - mean2) * rstd2
        grad = half_cols(ga2, near) * ga1[:, near * half_width : (near + 1) * half_width]
        low = (gain2 * rstd2 * (grad - tot[0:1] / count - normed * (tot[1:2] / count))).astype(BF16)
        gh2[near] = low
        gpad[near, 1 : SIDE + 1, 1 : SIDE + 1] = low.reshape(SIDE, SIDE, block, half_width)
    tot = sum_parts[4, y]
    own_cols = jnp.where(c == 0, tot[:, : half_width // 2], tot[:, half_width // 2 :])
    grad_shift_mid[...] = own_cols[0:1]
    grad_gain_mid[...] = own_cols[1:2]
    cut = quarter // 32 * 16
    far_pieces = [pl.ds(0, cut), pl.ds(cut, quarter - cut)]
    far_copies = [mail.send(gh2.at[1, far_pieces[0]], gh2_far.at[far_pieces[0]], opposite)]
    fold_last.pass_on(1, fold_last.size + 1)
    w2_here.wait()
    w2_far_here.wait()
    channels = w2.shape[1] // 9
    for tap in range(9):
        a, b = 2 - tap // 3, 2 - tap % 3
        taps = slice(tap * channels, (tap + 1) * channels)
        term = None
        for near, weight in enumerate((w2, w2_far)):
            window = gpad[near, a : a + SIDE, b : b + SIDE].reshape(quarter, half_width)
            both = jnp.concatenate([weight[0, taps], weight[1, taps]], axis=1)
            piece = dot_nt(window, both)
            term = piece if term is None else term + piece
        if tap == 0:
            ga1[...] = term
        else:
            ga1[...] += term
    h1q_here.wait()
    for half in range(2):
        gains = jnp.concatenate([smalls[2 * half], smalls[2 * half + 1]], axis=1)
        normed = (h1q[half] - stat1[half, 0:1]) * stat1[half, 1:2]
        cols = slice(half * half_width, (half + 1) * half_width)
        grad = ga1[:, cols] * silu_slope(normed * gains[0:1] + gains[1:2])
        ga2[:, cols] = grad
        st[half, 0:1] = jnp.sum(grad, axis=0, keepdims=True)
        st[half, 1:2] = jnp.sum(grad * normed, axis=0, keepdims=True)
    share_value(st, chan_slots.at[1], chan_sends.at[1], chan_recvs.at[1], chans)
    far_copies.append(mail.send(gh2.at[1, far_pieces[1]], gh2_far.at[far_pieces[1]], opposite))
    share_start(st, view_slots.at[1], group_sends.at[4], group_recvs.at[4], group)

    pad_here.wait()

    def tap_term(at, tap, grads):
        a, b = tap // 3, tap % 3
        window = pad[at, a : a + SIDE, b : b + SIDE].reshape(quarter, channels)
        return dot_tn(window, grads)

    for tap in range(9):
        total = tap_term(y, tap, gh2[0])
        taps = slice(tap * channels, (tap + 1) * channels)
        wsum[0, taps] = total[:, : half_width // 2]
        wsum[1, taps] = total[:, half_width // 2 :]
    share_end(st, view_slots.at[1], group_sends.at[4], group_recvs.at[4], group)
    totals1 = add_slots(view_slots.at[1], views)
    view_slots[1, 0] = totals1
    tot = view_slots[1, 0, y]
    own_cols = jnp.where(c == 0, tot[:, : half_width // 2], tot[:, half_width // 2 :])
    grad_shift_first[...] = own_cols[0:1]
    grad_gain_first[...] = own_cols[1:2]
    unperm_here.wait()
    gh1_across, gh1_beside = [], []
    for half in range(2):
        gains = jnp.concatenate([smalls[2 * half], smalls[2 * half + 1]], axis=1)
        normed = (h1q[half] - stat1[half, 0:1]) * stat1[half, 1:2]
        cols = slice(half * half_width, (half + 1) * half_width)
        tot = totals1[half]
        low = (
            gains[0:1]
            * stat1[half, 1:2]
            * (ga2[:, cols] - tot[0:1] / count - normed * (tot[1:2] / count))
        ).astype(BF16)
        gh1[half, chan_at] = dot(to_views[...], low).astype(BF16)
        spot = gh1.at[half, chan_at]
        gh1_across.append(mail.send(spot, spot, opposite))
        gh1_beside.append(mail.send(spot, spot, mate))

    for copy in far_copies:
        copy.wait_recv()
    for tap in range(9):
        total = tap_term(1 - y, tap, gh2_far[...])
        taps = slice(tap * channels, (tap + 1) * channels)
        wsum[0, taps] += total[:, : half_width // 2]
        wsum[1, taps] += total[:, half_width // 2 :]
    mid_rows = mid_parts.shape[1]
    mid_flat = mid_parts.reshape(views * mid_rows, mid_parts.shape[2])
    if mid_parts.dtype == F32:
        mid_mate = mail.send(wsum.at[1 - c], mid_flat, mate)
    else:
        w2_far[0] = wsum[1 - c].astype(BF16)
        mid_mate = mail.send(w2_far.at[0], mid_flat, mate)
    mid_mate.wait_recv()

    def mid_block(to, carry):
        rows = pl.ds(pl.multiple_of(to * mid_rows, mid_rows), mid_rows)
        mid_parts[to] = (wsum[c, rows] + mid_parts[to].astype(F32)).astype(mid_parts.dtype)
        return carry

    lax.fori_loop(0, views, mid_block, 0)
    fold_mid = Fold(mid_parts, mid_in, mid_slots, fold_sems(1), views, False)
    fold_mid.start()
    scatter_end(p1_parts, p1_slots, group_sends.at[1], group_recvs.at[1], group)
    few = pooled.shape[0]

    def head_first_term(at, total):
        views_at = pl.ds(at * few, few)
        copy = pltpu.make_async_copy(pooled_any.at[views_at], pooled, local_sems.at[29])
        copy.start()
        copy.wait()
        rows = pooled[...].astype(F32).reshape(-1, width)
        return total + exact(rows, p1_slots[views_at].reshape(rows.shape[0], -1), 0, 0)

    head_first_out[...] = over(
        views // few, head_first_term, exact(pooled_means[...], jnp.sum(p1_slots[...], axis=1), 0, 0)
    )
    share_end(means, mean_slots, group_sends.at[2], group_recvs.at[2], group)
    fold_last.end()
    rest, folds = [], []
    cuts = [1 + fold_mid.size * k // 4 for k in range(4)] + [fold_mid.size + 1]
    x_here.wait()
    for half in range(2):
        gh1_across[half].wait_recv()
        far_spot = gh1.at[half, 2 * (1 - y) + c]
        gh1_on = mail.send(far_spot, far_spot, mate)
        fold_mid.pass_on(cuts[2 * half], cuts[2 * half + 1])
        gh1_beside[half].wait_recv()
        gh1_on.wait_recv()
        rest.append(local.fetch(gh1.at[half], gh1_out.at[half]))
        total = None
        for q in range(4):
            term = dot_tn(x[q], gh1[half, q])
            total = term if total is None else total + term
        low = total.astype(first_parts.dtype)
        for to in range(views):
            first_parts[half, to] = low[to * share_rows : (to + 1) * share_rows]
        folds.append(Fold(first_parts.at[half], first_in.at[half], first_slots.at[half], fold_sems(2 + half), views))
        folds[half].start()
        fold_mid.pass_on(cuts[2 * half + 1], cuts[2 * half + 2])
    rest.append(local.fetch(mid_parts.at[view_at], mid_slots.at[fold_mid.outer]))

    scatter_end(hl_parts, hl_slots, group_sends.at[0], group_recvs.at[0], group)
    if hid_split == 4:
        head_last_out[chan_at] = add_slots(hl_slots, views)
        gather_start(head_last_out.at[chan_at], head_last_out, chan_sends.at[2], chan_recvs.at[2], chans)
    else:
        head_last_out[0] = add_slots(hl_slots, views)

    def blocks(kind, summed):
        wide = summed.shape[1] // 4
        for to in range(4):
            pair_parts[to, kind] = summed[:, to * wide : (to + 1) * wide]

    def summed_slots(slots):
        def add(at, total):
            return total + slots[at].astype(F32)

        return lax.fori_loop(1, slots.shape[0], add, slots[0].astype(F32))

    everywhere = short_product(mean_slots[:, 0], mean_slots[:, 1])
    ga1[: everywhere.shape[0]] = everywhere
    own_block = pl.ds(pl.multiple_of(view_at * share_rows, share_rows), share_rows)
    blocks(1, summed_slots(last_slots) + ga1[own_block])
    for fold in folds:
        fold.pass_on(1, fold.size + 1)
    for fold in folds:
        fold.end()
    blocks(0, jnp.concatenate([summed_slots(first_slots.at[half]) for half in range(2)], axis=1))
    row_views = views // 4
    to_view = chan_at * row_views + lax.div(view_at, 4)
    slot = lax.rem(view_at, 4)

    def pair_copy(to):
        return pltpu.make_async_remote_copy(
            src_ref=pair_parts.at[to],
            dst_ref=pair_out.at[slot],
            send_sem=pair_sends.at[to],
            recv_sem=pair_recvs.at[slot],
            device_id=(to_view, to),
            device_id_type=MESH,
        )

    def pair_arrival(origin):
        return pltpu.make_async_remote_copy(
            src_ref=pair_parts.at[0],
            dst_ref=pair_out.at[origin],
            send_sem=pair_sends.at[0],
            recv_sem=pair_recvs.at[origin],
            device_id=(from_view + origin, from_chan),
            device_id_type=MESH,
        )

    from_view, from_chan = 4 * lax.rem(view_at, row_views), lax.div(view_at, row_views)
    for to in range(4):
        own = jnp.logical_and(to_view == view_at, chan_at == to)

        @pl.when(own)
        def _():
            pair_out[slot] = pair_parts[to]

        @pl.when(jnp.logical_not(own))
        def _():
            pair_copy(to).start()

    for origin in range(4):
        own = jnp.logical_and(from_view + origin == view_at, chan_at == from_chan)

        @pl.when(jnp.logical_not(own))
        def _():
            pair_arrival(origin).wait_recv()

    for to in range(4):
        own = jnp.logical_and(to_view == view_at, chan_at == to)

        @pl.when(jnp.logical_not(own))
        def _():
            pair_copy(to).wait_send()

    if hid_split == 4:
        share_end(head_last_out.at[chan_at], head_last_out, chan_sends.at[2], chan_recvs.at[2], chans)
    fold_mid.end()
    for copy in rest:
        copy.wait()
    for copy in mail.copies[4:]:
        copy.wait_send()


def back_specs(views, front_outs):
    pad, w2, w3, act, h3, h2_near = (front_outs[at] for at in (0, 2, 4, 5, 6, 9))
    act4, grad_embed = front_outs[20], front_outs[21]
    h1q, slope, pooled_all, h2_far = front_outs[1], front_outs[7], front_outs[8], front_outs[10]
    perm_dims = (h3.shape[1], h3.shape[1])
    quarter, width = h3.shape[1], h3.shape[2]
    block = quarter // PIX
    own = 4 * block
    mid = pad.shape[4]
    half = mid // 2
    hid, emb = 2 * act4.shape[2], grad_embed.shape[1]
    taps = w2.shape[1]
    hid_split = 4 if hid // views % 32 == 0 else 1
    hid_block = hid // views // hid_split
    mid_kind, row_kind = link_kind(taps // views), link_kind(width // views)
    vm = pltpu.VMEM
    outs = (
        shape(2, 4, quarter, half, kind=BF16),
        shape(views // 2, taps // views, half // 2, kind=mid_kind),
        shape(4, 2, width // views, mid // 4),
        shape(hid_split, hid_block, emb),
        shape(width, hid // views),
        *[shape(1, half // 2)] * 4,
    )
    scratch = [
        vm((4, quarter, width), BF16),
        vm((4, quarter, width), BF16),
        vm(w3.shape, BF16),
        vm(h2_near.shape, BF16),
        vm(h2_near.shape, BF16),
        vm((2, 4, quarter, half), BF16),
        vm((4, quarter, width), BF16),
        vm((2, quarter, width), BF16),
        vm((2, quarter, half), BF16),
        vm((2, quarter, half), BF16),
        vm((quarter, mid), F32),
        vm((quarter, half), BF16),
        vm((2, PAD, PAD, block, half), BF16),
        vm((quarter, mid), F32),
        vm((2, 2, half), F32),
        vm((5, 2, 2, half), F32),
        vm((2, 4, 2, 2, half), F32),
        vm((2, views, 2, 2, half), F32),
        vm(perm_dims, BF16),
        vm(pad.shape, BF16),
        vm(h1q.shape, F32),
        vm(w2.shape, BF16),
        vm(w2.shape, BF16),
        vm(act.shape, BF16),
        vm((min(views, 8), own, width), BF16),
        vm((2, taps, half // 2), F32),
        vm((views, taps // views, half // 2), mid_kind),
        vm((views // 2, taps // views, half // 2), mid_kind),
        vm((views, width // views, mid), row_kind),
        vm((views // 2, width // views, mid), row_kind),
        vm((views // 2, width // views, mid), row_kind),
        vm((2, views, width // views, half), row_kind),
        vm((2, views // 2, width // views, half), row_kind),
        vm((2, views // 2, width // views, half), row_kind),
        vm((2, width), F32),
        vm((views, 2, width), F32),
        vm((4, 2, width // views, mid // 4), F32),
        vm((views, hid_block, emb), F32),
        vm((views, hid_block, emb), F32),
        vm((views, own, hid // views), F32),
        vm((views, own, hid // views), F32),
        dma(20),
        dma(20),
        dma(3, 4),
        dma(3, 4),
        dma(7, views),
        dma(7, views),
        dma(4),
        dma(4),
        *[dma(4, views // 2)] * 4,
        dma(30),
    ]
    return outs, scratch


def back_stage(views, front_outs, x, gain_last, perm, unperm, expand):
    (pad, h1q, w2, w2_far, w3, act, h3, slope, pooled_all, h2_near, h2_far, stat1, _, smalls, stat3,
     grad_shift_last, grad_gain_last, _, _, grad_pooled, act4, grad_embed, grad_p1, _,
     stats2, pooled_means, rows_sum) = front_outs
    outs, scratch = back_specs(views, front_outs)
    return call(
        functools.partial(back_body, views),
        "back",
        outs,
        28,
        scratch,
        collective=4,
        any_ins=range(14, 28),
        any_outs=range(2),
    )(
        stat3, grad_shift_last, grad_gain_last, grad_pooled, gain_last, expand,
        stats2, smalls, stat1, act4, grad_embed, grad_p1, pooled_means, rows_sum,
        h3, slope, w3, h2_near, h2_far, perm, unperm, pad, h1q, w2, w2_far, act,
        x.reshape(4, x.shape[0] // 4, x.shape[1]), pooled_all,
    )


def split_names(body, ins, outs):
    names = tuple(inspect.signature(body).parameters)[1:-1]
    return names[:ins], names[ins : ins + outs], names[ins + outs :]


FRONT_INS, FRONT_OUTS, FRONT_SCRATCH = split_names(front_body, 19, 27)
BACK_INS, BACK_OUTS, BACK_SCRATCH = split_names(back_body, 28, 9)
DROPPED = ("pad_out", "h1_out", "w2_out", "w3_out", "act_out", "h3_out", "h2_near")
KEPT = (
    "slope_out", "pooled_all", "w1_own", "grad_shift_last", "grad_gain_last",
    "grad_shift_head", "grad_gain_head", "grad_pooled_out", "loss_out",
)
SHARED = {
    "h3": "h3", "slope": "slope", "w3": "w3", "h2_near": "h2", "h2_far": "h2_far", "gh1": "act",
    "gh3": "slope", "pad": "pad", "w2": "w2", "w2_far": "w2_far", "act": "act",
}
SAME = {"stat1": "stat", "grad_pooled": "grad_pooled_out", "grad_embed": "grad_embed_out"}


def joined_names():
    held = [name for name in FRONT_OUTS if name not in DROPPED and name not in KEPT]
    fresh = [name for name in BACK_SCRATCH if name not in SHARED and name not in ("order", "h1q")]
    return held, fresh


def joined_body(views, *refs):
    held, fresh = joined_names()
    names = [*FRONT_INS, "expand", *KEPT, *BACK_OUTS, *FRONT_SCRATCH, *held]
    env = dict(zip(names, refs))
    back_env = dict(zip(fresh, refs[len(names) :]))
    front_body(views, *[env.get(name) for name in FRONT_INS + FRONT_OUTS + FRONT_SCRATCH], everyone=True)
    for name, other in SHARED.items():
        back_env[name] = env[other]
    back_env["h1q"] = env["h1"].at[:, place()[2]]
    for name in BACK_INS:
        if name.endswith("_any"):
            back_env[name] = back_env.get(name[:-4])
    back_env["perm_any"], back_env["unperm_any"] = env["perm"], env["unperm"]
    back_env["x_any"], back_env["pooled_any"] = env["x"], env["pooled_all"]

    def pick(name):
        return back_env[name] if name in back_env else env.get(SAME.get(name, name))

    back_body(views, *[pick(name) for name in BACK_INS + BACK_OUTS + BACK_SCRATCH], resident=True)


def joined_stage(views, x, weights, vectors, tables, perm, unperm, expand):
    conv_first, conv_mid, conv_last, head_first, head_last = weights
    outs, scratch = front_specs(views, x, weights)
    outs_at = dict(zip(FRONT_OUTS, outs))
    back_outs, back_scratch = back_specs(views, outs)
    back_at = dict(zip(BACK_SCRATCH, back_scratch))
    held, fresh = joined_names()
    front_scratch = dict(zip(FRONT_SCRATCH, scratch))
    more = [pltpu.VMEM(outs_at[name].shape, outs_at[name].dtype) for name in held]
    results = call(
        functools.partial(joined_body, views),
        "joined",
        (*[outs_at[name] for name in KEPT], *back_outs),
        20,
        [*front_scratch.values(), *more, *[back_at[name] for name in fresh]],
        collective=1,
        any_ins=range(11, 19),
        any_outs=(0, 1, len(KEPT), len(KEPT) + 1),
    )(
        *vectors, *tables, x.reshape(4, x.shape[0] // 4, x.shape[1]), conv_first, conv_mid, conv_last,
        perm, unperm, head_first, head_last, expand,
    )
    return dict(zip(KEPT, results)), results[len(KEPT) :]


def last_body(
    small_count, w1_any, grad_pooled, expand, gh1_any, slope_any, mid_any, pair_out, head_last_in, head_first_in, *more
):
    small_ins, outs = more[:small_count], more[small_count : 2 * small_count + 6]
    gh1, w1_own, slope, term, mid_slots, sems = more[2 * small_count + 6 :]
    grad_input, grad_mid, grad_first, grad_last, grad_head_last, grad_head_first, *small_outs = outs
    local = Local(sems)
    quarters, quarter, half = gh1.shape[1], gh1.shape[2], gh1.shape[3]
    w1_here = local.fetch(w1_any, w1_own)
    rows_here = [
        (local.fetch(gh1_any.at[:, q], gh1.at[:, q]), local.fetch(slope_any.at[q], slope.at[q]))
        for q in range(quarters)
    ]
    mid_here = local.fetch(mid_any, mid_slots)
    rest = []
    w1_here.wait()
    block = quarter // PIX
    for q in range(quarters):
        for copy in rows_here[q]:
            copy.wait()
        high, low = split_pair(grad_pooled[q * block : (q + 1) * block])
        spread = dot(expand[...], jnp.concatenate([high, low], axis=0))
        value = dot_nt(gh1[0, q], w1_own[:, :half]) + dot_nt(gh1[1, q], w1_own[:, half:])
        term[q] = value + spread * slope[q].astype(F32)
        rest.append(local.fetch(term.at[q], grad_input.at[q]))
    mid_here.wait()

    def add(slot, total):
        return total + mid_slots[slot].astype(F32)

    grad_mid[...] = lax.fori_loop(1, mid_slots.shape[0], add, mid_slots[0].astype(F32))
    grad_head_first[...] = head_first_in[...]
    for source, target in zip(small_ins, small_outs):
        target[...] = source[...]
    rows = pair_out.shape[2]
    for origin in range(4):
        grad_first[origin * rows : (origin + 1) * rows] = pair_out[origin, 0]
        grad_last[origin * rows : (origin + 1) * rows] = pair_out[origin, 1]
    rows = head_last_in.shape[1]
    for origin in range(head_last_in.shape[0]):
        grad_head_last[origin * rows : (origin + 1) * rows] = head_last_in[origin]
    for copy in rest:
        copy.wait()


def last_stage(
    gh1, w1_own, slope, grad_pooled, expand, mid_slots, pair_out, head_last_in, head_first_in, small
):
    quarter, half, width = gh1.shape[2], gh1.shape[3], slope.shape[2]
    outs = (
        shape(4, quarter, width),
        shape(*mid_slots.shape[1:]),
        shape(4 * pair_out.shape[2], pair_out.shape[3]),
        shape(4 * pair_out.shape[2], pair_out.shape[3]),
        shape(head_last_in.shape[0] * head_last_in.shape[1], head_last_in.shape[2]),
        shape(*head_first_in.shape),
        *[shape(*array.shape) for array in small],
    )
    ins = 9 + len(small)
    return call(
        functools.partial(last_body, len(small)),
        "results",
        outs,
        ins,
        [
            pltpu.VMEM(gh1.shape, BF16),
            pltpu.VMEM(w1_own.shape, BF16),
            pltpu.VMEM(slope.shape, BF16),
            pltpu.VMEM(slope.shape, F32),
            pltpu.VMEM(mid_slots.shape, mid_slots.dtype),
            dma(20),
        ],
        collective=None,
        any_ins=(0, 3, 4, 5),
        any_outs=(0,),
    )(w1_own, grad_pooled, expand, gh1, slope, mid_slots, pair_out, head_last_in, head_first_in, *small)


def per_device(
    views,
    block_input,
    conv_first,
    conv_mid,
    conv_last,
    gain_first,
    shift_first,
    gain_mid,
    shift_mid,
    gain_last,
    shift_last,
    head_first,
    gain_head,
    shift_head,
    head_last,
    image_of,
    partner,
    sub_of,
):
    rows, width = block_input.shape
    quarter = rows // 4
    block = quarter // PIX
    perm, unperm = orders(quarter)
    at_row = np.arange(quarter)
    twice = np.arange(2 * block) % block
    expand = jnp.asarray((at_row[:, None] // PIX == twice[None, :]).astype(BF16))

    def line(vector):
        return vector.reshape(1, -1)

    weights = (conv_first, conv_mid, conv_last, head_first, head_last)
    vectors = [
        line(v)
        for v in (gain_first, shift_first, gain_mid, shift_mid, gain_last, shift_last, gain_head, shift_head)
    ]
    tables = [line(v) for v in (sub_of, image_of, partner)]
    if views <= JOINED_VIEWS:
        kept, back_outs = joined_stage(views, block_input, weights, vectors, tables, perm, unperm, expand)
    else:
        front_outs = front_stage(views, block_input, weights, vectors, tables, perm, unperm)
        kept = dict(zip(FRONT_OUTS, front_outs))
        back_outs = back_stage(views, front_outs, block_input, line(gain_last), perm, unperm, expand)
    slope, w1_own, grad_pooled, loss = (
        kept[name] for name in ("slope_out", "w1_own", "grad_pooled_out", "loss_out")
    )
    (gh1, mid_slots, pair_out, head_last_in, head_first_in,
     grad_shift_mid, grad_gain_mid, grad_shift_first, grad_gain_first) = back_outs
    small = [
        grad_gain_first, grad_shift_first, grad_gain_mid, grad_shift_mid,
        kept["grad_gain_last"], kept["grad_shift_last"], kept["grad_gain_head"], kept["grad_shift_head"], loss,
    ]
    grad_input, grad_mid, grad_first, grad_last, grad_head_last, grad_head_first, *small = last_stage(
        gh1, w1_own, slope, grad_pooled, expand, mid_slots, pair_out, head_last_in, head_first_in, small
    )
    return (
        small[8].reshape(()),
        grad_input.reshape(rows, width),
        grad_first,
        grad_mid,
        grad_last,
        grad_head_first,
        grad_head_last,
        *[vector.reshape(-1) for vector in small[:8]],
    )


def solution(mesh):
    views = mesh.shape["views"]
    return jax.shard_map(
        functools.partial(per_device, views),
        mesh=mesh,
        in_specs=(
            P("views", "chan"),
            P(None, "chan"),
            P(None, "chan"),
            P(None, "chan"),
            P("chan"),
            P("chan"),
            P("chan"),
            P("chan"),
            P("chan"),
            P("chan"),
            P("chan", None),
            P(),
            P(),
            P(),
            P(),
            P(),
            P(),
        ),
        out_specs=(
            P(),
            P("views", "chan"),
            P("views", "chan"),
            P("views", "chan"),
            P("views", "chan"),
            P("chan", "views"),
            P("views", None),
            P("chan"),
            P("chan"),
            P("chan"),
            P("chan"),
            P("chan"),
            P("chan"),
            P(),
            P(),
        ),
        check_vma=False,
    )
```

```python
import functools
import inspect

import jax
import jax.numpy as jnp
import numpy as np
from jax import lax
from jax.experimental import pallas as pl
from jax.experimental.pallas import tpu as pltpu
from jax.sharding import PartitionSpec as P

SIDE = 7
PIX = SIDE * SIDE
PAD = SIDE + 2
SUB = 256
EPS = 1e-05
RIDGE = 0.5
MESH = pl.DeviceIdType.MESH
BF16 = jnp.bfloat16
F32 = jnp.float32
VMEM_BYTES = 62 << 20
JOINED_VIEWS = 8


def place():
    view_at, chan_at = lax.axis_index("views"), lax.axis_index("chan")
    return view_at, chan_at, lax.div(chan_at, 2), lax.rem(chan_at, 2)


def greet(peers, groups=()):
    barrier = pltpu.get_barrier_semaphore()
    total = len(peers)
    for peer in peers:
        pl.semaphore_signal(barrier, inc=1, device_id=peer, device_id_type=MESH)
    for size, own, device in groups:

        def tell(step, carry, size=size, own=own, device=device):
            pl.semaphore_signal(
                barrier, inc=1, device_id=device(lax.rem(own + step, size)), device_id_type=MESH
            )
            return carry

        lax.fori_loop(1, size, tell, 0)
        total += size - 1
    return lambda: pl.semaphore_wait(barrier, total)


class Mail:
    def __init__(self, send_sems, recv_sems):
        self.send_sems, self.recv_sems, self.copies = send_sems, recv_sems, []

    def send(self, source, target, peer):
        spot = len(self.copies)
        copy = pltpu.make_async_remote_copy(
            src_ref=source,
            dst_ref=target,
            send_sem=self.send_sems.at[spot],
            recv_sem=self.recv_sems.at[spot],
            device_id=peer,
            device_id_type=MESH,
        )
        copy.start()
        self.copies.append(copy)
        return copy

    def finish(self):
        for copy in self.copies:
            copy.wait_send()


class Done:
    def wait(self):
        pass


class Local:
    def __init__(self, sems):
        self.sems, self.used = sems, 0

    def fetch(self, source, target):
        if target is None or source is target:
            return Done()
        copy = pltpu.make_async_copy(source, target, self.sems.at[self.used])
        copy.start()
        self.used += 1
        return copy


def group_copy(source, slots, sends, recvs, size, own, device, step):
    to = lax.rem(own + step, size)
    return pltpu.make_async_remote_copy(
        src_ref=source,
        dst_ref=slots.at[own],
        send_sem=sends.at[step],
        recv_sem=recvs.at[own],
        device_id=device(to),
        device_id_type=MESH,
    )


def group_arrival(source, slots, sends, recvs, size, own, device, step):
    origin = lax.rem(own + step, size)
    return pltpu.make_async_remote_copy(
        src_ref=source,
        dst_ref=slots.at[origin],
        send_sem=sends.at[step],
        recv_sem=recvs.at[origin],
        device_id=device(origin),
        device_id_type=MESH,
    )


def share_start(source, slots, sends, recvs, group):
    def start(step, carry):
        group_copy(source, slots, sends, recvs, *group, step).start()
        return carry

    lax.fori_loop(1, group[0], start, 0)
    slots[group[1]] = source[...]


def share_end(source, slots, sends, recvs, group):
    def end(step, carry):
        group_arrival(source, slots, sends, recvs, *group, step).wait_recv()
        group_copy(source, slots, sends, recvs, *group, step).wait_send()
        return carry

    lax.fori_loop(1, group[0], end, 0)


def add_slots(slots, size):
    def add(at, total):
        return total + slots[at]

    return lax.fori_loop(1, size, add, slots[0])


def share(source, slots, sends, recvs, group):
    share_start(source, slots, sends, recvs, group)
    share_end(source, slots, sends, recvs, group)
    return add_slots(slots, group[0])


def gather_start(source, slots, sends, recvs, group):
    def start(step, carry):
        group_copy(source, slots, sends, recvs, *group, step).start()
        return carry

    lax.fori_loop(1, group[0], start, 0)


def scatter_start(parts, slots, sends, recvs, group, keep=True):
    size, own, device = group

    def start(step, carry):
        to = lax.rem(own + step, size)
        group_copy(parts.at[to], slots, sends, recvs, *group, step).start()
        return carry

    lax.fori_loop(1, size, start, 0)
    if keep:
        slots[own] = parts[own]


def scatter_end(parts, slots, sends, recvs, group):
    share_end(parts.at[group[1]], slots, sends, recvs, group)


class Fold:
    def __init__(self, parts, fold_in, slots, sems, views, keep=True):
        view_at, chan_at, _, _ = place()
        self.parts, self.fold_in, self.slots, self.sems, self.keep = parts, fold_in, slots, sems, keep
        self.size, self.outer, self.inner = views // 2, lax.div(view_at, 2), lax.rem(view_at, 2)
        self.pair = (2 * self.outer + 1 - self.inner, chan_at)
        self.chan_at = chan_at

    def block(self, step):
        return lax.rem(self.outer + step, self.size)

    def pair_copy(self, step):
        at = self.block(step)
        return pltpu.make_async_remote_copy(
            src_ref=self.parts.at[2 * at + 1 - self.inner],
            dst_ref=self.fold_in.at[at],
            send_sem=self.sems[0].at[at],
            recv_sem=self.sems[1].at[at],
            device_id=self.pair,
            device_id_type=MESH,
        )

    def out_copy(self, step, slot):
        at = self.block(step)
        return pltpu.make_async_remote_copy(
            src_ref=self.parts.at[2 * at + self.inner],
            dst_ref=self.slots.at[slot],
            send_sem=self.sems[2].at[at],
            recv_sem=self.sems[3].at[slot],
            device_id=(2 * at + self.inner, self.chan_at),
            device_id_type=MESH,
        )

    def start(self):
        def one(step, carry):
            self.pair_copy(step).start()
            return carry

        lax.fori_loop(1, self.size + 1, one, 0)

    def add(self, step):
        self.pair_copy(step).wait_recv()
        at, mine = self.block(step), 2 * self.block(step) + self.inner
        total = self.parts[mine].astype(F32) + self.fold_in[at].astype(F32)
        self.parts[mine] = total.astype(self.parts.dtype)

    def pass_on(self, first, last):
        def one(step, carry):
            self.add(step)
            self.out_copy(step, self.outer).start()
            return carry

        lax.fori_loop(first, min(last, self.size), one, 0)
        if last > self.size:
            self.add(self.size)
            if self.keep:
                self.slots[self.outer] = self.parts[2 * self.outer + self.inner]

    def end(self):
        def one(step, carry):
            self.out_copy(step, self.block(step)).wait_recv()
            self.out_copy(step, self.outer).wait_send()
            return carry

        lax.fori_loop(1, self.size, one, 0)

        def sent(step, carry):
            self.pair_copy(step).wait_send()
            return carry

        lax.fori_loop(1, self.size + 1, sent, 0)


def chan_group():
    view_at, chan_at, y, c = place()
    return (4, chan_at, lambda at: (view_at, at))


def half_group(views):
    view_at, chan_at, y, c = place()
    return (
        2 * views,
        2 * view_at + c,
        lambda at: (lax.div(at, 2), 2 * y + lax.rem(at, 2)),
    )


def view_group(views):
    view_at, chan_at, y, c = place()
    return (views, view_at, lambda at: (at, chan_at))


def all_group(views):
    view_at, chan_at, y, c = place()
    return (4 * views, 4 * view_at + chan_at, lambda at: (lax.div(at, 4), lax.rem(at, 4)))


def dot(left, right):
    return jnp.dot(left, right, preferred_element_type=F32)


def dot_nt(left, right):
    return lax.dot_general(left, right, (((1,), (1,)), ((), ())), preferred_element_type=F32)


def dot_tn(left, right):
    return lax.dot_general(left, right, (((0,), (0,)), ((), ())), preferred_element_type=F32)


def gate(level):
    return 0.5 + 0.5 * jnp.tanh(0.5 * level)


def silu_slope(level):
    open_part = gate(level)
    return open_part * (1.0 + level * (1.0 - open_part))


def call(body, name, outs, ins, scratch, collective, any_ins=(), any_outs=()):
    def spec(at, places):
        return pl.BlockSpec(memory_space=pl.ANY if at in places else pltpu.VMEM)

    return pl.pallas_call(
        body,
        out_shape=outs,
        in_specs=[spec(at, any_ins) for at in range(ins)],
        out_specs=tuple(spec(at, any_outs) for at in range(len(outs))),
        scratch_shapes=scratch,
        name=name,
        compiler_params=pltpu.CompilerParams(
            collective_id=collective,
            has_side_effects=collective is not None,
            vmem_limit_bytes=VMEM_BYTES,
        ),
    )


def shape(*dims, kind=F32):
    return jax.ShapeDtypeStruct(dims, kind)


def dma(*dims):
    return pltpu.SemaphoreType.DMA(dims)


def split_rows(value):
    high = value.astype(BF16)
    rest = value - high.astype(F32)
    middle = rest.astype(BF16)
    low = (rest - middle.astype(F32)).astype(BF16)
    return jnp.concatenate([high, middle, low], axis=0)


def join_rows(stacked):
    rows = stacked.shape[0] // 3
    return stacked[2 * rows :] + stacked[rows : 2 * rows] + stacked[:rows]


def split_pair(value):
    high = value.astype(BF16)
    return high, (value - high.astype(F32)).astype(BF16)


def exact(left, right, left_dim, right_dim):
    return lax.dot_general(
        left,
        right,
        (((left_dim,), (right_dim,)), ((), ())),
        precision=lax.Precision.HIGHEST,
        preferred_element_type=F32,
    )


def over(count, body, start):
    return body(0, start) if count == 1 else lax.fori_loop(0, count, body, start)


def split_three(value):
    high = value.astype(BF16)
    rest = value - high.astype(F32)
    middle = rest.astype(BF16)
    return high, middle, (rest - middle.astype(F32)).astype(BF16)


def short_product(left, right):
    lh, lm, ll = split_three(left)
    rh, rm, rl = split_three(right)
    return dot_tn(
        jnp.concatenate([lh, lh, lm, lh, lm, ll], axis=0),
        jnp.concatenate([rh, rm, rh, rl, rm, rh], axis=0),
    )


def outer_product(left, right):
    def rows(value, high_at, middle_at, low_at):
        parts = [part.astype(F32) for part in split_three(value)]
        row = lax.broadcasted_iota(jnp.int32, (16, value.shape[1]), 0)
        total = jnp.zeros((16, value.shape[1]), F32)
        for part, places in zip(parts, (high_at, middle_at, low_at)):
            for place_at in places:
                total = jnp.where(row == place_at, part, total)
        return total.astype(BF16)

    return dot_tn(rows(left, (0, 1, 3), (2, 4), (5,)), rows(right, (0, 2, 5), (1, 4), (3,)))


def factor_inverse(work, inverse, subs, width):
    panel = 16
    row = lax.broadcasted_iota(jnp.int32, (panel, width), 0)

    def wide(part):
        return jnp.broadcast_to(part, (panel, width))

    def eliminate(s, first):
        rows = work[s, first : first + panel]
        columns = [wide(rows[:, first + j : first + j + 1]) for j in range(panel)]
        diagonal = jnp.zeros((panel, width), F32)
        for j in range(panel):
            pivot = wide(columns[j][j : j + 1])
            diagonal = jnp.where(row == j, pivot, diagonal)
            if j == panel - 1:
                break
            ratio = jnp.where(row > j, columns[j] * (1.0 / pivot), 0.0)
            for k in range(j + 1, panel):
                columns[k] = columns[k] - ratio * wide(columns[k][j : j + 1])
            rows = rows - jnp.concatenate([ratio, ratio], axis=1) * rows[j : j + 1]
        inverse[s, first : first + panel] = rows[:, width:] * lax.rsqrt(diagonal)
        if first + panel < width:
            scaled = rows[:, :width] / diagonal
            work[s, first + panel :] -= short_product(scaled, rows)[first + panel :]

    def some(at, carry):
        for first in range(0, width, panel):
            for k in range(2):
                eliminate(2 * at + k, first)
        return carry

    over(subs // 2, some, 0)


def view_sums(value, block):
    return jnp.concatenate(
        [jnp.sum(value[PIX * v : PIX * (v + 1)], axis=0, keepdims=True) for v in range(block)], axis=0
    )


def columns_of(row, column):
    tile = column.shape[1]

    def one(at, carry):
        cols = pl.ds(pl.multiple_of(at * tile, tile), tile)
        column[cols] = jnp.broadcast_to(row[:, cols].astype(F32), (tile, tile)).T
        return carry

    lax.fori_loop(0, row.shape[1] // tile, one, 0)


def whiten(embed, sub_col, image_col, image_row, partner_col, partner_row, refs, own_rows):
    work, inverse, white, unit, unit_parts, back = refs
    total, width = embed.shape
    subs = inverse.shape[0]
    eye = (
        lax.broadcasted_iota(jnp.int32, (width, width), 0)
        == lax.broadcasted_iota(jnp.int32, (width, width), 1)
    ).astype(F32)
    size = min(total, 512)
    pieces = total // size

    def rows_at(at):
        return pl.ds(pl.multiple_of(at * size, size), size)

    means = []

    def masks(rows, s):
        column = sub_col[rows]
        return (column == float(s)).astype(F32), (column == float(s + 1)).astype(F32)

    for s in range(0, subs, 2):

        def moments(at, sums, s=s):
            rows = rows_at(at)
            value = embed[rows]
            picked = jnp.concatenate([value * mask for mask in masks(rows, s)], axis=1)
            first = sums[0] + jnp.sum(picked, axis=0, keepdims=True)
            return first, sums[1] + exact(picked, value, 0, 0)

        first, second = over(
            pieces, moments, (jnp.zeros((1, 2 * width), F32), jnp.zeros((2 * width, width), F32))
        )
        for k in range(2):
            mean = first[:, k * width : (k + 1) * width] / SUB
            cov = second[k * width : (k + 1) * width] / SUB - exact(mean, mean, 0, 0)
            work[s + k, :, :width] = cov + RIDGE * eye
            work[s + k, :, width:] = eye
            means.append(mean)
    factor_inverse(work, inverse, subs, width)

    def whitening(at, carry):
        rows = rows_at(at)
        value = None
        for s in range(0, subs, 2):
            centred = jnp.concatenate(
                [(embed[rows] - means[s + k]) * mask for k, mask in enumerate(masks(rows, s))], axis=1
            )
            term = exact(centred, jnp.concatenate([inverse[s], inverse[s + 1]], axis=1), 1, 1)
            value = term if value is None else value + term
        white[rows] = value
        value = value * lax.rsqrt(jnp.sum(value * value, axis=1, keepdims=True) + EPS)
        unit[rows] = value
        high = value.astype(BF16)
        rest = value - high.astype(F32)
        middle = rest.astype(BF16)
        unit_parts[rows] = jnp.concatenate(
            [high, middle, (rest - middle.astype(F32)).astype(BF16)], axis=1
        )
        return carry

    over(pieces, whitening, 0)
    chunk = min(total, 262144 // total)

    def pairs(at, loss):
        rows = pl.ds(pl.multiple_of(at * chunk, chunk), chunk)
        across = lax.broadcasted_iota(jnp.int32, (chunk, total), 1).astype(F32)
        down = lax.broadcasted_iota(jnp.int32, (chunk, total), 0) + at * chunk

        def pick(hot):
            found = dot(hot.astype(F32).astype(BF16), unit_parts[...])
            return found[:, 2 * width :] + found[:, width : 2 * width] + found[:, :width]

        mine = unit[rows]
        ahead = pick(partner_col[rows][:, :1] == across)
        behind = pick(partner_row[...] == down)
        members = jnp.sum(
            (image_col[rows][:, :1] == image_row[...].astype(F32)).astype(F32), axis=1, keepdims=True
        )
        weight = 1.0 / members
        apart = mine - ahead
        grad = (4.0 / total) * weight * (2.0 * mine - ahead - behind)
        length = lax.rsqrt(jnp.sum(white[rows] * white[rows], axis=1, keepdims=True) + EPS)
        back[rows] = length * (grad - mine * jnp.sum(mine * grad, axis=1, keepdims=True))
        per_view = jnp.sum(apart * apart, axis=1, keepdims=True) * weight
        return loss + jnp.sum(per_view, axis=0, keepdims=True)

    loss = over(total // chunk, pairs, jnp.zeros((1, 1), F32)) * (2.0 / total)
    lower = lax.broadcasted_iota(jnp.int32, (width, width), 0) >= lax.broadcasted_iota(
        jnp.int32, (width, width), 1
    )
    own_white, own_back = white[own_rows], back[own_rows]
    gradient = jnp.zeros(own_white.shape, F32)
    for s in range(0, subs, 2):

        def pulled(at, sums, s=s):
            rows = rows_at(at)
            picked = jnp.concatenate([back[rows] * mask for mask in masks(rows, s)], axis=1)
            spread = sums[0] + jnp.sum(picked, axis=0, keepdims=True)
            return spread, sums[1] + exact(picked, white[rows], 0, 0)

        spread, sums = over(
            pieces, pulled, (jnp.zeros((1, 2 * width), F32), jnp.zeros((2 * width, width), F32))
        )
        for k, own_mask in enumerate(masks(own_rows, s)):
            cols = slice(k * width, (k + 1) * width)
            low_part = jnp.where(lower, sums[cols], 0.0)
            mirrored = low_part + low_part.T - sums[cols] * eye
            moved = own_back - (exact(own_white, mirrored, 1, 0) + spread[:, cols]) / SUB
            gradient = gradient + own_mask * exact(moved, inverse[s + k], 1, 0)
    return loss, gradient


MIDDLE_TAPS = 3
EARLY_TAPS = 3


def orders(quarter):
    block = quarter // PIX
    row = np.arange(quarter)
    source = (row % block) * PIX + row // block
    hot = (source[:, None] == row[None, :]).astype(BF16)
    return jnp.asarray(hot), jnp.asarray(hot.T)


def front_body(
    views, g1, b1, g2, b2, gain_last, shift_last, gain_head, shift_head, sub_row, image_row, partner_row,
    x_any, w1in, w2in, w3in, perm_any, unperm_any, head_first_any, head_last_any,
    pad_out, h1_out, w2_out, w2_far, w3_out, act_out, h3_out, slope_out, pooled_all, h2_near, h2_far,
    stat, w1_own, smalls, stat3, grad_shift_last, grad_gain_last, grad_shift_head, grad_gain_head,
    grad_pooled_out, act4, grad_embed_out, grad_p1, loss_out, stats2, pooled_means, rows_sum,
    x, w1, act, h3, h1, st, slots, st2, slots2, perm, unperm, pad, w2, w3, hidden, h2, small,
    head_first, head_last, slope, pooled_own, pooled_low, sub_col, image_col, partner_col,
    embed_all, part, part_in, mean_sums, slope_sums, st3, slots3, st4, slots4, bk4, bslots4, bk3, bslots3, embed_own,
    work, inverse, white, unit, unit_parts, back,
    sends, recvs, part_sends, part_recvs, half_sends, half_recvs, group_sends, group_recvs, local_sems,
    everyone=False,
):
    view_at, chan_at, y, c = place()
    mate, opposite = (view_at, 2 * y + 1 - c), (view_at, 2 * (1 - y) + c)
    diagonal = (view_at, 2 * (1 - y) + 1 - c)
    half_peers, group = half_group(views), view_group(views)
    quarter, depth = x.shape[1], x.shape[2]
    width = h3.shape[2]
    block = quarter // PIX
    views_own = 4 * block
    parts = act.reshape(2, 2, 2, quarter, act.shape[3])
    out_part, in_part = parts.at[0], parts.at[1]
    xm = h3.at[pl.ds(0, 2)]
    near, far = 2 * y + c, 2 * (1 - y) + c
    near_rows = pl.ds(pl.multiple_of(2 * depth * y, 2 * depth), 2 * depth)
    far_rows = pl.ds(pl.multiple_of(2 * depth * (1 - y), 2 * depth), 2 * depth)
    met = greet([], [all_group(views)]) if everyone else greet([opposite, diagonal], [half_peers])
    local = Local(local_sems)
    w1_here = local.fetch(w1in.at[near_rows], w1.at[near])
    perm_here = local.fetch(perm_any, perm)
    x_own = [local.fetch(x_any.at[2 * q + c], x.at[2 * q + c]) for q in range(2)]
    w2_here = local.fetch(w2in, w2.at[c])
    unperm_here = local.fetch(unperm_any, unperm)
    rest = [local.fetch(w3in.at[near_rows], w3.at[near])]
    for at, vector in enumerate((g1, b1, g2, b2)):
        small[at : at + 1] = vector[...]
        small[4 + at : 5 + at] = vector[...]
    smalls[chan_at] = small[...]
    pad[...] = jnp.zeros(pad.shape, pad.dtype)
    met()
    mail = Mail(sends, recvs)
    w1_mate = mail.send(w1in.at[near_rows], w1.at[near], mate)
    x_mate = [mail.send(x_any.at[1 - c], xm.at[0], mate)]
    w1_far = mail.send(w1in.at[far_rows], w1.at[near], opposite)
    x_mate.append(mail.send(x_any.at[3 - c], xm.at[1], mate))
    small_copies = [mail.send(small, smalls.at[chan_at], to) for to in (mate, opposite, diagonal)]
    w2_mate = mail.send(w2in, w2.at[c], mate)
    w3_mate = mail.send(w3in.at[near_rows], w3.at[near], mate)

    def part_copy(half, q):
        return pltpu.make_async_remote_copy(
            src_ref=out_part.at[half, q],
            dst_ref=in_part.at[half, q],
            send_sem=part_sends.at[half, q],
            recv_sem=part_recvs.at[half, q],
            device_id=opposite,
            device_id_type=MESH,
        )

    own_in, mate_in = (
        pl.ds(pl.multiple_of(depth * k, depth), depth) for k in (c, 1 - c)
    )

    def send_part(half, q):
        def weight(rows):
            return jnp.concatenate([w1[2 * half, rows], w1[2 * half + 1, rows]], axis=1)

        value = dot(x[2 * q + c], weight(own_in)) + dot(xm[q], weight(mate_in))
        out_part[half, q] = dot(perm[...], value.astype(BF16)).astype(BF16)
        part_copy(half, q).start()

    w1_here.wait()
    w1_mate.wait_recv()
    perm_here.wait()
    for q in range(2):
        x_own[q].wait()
        x_mate[q].wait_recv()
        send_part(y, q)
    w1_far.wait_recv()
    w1_on = mail.send(w1.at[far], w1.at[far], mate)
    w1_on.wait_recv()
    for q in range(2):
        send_part(1 - y, q)
    x_rest = [local.fetch(x_any.at[2 * q + 1 - c], x.at[2 * q + 1 - c]) for q in range(2)]
    w2_here.wait()
    w2_mate.wait_recv()
    rest.append(local.fetch(w2, w2_out))
    own_rows = pl.ds(pl.multiple_of(depth * c, depth), depth)
    w1_own[...] = jnp.concatenate([w1[k, own_rows] for k in range(4)], axis=1)
    st[...] = jnp.zeros(st.shape, st.dtype)
    step_rows = quarter // SIDE

    def sums(half):
        def one(q, carry):
            part_copy(half, q).wait_recv()

            def rows_of(at, inner):
                rows = pl.ds(at * step_rows, step_rows)
                value = out_part[half, q, rows].astype(F32) + in_part[half, q, rows].astype(F32)
                h1[half, q, rows] = value
                st[half, 0:1] += jnp.sum(value, axis=0, keepdims=True)
                st[half, 1:2] += jnp.sum(value * value, axis=0, keepdims=True)
                return inner

            return lax.fori_loop(0, SIDE, rows_of, carry)

        lax.fori_loop(0, 2, one, 0)

    sums(1 - y)
    sums(y)
    for half in range(2):
        for q in range(2):
            part_copy(half, q).wait_send()
    share_start(st, slots, half_sends.at[0], half_recvs.at[0], half_peers)
    w3_far = mail.send(w3in.at[far_rows], w3.at[near], opposite)
    channels = pad.shape[4]
    early_taps = []
    for tap in range(EARLY_TAPS):
        rows = pl.ds(tap * channels, channels)
        early_taps.append(mail.send(w2in.at[rows], w2_far.at[c, rows], opposite))
    share_end(st, slots, half_sends.at[0], half_recvs.at[0], half_peers)
    totals = add_slots(slots, half_peers[0])
    count = float(views * 4 * quarter)
    for copy in small_copies:
        copy.wait_recv()
    mean = totals[:, 0:1] / count
    rstd = lax.rsqrt(totals[:, 1:2] / count - mean * mean + EPS)
    stat[...] = jnp.concatenate([mean, rstd], axis=1)
    for half in range(2):
        gains = jnp.concatenate([smalls[2 * half], smalls[2 * half + 1]], axis=1)
        scale = rstd[half] * gains[0:1]
        bias = gains[1:2] - mean[half] * scale

        def act_rows(at, carry, half=half, scale=scale, bias=bias):
            q, i = lax.div(at, SIDE), lax.rem(at, SIDE)
            level = h1[half, q, pl.ds(i * step_rows, step_rows)] * scale + bias
            value = (level * gate(level)).astype(BF16)
            pad[q, i + 1, 1 : SIDE + 1, :, 256 * half : 256 * half + 256] = value.reshape(
                SIDE, step_rows // SIDE, 256
            )
            return carry

        lax.fori_loop(0, 2 * SIDE, act_rows, 0)
    rest.append(local.fetch(pad, pad_out))
    rest.append(local.fetch(h1, h1_out))
    w3_far.wait_recv()
    w3_on = mail.send(w3.at[far], w3.at[far], mate)
    st2[...] = jnp.zeros(st2.shape, F32)

    def convolve(q, carry):
        for tap in range(9):
            a, b = tap // 3, tap % 3
            window = pad[q, a : a + SIDE, b : b + SIDE].reshape(quarter, channels)
            taps = slice(tap * channels, (tap + 1) * channels)
            term = dot(window, jnp.concatenate([w2[0, taps], w2[1, taps]], axis=1))
            if tap == 0:
                hidden[q] = term
            else:
                hidden[q] += term
        value = hidden[q]
        h2[q] = value.astype(BF16)
        st2[0:1] += jnp.sum(value, axis=0, keepdims=True)
        st2[1:2] += jnp.sum(value * value, axis=0, keepdims=True)
        return carry

    lax.fori_loop(0, 2, convolve, 0)
    share_start(st2, slots2, half_sends.at[1], half_recvs.at[1], half_peers)
    rest.append(local.fetch(h2, h2_near))
    w2_on = []

    def pass_on(taps):
        for tap in taps:
            early_taps[tap].wait_recv()
            rows = pl.ds(tap * channels, channels)
            w2_on.append(mail.send(w2_far.at[c, rows], w2_far.at[c, rows], mate))

    pass_on(range(EARLY_TAPS - 1))
    share_end(st2, slots2, half_sends.at[1], half_recvs.at[1], half_peers)
    totals2 = add_slots(slots2, half_peers[0])
    mean2 = totals2[0:1] / count
    rstd2 = lax.rsqrt(totals2[1:2] / count - mean2 * mean2 + EPS)
    stats2[y] = jnp.concatenate([mean2, rstd2], axis=0)
    gains = jnp.concatenate([smalls[2 * y], smalls[2 * y + 1]], axis=1)
    scale2 = rstd2 * gains[2:3]
    bias2 = gains[3:4] - mean2 * scale2
    across, beside = [], []
    unperm_here.wait()
    for q in range(2):
        level = hidden[q] * scale2 + bias2
        value = (level * gate(level)).astype(BF16)
        act[y, 2 * q + c] = dot(unperm[...], value).astype(BF16)
        spot = act.at[y, 2 * q + c]
        across.append(mail.send(spot, spot, opposite))
        beside.append(mail.send(spot, spot, mate))
    pass_on(range(EARLY_TAPS - 1, EARLY_TAPS))
    stat2_far = mail.send(stats2.at[y], stats2.at[y], opposite)

    own_out = pl.ds(pl.multiple_of(width * c, width), width)
    st3[...] = jnp.zeros(st3.shape, F32)
    head_first_here = local.fetch(head_first_any, head_first)
    head_last_here = local.fetch(head_last_any, head_last)
    for copy in (w3_mate, w3_on):
        copy.wait_recv()
    rest[0].wait()
    w3_kept = local.fetch(w3, w3_out)

    def last_conv(q):
        total = None
        for half in range(2):
            weight = jnp.concatenate([w3[2 * half, own_out], w3[2 * half + 1, own_out]], axis=1)
            term = dot_nt(act[half, q], weight)
            total = term if total is None else total + term
        low = total.astype(BF16)
        h3[q] = low
        value = low.astype(F32)
        st3[0:1] += jnp.sum(value, axis=0, keepdims=True)
        st3[1:2] += jnp.sum(value * value, axis=0, keepdims=True)

    for row, column in ((sub_row, sub_col), (image_row, image_col), (partner_row, partner_col)):
        columns_of(row, column)
    for q in range(2):
        across[q].wait_recv()
        spot = act.at[1 - y, 2 * q + c]
        passed = mail.send(spot, spot, mate)
        last_conv(2 * q + c)
        beside[q].wait_recv()
        passed.wait_recv()
        last_conv(2 * q + 1 - c)
    for copy in w2_on:
        copy.wait_recv()
    act_kept = local.fetch(act, act_out)
    middle_rows = pl.ds(EARLY_TAPS * channels, MIDDLE_TAPS * channels)
    w2_middle = mail.send(w2in.at[middle_rows], w2_far.at[c, middle_rows], opposite)
    share_start(st3, slots3, group_sends.at[0], group_recvs.at[0], group)
    rest.append(local.fetch(h3, h3_out))
    share_end(st3, slots3, group_sends.at[0], group_recvs.at[0], group)
    totals = add_slots(slots3, views)
    count = float(views * 4 * quarter)
    mean = totals[0:1] / count
    rstd = lax.rsqrt(totals[1:2] / count - mean * mean + EPS)
    stat3[...] = jnp.concatenate([mean, rstd], axis=0)
    scale = rstd * gain_last[...]
    bias = shift_last[...] - mean * scale
    for copy in x_rest:
        copy.wait()

    def pool_block(q, carry):
        before = x[q].astype(F32) + (h3[q].astype(F32) * scale + bias)
        sums = view_sums(before * gate(before), block)
        pooled_own[pl.ds(pl.multiple_of(q * block, block), block)] = sums * (1.0 / PIX)
        return carry

    lax.fori_loop(0, 4, pool_block, 0)
    head_first_here.wait()
    hidden = join_rows(dot(split_rows(pooled_own[...]), head_first[...]))
    wide = hidden.shape[1] // 2
    part[0] = hidden[:, :wide]
    part[1] = hidden[:, wide:]
    swap = mail.send(part, part_in.at[pl.ds(0, 2)], mate)

    def slope_block(q, carry):
        level3 = h3[q].astype(F32)
        before = x[q].astype(F32) + (level3 * scale + bias)
        low = silu_slope(before).astype(BF16)
        slope[q] = low
        normed = (level3 - mean) * rstd
        kept = low.astype(F32)
        rows = pl.ds(pl.multiple_of(q * block, block), block)
        slope_sums[0, rows] = view_sums(kept, block)
        slope_sums[1, rows] = view_sums(kept * normed, block)
        return carry

    swap.wait()
    mean_sums[...] = part[...] + part_in[0:2]
    across_p1 = mail.send(mean_sums.at[c], part_in.at[2], opposite)
    lax.fori_loop(0, 2, slope_block, 0)
    across_p1.wait_recv()
    part_in[4 + c] = mean_sums[c] + part_in[2]
    gathered = mail.send(part_in.at[4 + c], part_in.at[4 + c], mate)
    h2_over = mail.send(h2, h2_far, opposite)
    w2_middle.wait_recv()
    w2_middle_on = mail.send(w2_far.at[c, middle_rows], w2_far.at[c, middle_rows], mate)
    before_late = (EARLY_TAPS + MIDDLE_TAPS) * channels
    late_rows = pl.ds(before_late, w2in.shape[0] - before_late)
    w2_over = mail.send(w2in.at[late_rows], w2_far.at[c, late_rows], opposite)
    gathered.wait_recv()
    p1 = part_in[4:6]
    st4[0:2] = jnp.sum(p1, axis=1)
    st4[2:4] = jnp.sum(p1 * p1, axis=1)
    share_start(st4, slots4, group_sends.at[1], group_recvs.at[1], group)
    lax.fori_loop(2, 4, slope_block, 0)
    slope_kept = local.fetch(slope, slope_out)
    share_end(st4, slots4, group_sends.at[1], group_recvs.at[1], group)
    totals4 = add_slots(slots4, views)
    count4 = float(views * views_own)
    mean4 = totals4[0:2] / count4
    rstd4 = lax.rsqrt(totals4[2:4] / count4 - mean4 * mean4 + EPS)
    head_last_here.wait()

    def level4(half):
        cols = slice(half * wide, (half + 1) * wide)
        normed = (part_in[4 + half] - mean4[half : half + 1]) * rstd4[half : half + 1]
        return normed, normed * gain_head[:, cols] + shift_head[:, cols]

    embed = None
    for half in range(2):
        normed, level = level4(half)
        value = level * gate(level)
        act4[half] = value
        term = join_rows(dot(split_rows(value), head_last[half * wide : (half + 1) * wide]))
        embed = term if embed is None else embed + term
    embed_own[...] = embed
    share_start(embed_own, embed_all, group_sends.at[2], group_recvs.at[2], group)
    share_end(embed_own, embed_all, group_sends.at[2], group_recvs.at[2], group)
    pooled_mean = jnp.sum(pooled_own[...], axis=0, keepdims=True) / views_own
    bk3[2:3] = pooled_mean
    pooled_low[...] = (pooled_own[...] - pooled_mean).astype(BF16)
    gather_start(pooled_low, pooled_all, group_sends.at[5], group_recvs.at[5], group)
    rest.append(local.fetch(pooled_low, pooled_all.at[view_at]))
    own_rows = pl.ds(pl.multiple_of(view_at * views_own, views_own), views_own)
    every = embed_all.reshape(views * views_own, embed.shape[1])
    loss, grad_embed = whiten(
        every, sub_col, image_col, image_row, partner_col, partner_row,
        (work, inverse, white, unit, unit_parts, back), own_rows,
    )
    loss_out[...] = loss
    grad_embed_out[...] = grad_embed
    stacked = split_rows(grad_embed)
    for half in range(2):
        normed, level = level4(half)
        grad = join_rows(dot_nt(stacked, head_last[half * wide : (half + 1) * wide]))
        grad = grad * silu_slope(level)
        part[half] = grad
        bk4[half : half + 1] = jnp.sum(grad, axis=0, keepdims=True)
        bk4[2 + half : 3 + half] = jnp.sum(grad * normed, axis=0, keepdims=True)
    tot4 = share(bk4, bslots4, group_sends.at[3], group_recvs.at[3], group)
    grad_pooled = None
    for half in range(2):
        cols = slice(half * wide, (half + 1) * wide)
        normed, level = level4(half)
        shift_sum, gain_sum = tot4[half : half + 1], tot4[2 + half : 3 + half]
        grad_shift_head[:, cols] = shift_sum
        grad_gain_head[:, cols] = gain_sum
        grad = (
            gain_head[:, cols]
            * rstd4[half : half + 1]
            * (part[half] - shift_sum / count4 - normed * (gain_sum / count4))
        )
        grad_p1[half] = grad
        term = join_rows(dot_nt(split_rows(grad), head_first[:, cols]))
        grad_pooled = term if grad_pooled is None else grad_pooled + term
    grad_pooled = grad_pooled * (1.0 / PIX)
    grad_pooled_out[...] = grad_pooled
    bk3[0:1] = jnp.sum(grad_pooled * slope_sums[0], axis=0, keepdims=True)
    bk3[1:2] = jnp.sum(grad_pooled * slope_sums[1], axis=0, keepdims=True)
    share_start(bk3, bslots3, group_sends.at[4], group_recvs.at[4], group)
    share_end(bk3, bslots3, group_sends.at[4], group_recvs.at[4], group)
    tot3 = add_slots(bslots3, views)
    grad_shift_last[...] = tot3[0:1]
    grad_gain_last[...] = tot3[1:2]
    own_count = float(4 * quarter)
    normed_sum = (st3[0:1] - own_count * mean) * rstd
    rows_sum[...] = scale * (
        bk3[0:1] - tot3[0:1] * (own_count / count) - normed_sum * (tot3[1:2] / count)
    )
    pooled_means[...] = bslots3[:, 2]

    def finish():
        w2_over.wait_recv()
        w2_last = mail.send(w2_far.at[c, late_rows], w2_far.at[c, late_rows], mate)
        h2_over.wait_recv()
        stat2_far.wait_recv()
        w2_last.wait_recv()
        w2_middle_on.wait_recv()
        share_end(pooled_low, pooled_all, group_sends.at[5], group_recvs.at[5], group)
        for copy in [*rest[1:], w3_kept, act_kept]:
            copy.wait()
        for copy in mail.copies:
            if copy is not swap:
                copy.wait_send()

    slope_kept.wait()
    if everyone:
        return finish
    finish()
    return None


def front_specs(views, x, weights):
    conv_mid, head_first, head_last = weights[1], weights[3], weights[4]
    quarter, depth = x.shape[0] // 4, x.shape[1]
    width = depth
    mid = conv_mid.shape[1] * 4
    half = mid // 2
    block = quarter // PIX
    own = 4 * block
    total = views * own
    hid, emb = head_last.shape
    wide = hid // 2
    subs = total // SUB
    peers = 2 * views
    vm = pltpu.VMEM
    wide_rows = (4, quarter, width)
    outs = (
        shape(2, PAD, PAD, block, mid, kind=BF16),
        shape(2, 2, quarter, half),
        shape(2, *conv_mid.shape, kind=BF16),
        shape(2, *conv_mid.shape, kind=BF16),
        shape(4, 2 * depth, mid // 4, kind=BF16),
        shape(2, 4, quarter, half, kind=BF16),
        shape(*wide_rows, kind=BF16),
        shape(*wide_rows, kind=BF16),
        shape(views, own, width, kind=BF16),
        shape(2, quarter, half, kind=BF16),
        shape(2, quarter, half, kind=BF16),
        shape(2, 2, half),
        shape(depth, mid, kind=BF16),
        shape(4, 8, mid // 4),
        shape(2, width),
        shape(1, width),
        shape(1, width),
        shape(1, hid),
        shape(1, hid),
        shape(own, width),
        shape(2, own, wide),
        shape(own, emb),
        shape(2, own, wide),
        shape(1, 1),
        shape(2, 2, half),
        shape(views, width),
        shape(1, width),
    )
    scratch = [
        vm(wide_rows, BF16),
        vm((4, 2 * depth, mid // 4), BF16),
        vm((2, 4, quarter, half), BF16),
        vm(wide_rows, BF16),
        vm((2, 2, quarter, half), F32),
        vm((2, 2, half), F32),
        vm((peers, 2, 2, half), F32),
        vm((2, half), F32),
        vm((peers, 2, half), F32),
        vm((quarter, quarter), BF16),
        vm((quarter, quarter), BF16),
        vm((2, PAD, PAD, block, mid), BF16),
        vm((2, *conv_mid.shape), BF16),
        vm((4, 2 * depth, mid // 4), BF16),
        vm((2, quarter, half), F32),
        vm((2, quarter, half), BF16),
        vm((8, mid // 4), F32),
        vm(head_first.shape, BF16),
        vm(head_last.shape, BF16),
        vm(wide_rows, BF16),
        vm((own, width), F32),
        vm((own, width), BF16),
        vm((total, 128), F32),
        vm((total, 128), F32),
        vm((total, 128), F32),
        vm((views, own, emb), F32),
        vm((2, own, wide), F32),
        vm((6, own, wide), F32),
        vm((2, own, wide), F32),
        vm((2, own, width), F32),
        vm((2, width), F32),
        vm((views, 2, width), F32),
        vm((4, wide), F32),
        vm((views, 4, wide), F32),
        vm((4, wide), F32),
        vm((views, 4, wide), F32),
        vm((3, width), F32),
        vm((views, 3, width), F32),
        vm((own, emb), F32),
        vm((subs, emb, 2 * emb), F32),
        vm((subs, emb, emb), F32),
        vm((total, emb), F32),
        vm((total, emb), F32),
        vm((total, 3 * emb), BF16),
        vm((total, emb), F32),
        dma(40),
        dma(40),
        dma(2, 2),
        dma(2, 2),
        dma(2, peers),
        dma(2, peers),
        dma(6, views),
        dma(6, views),
        dma(32),
    ]
    return outs, scratch


def front_stage(views, x, weights, vectors, tables, perm, unperm):
    conv_first, conv_mid, conv_last, head_first, head_last = weights
    outs, scratch = front_specs(views, x, weights)
    return call(
        functools.partial(front_body, views),
        "front",
        outs,
        19,
        scratch,
        collective=1,
        any_ins=range(11, 19),
        any_outs=range(11),
    )(
        *vectors, *tables, x.reshape(4, x.shape[0] // 4, x.shape[1]), conv_first, conv_mid, conv_last,
        perm, unperm, head_first, head_last,
    )


def link_kind(rows):
    return BF16 if rows % 16 == 0 else F32


def back_body(
    views, stat3, grad_shift_last, grad_gain_last, grad_pooled, gain_last, expand,
    stats2, smalls, stat1, act4, grad_embed, grad_p1, pooled_means, rows_sum,
    h3_any, slope_any, w3_any, h2_near_any, h2_far_any, perm_any, unperm_any, pad_any, h1q_any, w2_any,
    w2_far_any, act_any, x_any, pooled_any,
    gh1_out, mid_slots, pair_out, head_last_out, head_first_out,
    grad_shift_mid, grad_gain_mid, grad_shift_first, grad_gain_first,
    h3, slope, w3, h2_near, h2_far, gh1, gh3, gh3_mate, out_part, in_part, ga2, gh2_far, gpad, ga1, st, sum_parts, chan_slots, view_slots,
    order, pad, h1q, w2, w2_far, act, pooled,
    wsum, mid_parts, mid_in, last_parts, last_in, last_slots, first_parts, first_in, first_slots, means, mean_slots, pair_parts,
    hl_parts, hl_slots, p1_parts, p1_slots,
    sends, recvs, chan_sends, chan_recvs, group_sends, group_recvs, pair_sends, pair_recvs,
    pair1_sends, pair1_recvs, pair2_sends, pair2_recvs, local_sems,
    resident=None,
):
    view_at, chan_at, y, c = place()
    mate, opposite = (view_at, 2 * y + 1 - c), (view_at, 2 * (1 - y) + c)
    group, chans, everyone = view_group(views), chan_group(), all_group(views)
    quarter, width = h3.shape[1], h3.shape[2]
    block = quarter // PIX
    half_width = h2_near.shape[2]
    met = (lambda: None) if resident else greet([], [everyone])
    to_pixels, to_views = (perm_any, unperm_any) if resident else (order, order)
    local = Local(local_sems)
    near_half, own_half = [2 * i + 1 - c for i in (1 - y, y)], [2 * i + c for i in (1 - y, y)]
    rows_here = []

    def fetch_rows(q):
        if not resident:
            rows_here.append((local.fetch(h3_any.at[q], h3.at[q]), local.fetch(slope_any.at[q], slope.at[q])))
        else:
            rows_here.append(())

    for q in near_half:
        fetch_rows(q)
    count = float(views * 4 * quarter)
    mean, rstd = stat3[0:1], stat3[1:2]
    scale = rstd * gain_last[...]
    shift_part, gain_part = grad_shift_last[...] / count, grad_gain_last[...] / count

    def grad_rows(q):
        rows = pl.ds(pl.multiple_of(q * block, block), block)
        high, low = split_pair(grad_pooled[rows])
        spread = dot(expand[...], jnp.concatenate([high, low], axis=0))
        grad = spread * slope[q].astype(F32)
        normed = (h3[q].astype(F32) - mean) * rstd
        gh3[q] = (scale * (grad - shift_part - normed * gain_part)).astype(BF16)

    mate_out = pl.ds(pl.multiple_of(width * (1 - c), width), width)
    own_out = pl.ds(pl.multiple_of(width * c, width), width)

    def part_of(i):
        def weight(rows):
            return jnp.concatenate([w3[k, rows] for k in range(4)], axis=1)

        value = dot(gh3[2 * i + c], weight(own_out)) + dot(gh3_mate[i], weight(mate_out))
        return dot(to_pixels[...], value.astype(BF16))

    mail = Mail(sends, recvs)
    beside = []
    for at, i in enumerate((1 - y, y)):
        for copy in rows_here[at]:
            copy.wait()
        grad_rows(2 * i + 1 - c)
        if at == 0:
            met()
        beside.append(mail.send(gh3.at[2 * i + 1 - c], gh3_mate.at[i], mate))
        if at == 0:
            for q in own_half:
                fetch_rows(q)
            w3_here = local.fetch(w3_any, w3)
            perm_here = local.fetch(perm_any, order)
    for at, i in enumerate((1 - y, y)):
        for copy in rows_here[2 + at]:
            copy.wait()
        grad_rows(2 * i + c)
        if at == 0:
            w3_here.wait()
            perm_here.wait()
            beside[0].wait_recv()
            value = part_of(1 - y).astype(BF16)
            for half in range(2):
                out_part[half] = value[:, half * half_width : (half + 1) * half_width]
            across = [mail.send(out_part.at[half], in_part.at[half], opposite) for half in range(2)]
            if resident:
                resident()
            h2_here = [local.fetch(h2_near_any, h2_near), local.fetch(h2_far_any, h2_far)]
            act_here = local.fetch(act_any, act)
            w2_here = local.fetch(w2_any, w2)
            w2_far_here = local.fetch(w2_far_any, w2_far)
            h1q_here = local.fetch(h1q_any, h1q)
            pad_here = local.fetch(pad_any, pad)
    beside[1].wait_recv()
    ga2[...] = part_of(y)
    unperm_here = local.fetch(unperm_any, order)

    def fold_sems(at):
        return [sems.at[at] for sems in (pair1_sends, pair1_recvs, pair2_sends, pair2_recvs)]

    halves = (y, 1 - y)

    def mid_norm(near):
        half = halves[near]
        gains = jnp.concatenate([smalls[2 * half], smalls[2 * half + 1]], axis=1)
        mean2, rstd2 = stats2[half, 0:1], stats2[half, 1:2]
        return mean2, rstd2, gains[2:3], gains[3:4]

    def half_cols(ref, near):
        low, high = ref[:, :half_width], ref[:, half_width:]
        return jnp.where(halves[near] == 0, low, high)

    for copy in h2_here:
        copy.wait()
    for near, h2 in enumerate((h2_near, h2_far)):
        mean2, rstd2, gain2, shift2 = mid_norm(near)
        normed = (h2[1 - y].astype(F32) - mean2) * rstd2
        grad = out_part[halves[near]].astype(F32) * silu_slope(normed * gain2 + shift2)
        st[halves[near], 0:1] = jnp.sum(grad, axis=0, keepdims=True)
        st[halves[near], 1:2] = jnp.sum(grad * normed, axis=0, keepdims=True)
        normed = (h2[y].astype(F32) - mean2) * rstd2
        kept = silu_slope(normed * gain2 + shift2)
        ga1[:, near * half_width : (near + 1) * half_width] = kept
        grad = half_cols(ga2, near) * kept
        st[halves[near], 0:1] += jnp.sum(grad, axis=0, keepdims=True)
        st[halves[near], 1:2] += jnp.sum(grad * normed, axis=0, keepdims=True)
    share_start(st, view_slots.at[0], group_sends.at[3], group_recvs.at[3], group)

    hid_block, hid_split = hl_parts.shape[1], head_last_out.shape[0]
    for half in range(2):
        product = exact(act4[half], grad_embed[...], 0, 0)
        wsum[0, : product.shape[0]] = product
        per_half = views // 2

        def spread_hidden(to, carry, half=half, per_half=per_half):
            spot = (4 * to + chan_at) * hid_block if hid_split == 4 else to * hid_block
            rows = pl.ds(pl.multiple_of(spot, hid_block), hid_block)
            hl_parts[half * per_half + to] = wsum[0, rows]
            return carry

        lax.fori_loop(0, per_half, spread_hidden, 0)
        wide = grad_p1.shape[2] // per_half
        for to in range(per_half):
            p1_parts[half * per_half + to] = grad_p1[half, :, to * wide : (to + 1) * wide]
    act_here.wait()
    share_rows = last_parts.shape[1]
    means[0:1] = rows_sum[...]
    few_rows = quarter // SIDE
    for half in range(2):
        cols = slice(half * half_width, (half + 1) * half_width)
        sampled = [jnp.sum(act[half, q, :few_rows].astype(F32), axis=0, keepdims=True) for q in range(4)]
        means[1:2, cols] = sum(sampled) / (4 * few_rows)
    for half in range(2):
        cols = slice(half * half_width, (half + 1) * half_width)
        total = None
        for q in range(4):
            term = dot_tn(gh3[q], act[half, q])
            total = term if total is None else total + term
        wsum[0, :width] = total[:, : half_width // 2]
        wsum[1, :width] = total[:, half_width // 2 :]
        low = (
            jnp.concatenate([wsum[0, :width], wsum[1, :width]], axis=1)
            - outer_product(means[0:1], means[1:2, cols])
        ).astype(last_parts.dtype)
        for to in range(views):
            last_parts[to, :, half * half_width : (half + 1) * half_width] = low[
                to * share_rows : (to + 1) * share_rows
            ]
    share_end(st, view_slots.at[0], group_sends.at[3], group_recvs.at[3], group)
    sum_parts[0] = add_slots(view_slots.at[0], views)
    sums_beside = mail.send(sum_parts.at[0], sum_parts.at[1], mate)
    scatter_start(hl_parts, hl_slots, group_sends.at[0], group_recvs.at[0], group)
    scatter_start(p1_parts, p1_slots, group_sends.at[1], group_recvs.at[1], group)
    share_start(means, mean_slots, group_sends.at[2], group_recvs.at[2], group)
    fold_last = Fold(last_parts, last_in, last_slots, fold_sems(0), views)
    fold_last.start()
    sums_beside.wait_recv()
    sum_parts[2] = sum_parts[0] + sum_parts[1]
    sums_across = mail.send(sum_parts.at[2], sum_parts.at[3], opposite)
    for copy in beside:
        copy.wait_send()
    x = x_any if resident else gh3
    x_here = local.fetch(x_any, x)

    gpad[...] = jnp.zeros(gpad.shape, gpad.dtype)
    for half in range(2):
        across[half].wait()
        cols = slice(half * half_width, (half + 1) * half_width)
        ga2[:, cols] += in_part[half].astype(F32)
    gh2 = out_part
    sums_across.wait_recv()
    sum_parts[4] = sum_parts[2] + sum_parts[3]
    for near, h2 in enumerate((h2_near, h2_far)):
        mean2, rstd2, gain2, shift2 = mid_norm(near)
        tot = sum_parts[4, halves[near]]
        normed = (h2[y].astype(F32) - mean2) * rstd2
        grad = half_cols(ga2, near) * ga1[:, near * half_width : (near + 1) * half_width]
        low = (gain2 * rstd2 * (grad - tot[0:1] / count - normed * (tot[1:2] / count))).astype(BF16)
        gh2[near] = low
        gpad[near, 1 : SIDE + 1, 1 : SIDE + 1] = low.reshape(SIDE, SIDE, block, half_width)
    tot = sum_parts[4, y]
    own_cols = jnp.where(c == 0, tot[:, : half_width // 2], tot[:, half_width // 2 :])
    grad_shift_mid[...] = own_cols[0:1]
    grad_gain_mid[...] = own_cols[1:2]
    far_copy = mail.send(gh2.at[1], gh2_far, opposite)
    fold_last.pass_on(1, fold_last.size + 1)
    w2_here.wait()
    w2_far_here.wait()
    channels = w2.shape[1] // 9
    for tap in range(9):
        a, b = 2 - tap // 3, 2 - tap % 3
        taps = slice(tap * channels, (tap + 1) * channels)
        term = None
        for near, weight in enumerate((w2, w2_far)):
            window = gpad[near, a : a + SIDE, b : b + SIDE].reshape(quarter, half_width)
            both = jnp.concatenate([weight[0, taps], weight[1, taps]], axis=1)
            piece = dot_nt(window, both)
            term = piece if term is None else term + piece
        if tap == 0:
            ga1[...] = term
        else:
            ga1[...] += term
    h1q_here.wait()

    def first_norm(half, quarter_at):
        gains = jnp.concatenate([smalls[2 * half], smalls[2 * half + 1]], axis=1)
        normed = (h1q[half, quarter_at] - stat1[half, 0:1]) * stat1[half, 1:2]
        return normed, gains[0:1], gains[1:2], gains[0:1] * stat1[half, 1:2]

    for half in range(2):
        cols = slice(half * half_width, (half + 1) * half_width)
        normed, gain1, shift1, scale1 = first_norm(half, y)
        grad = ga1[:, cols] * silu_slope(normed * gain1 + shift1)
        ga2[:, cols] = grad
        in_part[half] = (scale1 * grad).astype(BF16)
        st[half, 0:1] = jnp.sum(grad, axis=0, keepdims=True)
        st[half, 1:2] = jnp.sum(grad * normed, axis=0, keepdims=True)
    share_start(st, chan_slots.at[1], chan_sends.at[1], chan_recvs.at[1], chans)
    scaled = []
    for half in range(2):
        spot = gh3_mate.at[0, :, half * half_width : (half + 1) * half_width]
        scaled.append(mail.send(in_part.at[half], spot, opposite))

    pad_here.wait()

    def tap_term(at, tap, grads):
        a, b = tap // 3, tap % 3
        window = pad[at, a : a + SIDE, b : b + SIDE].reshape(quarter, channels)
        return dot_tn(window, grads)

    for tap in range(9):
        total = tap_term(y, tap, gh2[0])
        taps = slice(tap * channels, (tap + 1) * channels)
        wsum[0, taps] = total[:, : half_width // 2]
        wsum[1, taps] = total[:, half_width // 2 :]
    share_end(st, chan_slots.at[1], chan_sends.at[1], chan_recvs.at[1], chans)
    st[...] = add_slots(chan_slots.at[1], 4)
    share_start(st, view_slots.at[1], group_sends.at[4], group_recvs.at[4], group)
    far_copy.wait_recv()
    for tap in range(9):
        total = tap_term(1 - y, tap, gh2_far[...])
        taps = slice(tap * channels, (tap + 1) * channels)
        wsum[0, taps] += total[:, : half_width // 2]
        wsum[1, taps] += total[:, half_width // 2 :]
    mid_rows = mid_parts.shape[1]
    mid_flat = mid_parts.reshape(views * mid_rows, mid_parts.shape[2])
    if mid_parts.dtype == F32:
        mid_mate = mail.send(wsum.at[1 - c], mid_flat, mate)
    else:
        w2_far[0] = wsum[1 - c].astype(BF16)
        mid_mate = mail.send(w2_far.at[0], mid_flat, mate)
    share_end(st, view_slots.at[1], group_sends.at[4], group_recvs.at[4], group)
    totals1 = add_slots(view_slots.at[1], views)
    view_slots[1, 0] = totals1
    tot = view_slots[1, 0, y]
    own_cols = jnp.where(c == 0, tot[:, : half_width // 2], tot[:, half_width // 2 :])
    grad_shift_first[...] = own_cols[0:1]
    grad_gain_first[...] = own_cols[1:2]
    unperm_here.wait()
    gh1_beside = []
    for half in range(2):
        cols = slice(half * half_width, (half + 1) * half_width)
        normed, _, _, scale1 = first_norm(half, y)
        tot = totals1[half]
        low = (scale1 * (ga2[:, cols] - tot[0:1] / count - normed * (tot[1:2] / count))).astype(BF16)
        gh1[half, chan_at] = dot(to_views[...], low).astype(BF16)
        spot = gh1.at[half, chan_at]
        gh1_beside.append(mail.send(spot, spot, mate))
    mid_mate.wait_recv()

    def mid_block(to, carry):
        rows = pl.ds(pl.multiple_of(to * mid_rows, mid_rows), mid_rows)
        mid_parts[to] = (wsum[c, rows] + mid_parts[to].astype(F32)).astype(mid_parts.dtype)
        return carry

    lax.fori_loop(0, views, mid_block, 0)
    fold_mid = Fold(mid_parts, mid_in, mid_slots, fold_sems(1), views, False)
    fold_mid.start()
    scatter_end(p1_parts, p1_slots, group_sends.at[1], group_recvs.at[1], group)
    few = pooled.shape[0]

    def head_first_term(at, total):
        views_at = pl.ds(at * few, few)
        copy = pltpu.make_async_copy(pooled_any.at[views_at], pooled, local_sems.at[29])
        copy.start()
        copy.wait()
        rows = pooled[...].astype(F32).reshape(-1, width)
        return total + exact(rows, p1_slots[views_at].reshape(rows.shape[0], -1), 0, 0)

    head_first_out[...] = over(
        views // few, head_first_term, exact(pooled_means[...], jnp.sum(p1_slots[...], axis=1), 0, 0)
    )
    share_end(means, mean_slots, group_sends.at[2], group_recvs.at[2], group)
    fold_last.end()
    rest, folds = [], []
    cuts = [1 + fold_mid.size * k // 4 for k in range(4)] + [fold_mid.size + 1]
    x_here.wait()
    for half in range(2):
        scaled[half].wait_recv()
        cols = slice(half * half_width, (half + 1) * half_width)
        normed, _, _, scale1 = first_norm(half, 1 - y)
        tot = view_slots[1, 0, half]
        value = gh3_mate[0, :, cols].astype(F32)
        low = (value - scale1 * (tot[0:1] / count + normed * (tot[1:2] / count))).astype(BF16)
        gh1[half, 2 * (1 - y) + c] = dot(to_views[...], low).astype(BF16)
        far_spot = gh1.at[half, 2 * (1 - y) + c]
        gh1_on = mail.send(far_spot, far_spot, mate)
        fold_mid.pass_on(cuts[2 * half], cuts[2 * half + 1])
        gh1_beside[half].wait_recv()
        gh1_on.wait_recv()
        rest.append(local.fetch(gh1.at[half], gh1_out.at[half]))
        total = None
        for q in range(4):
            term = dot_tn(x[q], gh1[half, q])
            total = term if total is None else total + term
        low = total.astype(first_parts.dtype)
        for to in range(views):
            first_parts[half, to] = low[to * share_rows : (to + 1) * share_rows]
        folds.append(Fold(first_parts.at[half], first_in.at[half], first_slots.at[half], fold_sems(2 + half), views))
        folds[half].start()
        fold_mid.pass_on(cuts[2 * half + 1], cuts[2 * half + 2])
    rest.append(local.fetch(mid_parts.at[view_at], mid_slots.at[fold_mid.outer]))

    scatter_end(hl_parts, hl_slots, group_sends.at[0], group_recvs.at[0], group)
    if hid_split == 4:
        head_last_out[chan_at] = add_slots(hl_slots, views)
        gather_start(head_last_out.at[chan_at], head_last_out, chan_sends.at[2], chan_recvs.at[2], chans)
    else:
        head_last_out[0] = add_slots(hl_slots, views)

    def blocks(kind, summed):
        wide = summed.shape[1] // 4
        for to in range(4):
            pair_parts[to, kind] = summed[:, to * wide : (to + 1) * wide]

    def summed_slots(slots):
        def add(at, total):
            return total + slots[at].astype(F32)

        return lax.fori_loop(1, slots.shape[0], add, slots[0].astype(F32))

    everywhere = short_product(mean_slots[:, 0], mean_slots[:, 1])
    ga1[: everywhere.shape[0]] = everywhere
    own_block = pl.ds(pl.multiple_of(view_at * share_rows, share_rows), share_rows)
    blocks(1, summed_slots(last_slots) + ga1[own_block])
    for fold in folds:
        fold.pass_on(1, fold.size + 1)
    for fold in folds:
        fold.end()
    blocks(0, jnp.concatenate([summed_slots(first_slots.at[half]) for half in range(2)], axis=1))
    row_views = views // 4
    to_view = chan_at * row_views + lax.div(view_at, 4)
    slot = lax.rem(view_at, 4)

    def pair_copy(to):
        return pltpu.make_async_remote_copy(
            src_ref=pair_parts.at[to],
            dst_ref=pair_out.at[slot],
            send_sem=pair_sends.at[to],
            recv_sem=pair_recvs.at[slot],
            device_id=(to_view, to),
            device_id_type=MESH,
        )

    def pair_arrival(origin):
        return pltpu.make_async_remote_copy(
            src_ref=pair_parts.at[0],
            dst_ref=pair_out.at[origin],
            send_sem=pair_sends.at[0],
            recv_sem=pair_recvs.at[origin],
            device_id=(from_view + origin, from_chan),
            device_id_type=MESH,
        )

    from_view, from_chan = 4 * lax.rem(view_at, row_views), lax.div(view_at, row_views)
    for to in range(4):
        own = jnp.logical_and(to_view == view_at, chan_at == to)

        @pl.when(own)
        def _():
            pair_out[slot] = pair_parts[to]

        @pl.when(jnp.logical_not(own))
        def _():
            pair_copy(to).start()

    for origin in range(4):
        own = jnp.logical_and(from_view + origin == view_at, chan_at == from_chan)

        @pl.when(jnp.logical_not(own))
        def _():
            pair_arrival(origin).wait_recv()

    for to in range(4):
        own = jnp.logical_and(to_view == view_at, chan_at == to)

        @pl.when(jnp.logical_not(own))
        def _():
            pair_copy(to).wait_send()

    if hid_split == 4:
        share_end(head_last_out.at[chan_at], head_last_out, chan_sends.at[2], chan_recvs.at[2], chans)
    fold_mid.end()
    for copy in rest:
        copy.wait()
    for copy in mail.copies[4:]:
        copy.wait_send()


def back_specs(views, front_outs):
    pad, w2, w3, act, h3, h2_near = (front_outs[at] for at in (0, 2, 4, 5, 6, 9))
    act4, grad_embed = front_outs[20], front_outs[21]
    h1q, slope, pooled_all, h2_far = front_outs[1], front_outs[7], front_outs[8], front_outs[10]
    perm_dims = (h3.shape[1], h3.shape[1])
    quarter, width = h3.shape[1], h3.shape[2]
    block = quarter // PIX
    own = 4 * block
    mid = pad.shape[4]
    half = mid // 2
    hid, emb = 2 * act4.shape[2], grad_embed.shape[1]
    taps = w2.shape[1]
    hid_split = 4 if hid // views % 32 == 0 else 1
    hid_block = hid // views // hid_split
    mid_kind, row_kind = link_kind(taps // views), link_kind(width // views)
    vm = pltpu.VMEM
    outs = (
        shape(2, 4, quarter, half, kind=BF16),
        shape(views // 2, taps // views, half // 2, kind=mid_kind),
        shape(4, 2, width // views, mid // 4),
        shape(hid_split, hid_block, emb),
        shape(width, hid // views),
        *[shape(1, half // 2)] * 4,
    )
    scratch = [
        vm((4, quarter, width), BF16),
        vm((4, quarter, width), BF16),
        vm(w3.shape, BF16),
        vm(h2_near.shape, BF16),
        vm(h2_near.shape, BF16),
        vm((2, 4, quarter, half), BF16),
        vm((4, quarter, width), BF16),
        vm((2, quarter, width), BF16),
        vm((2, quarter, half), BF16),
        vm((2, quarter, half), BF16),
        vm((quarter, mid), F32),
        vm((quarter, half), BF16),
        vm((2, PAD, PAD, block, half), BF16),
        vm((quarter, mid), F32),
        vm((2, 2, half), F32),
        vm((5, 2, 2, half), F32),
        vm((2, 4, 2, 2, half), F32),
        vm((2, views, 2, 2, half), F32),
        vm(perm_dims, BF16),
        vm(pad.shape, BF16),
        vm(h1q.shape, F32),
        vm(w2.shape, BF16),
        vm(w2.shape, BF16),
        vm(act.shape, BF16),
        vm((min(views, 8), own, width), BF16),
        vm((2, taps, half // 2), F32),
        vm((views, taps // views, half // 2), mid_kind),
        vm((views // 2, taps // views, half // 2), mid_kind),
        vm((views, width // views, mid), row_kind),
        vm((views // 2, width // views, mid), row_kind),
        vm((views // 2, width // views, mid), row_kind),
        vm((2, views, width // views, half), row_kind),
        vm((2, views // 2, width // views, half), row_kind),
        vm((2, views // 2, width // views, half), row_kind),
        vm((2, width), F32),
        vm((views, 2, width), F32),
        vm((4, 2, width // views, mid // 4), F32),
        vm((views, hid_block, emb), F32),
        vm((views, hid_block, emb), F32),
        vm((views, own, hid // views), F32),
        vm((views, own, hid // views), F32),
        dma(20),
        dma(20),
        dma(3, 4),
        dma(3, 4),
        dma(7, views),
        dma(7, views),
        dma(4),
        dma(4),
        *[dma(4, views // 2)] * 4,
        dma(30),
    ]
    return outs, scratch


def back_stage(views, front_outs, x, gain_last, perm, unperm, expand):
    (pad, h1q, w2, w2_far, w3, act, h3, slope, pooled_all, h2_near, h2_far, stat1, _, smalls, stat3,
     grad_shift_last, grad_gain_last, _, _, grad_pooled, act4, grad_embed, grad_p1, _,
     stats2, pooled_means, rows_sum) = front_outs
    outs, scratch = back_specs(views, front_outs)
    return call(
        functools.partial(back_body, views),
        "back",
        outs,
        28,
        scratch,
        collective=4,
        any_ins=range(14, 28),
        any_outs=range(2),
    )(
        stat3, grad_shift_last, grad_gain_last, grad_pooled, gain_last, expand,
        stats2, smalls, stat1, act4, grad_embed, grad_p1, pooled_means, rows_sum,
        h3, slope, w3, h2_near, h2_far, perm, unperm, pad, h1q, w2, w2_far, act,
        x.reshape(4, x.shape[0] // 4, x.shape[1]), pooled_all,
    )


def split_names(body, ins, outs):
    names = tuple(inspect.signature(body).parameters)[1:-1]
    return names[:ins], names[ins : ins + outs], names[ins + outs :]


FRONT_INS, FRONT_OUTS, FRONT_SCRATCH = split_names(front_body, 19, 27)
BACK_INS, BACK_OUTS, BACK_SCRATCH = split_names(back_body, 28, 9)
DROPPED = ("pad_out", "h1_out", "w2_out", "w3_out", "act_out", "h3_out", "h2_near")
KEPT = (
    "slope_out", "pooled_all", "w1_own", "grad_shift_last", "grad_gain_last",
    "grad_shift_head", "grad_gain_head", "grad_pooled_out", "loss_out",
)
SHARED = {
    "h3": "h3", "slope": "slope", "w3": "w3", "h2_near": "h2", "h2_far": "h2_far", "gh1": "act",
    "gh3": "slope", "pad": "pad", "w2": "w2", "w2_far": "w2_far", "act": "act", "h1q": "h1",
}
SAME = {"stat1": "stat", "grad_pooled": "grad_pooled_out", "grad_embed": "grad_embed_out"}


def joined_names():
    held = [name for name in FRONT_OUTS if name not in DROPPED and name not in KEPT]
    fresh = [name for name in BACK_SCRATCH if name not in SHARED and name != "order"]
    return held, fresh


def joined_body(views, *refs):
    held, fresh = joined_names()
    names = [*FRONT_INS, "expand", *KEPT, *BACK_OUTS, *FRONT_SCRATCH, *held]
    env = dict(zip(names, refs))
    back_env = dict(zip(fresh, refs[len(names) :]))
    finish = front_body(views, *[env.get(name) for name in FRONT_INS + FRONT_OUTS + FRONT_SCRATCH], everyone=True)
    for name, other in SHARED.items():
        back_env[name] = env[other]
    for name in BACK_INS:
        if name.endswith("_any"):
            back_env[name] = back_env.get(name[:-4])
    back_env["perm_any"], back_env["unperm_any"] = env["perm"], env["unperm"]
    back_env["x_any"], back_env["pooled_any"] = env["x"], env["pooled_all"]

    def pick(name):
        return back_env[name] if name in back_env else env.get(SAME.get(name, name))

    back_body(views, *[pick(name) for name in BACK_INS + BACK_OUTS + BACK_SCRATCH], resident=finish)


def joined_stage(views, x, weights, vectors, tables, perm, unperm, expand):
    conv_first, conv_mid, conv_last, head_first, head_last = weights
    outs, scratch = front_specs(views, x, weights)
    outs_at = dict(zip(FRONT_OUTS, outs))
    back_outs, back_scratch = back_specs(views, outs)
    back_at = dict(zip(BACK_SCRATCH, back_scratch))
    held, fresh = joined_names()
    front_scratch = dict(zip(FRONT_SCRATCH, scratch))
    more = [pltpu.VMEM(outs_at[name].shape, outs_at[name].dtype) for name in held]
    results = call(
        functools.partial(joined_body, views),
        "joined",
        (*[outs_at[name] for name in KEPT], *back_outs),
        20,
        [*front_scratch.values(), *more, *[back_at[name] for name in fresh]],
        collective=1,
        any_ins=range(11, 19),
        any_outs=(0, 1, len(KEPT), len(KEPT) + 1),
    )(
        *vectors, *tables, x.reshape(4, x.shape[0] // 4, x.shape[1]), conv_first, conv_mid, conv_last,
        perm, unperm, head_first, head_last, expand,
    )
    return dict(zip(KEPT, results)), results[len(KEPT) :]


def last_body(
    small_count, w1_any, grad_pooled, expand, gh1_any, slope_any, mid_any, pair_out, head_last_in, head_first_in, *more
):
    small_ins, outs = more[:small_count], more[small_count : 2 * small_count + 6]
    gh1, w1_own, slope, term, mid_slots, sems = more[2 * small_count + 6 :]
    grad_input, grad_mid, grad_first, grad_last, grad_head_last, grad_head_first, *small_outs = outs
    local = Local(sems)
    quarters, quarter, half = gh1.shape[1], gh1.shape[2], gh1.shape[3]
    w1_here = local.fetch(w1_any, w1_own)
    rows_here = [
        (local.fetch(gh1_any.at[:, q], gh1.at[:, q]), local.fetch(slope_any.at[q], slope.at[q]))
        for q in range(quarters)
    ]
    mid_here = local.fetch(mid_any, mid_slots)
    rest = []
    w1_here.wait()
    block = quarter // PIX
    for q in range(quarters):
        for copy in rows_here[q]:
            copy.wait()
        high, low = split_pair(grad_pooled[q * block : (q + 1) * block])
        spread = dot(expand[...], jnp.concatenate([high, low], axis=0))
        value = dot_nt(gh1[0, q], w1_own[:, :half]) + dot_nt(gh1[1, q], w1_own[:, half:])
        term[q] = value + spread * slope[q].astype(F32)
        rest.append(local.fetch(term.at[q], grad_input.at[q]))
    mid_here.wait()

    def add(slot, total):
        return total + mid_slots[slot].astype(F32)

    grad_mid[...] = lax.fori_loop(1, mid_slots.shape[0], add, mid_slots[0].astype(F32))
    grad_head_first[...] = head_first_in[...]
    for source, target in zip(small_ins, small_outs):
        target[...] = source[...]
    rows = pair_out.shape[2]
    for origin in range(4):
        grad_first[origin * rows : (origin + 1) * rows] = pair_out[origin, 0]
        grad_last[origin * rows : (origin + 1) * rows] = pair_out[origin, 1]
    rows = head_last_in.shape[1]
    for origin in range(head_last_in.shape[0]):
        grad_head_last[origin * rows : (origin + 1) * rows] = head_last_in[origin]
    for copy in rest:
        copy.wait()


def last_stage(
    gh1, w1_own, slope, grad_pooled, expand, mid_slots, pair_out, head_last_in, head_first_in, small
):
    quarter, half, width = gh1.shape[2], gh1.shape[3], slope.shape[2]
    outs = (
        shape(4, quarter, width),
        shape(*mid_slots.shape[1:]),
        shape(4 * pair_out.shape[2], pair_out.shape[3]),
        shape(4 * pair_out.shape[2], pair_out.shape[3]),
        shape(head_last_in.shape[0] * head_last_in.shape[1], head_last_in.shape[2]),
        shape(*head_first_in.shape),
        *[shape(*array.shape) for array in small],
    )
    ins = 9 + len(small)
    return call(
        functools.partial(last_body, len(small)),
        "results",
        outs,
        ins,
        [
            pltpu.VMEM(gh1.shape, BF16),
            pltpu.VMEM(w1_own.shape, BF16),
            pltpu.VMEM(slope.shape, BF16),
            pltpu.VMEM(slope.shape, F32),
            pltpu.VMEM(mid_slots.shape, mid_slots.dtype),
            dma(20),
        ],
        collective=None,
        any_ins=(0, 3, 4, 5),
        any_outs=(0,),
    )(w1_own, grad_pooled, expand, gh1, slope, mid_slots, pair_out, head_last_in, head_first_in, *small)


def per_device(
    views,
    block_input,
    conv_first,
    conv_mid,
    conv_last,
    gain_first,
    shift_first,
    gain_mid,
    shift_mid,
    gain_last,
    shift_last,
    head_first,
    gain_head,
    shift_head,
    head_last,
    image_of,
    partner,
    sub_of,
):
    rows, width = block_input.shape
    quarter = rows // 4
    block = quarter // PIX
    perm, unperm = orders(quarter)
    at_row = np.arange(quarter)
    twice = np.arange(2 * block) % block
    expand = jnp.asarray((at_row[:, None] // PIX == twice[None, :]).astype(BF16))

    def line(vector):
        return vector.reshape(1, -1)

    weights = (conv_first, conv_mid, conv_last, head_first, head_last)
    vectors = [
        line(v)
        for v in (gain_first, shift_first, gain_mid, shift_mid, gain_last, shift_last, gain_head, shift_head)
    ]
    tables = [line(v) for v in (sub_of, image_of, partner)]
    if views <= JOINED_VIEWS:
        kept, back_outs = joined_stage(views, block_input, weights, vectors, tables, perm, unperm, expand)
    else:
        front_outs = front_stage(views, block_input, weights, vectors, tables, perm, unperm)
        kept = dict(zip(FRONT_OUTS, front_outs))
        back_outs = back_stage(views, front_outs, block_input, line(gain_last), perm, unperm, expand)
    slope, w1_own, grad_pooled, loss = (
        kept[name] for name in ("slope_out", "w1_own", "grad_pooled_out", "loss_out")
    )
    (gh1, mid_slots, pair_out, head_last_in, head_first_in,
     grad_shift_mid, grad_gain_mid, grad_shift_first, grad_gain_first) = back_outs
    small = [
        grad_gain_first, grad_shift_first, grad_gain_mid, grad_shift_mid,
        kept["grad_gain_last"], kept["grad_shift_last"], kept["grad_gain_head"], kept["grad_shift_head"], loss,
    ]
    grad_input, grad_mid, grad_first, grad_last, grad_head_last, grad_head_first, *small = last_stage(
        gh1, w1_own, slope, grad_pooled, expand, mid_slots, pair_out, head_last_in, head_first_in, small
    )
    return (
        small[8].reshape(()),
        grad_input.reshape(rows, width),
        grad_first,
        grad_mid,
        grad_last,
        grad_head_first,
        grad_head_last,
        *[vector.reshape(-1) for vector in small[:8]],
    )


def solution(mesh):
    views = mesh.shape["views"]
    return jax.shard_map(
        functools.partial(per_device, views),
        mesh=mesh,
        in_specs=(
            P("views", "chan"),
            P(None, "chan"),
            P(None, "chan"),
            P(None, "chan"),
            P("chan"),
            P("chan"),
            P("chan"),
            P("chan"),
            P("chan"),
            P("chan"),
            P("chan", None),
            P(),
            P(),
            P(),
            P(),
            P(),
            P(),
        ),
        out_specs=(
            P(),
            P("views", "chan"),
            P("views", "chan"),
            P("views", "chan"),
            P("views", "chan"),
            P("chan", "views"),
            P("views", None),
            P("chan"),
            P("chan"),
            P("chan"),
            P("chan"),
            P("chan"),
            P("chan"),
            P(),
            P(),
        ),
        check_vma=False,
    )
```

```python
import functools
import inspect

import jax
import jax.numpy as jnp
import numpy as np
from jax import lax
from jax.experimental import pallas as pl
from jax.experimental.pallas import tpu as pltpu
from jax.sharding import PartitionSpec as P

SIDE = 7
PIX = SIDE * SIDE
PAD = SIDE + 2
SUB = 256
EPS = 1e-05
RIDGE = 0.5
MESH = pl.DeviceIdType.MESH
BF16 = jnp.bfloat16
F32 = jnp.float32
VMEM_BYTES = 62 << 20
JOINED_VIEWS = 8


def place():
    view_at, chan_at = lax.axis_index("views"), lax.axis_index("chan")
    return view_at, chan_at, lax.div(chan_at, 2), lax.rem(chan_at, 2)


def greet(peers, groups=()):
    barrier = pltpu.get_barrier_semaphore()
    total = len(peers)
    for peer in peers:
        pl.semaphore_signal(barrier, inc=1, device_id=peer, device_id_type=MESH)
    for size, own, device in groups:

        def tell(step, carry, size=size, own=own, device=device):
            pl.semaphore_signal(
                barrier, inc=1, device_id=device(lax.rem(own + step, size)), device_id_type=MESH
            )
            return carry

        lax.fori_loop(1, size, tell, 0)
        total += size - 1
    return lambda: pl.semaphore_wait(barrier, total)


class Mail:
    def __init__(self, send_sems, recv_sems):
        self.send_sems, self.recv_sems, self.copies = send_sems, recv_sems, []

    def send(self, source, target, peer):
        spot = len(self.copies)
        copy = pltpu.make_async_remote_copy(
            src_ref=source,
            dst_ref=target,
            send_sem=self.send_sems.at[spot],
            recv_sem=self.recv_sems.at[spot],
            device_id=peer,
            device_id_type=MESH,
        )
        copy.start()
        self.copies.append(copy)
        return copy

    def finish(self):
        for copy in self.copies:
            copy.wait_send()


class Done:
    def wait(self):
        pass


class Local:
    def __init__(self, sems):
        self.sems, self.used = sems, 0

    def fetch(self, source, target):
        if target is None or source is target:
            return Done()
        copy = pltpu.make_async_copy(source, target, self.sems.at[self.used])
        copy.start()
        self.used += 1
        return copy


def group_copy(source, slots, sends, recvs, size, own, device, step):
    to = lax.rem(own + step, size)
    return pltpu.make_async_remote_copy(
        src_ref=source,
        dst_ref=slots.at[own],
        send_sem=sends.at[step],
        recv_sem=recvs.at[own],
        device_id=device(to),
        device_id_type=MESH,
    )


def group_arrival(source, slots, sends, recvs, size, own, device, step):
    origin = lax.rem(own + step, size)
    return pltpu.make_async_remote_copy(
        src_ref=source,
        dst_ref=slots.at[origin],
        send_sem=sends.at[step],
        recv_sem=recvs.at[origin],
        device_id=device(origin),
        device_id_type=MESH,
    )


def share_start(source, slots, sends, recvs, group):
    def start(step, carry):
        group_copy(source, slots, sends, recvs, *group, step).start()
        return carry

    lax.fori_loop(1, group[0], start, 0)
    slots[group[1]] = source[...]


def share_end(source, slots, sends, recvs, group):
    def end(step, carry):
        group_arrival(source, slots, sends, recvs, *group, step).wait_recv()
        group_copy(source, slots, sends, recvs, *group, step).wait_send()
        return carry

    lax.fori_loop(1, group[0], end, 0)


def add_slots(slots, size):
    def add(at, total):
        return total + slots[at]

    return lax.fori_loop(1, size, add, slots[0])


def share(source, slots, sends, recvs, group):
    share_start(source, slots, sends, recvs, group)
    share_end(source, slots, sends, recvs, group)
    return add_slots(slots, group[0])


def gather_start(source, slots, sends, recvs, group):
    def start(step, carry):
        group_copy(source, slots, sends, recvs, *group, step).start()
        return carry

    lax.fori_loop(1, group[0], start, 0)


def scatter_start(parts, slots, sends, recvs, group, keep=True):
    size, own, device = group

    def start(step, carry):
        to = lax.rem(own + step, size)
        group_copy(parts.at[to], slots, sends, recvs, *group, step).start()
        return carry

    lax.fori_loop(1, size, start, 0)
    if keep:
        slots[own] = parts[own]


def scatter_end(parts, slots, sends, recvs, group):
    share_end(parts.at[group[1]], slots, sends, recvs, group)


class Fold:
    def __init__(self, parts, fold_in, slots, sems, views, keep=True):
        view_at, chan_at, _, _ = place()
        self.parts, self.fold_in, self.slots, self.sems, self.keep = parts, fold_in, slots, sems, keep
        self.size, self.outer, self.inner = views // 2, lax.div(view_at, 2), lax.rem(view_at, 2)
        self.pair = (2 * self.outer + 1 - self.inner, chan_at)
        self.chan_at = chan_at

    def block(self, step):
        return lax.rem(self.outer + step, self.size)

    def pair_copy(self, step):
        at = self.block(step)
        return pltpu.make_async_remote_copy(
            src_ref=self.parts.at[2 * at + 1 - self.inner],
            dst_ref=self.fold_in.at[at],
            send_sem=self.sems[0].at[at],
            recv_sem=self.sems[1].at[at],
            device_id=self.pair,
            device_id_type=MESH,
        )

    def out_copy(self, step, slot):
        at = self.block(step)
        return pltpu.make_async_remote_copy(
            src_ref=self.parts.at[2 * at + self.inner],
            dst_ref=self.slots.at[slot],
            send_sem=self.sems[2].at[at],
            recv_sem=self.sems[3].at[slot],
            device_id=(2 * at + self.inner, self.chan_at),
            device_id_type=MESH,
        )

    def start(self):
        def one(step, carry):
            self.pair_copy(step).start()
            return carry

        lax.fori_loop(1, self.size + 1, one, 0)

    def add(self, step):
        self.pair_copy(step).wait_recv()
        at, mine = self.block(step), 2 * self.block(step) + self.inner
        total = self.parts[mine].astype(F32) + self.fold_in[at].astype(F32)
        self.parts[mine] = total.astype(self.parts.dtype)

    def pass_on(self, first, last):
        def one(step, carry):
            self.add(step)
            self.out_copy(step, self.outer).start()
            return carry

        lax.fori_loop(first, min(last, self.size), one, 0)
        if last > self.size:
            self.add(self.size)
            if self.keep:
                self.slots[self.outer] = self.parts[2 * self.outer + self.inner]

    def end(self):
        def one(step, carry):
            self.out_copy(step, self.block(step)).wait_recv()
            self.out_copy(step, self.outer).wait_send()
            return carry

        lax.fori_loop(1, self.size, one, 0)

        def sent(step, carry):
            self.pair_copy(step).wait_send()
            return carry

        lax.fori_loop(1, self.size + 1, sent, 0)


def chan_group():
    view_at, chan_at, y, c = place()
    return (4, chan_at, lambda at: (view_at, at))


def half_group(views):
    view_at, chan_at, y, c = place()
    return (
        2 * views,
        2 * view_at + c,
        lambda at: (lax.div(at, 2), 2 * y + lax.rem(at, 2)),
    )


def view_group(views):
    view_at, chan_at, y, c = place()
    return (views, view_at, lambda at: (at, chan_at))


def all_group(views):
    view_at, chan_at, y, c = place()
    return (4 * views, 4 * view_at + chan_at, lambda at: (lax.div(at, 4), lax.rem(at, 4)))


def dot(left, right):
    return jnp.dot(left, right, preferred_element_type=F32)


def dot_nt(left, right):
    return lax.dot_general(left, right, (((1,), (1,)), ((), ())), preferred_element_type=F32)


def dot_tn(left, right):
    return lax.dot_general(left, right, (((0,), (0,)), ((), ())), preferred_element_type=F32)


def gate(level):
    return 0.5 + 0.5 * jnp.tanh(0.5 * level)


def silu_slope(level):
    open_part = gate(level)
    return open_part * (1.0 + level * (1.0 - open_part))


def call(body, name, outs, ins, scratch, collective, any_ins=(), any_outs=()):
    def spec(at, places):
        return pl.BlockSpec(memory_space=pl.ANY if at in places else pltpu.VMEM)

    return pl.pallas_call(
        body,
        out_shape=outs,
        in_specs=[spec(at, any_ins) for at in range(ins)],
        out_specs=tuple(spec(at, any_outs) for at in range(len(outs))),
        scratch_shapes=scratch,
        name=name,
        compiler_params=pltpu.CompilerParams(
            collective_id=collective,
            has_side_effects=collective is not None,
            vmem_limit_bytes=VMEM_BYTES,
        ),
    )


def shape(*dims, kind=F32):
    return jax.ShapeDtypeStruct(dims, kind)


def dma(*dims):
    return pltpu.SemaphoreType.DMA(dims)


def split_rows(value):
    high = value.astype(BF16)
    rest = value - high.astype(F32)
    middle = rest.astype(BF16)
    low = (rest - middle.astype(F32)).astype(BF16)
    return jnp.concatenate([high, middle, low], axis=0)


def join_rows(stacked):
    rows = stacked.shape[0] // 3
    return stacked[2 * rows :] + stacked[rows : 2 * rows] + stacked[:rows]


def split_pair(value):
    high = value.astype(BF16)
    return high, (value - high.astype(F32)).astype(BF16)


def exact(left, right, left_dim, right_dim):
    return lax.dot_general(
        left,
        right,
        (((left_dim,), (right_dim,)), ((), ())),
        precision=lax.Precision.HIGHEST,
        preferred_element_type=F32,
    )


def over(count, body, start):
    return body(0, start) if count == 1 else lax.fori_loop(0, count, body, start)


def split_three(value):
    high = value.astype(BF16)
    rest = value - high.astype(F32)
    middle = rest.astype(BF16)
    return high, middle, (rest - middle.astype(F32)).astype(BF16)


def short_product(left, right):
    lh, lm, ll = split_three(left)
    rh, rm, rl = split_three(right)
    return dot_tn(
        jnp.concatenate([lh, lh, lm, lh, lm, ll], axis=0),
        jnp.concatenate([rh, rm, rh, rl, rm, rh], axis=0),
    )


def outer_product(left, right):
    def rows(value, high_at, middle_at, low_at):
        parts = [part.astype(F32) for part in split_three(value)]
        row = lax.broadcasted_iota(jnp.int32, (16, value.shape[1]), 0)
        total = jnp.zeros((16, value.shape[1]), F32)
        for part, places in zip(parts, (high_at, middle_at, low_at)):
            for place_at in places:
                total = jnp.where(row == place_at, part, total)
        return total.astype(BF16)

    return dot_tn(rows(left, (0, 1, 3), (2, 4), (5,)), rows(right, (0, 2, 5), (1, 4), (3,)))


def factor_inverse(work, inverse, subs, width):
    panel = 16
    row = lax.broadcasted_iota(jnp.int32, (panel, width), 0)

    def wide(part):
        return jnp.broadcast_to(part, (panel, width))

    def eliminate(s, first):
        rows = work[s, first : first + panel]
        columns = [wide(rows[:, first + j : first + j + 1]) for j in range(panel)]
        diagonal = jnp.zeros((panel, width), F32)
        for j in range(panel):
            pivot = wide(columns[j][j : j + 1])
            diagonal = jnp.where(row == j, pivot, diagonal)
            if j == panel - 1:
                break
            ratio = jnp.where(row > j, columns[j] * (1.0 / pivot), 0.0)
            for k in range(j + 1, panel):
                columns[k] = columns[k] - ratio * wide(columns[k][j : j + 1])
            rows = rows - jnp.concatenate([ratio, ratio], axis=1) * rows[j : j + 1]
        inverse[s, first : first + panel] = rows[:, width:] * lax.rsqrt(diagonal)
        if first + panel < width:
            scaled = rows[:, :width] / diagonal
            work[s, first + panel :] -= short_product(scaled, rows)[first + panel :]

    def some(at, carry):
        for first in range(0, width, panel):
            for k in range(2):
                eliminate(2 * at + k, first)
        return carry

    over(subs // 2, some, 0)


def view_sums(value, block):
    return jnp.concatenate(
        [jnp.sum(value[PIX * v : PIX * (v + 1)], axis=0, keepdims=True) for v in range(block)], axis=0
    )


def columns_of(row, column):
    tile = column.shape[1]

    def one(at, carry):
        cols = pl.ds(pl.multiple_of(at * tile, tile), tile)
        column[cols] = jnp.broadcast_to(row[:, cols].astype(F32), (tile, tile)).T
        return carry

    lax.fori_loop(0, row.shape[1] // tile, one, 0)


def whiten(embed, sub_col, image_col, image_row, partner_col, partner_row, refs, own_rows):
    work, inverse, white, unit, unit_parts, back = refs
    total, width = embed.shape
    subs = inverse.shape[0]
    eye = (
        lax.broadcasted_iota(jnp.int32, (width, width), 0)
        == lax.broadcasted_iota(jnp.int32, (width, width), 1)
    ).astype(F32)
    size = min(total, 512)
    pieces = total // size

    def rows_at(at):
        return pl.ds(pl.multiple_of(at * size, size), size)

    means = []

    def masks(rows, s):
        column = sub_col[rows]
        return (column == float(s)).astype(F32), (column == float(s + 1)).astype(F32)

    for s in range(0, subs, 2):

        def moments(at, sums, s=s):
            rows = rows_at(at)
            value = embed[rows]
            picked = jnp.concatenate([value * mask for mask in masks(rows, s)], axis=1)
            first = sums[0] + jnp.sum(picked, axis=0, keepdims=True)
            return first, sums[1] + exact(picked, value, 0, 0)

        first, second = over(
            pieces, moments, (jnp.zeros((1, 2 * width), F32), jnp.zeros((2 * width, width), F32))
        )
        for k in range(2):
            mean = first[:, k * width : (k + 1) * width] / SUB
            cov = second[k * width : (k + 1) * width] / SUB - exact(mean, mean, 0, 0)
            work[s + k, :, :width] = cov + RIDGE * eye
            work[s + k, :, width:] = eye
            means.append(mean)
    factor_inverse(work, inverse, subs, width)

    def whitening(at, carry):
        rows = rows_at(at)
        value = None
        for s in range(0, subs, 2):
            centred = jnp.concatenate(
                [(embed[rows] - means[s + k]) * mask for k, mask in enumerate(masks(rows, s))], axis=1
            )
            term = exact(centred, jnp.concatenate([inverse[s], inverse[s + 1]], axis=1), 1, 1)
            value = term if value is None else value + term
        white[rows] = value
        value = value * lax.rsqrt(jnp.sum(value * value, axis=1, keepdims=True) + EPS)
        unit[rows] = value
        high = value.astype(BF16)
        rest = value - high.astype(F32)
        middle = rest.astype(BF16)
        unit_parts[rows] = jnp.concatenate(
            [high, middle, (rest - middle.astype(F32)).astype(BF16)], axis=1
        )
        return carry

    over(pieces, whitening, 0)
    chunk = min(total, 262144 // total)

    def pairs(at, loss):
        rows = pl.ds(pl.multiple_of(at * chunk, chunk), chunk)
        across = lax.broadcasted_iota(jnp.int32, (chunk, total), 1).astype(F32)
        down = lax.broadcasted_iota(jnp.int32, (chunk, total), 0) + at * chunk

        def pick(hot):
            found = dot(hot.astype(F32).astype(BF16), unit_parts[...])
            return found[:, 2 * width :] + found[:, width : 2 * width] + found[:, :width]

        mine = unit[rows]
        ahead = pick(partner_col[rows][:, :1] == across)
        behind = pick(partner_row[...] == down)
        members = jnp.sum(
            (image_col[rows][:, :1] == image_row[...].astype(F32)).astype(F32), axis=1, keepdims=True
        )
        weight = 1.0 / members
        apart = mine - ahead
        grad = (4.0 / total) * weight * (2.0 * mine - ahead - behind)
        length = lax.rsqrt(jnp.sum(white[rows] * white[rows], axis=1, keepdims=True) + EPS)
        back[rows] = length * (grad - mine * jnp.sum(mine * grad, axis=1, keepdims=True))
        per_view = jnp.sum(apart * apart, axis=1, keepdims=True) * weight
        return loss + jnp.sum(per_view, axis=0, keepdims=True)

    loss = over(total // chunk, pairs, jnp.zeros((1, 1), F32)) * (2.0 / total)
    lower = lax.broadcasted_iota(jnp.int32, (width, width), 0) >= lax.broadcasted_iota(
        jnp.int32, (width, width), 1
    )
    own_white, own_back = white[own_rows], back[own_rows]
    gradient = jnp.zeros(own_white.shape, F32)
    for s in range(0, subs, 2):

        def pulled(at, sums, s=s):
            rows = rows_at(at)
            picked = jnp.concatenate([back[rows] * mask for mask in masks(rows, s)], axis=1)
            spread = sums[0] + jnp.sum(picked, axis=0, keepdims=True)
            return spread, sums[1] + exact(picked, white[rows], 0, 0)

        spread, sums = over(
            pieces, pulled, (jnp.zeros((1, 2 * width), F32), jnp.zeros((2 * width, width), F32))
        )
        for k, own_mask in enumerate(masks(own_rows, s)):
            cols = slice(k * width, (k + 1) * width)
            low_part = jnp.where(lower, sums[cols], 0.0)
            mirrored = low_part + low_part.T - sums[cols] * eye
            moved = own_back - (exact(own_white, mirrored, 1, 0) + spread[:, cols]) / SUB
            gradient = gradient + own_mask * exact(moved, inverse[s + k], 1, 0)
    return loss, gradient


MIDDLE_TAPS = 3
EARLY_TAPS = 3


def orders(quarter):
    block = quarter // PIX
    row = np.arange(quarter)
    source = (row % block) * PIX + row // block
    hot = (source[:, None] == row[None, :]).astype(BF16)
    return jnp.asarray(hot), jnp.asarray(hot.T)


def front_body(
    views, g1, b1, g2, b2, gain_last, shift_last, gain_head, shift_head, sub_row, image_row, partner_row,
    x_any, w1in, w2in, w3in, perm_any, unperm_any, head_first_any, head_last_any,
    pad_out, h1_out, w2_out, w2_far, w3_out, act_out, h3_out, slope_out, pooled_all, h2_near, h2_far,
    stat, w1_own, smalls, stat3, grad_shift_last, grad_gain_last, grad_shift_head, grad_gain_head,
    grad_pooled_out, act4, grad_embed_out, grad_p1, loss_out, stats2, pooled_means, rows_sum,
    x, w1, act, h3, h1, st, slots, st2, slots2, perm, unperm, pad, w2, w3, hidden, h2, small,
    head_first, head_last, slope, pooled_own, pooled_low, sub_col, image_col, partner_col,
    embed_all, part, part_in, mean_sums, slope_sums, st3, slots3, st4, slots4, bk4, bslots4, bk3, bslots3, embed_own,
    work, inverse, white, unit, unit_parts, back,
    sends, recvs, part_sends, part_recvs, half_sends, half_recvs, group_sends, group_recvs, local_sems,
    everyone=False,
):
    view_at, chan_at, y, c = place()
    mate, opposite = (view_at, 2 * y + 1 - c), (view_at, 2 * (1 - y) + c)
    diagonal = (view_at, 2 * (1 - y) + 1 - c)
    half_peers, group = half_group(views), view_group(views)
    quarter, depth = x.shape[1], x.shape[2]
    width = h3.shape[2]
    block = quarter // PIX
    views_own = 4 * block
    parts = act.reshape(2, 2, 2, quarter, act.shape[3])
    out_part, in_part = parts.at[0], parts.at[1]
    xm = h3.at[pl.ds(0, 2)]
    near, far = 2 * y + c, 2 * (1 - y) + c
    near_rows = pl.ds(pl.multiple_of(2 * depth * y, 2 * depth), 2 * depth)
    far_rows = pl.ds(pl.multiple_of(2 * depth * (1 - y), 2 * depth), 2 * depth)
    met = greet([], [all_group(views)]) if everyone else greet([opposite, diagonal], [half_peers])
    local = Local(local_sems)
    w1_here = local.fetch(w1in.at[near_rows], w1.at[near])
    perm_here = local.fetch(perm_any, perm)
    x_own = [local.fetch(x_any.at[2 * q + c], x.at[2 * q + c]) for q in range(2)]
    w2_here = local.fetch(w2in, w2.at[c])
    unperm_here = local.fetch(unperm_any, unperm)
    rest = [local.fetch(w3in.at[near_rows], w3.at[near])]
    for at, vector in enumerate((g1, b1, g2, b2)):
        small[at : at + 1] = vector[...]
        small[4 + at : 5 + at] = vector[...]
    smalls[chan_at] = small[...]
    pad[...] = jnp.zeros(pad.shape, pad.dtype)
    met()
    mail = Mail(sends, recvs)
    w1_mate = mail.send(w1in.at[near_rows], w1.at[near], mate)
    x_mate = [mail.send(x_any.at[1 - c], xm.at[0], mate)]
    w1_far = mail.send(w1in.at[far_rows], w1.at[near], opposite)
    x_mate.append(mail.send(x_any.at[3 - c], xm.at[1], mate))
    small_copies = [mail.send(small, smalls.at[chan_at], to) for to in (mate, opposite, diagonal)]
    w2_mate = mail.send(w2in, w2.at[c], mate)
    w3_mate = mail.send(w3in.at[near_rows], w3.at[near], mate)

    def part_copy(half, q):
        return pltpu.make_async_remote_copy(
            src_ref=out_part.at[half, q],
            dst_ref=in_part.at[half, q],
            send_sem=part_sends.at[half, q],
            recv_sem=part_recvs.at[half, q],
            device_id=opposite,
            device_id_type=MESH,
        )

    own_in, mate_in = (
        pl.ds(pl.multiple_of(depth * k, depth), depth) for k in (c, 1 - c)
    )

    def send_part(half, q):
        def weight(rows):
            return jnp.concatenate([w1[2 * half, rows], w1[2 * half + 1, rows]], axis=1)

        value = dot(x[2 * q + c], weight(own_in)) + dot(xm[q], weight(mate_in))
        out_part[half, q] = dot(perm[...], value.astype(BF16)).astype(BF16)
        part_copy(half, q).start()

    w1_here.wait()
    w1_mate.wait_recv()
    perm_here.wait()
    for q in range(2):
        x_own[q].wait()
        x_mate[q].wait_recv()
        send_part(y, q)
    w1_far.wait_recv()
    w1_on = mail.send(w1.at[far], w1.at[far], mate)
    w1_on.wait_recv()
    for q in range(2):
        send_part(1 - y, q)
    x_rest = [local.fetch(x_any.at[2 * q + 1 - c], x.at[2 * q + 1 - c]) for q in range(2)]
    w2_here.wait()
    w2_mate.wait_recv()
    rest.append(local.fetch(w2, w2_out))
    own_rows = pl.ds(pl.multiple_of(depth * c, depth), depth)
    w1_own[...] = jnp.concatenate([w1[k, own_rows] for k in range(4)], axis=1)
    st[...] = jnp.zeros(st.shape, st.dtype)
    step_rows = quarter // SIDE

    def sums(half):
        def one(q, carry):
            part_copy(half, q).wait_recv()

            def rows_of(at, inner):
                rows = pl.ds(at * step_rows, step_rows)
                value = out_part[half, q, rows].astype(F32) + in_part[half, q, rows].astype(F32)
                h1[half, q, rows] = value
                st[half, 0:1] += jnp.sum(value, axis=0, keepdims=True)
                st[half, 1:2] += jnp.sum(value * value, axis=0, keepdims=True)
                return inner

            return lax.fori_loop(0, SIDE, rows_of, carry)

        lax.fori_loop(0, 2, one, 0)

    sums(1 - y)
    sums(y)
    for half in range(2):
        for q in range(2):
            part_copy(half, q).wait_send()
    share_start(st, slots, half_sends.at[0], half_recvs.at[0], half_peers)
    w3_far = mail.send(w3in.at[far_rows], w3.at[near], opposite)
    channels = pad.shape[4]
    early_taps = []
    for tap in range(EARLY_TAPS):
        rows = pl.ds(tap * channels, channels)
        early_taps.append(mail.send(w2in.at[rows], w2_far.at[c, rows], opposite))
    share_end(st, slots, half_sends.at[0], half_recvs.at[0], half_peers)
    totals = add_slots(slots, half_peers[0])
    count = float(views * 4 * quarter)
    for copy in small_copies:
        copy.wait_recv()
    mean = totals[:, 0:1] / count
    rstd = lax.rsqrt(totals[:, 1:2] / count - mean * mean + EPS)
    stat[...] = jnp.concatenate([mean, rstd], axis=1)
    for half in range(2):
        gains = jnp.concatenate([smalls[2 * half], smalls[2 * half + 1]], axis=1)
        scale = rstd[half] * gains[0:1]
        bias = gains[1:2] - mean[half] * scale

        def act_rows(at, carry, half=half, scale=scale, bias=bias):
            q, i = lax.div(at, SIDE), lax.rem(at, SIDE)
            level = h1[half, q, pl.ds(i * step_rows, step_rows)] * scale + bias
            value = (level * gate(level)).astype(BF16)
            pad[q, i + 1, 1 : SIDE + 1, :, 256 * half : 256 * half + 256] = value.reshape(
                SIDE, step_rows // SIDE, 256
            )
            return carry

        lax.fori_loop(0, 2 * SIDE, act_rows, 0)
    rest.append(local.fetch(pad, pad_out))
    rest.append(local.fetch(h1, h1_out))
    w3_far.wait_recv()
    w3_on = mail.send(w3.at[far], w3.at[far], mate)
    st2[...] = jnp.zeros(st2.shape, F32)

    def convolve(q, carry):
        for tap in range(9):
            a, b = tap // 3, tap % 3
            window = pad[q, a : a + SIDE, b : b + SIDE].reshape(quarter, channels)
            taps = slice(tap * channels, (tap + 1) * channels)
            term = dot(window, jnp.concatenate([w2[0, taps], w2[1, taps]], axis=1))
            if tap == 0:
                hidden[q] = term
            else:
                hidden[q] += term
        value = hidden[q]
        h2[q] = value.astype(BF16)
        st2[0:1] += jnp.sum(value, axis=0, keepdims=True)
        st2[1:2] += jnp.sum(value * value, axis=0, keepdims=True)
        return carry

    lax.fori_loop(0, 2, convolve, 0)
    share_start(st2, slots2, half_sends.at[1], half_recvs.at[1], half_peers)
    rest.append(local.fetch(h2, h2_near))
    w2_on = []

    def pass_on(taps):
        for tap in taps:
            early_taps[tap].wait_recv()
            rows = pl.ds(tap * channels, channels)
            w2_on.append(mail.send(w2_far.at[c, rows], w2_far.at[c, rows], mate))

    pass_on(range(EARLY_TAPS - 1))
    share_end(st2, slots2, half_sends.at[1], half_recvs.at[1], half_peers)
    totals2 = add_slots(slots2, half_peers[0])
    mean2 = totals2[0:1] / count
    rstd2 = lax.rsqrt(totals2[1:2] / count - mean2 * mean2 + EPS)
    stats2[y] = jnp.concatenate([mean2, rstd2], axis=0)
    gains = jnp.concatenate([smalls[2 * y], smalls[2 * y + 1]], axis=1)
    scale2 = rstd2 * gains[2:3]
    bias2 = gains[3:4] - mean2 * scale2
    across, beside = [], []
    unperm_here.wait()
    for q in range(2):
        level = hidden[q] * scale2 + bias2
        value = (level * gate(level)).astype(BF16)
        act[y, 2 * q + c] = dot(unperm[...], value).astype(BF16)
        spot = act.at[y, 2 * q + c]
        across.append(mail.send(spot, spot, opposite))
        beside.append(mail.send(spot, spot, mate))
    pass_on(range(EARLY_TAPS - 1, EARLY_TAPS))
    stat2_far = mail.send(stats2.at[y], stats2.at[y], opposite)

    own_out = pl.ds(pl.multiple_of(width * c, width), width)
    st3[...] = jnp.zeros(st3.shape, F32)
    head_first_here = local.fetch(head_first_any, head_first)
    head_last_here = local.fetch(head_last_any, head_last)
    for copy in (w3_mate, w3_on):
        copy.wait_recv()
    rest[0].wait()
    w3_kept = local.fetch(w3, w3_out)

    def last_conv(q):
        total = None
        for half in range(2):
            weight = jnp.concatenate([w3[2 * half, own_out], w3[2 * half + 1, own_out]], axis=1)
            term = dot_nt(act[half, q], weight)
            total = term if total is None else total + term
        low = total.astype(BF16)
        h3[q] = low
        value = low.astype(F32)
        st3[0:1] += jnp.sum(value, axis=0, keepdims=True)
        st3[1:2] += jnp.sum(value * value, axis=0, keepdims=True)

    for row, column in ((sub_row, sub_col), (image_row, image_col), (partner_row, partner_col)):
        columns_of(row, column)
    for q in range(2):
        across[q].wait_recv()
        spot = act.at[1 - y, 2 * q + c]
        passed = mail.send(spot, spot, mate)
        last_conv(2 * q + c)
        beside[q].wait_recv()
        passed.wait_recv()
        last_conv(2 * q + 1 - c)
    for copy in w2_on:
        copy.wait_recv()
    act_kept = local.fetch(act, act_out)
    middle_rows = pl.ds(EARLY_TAPS * channels, MIDDLE_TAPS * channels)
    w2_middle = mail.send(w2in.at[middle_rows], w2_far.at[c, middle_rows], opposite)
    share_start(st3, slots3, group_sends.at[0], group_recvs.at[0], group)
    rest.append(local.fetch(h3, h3_out))
    share_end(st3, slots3, group_sends.at[0], group_recvs.at[0], group)
    totals = add_slots(slots3, views)
    count = float(views * 4 * quarter)
    mean = totals[0:1] / count
    rstd = lax.rsqrt(totals[1:2] / count - mean * mean + EPS)
    stat3[...] = jnp.concatenate([mean, rstd], axis=0)
    scale = rstd * gain_last[...]
    bias = shift_last[...] - mean * scale
    for copy in x_rest:
        copy.wait()

    def pool_block(q, carry):
        before = x[q].astype(F32) + (h3[q].astype(F32) * scale + bias)
        sums = view_sums(before * gate(before), block)
        pooled_own[pl.ds(pl.multiple_of(q * block, block), block)] = sums * (1.0 / PIX)
        return carry

    lax.fori_loop(0, 4, pool_block, 0)
    head_first_here.wait()
    hidden = join_rows(dot(split_rows(pooled_own[...]), head_first[...]))
    wide = hidden.shape[1] // 2
    part[0] = hidden[:, :wide]
    part[1] = hidden[:, wide:]
    swap = mail.send(part, part_in.at[pl.ds(0, 2)], mate)

    def slope_block(q, carry):
        level3 = h3[q].astype(F32)
        before = x[q].astype(F32) + (level3 * scale + bias)
        low = silu_slope(before).astype(BF16)
        slope[q] = low
        normed = (level3 - mean) * rstd
        kept = low.astype(F32)
        rows = pl.ds(pl.multiple_of(q * block, block), block)
        slope_sums[0, rows] = view_sums(kept, block)
        slope_sums[1, rows] = view_sums(kept * normed, block)
        return carry

    swap.wait()
    mean_sums[...] = part[...] + part_in[0:2]
    across_p1 = mail.send(mean_sums.at[c], part_in.at[2], opposite)
    lax.fori_loop(0, 2, slope_block, 0)
    across_p1.wait_recv()
    part_in[4 + c] = mean_sums[c] + part_in[2]
    gathered = mail.send(part_in.at[4 + c], part_in.at[4 + c], mate)
    h2_over = mail.send(h2, h2_far, opposite)
    w2_middle.wait_recv()
    w2_middle_on = mail.send(w2_far.at[c, middle_rows], w2_far.at[c, middle_rows], mate)
    before_late = (EARLY_TAPS + MIDDLE_TAPS) * channels
    late_rows = pl.ds(before_late, w2in.shape[0] - before_late)
    w2_over = mail.send(w2in.at[late_rows], w2_far.at[c, late_rows], opposite)
    gathered.wait_recv()
    p1 = part_in[4:6]
    st4[0:2] = jnp.sum(p1, axis=1)
    st4[2:4] = jnp.sum(p1 * p1, axis=1)
    share_start(st4, slots4, group_sends.at[1], group_recvs.at[1], group)
    lax.fori_loop(2, 4, slope_block, 0)
    slope_kept = local.fetch(slope, slope_out)
    share_end(st4, slots4, group_sends.at[1], group_recvs.at[1], group)
    totals4 = add_slots(slots4, views)
    count4 = float(views * views_own)
    mean4 = totals4[0:2] / count4
    rstd4 = lax.rsqrt(totals4[2:4] / count4 - mean4 * mean4 + EPS)
    head_last_here.wait()

    def level4(half):
        cols = slice(half * wide, (half + 1) * wide)
        normed = (part_in[4 + half] - mean4[half : half + 1]) * rstd4[half : half + 1]
        return normed, normed * gain_head[:, cols] + shift_head[:, cols]

    embed = None
    for half in range(2):
        normed, level = level4(half)
        value = level * gate(level)
        act4[half] = value
        term = join_rows(dot(split_rows(value), head_last[half * wide : (half + 1) * wide]))
        embed = term if embed is None else embed + term
    embed_own[...] = embed
    share_start(embed_own, embed_all, group_sends.at[2], group_recvs.at[2], group)
    share_end(embed_own, embed_all, group_sends.at[2], group_recvs.at[2], group)
    pooled_mean = jnp.sum(pooled_own[...], axis=0, keepdims=True) / views_own
    bk3[2:3] = pooled_mean
    pooled_low[...] = (pooled_own[...] - pooled_mean).astype(BF16)
    gather_start(pooled_low, pooled_all, group_sends.at[5], group_recvs.at[5], group)
    rest.append(local.fetch(pooled_low, pooled_all.at[view_at]))
    own_rows = pl.ds(pl.multiple_of(view_at * views_own, views_own), views_own)
    every = embed_all.reshape(views * views_own, embed.shape[1])
    loss, grad_embed = whiten(
        every, sub_col, image_col, image_row, partner_col, partner_row,
        (work, inverse, white, unit, unit_parts, back), own_rows,
    )
    loss_out[...] = loss
    grad_embed_out[...] = grad_embed
    stacked = split_rows(grad_embed)
    for half in range(2):
        normed, level = level4(half)
        grad = join_rows(dot_nt(stacked, head_last[half * wide : (half + 1) * wide]))
        grad = grad * silu_slope(level)
        part[half] = grad
        bk4[half : half + 1] = jnp.sum(grad, axis=0, keepdims=True)
        bk4[2 + half : 3 + half] = jnp.sum(grad * normed, axis=0, keepdims=True)
    tot4 = share(bk4, bslots4, group_sends.at[3], group_recvs.at[3], group)
    grad_pooled = None
    for half in range(2):
        cols = slice(half * wide, (half + 1) * wide)
        normed, level = level4(half)
        shift_sum, gain_sum = tot4[half : half + 1], tot4[2 + half : 3 + half]
        grad_shift_head[:, cols] = shift_sum
        grad_gain_head[:, cols] = gain_sum
        grad = (
            gain_head[:, cols]
            * rstd4[half : half + 1]
            * (part[half] - shift_sum / count4 - normed * (gain_sum / count4))
        )
        grad_p1[half] = grad
        term = join_rows(dot_nt(split_rows(grad), head_first[:, cols]))
        grad_pooled = term if grad_pooled is None else grad_pooled + term
    grad_pooled = grad_pooled * (1.0 / PIX)
    grad_pooled_out[...] = grad_pooled
    bk3[0:1] = jnp.sum(grad_pooled * slope_sums[0], axis=0, keepdims=True)
    bk3[1:2] = jnp.sum(grad_pooled * slope_sums[1], axis=0, keepdims=True)
    share_start(bk3, bslots3, group_sends.at[4], group_recvs.at[4], group)
    share_end(bk3, bslots3, group_sends.at[4], group_recvs.at[4], group)
    tot3 = add_slots(bslots3, views)
    grad_shift_last[...] = tot3[0:1]
    grad_gain_last[...] = tot3[1:2]
    own_count = float(4 * quarter)
    normed_sum = (st3[0:1] - own_count * mean) * rstd
    rows_sum[...] = scale * (
        bk3[0:1] - tot3[0:1] * (own_count / count) - normed_sum * (tot3[1:2] / count)
    )
    pooled_means[...] = bslots3[:, 2]

    def finish():
        w2_over.wait_recv()
        w2_last = mail.send(w2_far.at[c, late_rows], w2_far.at[c, late_rows], mate)
        h2_over.wait_recv()
        stat2_far.wait_recv()
        w2_last.wait_recv()
        w2_middle_on.wait_recv()
        share_end(pooled_low, pooled_all, group_sends.at[5], group_recvs.at[5], group)
        for copy in [*rest[1:], w3_kept, act_kept]:
            copy.wait()
        for copy in mail.copies:
            if copy is not swap:
                copy.wait_send()

    slope_kept.wait()
    if everyone:
        return finish
    finish()
    return None


def front_specs(views, x, weights):
    conv_mid, head_first, head_last = weights[1], weights[3], weights[4]
    quarter, depth = x.shape[0] // 4, x.shape[1]
    width = depth
    mid = conv_mid.shape[1] * 4
    half = mid // 2
    block = quarter // PIX
    own = 4 * block
    total = views * own
    hid, emb = head_last.shape
    wide = hid // 2
    subs = total // SUB
    peers = 2 * views
    vm = pltpu.VMEM
    wide_rows = (4, quarter, width)
    outs = (
        shape(2, PAD, PAD, block, mid, kind=BF16),
        shape(2, 2, quarter, half),
        shape(2, *conv_mid.shape, kind=BF16),
        shape(2, *conv_mid.shape, kind=BF16),
        shape(4, 2 * depth, mid // 4, kind=BF16),
        shape(2, 4, quarter, half, kind=BF16),
        shape(*wide_rows, kind=BF16),
        shape(*wide_rows, kind=BF16),
        shape(views, own, width, kind=BF16),
        shape(2, quarter, half, kind=BF16),
        shape(2, quarter, half, kind=BF16),
        shape(2, 2, half),
        shape(depth, mid, kind=BF16),
        shape(4, 8, mid // 4),
        shape(2, width),
        shape(1, width),
        shape(1, width),
        shape(1, hid),
        shape(1, hid),
        shape(own, width),
        shape(2, own, wide),
        shape(own, emb),
        shape(2, own, wide),
        shape(1, 1),
        shape(2, 2, half),
        shape(views, width),
        shape(1, width),
    )
    scratch = [
        vm(wide_rows, BF16),
        vm((4, 2 * depth, mid // 4), BF16),
        vm((2, 4, quarter, half), BF16),
        vm(wide_rows, BF16),
        vm((2, 2, quarter, half), F32),
        vm((2, 2, half), F32),
        vm((peers, 2, 2, half), F32),
        vm((2, half), F32),
        vm((peers, 2, half), F32),
        vm((quarter, quarter), BF16),
        vm((quarter, quarter), BF16),
        vm((2, PAD, PAD, block, mid), BF16),
        vm((2, *conv_mid.shape), BF16),
        vm((4, 2 * depth, mid // 4), BF16),
        vm((2, quarter, half), F32),
        vm((2, quarter, half), BF16),
        vm((8, mid // 4), F32),
        vm(head_first.shape, BF16),
        vm(head_last.shape, BF16),
        vm(wide_rows, BF16),
        vm((own, width), F32),
        vm((own, width), BF16),
        vm((total, 128), F32),
        vm((total, 128), F32),
        vm((total, 128), F32),
        vm((views, own, emb), F32),
        vm((2, own, wide), F32),
        vm((6, own, wide), F32),
        vm((2, own, wide), F32),
        vm((2, own, width), F32),
        vm((2, width), F32),
        vm((views, 2, width), F32),
        vm((4, wide), F32),
        vm((views, 4, wide), F32),
        vm((4, wide), F32),
        vm((views, 4, wide), F32),
        vm((3, width), F32),
        vm((views, 3, width), F32),
        vm((own, emb), F32),
        vm((subs, emb, 2 * emb), F32),
        vm((subs, emb, emb), F32),
        vm((total, emb), F32),
        vm((total, emb), F32),
        vm((total, 3 * emb), BF16),
        vm((total, emb), F32),
        dma(40),
        dma(40),
        dma(2, 2),
        dma(2, 2),
        dma(2, peers),
        dma(2, peers),
        dma(6, views),
        dma(6, views),
        dma(32),
    ]
    return outs, scratch


def front_stage(views, x, weights, vectors, tables, perm, unperm):
    conv_first, conv_mid, conv_last, head_first, head_last = weights
    outs, scratch = front_specs(views, x, weights)
    return call(
        functools.partial(front_body, views),
        "front",
        outs,
        19,
        scratch,
        collective=1,
        any_ins=range(11, 19),
        any_outs=range(11),
    )(
        *vectors, *tables, x.reshape(4, x.shape[0] // 4, x.shape[1]), conv_first, conv_mid, conv_last,
        perm, unperm, head_first, head_last,
    )


def link_kind(rows):
    return BF16 if rows % 16 == 0 else F32


def back_body(
    views, stat3, grad_shift_last, grad_gain_last, grad_pooled, gain_last, expand,
    stats2, smalls, stat1, act4, grad_embed, grad_p1, pooled_means, rows_sum,
    h3_any, slope_any, w3_any, h2_near_any, h2_far_any, perm_any, unperm_any, pad_any, h1q_any, w2_any,
    w2_far_any, act_any, x_any, pooled_any,
    gh1_out, mid_slots, pair_out, head_last_out, head_first_out,
    grad_shift_mid, grad_gain_mid, grad_shift_first, grad_gain_first,
    h3, slope, w3, h2_near, h2_far, gh1, gh3, gh3_mate, out_part, in_part, ga2, gh2_far, gpad, ga1, st, sum_parts, chan_slots, view_slots,
    order, pad, h1q, w2, w2_far, act, pooled,
    wsum, mid_parts, mid_in, last_parts, last_in, last_slots, first_parts, first_in, first_slots, means, mean_slots, pair_parts,
    hl_parts, hl_slots, p1_parts, p1_slots,
    sends, recvs, chan_sends, chan_recvs, group_sends, group_recvs, pair_sends, pair_recvs,
    pair1_sends, pair1_recvs, pair2_sends, pair2_recvs, local_sems,
    resident=None,
):
    view_at, chan_at, y, c = place()
    mate, opposite = (view_at, 2 * y + 1 - c), (view_at, 2 * (1 - y) + c)
    group, chans, everyone = view_group(views), chan_group(), all_group(views)
    quarter, width = h3.shape[1], h3.shape[2]
    block = quarter // PIX
    half_width = h2_near.shape[2]
    met = (lambda: None) if resident else greet([], [everyone])
    to_pixels, to_views = (perm_any, unperm_any) if resident else (order, order)
    local = Local(local_sems)
    near_half, own_half = [2 * i + 1 - c for i in (1 - y, y)], [2 * i + c for i in (1 - y, y)]
    rows_here = []

    def fetch_rows(q):
        if not resident:
            rows_here.append((local.fetch(h3_any.at[q], h3.at[q]), local.fetch(slope_any.at[q], slope.at[q])))
        else:
            rows_here.append(())

    for q in near_half:
        fetch_rows(q)
    count = float(views * 4 * quarter)
    mean, rstd = stat3[0:1], stat3[1:2]
    scale = rstd * gain_last[...]
    shift_part, gain_part = grad_shift_last[...] / count, grad_gain_last[...] / count

    def grad_rows(q):
        rows = pl.ds(pl.multiple_of(q * block, block), block)
        high, low = split_pair(grad_pooled[rows])
        spread = dot(expand[...], jnp.concatenate([high, low], axis=0))
        grad = spread * slope[q].astype(F32)
        normed = (h3[q].astype(F32) - mean) * rstd
        gh3[q] = (scale * (grad - shift_part - normed * gain_part)).astype(BF16)

    mate_out = pl.ds(pl.multiple_of(width * (1 - c), width), width)
    own_out = pl.ds(pl.multiple_of(width * c, width), width)

    def part_of(i):
        def weight(rows):
            return jnp.concatenate([w3[k, rows] for k in range(4)], axis=1)

        value = dot(gh3[2 * i + c], weight(own_out)) + dot(gh3_mate[i], weight(mate_out))
        return dot(to_pixels[...], value.astype(BF16))

    mail = Mail(sends, recvs)
    beside = []
    for at, i in enumerate((1 - y, y)):
        for copy in rows_here[at]:
            copy.wait()
        grad_rows(2 * i + 1 - c)
        if at == 0:
            met()
        beside.append(mail.send(gh3.at[2 * i + 1 - c], gh3_mate.at[i], mate))
        if at == 0:
            for q in own_half:
                fetch_rows(q)
            w3_here = local.fetch(w3_any, w3)
            perm_here = local.fetch(perm_any, order)
    for at, i in enumerate((1 - y, y)):
        for copy in rows_here[2 + at]:
            copy.wait()
        grad_rows(2 * i + c)
        if at == 0:
            w3_here.wait()
            perm_here.wait()
            beside[0].wait_recv()
            value = part_of(1 - y).astype(BF16)
            for half in range(2):
                out_part[half] = value[:, half * half_width : (half + 1) * half_width]
            across = [mail.send(out_part.at[half], in_part.at[half], opposite) for half in range(2)]
            if resident:
                resident()
            h2_here = [local.fetch(h2_near_any, h2_near), local.fetch(h2_far_any, h2_far)]
            act_here = local.fetch(act_any, act)
            w2_here = local.fetch(w2_any, w2)
            w2_far_here = local.fetch(w2_far_any, w2_far)
            h1q_here = local.fetch(h1q_any, h1q)
            pad_here = local.fetch(pad_any, pad)
    beside[1].wait_recv()
    ga2[...] = part_of(y)
    unperm_here = local.fetch(unperm_any, order)

    def fold_sems(at):
        return [sems.at[at] for sems in (pair1_sends, pair1_recvs, pair2_sends, pair2_recvs)]

    halves = (y, 1 - y)

    def mid_norm(near):
        half = halves[near]
        gains = jnp.concatenate([smalls[2 * half], smalls[2 * half + 1]], axis=1)
        mean2, rstd2 = stats2[half, 0:1], stats2[half, 1:2]
        return mean2, rstd2, gains[2:3], gains[3:4]

    def half_cols(ref, near):
        low, high = ref[:, :half_width], ref[:, half_width:]
        return jnp.where(halves[near] == 0, low, high)

    for copy in h2_here:
        copy.wait()
    for near, h2 in enumerate((h2_near, h2_far)):
        mean2, rstd2, gain2, shift2 = mid_norm(near)
        normed = (h2[1 - y].astype(F32) - mean2) * rstd2
        grad = out_part[halves[near]].astype(F32) * silu_slope(normed * gain2 + shift2)
        st[halves[near], 0:1] = jnp.sum(grad, axis=0, keepdims=True)
        st[halves[near], 1:2] = jnp.sum(grad * normed, axis=0, keepdims=True)
        normed = (h2[y].astype(F32) - mean2) * rstd2
        kept = silu_slope(normed * gain2 + shift2)
        ga1[:, near * half_width : (near + 1) * half_width] = kept
        grad = half_cols(ga2, near) * kept
        st[halves[near], 0:1] += jnp.sum(grad, axis=0, keepdims=True)
        st[halves[near], 1:2] += jnp.sum(grad * normed, axis=0, keepdims=True)
    share_start(st, view_slots.at[0], group_sends.at[3], group_recvs.at[3], group)

    hid_block, hid_split = hl_parts.shape[1], head_last_out.shape[0]
    for half in range(2):
        product = exact(act4[half], grad_embed[...], 0, 0)
        wsum[0, : product.shape[0]] = product
        per_half = views // 2

        def spread_hidden(to, carry, half=half, per_half=per_half):
            spot = (4 * to + chan_at) * hid_block if hid_split == 4 else to * hid_block
            rows = pl.ds(pl.multiple_of(spot, hid_block), hid_block)
            hl_parts[half * per_half + to] = wsum[0, rows]
            return carry

        lax.fori_loop(0, per_half, spread_hidden, 0)
        wide = grad_p1.shape[2] // per_half
        for to in range(per_half):
            p1_parts[half * per_half + to] = grad_p1[half, :, to * wide : (to + 1) * wide]
    act_here.wait()
    share_rows = last_parts.shape[1]
    means[0:1] = rows_sum[...]
    few_rows = quarter // SIDE
    for half in range(2):
        cols = slice(half * half_width, (half + 1) * half_width)
        sampled = [jnp.sum(act[half, q, :few_rows].astype(F32), axis=0, keepdims=True) for q in range(4)]
        means[1:2, cols] = sum(sampled) / (4 * few_rows)
    for half in range(2):
        cols = slice(half * half_width, (half + 1) * half_width)
        total = None
        for q in range(4):
            term = dot_tn(gh3[q], act[half, q])
            total = term if total is None else total + term
        wsum[0, :width] = total[:, : half_width // 2]
        wsum[1, :width] = total[:, half_width // 2 :]
        low = (
            jnp.concatenate([wsum[0, :width], wsum[1, :width]], axis=1)
            - outer_product(means[0:1], means[1:2, cols])
        ).astype(last_parts.dtype)
        for to in range(views):
            last_parts[to, :, half * half_width : (half + 1) * half_width] = low[
                to * share_rows : (to + 1) * share_rows
            ]
    share_end(st, view_slots.at[0], group_sends.at[3], group_recvs.at[3], group)
    sum_parts[0] = add_slots(view_slots.at[0], views)
    sums_beside = mail.send(sum_parts.at[0], sum_parts.at[1], mate)
    scatter_start(hl_parts, hl_slots, group_sends.at[0], group_recvs.at[0], group)
    scatter_start(p1_parts, p1_slots, group_sends.at[1], group_recvs.at[1], group)
    share_start(means, mean_slots, group_sends.at[2], group_recvs.at[2], group)
    fold_last = Fold(last_parts, last_in, last_slots, fold_sems(0), views)
    fold_last.start()
    sums_beside.wait_recv()
    sum_parts[2] = sum_parts[0] + sum_parts[1]
    sums_across = mail.send(sum_parts.at[2], sum_parts.at[3], opposite)
    for copy in beside:
        copy.wait_send()
    x = x_any if resident else gh3
    x_here = local.fetch(x_any, x)

    gpad[...] = jnp.zeros(gpad.shape, gpad.dtype)
    for half in range(2):
        across[half].wait()
        cols = slice(half * half_width, (half + 1) * half_width)
        ga2[:, cols] += in_part[half].astype(F32)
    gh2 = out_part
    sums_across.wait_recv()
    sum_parts[4] = sum_parts[2] + sum_parts[3]
    for near, h2 in enumerate((h2_near, h2_far)):
        mean2, rstd2, gain2, shift2 = mid_norm(near)
        tot = sum_parts[4, halves[near]]
        normed = (h2[y].astype(F32) - mean2) * rstd2
        grad = half_cols(ga2, near) * ga1[:, near * half_width : (near + 1) * half_width]
        low = (gain2 * rstd2 * (grad - tot[0:1] / count - normed * (tot[1:2] / count))).astype(BF16)
        gh2[near] = low
        gpad[near, 1 : SIDE + 1, 1 : SIDE + 1] = low.reshape(SIDE, SIDE, block, half_width)
    tot = sum_parts[4, y]
    own_cols = jnp.where(c == 0, tot[:, : half_width // 2], tot[:, half_width // 2 :])
    grad_shift_mid[...] = own_cols[0:1]
    grad_gain_mid[...] = own_cols[1:2]
    far_copy = mail.send(gh2.at[1], gh2_far, opposite)
    fold_last.pass_on(1, fold_last.size + 1)
    w2_here.wait()
    w2_far_here.wait()
    channels = w2.shape[1] // 9
    for tap in range(9):
        a, b = 2 - tap // 3, 2 - tap % 3
        taps = slice(tap * channels, (tap + 1) * channels)
        term = None
        for near, weight in enumerate((w2, w2_far)):
            window = gpad[near, a : a + SIDE, b : b + SIDE].reshape(quarter, half_width)
            both = jnp.concatenate([weight[0, taps], weight[1, taps]], axis=1)
            piece = dot_nt(window, both)
            term = piece if term is None else term + piece
        if tap == 0:
            ga1[...] = term
        else:
            ga1[...] += term
    h1q_here.wait()

    def first_norm(half, quarter_at):
        gains = jnp.concatenate([smalls[2 * half], smalls[2 * half + 1]], axis=1)
        normed = (h1q[half, quarter_at] - stat1[half, 0:1]) * stat1[half, 1:2]
        return normed, gains[0:1], gains[1:2], gains[0:1] * stat1[half, 1:2]

    for half in range(2):
        cols = slice(half * half_width, (half + 1) * half_width)
        normed, gain1, shift1, scale1 = first_norm(half, y)
        grad = ga1[:, cols] * silu_slope(normed * gain1 + shift1)
        ga2[:, cols] = grad
        in_part[half] = (scale1 * grad).astype(BF16)
        st[half, 0:1] = jnp.sum(grad, axis=0, keepdims=True)
        st[half, 1:2] = jnp.sum(grad * normed, axis=0, keepdims=True)
    share_start(st, chan_slots.at[1], chan_sends.at[1], chan_recvs.at[1], chans)
    scaled = []
    for half in range(2):
        spot = gh3_mate.at[0, :, half * half_width : (half + 1) * half_width]
        scaled.append(mail.send(in_part.at[half], spot, opposite))

    pad_here.wait()

    def tap_term(at, tap, grads):
        a, b = tap // 3, tap % 3
        window = pad[at, a : a + SIDE, b : b + SIDE].reshape(quarter, channels)
        return dot_tn(window, grads)

    for tap in range(9):
        total = tap_term(y, tap, gh2[0])
        taps = slice(tap * channels, (tap + 1) * channels)
        wsum[0, taps] = total[:, : half_width // 2]
        wsum[1, taps] = total[:, half_width // 2 :]
    share_end(st, chan_slots.at[1], chan_sends.at[1], chan_recvs.at[1], chans)
    st[...] = add_slots(chan_slots.at[1], 4)
    share_start(st, view_slots.at[1], group_sends.at[4], group_recvs.at[4], group)
    far_copy.wait_recv()
    for tap in range(9):
        total = tap_term(1 - y, tap, gh2_far[...])
        taps = slice(tap * channels, (tap + 1) * channels)
        wsum[0, taps] += total[:, : half_width // 2]
        wsum[1, taps] += total[:, half_width // 2 :]
    mid_rows = mid_parts.shape[1]
    mid_flat = mid_parts.reshape(views * mid_rows, mid_parts.shape[2])
    if mid_parts.dtype == F32:
        mid_mate = mail.send(wsum.at[1 - c], mid_flat, mate)
    else:
        w2_far[0] = wsum[1 - c].astype(BF16)
        mid_mate = mail.send(w2_far.at[0], mid_flat, mate)
    share_end(st, view_slots.at[1], group_sends.at[4], group_recvs.at[4], group)
    totals1 = add_slots(view_slots.at[1], views)
    view_slots[1, 0] = totals1
    tot = view_slots[1, 0, y]
    own_cols = jnp.where(c == 0, tot[:, : half_width // 2], tot[:, half_width // 2 :])
    grad_shift_first[...] = own_cols[0:1]
    grad_gain_first[...] = own_cols[1:2]
    unperm_here.wait()
    gh1_beside = []
    for half in range(2):
        cols = slice(half * half_width, (half + 1) * half_width)
        normed, _, _, scale1 = first_norm(half, y)
        tot = totals1[half]
        low = (scale1 * (ga2[:, cols] - tot[0:1] / count - normed * (tot[1:2] / count))).astype(BF16)
        gh1[half, chan_at] = dot(to_views[...], low).astype(BF16)
        spot = gh1.at[half, chan_at]
        gh1_beside.append(mail.send(spot, spot, mate))
    mid_mate.wait_recv()

    def mid_block(to, carry):
        rows = pl.ds(pl.multiple_of(to * mid_rows, mid_rows), mid_rows)
        mid_parts[to] = (wsum[c, rows] + mid_parts[to].astype(F32)).astype(mid_parts.dtype)
        return carry

    lax.fori_loop(0, views, mid_block, 0)
    fold_mid = Fold(mid_parts, mid_in, mid_slots, fold_sems(1), views, False)
    fold_mid.start()
    scatter_end(p1_parts, p1_slots, group_sends.at[1], group_recvs.at[1], group)
    few = pooled.shape[0]

    def head_first_term(at, total):
        views_at = pl.ds(at * few, few)
        copy = pltpu.make_async_copy(pooled_any.at[views_at], pooled, local_sems.at[29])
        copy.start()
        copy.wait()
        rows = pooled[...].astype(F32).reshape(-1, width)
        return total + exact(rows, p1_slots[views_at].reshape(rows.shape[0], -1), 0, 0)

    head_first_out[...] = over(
        views // few, head_first_term, exact(pooled_means[...], jnp.sum(p1_slots[...], axis=1), 0, 0)
    )
    share_end(means, mean_slots, group_sends.at[2], group_recvs.at[2], group)
    fold_last.end()
    rest, folds = [], []
    cuts = [1 + fold_mid.size * k // 4 for k in range(4)] + [fold_mid.size + 1]
    x_here.wait()
    for half in range(2):
        scaled[half].wait_recv()
        cols = slice(half * half_width, (half + 1) * half_width)
        normed, _, _, scale1 = first_norm(half, 1 - y)
        tot = view_slots[1, 0, half]
        value = gh3_mate[0, :, cols].astype(F32)
        low = (value - scale1 * (tot[0:1] / count + normed * (tot[1:2] / count))).astype(BF16)
        gh1[half, 2 * (1 - y) + c] = dot(to_views[...], low).astype(BF16)
        far_spot = gh1.at[half, 2 * (1 - y) + c]
        gh1_on = mail.send(far_spot, far_spot, mate)
        fold_mid.pass_on(cuts[2 * half], cuts[2 * half + 1])
        gh1_beside[half].wait_recv()
        gh1_on.wait_recv()
        rest.append(local.fetch(gh1.at[half], gh1_out.at[half]))
        total = None
        for q in range(4):
            term = dot_tn(x[q], gh1[half, q])
            total = term if total is None else total + term
        low = total.astype(first_parts.dtype)
        for to in range(views):
            first_parts[half, to] = low[to * share_rows : (to + 1) * share_rows]
        folds.append(Fold(first_parts.at[half], first_in.at[half], first_slots.at[half], fold_sems(2 + half), views))
        folds[half].start()
        fold_mid.pass_on(cuts[2 * half + 1], cuts[2 * half + 2])
    rest.append(local.fetch(mid_parts.at[view_at], mid_slots.at[fold_mid.outer]))
    folds[0].pass_on(1, folds[0].size + 1)

    scatter_end(hl_parts, hl_slots, group_sends.at[0], group_recvs.at[0], group)
    if hid_split == 4:
        head_last_out[chan_at] = add_slots(hl_slots, views)
        gather_start(head_last_out.at[chan_at], head_last_out, chan_sends.at[2], chan_recvs.at[2], chans)
    else:
        head_last_out[0] = add_slots(hl_slots, views)

    def blocks(kind, summed):
        wide = summed.shape[1] // 4
        for to in range(4):
            pair_parts[to, kind] = summed[:, to * wide : (to + 1) * wide]

    def summed_slots(slots):
        def add(at, total):
            return total + slots[at].astype(F32)

        return lax.fori_loop(1, slots.shape[0], add, slots[0].astype(F32))

    everywhere = short_product(mean_slots[:, 0], mean_slots[:, 1])
    ga1[: everywhere.shape[0]] = everywhere
    own_block = pl.ds(pl.multiple_of(view_at * share_rows, share_rows), share_rows)
    blocks(1, summed_slots(last_slots) + ga1[own_block])
    folds[1].pass_on(1, folds[1].size + 1)
    for fold in folds:
        fold.end()
    blocks(0, jnp.concatenate([summed_slots(first_slots.at[half]) for half in range(2)], axis=1))
    row_views = views // 4
    to_view = chan_at * row_views + lax.div(view_at, 4)
    slot = lax.rem(view_at, 4)

    def pair_copy(to):
        return pltpu.make_async_remote_copy(
            src_ref=pair_parts.at[to],
            dst_ref=pair_out.at[slot],
            send_sem=pair_sends.at[to],
            recv_sem=pair_recvs.at[slot],
            device_id=(to_view, to),
            device_id_type=MESH,
        )

    def pair_arrival(origin):
        return pltpu.make_async_remote_copy(
            src_ref=pair_parts.at[0],
            dst_ref=pair_out.at[origin],
            send_sem=pair_sends.at[0],
            recv_sem=pair_recvs.at[origin],
            device_id=(from_view + origin, from_chan),
            device_id_type=MESH,
        )

    from_view, from_chan = 4 * lax.rem(view_at, row_views), lax.div(view_at, row_views)
    for to in range(4):
        own = jnp.logical_and(to_view == view_at, chan_at == to)

        @pl.when(own)
        def _():
            pair_out[slot] = pair_parts[to]

        @pl.when(jnp.logical_not(own))
        def _():
            pair_copy(to).start()

    for origin in range(4):
        own = jnp.logical_and(from_view + origin == view_at, chan_at == from_chan)

        @pl.when(jnp.logical_not(own))
        def _():
            pair_arrival(origin).wait_recv()

    for to in range(4):
        own = jnp.logical_and(to_view == view_at, chan_at == to)

        @pl.when(jnp.logical_not(own))
        def _():
            pair_copy(to).wait_send()

    if hid_split == 4:
        share_end(head_last_out.at[chan_at], head_last_out, chan_sends.at[2], chan_recvs.at[2], chans)
    fold_mid.end()
    for copy in rest:
        copy.wait()
    for copy in mail.copies[4:]:
        copy.wait_send()


def back_specs(views, front_outs):
    pad, w2, w3, act, h3, h2_near = (front_outs[at] for at in (0, 2, 4, 5, 6, 9))
    act4, grad_embed = front_outs[20], front_outs[21]
    h1q, slope, pooled_all, h2_far = front_outs[1], front_outs[7], front_outs[8], front_outs[10]
    perm_dims = (h3.shape[1], h3.shape[1])
    quarter, width = h3.shape[1], h3.shape[2]
    block = quarter // PIX
    own = 4 * block
    mid = pad.shape[4]
    half = mid // 2
    hid, emb = 2 * act4.shape[2], grad_embed.shape[1]
    taps = w2.shape[1]
    hid_split = 4 if hid // views % 32 == 0 else 1
    hid_block = hid // views // hid_split
    mid_kind, row_kind = link_kind(taps // views), link_kind(width // views)
    vm = pltpu.VMEM
    outs = (
        shape(2, 4, quarter, half, kind=BF16),
        shape(views // 2, taps // views, half // 2, kind=mid_kind),
        shape(4, 2, width // views, mid // 4),
        shape(hid_split, hid_block, emb),
        shape(width, hid // views),
        *[shape(1, half // 2)] * 4,
    )
    scratch = [
        vm((4, quarter, width), BF16),
        vm((4, quarter, width), BF16),
        vm(w3.shape, BF16),
        vm(h2_near.shape, BF16),
        vm(h2_near.shape, BF16),
        vm((2, 4, quarter, half), BF16),
        vm((4, quarter, width), BF16),
        vm((2, quarter, width), BF16),
        vm((2, quarter, half), BF16),
        vm((2, quarter, half), BF16),
        vm((quarter, mid), F32),
        vm((quarter, half), BF16),
        vm((2, PAD, PAD, block, half), BF16),
        vm((quarter, mid), F32),
        vm((2, 2, half), F32),
        vm((5, 2, 2, half), F32),
        vm((2, 4, 2, 2, half), F32),
        vm((2, views, 2, 2, half), F32),
        vm(perm_dims, BF16),
        vm(pad.shape, BF16),
        vm(h1q.shape, F32),
        vm(w2.shape, BF16),
        vm(w2.shape, BF16),
        vm(act.shape, BF16),
        vm((min(views, 8), own, width), BF16),
        vm((2, taps, half // 2), F32),
        vm((views, taps // views, half // 2), mid_kind),
        vm((views // 2, taps // views, half // 2), mid_kind),
        vm((views, width // views, mid), row_kind),
        vm((views // 2, width // views, mid), row_kind),
        vm((views // 2, width // views, mid), row_kind),
        vm((2, views, width // views, half), row_kind),
        vm((2, views // 2, width // views, half), row_kind),
        vm((2, views // 2, width // views, half), row_kind),
        vm((2, width), F32),
        vm((views, 2, width), F32),
        vm((4, 2, width // views, mid // 4), F32),
        vm((views, hid_block, emb), F32),
        vm((views, hid_block, emb), F32),
        vm((views, own, hid // views), F32),
        vm((views, own, hid // views), F32),
        dma(20),
        dma(20),
        dma(3, 4),
        dma(3, 4),
        dma(7, views),
        dma(7, views),
        dma(4),
        dma(4),
        *[dma(4, views // 2)] * 4,
        dma(30),
    ]
    return outs, scratch


def back_stage(views, front_outs, x, gain_last, perm, unperm, expand):
    (pad, h1q, w2, w2_far, w3, act, h3, slope, pooled_all, h2_near, h2_far, stat1, _, smalls, stat3,
     grad_shift_last, grad_gain_last, _, _, grad_pooled, act4, grad_embed, grad_p1, _,
     stats2, pooled_means, rows_sum) = front_outs
    outs, scratch = back_specs(views, front_outs)
    return call(
        functools.partial(back_body, views),
        "back",
        outs,
        28,
        scratch,
        collective=4,
        any_ins=range(14, 28),
        any_outs=range(2),
    )(
        stat3, grad_shift_last, grad_gain_last, grad_pooled, gain_last, expand,
        stats2, smalls, stat1, act4, grad_embed, grad_p1, pooled_means, rows_sum,
        h3, slope, w3, h2_near, h2_far, perm, unperm, pad, h1q, w2, w2_far, act,
        x.reshape(4, x.shape[0] // 4, x.shape[1]), pooled_all,
    )


def split_names(body, ins, outs):
    names = tuple(inspect.signature(body).parameters)[1:-1]
    return names[:ins], names[ins : ins + outs], names[ins + outs :]


FRONT_INS, FRONT_OUTS, FRONT_SCRATCH = split_names(front_body, 19, 27)
BACK_INS, BACK_OUTS, BACK_SCRATCH = split_names(back_body, 28, 9)
DROPPED = ("pad_out", "h1_out", "w2_out", "w3_out", "act_out", "h3_out", "h2_near")
KEPT = (
    "slope_out", "pooled_all", "w1_own", "grad_shift_last", "grad_gain_last",
    "grad_shift_head", "grad_gain_head", "grad_pooled_out", "loss_out",
)
SHARED = {
    "h3": "h3", "slope": "slope", "w3": "w3", "h2_near": "h2", "h2_far": "h2_far", "gh1": "act",
    "gh3": "slope", "pad": "pad", "w2": "w2", "w2_far": "w2_far", "act": "act", "h1q": "h1",
}
SAME = {"stat1": "stat", "grad_pooled": "grad_pooled_out", "grad_embed": "grad_embed_out"}


def joined_names():
    held = [name for name in FRONT_OUTS if name not in DROPPED and name not in KEPT]
    fresh = [name for name in BACK_SCRATCH if name not in SHARED and name != "order"]
    return held, fresh


def joined_body(views, *refs):
    held, fresh = joined_names()
    names = [*FRONT_INS, "expand", *KEPT, *BACK_OUTS, *FRONT_SCRATCH, *held]
    env = dict(zip(names, refs))
    back_env = dict(zip(fresh, refs[len(names) :]))
    finish = front_body(views, *[env.get(name) for name in FRONT_INS + FRONT_OUTS + FRONT_SCRATCH], everyone=True)
    for name, other in SHARED.items():
        back_env[name] = env[other]
    for name in BACK_INS:
        if name.endswith("_any"):
            back_env[name] = back_env.get(name[:-4])
    back_env["perm_any"], back_env["unperm_any"] = env["perm"], env["unperm"]
    back_env["x_any"], back_env["pooled_any"] = env["x"], env["pooled_all"]

    def pick(name):
        return back_env[name] if name in back_env else env.get(SAME.get(name, name))

    back_body(views, *[pick(name) for name in BACK_INS + BACK_OUTS + BACK_SCRATCH], resident=finish)


def joined_stage(views, x, weights, vectors, tables, perm, unperm, expand):
    conv_first, conv_mid, conv_last, head_first, head_last = weights
    outs, scratch = front_specs(views, x, weights)
    outs_at = dict(zip(FRONT_OUTS, outs))
    back_outs, back_scratch = back_specs(views, outs)
    back_at = dict(zip(BACK_SCRATCH, back_scratch))
    held, fresh = joined_names()
    front_scratch = dict(zip(FRONT_SCRATCH, scratch))
    more = [pltpu.VMEM(outs_at[name].shape, outs_at[name].dtype) for name in held]
    results = call(
        functools.partial(joined_body, views),
        "joined",
        (*[outs_at[name] for name in KEPT], *back_outs),
        20,
        [*front_scratch.values(), *more, *[back_at[name] for name in fresh]],
        collective=1,
        any_ins=range(11, 19),
        any_outs=(0, 1, len(KEPT), len(KEPT) + 1),
    )(
        *vectors, *tables, x.reshape(4, x.shape[0] // 4, x.shape[1]), conv_first, conv_mid, conv_last,
        perm, unperm, head_first, head_last, expand,
    )
    return dict(zip(KEPT, results)), results[len(KEPT) :]


def last_body(
    small_count, w1_any, grad_pooled, expand, gh1_any, slope_any, mid_any, pair_out, head_last_in, head_first_in, *more
):
    small_ins, outs = more[:small_count], more[small_count : 2 * small_count + 6]
    gh1, w1_own, slope, term, mid_slots, sems = more[2 * small_count + 6 :]
    grad_input, grad_mid, grad_first, grad_last, grad_head_last, grad_head_first, *small_outs = outs
    local = Local(sems)
    quarters, quarter, half = gh1.shape[1], gh1.shape[2], gh1.shape[3]
    w1_here = local.fetch(w1_any, w1_own)
    rows_here = [
        (local.fetch(gh1_any.at[:, q], gh1.at[:, q]), local.fetch(slope_any.at[q], slope.at[q]))
        for q in range(quarters)
    ]
    mid_here = local.fetch(mid_any, mid_slots)
    rest = []
    w1_here.wait()
    block = quarter // PIX
    for q in range(quarters):
        for copy in rows_here[q]:
            copy.wait()
        high, low = split_pair(grad_pooled[q * block : (q + 1) * block])
        spread = dot(expand[...], jnp.concatenate([high, low], axis=0))
        value = dot_nt(gh1[0, q], w1_own[:, :half]) + dot_nt(gh1[1, q], w1_own[:, half:])
        term[q] = value + spread * slope[q].astype(F32)
        rest.append(local.fetch(term.at[q], grad_input.at[q]))
    mid_here.wait()

    def add(slot, total):
        return total + mid_slots[slot].astype(F32)

    grad_mid[...] = lax.fori_loop(1, mid_slots.shape[0], add, mid_slots[0].astype(F32))
    grad_head_first[...] = head_first_in[...]
    for source, target in zip(small_ins, small_outs):
        target[...] = source[...]
    rows = pair_out.shape[2]
    for origin in range(4):
        grad_first[origin * rows : (origin + 1) * rows] = pair_out[origin, 0]
        grad_last[origin * rows : (origin + 1) * rows] = pair_out[origin, 1]
    rows = head_last_in.shape[1]
    for origin in range(head_last_in.shape[0]):
        grad_head_last[origin * rows : (origin + 1) * rows] = head_last_in[origin]
    for copy in rest:
        copy.wait()


def last_stage(
    gh1, w1_own, slope, grad_pooled, expand, mid_slots, pair_out, head_last_in, head_first_in, small
):
    quarter, half, width = gh1.shape[2], gh1.shape[3], slope.shape[2]
    outs = (
        shape(4, quarter, width),
        shape(*mid_slots.shape[1:]),
        shape(4 * pair_out.shape[2], pair_out.shape[3]),
        shape(4 * pair_out.shape[2], pair_out.shape[3]),
        shape(head_last_in.shape[0] * head_last_in.shape[1], head_last_in.shape[2]),
        shape(*head_first_in.shape),
        *[shape(*array.shape) for array in small],
    )
    ins = 9 + len(small)
    return call(
        functools.partial(last_body, len(small)),
        "results",
        outs,
        ins,
        [
            pltpu.VMEM(gh1.shape, BF16),
            pltpu.VMEM(w1_own.shape, BF16),
            pltpu.VMEM(slope.shape, BF16),
            pltpu.VMEM(slope.shape, F32),
            pltpu.VMEM(mid_slots.shape, mid_slots.dtype),
            dma(20),
        ],
        collective=None,
        any_ins=(0, 3, 4, 5),
        any_outs=(0,),
    )(w1_own, grad_pooled, expand, gh1, slope, mid_slots, pair_out, head_last_in, head_first_in, *small)


def per_device(
    views,
    block_input,
    conv_first,
    conv_mid,
    conv_last,
    gain_first,
    shift_first,
    gain_mid,
    shift_mid,
    gain_last,
    shift_last,
    head_first,
    gain_head,
    shift_head,
    head_last,
    image_of,
    partner,
    sub_of,
):
    rows, width = block_input.shape
    quarter = rows // 4
    block = quarter // PIX
    perm, unperm = orders(quarter)
    at_row = np.arange(quarter)
    twice = np.arange(2 * block) % block
    expand = jnp.asarray((at_row[:, None] // PIX == twice[None, :]).astype(BF16))

    def line(vector):
        return vector.reshape(1, -1)

    weights = (conv_first, conv_mid, conv_last, head_first, head_last)
    vectors = [
        line(v)
        for v in (gain_first, shift_first, gain_mid, shift_mid, gain_last, shift_last, gain_head, shift_head)
    ]
    tables = [line(v) for v in (sub_of, image_of, partner)]
    if views <= JOINED_VIEWS:
        kept, back_outs = joined_stage(views, block_input, weights, vectors, tables, perm, unperm, expand)
    else:
        front_outs = front_stage(views, block_input, weights, vectors, tables, perm, unperm)
        kept = dict(zip(FRONT_OUTS, front_outs))
        back_outs = back_stage(views, front_outs, block_input, line(gain_last), perm, unperm, expand)
    slope, w1_own, grad_pooled, loss = (
        kept[name] for name in ("slope_out", "w1_own", "grad_pooled_out", "loss_out")
    )
    (gh1, mid_slots, pair_out, head_last_in, head_first_in,
     grad_shift_mid, grad_gain_mid, grad_shift_first, grad_gain_first) = back_outs
    small = [
        grad_gain_first, grad_shift_first, grad_gain_mid, grad_shift_mid,
        kept["grad_gain_last"], kept["grad_shift_last"], kept["grad_gain_head"], kept["grad_shift_head"], loss,
    ]
    grad_input, grad_mid, grad_first, grad_last, grad_head_last, grad_head_first, *small = last_stage(
        gh1, w1_own, slope, grad_pooled, expand, mid_slots, pair_out, head_last_in, head_first_in, small
    )
    return (
        small[8].reshape(()),
        grad_input.reshape(rows, width),
        grad_first,
        grad_mid,
        grad_last,
        grad_head_first,
        grad_head_last,
        *[vector.reshape(-1) for vector in small[:8]],
    )


def solution(mesh):
    views = mesh.shape["views"]
    return jax.shard_map(
        functools.partial(per_device, views),
        mesh=mesh,
        in_specs=(
            P("views", "chan"),
            P(None, "chan"),
            P(None, "chan"),
            P(None, "chan"),
            P("chan"),
            P("chan"),
            P("chan"),
            P("chan"),
            P("chan"),
            P("chan"),
            P("chan", None),
            P(),
            P(),
            P(),
            P(),
            P(),
            P(),
        ),
        out_specs=(
            P(),
            P("views", "chan"),
            P("views", "chan"),
            P("views", "chan"),
            P("views", "chan"),
            P("chan", "views"),
            P("views", None),
            P("chan"),
            P("chan"),
            P("chan"),
            P("chan"),
            P("chan"),
            P("chan"),
            P(),
            P(),
        ),
        check_vma=False,
    )
```
